32 devices in a mesh: dp: 8 (over z, core), ctx: 4 (over y, x).
Axes of the slice: x: 2, y: 2, z: 4, core: 2. Of those that a mesh axis runs over, the one named last changes fastest.
Arguments:
- queries: bfloat16 [8, 512, 4096], P('dp', 'ctx'), may hold values from -8 to 8
- key_rows: bfloat16 [8, 512, 512], P('dp', 'ctx'), may hold values from -8 to 8
- values: bfloat16 [8, 512, 512], P('dp', 'ctx'), may hold values from -6 to 6
- outputs: bfloat16 [8, 512, 4096], P('dp', 'ctx'), may hold values from -4 to 4
- out_grads: bfloat16 [8, 512, 4096], P('dp', 'ctx'), may hold values from -6 to 6
- depths: int32 [8, 512], P('dp', 'ctx'), may hold values from 0 to 63, as said below
- subtree_end: int32 [8, 512], P('dp', 'ctx'), may hold values from 64 to 512, as said below
- file_lengths: int32 [8, 8], P('dp'), may hold values from 1 to 384, 512 in all within a row
- slopes: float32 [32], replicated, may hold values from 0.02 to 0.5
- ancestor_gain: float32 [32], replicated, may hold values from 0.5 to 3
Outputs:
- query_grads: bfloat16 [8, 512, 4096], P('dp', 'ctx')
- key_grads: bfloat16 [8, 512, 512], P('dp', 'ctx')
- value_grads: bfloat16 [8, 512, 512], P('dp', 'ctx')
- bias_grads: float32 [32, 2], P('ctx')
The draws below stay inside these ranges and needn't reach their ends.
Inputs may be any that keep to these rules, and one draw needn't show every extreme that they name: `depths`: token t has depth t for t < 64; afterwards the depth changes by at most one from a token to the next. `subtree_end`: the first later position of the same sequence whose depth is not above the token's depth, or 512 where there is none.
All inputs are finite; a program needn't handle non-finite values.
Results may differ from the reference program's by a relative error of at most 0.012.
Values may be sent and summed in bfloat16 or wider, within the bound.
No kernel may reach another device: no remote copies, remote signals or barrier semaphores. Data moves between devices by JAX's collectives and lax.ppermute only.
A program may use at most 64 MiB of HBM per device.

```python
import math
import jax
import jax.numpy as jnp
import numpy as np
from jax import lax

QUERY_HEADS = 32
KEY_VALUE_HEADS = 4
HEAD_WIDTH = 128
DEPTHS = 64
FILES = 8
SEQUENCE_LENGTH = 512
SEQUENCE_COUNT = 8


def drawn_pair(key):
    base_key = jax.random.fold_in(key, 101)
    query_key, key_random_seed = jax.random.split(base_key, 2)
    query_draw = jax.random.normal(query_key, (SEQUENCE_COUNT, SEQUENCE_LENGTH, QUERY_HEADS * HEAD_WIDTH), jnp.float32)
    key_sample = jax.random.normal(key_random_seed, (SEQUENCE_COUNT, SEQUENCE_LENGTH, KEY_VALUE_HEADS * HEAD_WIDTH), jnp.float32)
    return (jnp.clip(query_draw, -8.0, 8.0), jnp.clip(key_sample, -8.0, 8.0))


def draw_queries(key, part):
    return drawn_pair(key)[0].astype(jnp.bfloat16)


def draw_key_rows(key, part):
    return drawn_pair(key)[1].astype(jnp.bfloat16)


def tree_shape(key):
    base_key = jax.random.fold_in(key, 202)
    step_draws = jax.random.randint(base_key, (SEQUENCE_COUNT, SEQUENCE_LENGTH), -1, 2)
    positions = jnp.arange(SEQUENCE_LENGTH, dtype=jnp.int32)

    def advance(current, element):
        step_now, position = element
        following = jnp.where(position < DEPTHS, position, jnp.clip(current + step_now, 0, DEPTHS - 1))
        return (following, following)
    _, walked = lax.scan(advance, jnp.zeros((SEQUENCE_COUNT,), jnp.int32), (step_draws.T, positions))
    depth_rows = walked.T.astype(jnp.int32)

    def subtree_ends(depth_row):
        later = (positions[None, :] > positions[:, None]) & (depth_row[None, :] <= depth_row[:, None])
        return jnp.min(jnp.where(later, positions[None, :], SEQUENCE_LENGTH), axis=1).astype(jnp.int32)
    return (depth_rows, lax.map(subtree_ends, depth_rows))


def draw_depths(key, part):
    return tree_shape(key)[0]


def draw_subtree_end(key, part):
    return tree_shape(key)[1]


def block_levels(own_key, shape, pieces, low, high):
    level = 1.0
    for dim, shards_of in pieces:
        steps = jax.random.uniform(jax.random.fold_in(jax.random.fold_in(own_key, 6), dim), (shards_of,), jnp.float32, low / len(pieces), high / len(pieces))
        level = level * jnp.repeat(jnp.exp(steps), shape[dim] // shards_of).reshape((-1,) + (1,) * (len(shape) - 1 - dim))
    return level


def split_up(amount, total, bound, lean):
    loads = [(1 << 20) // math.isqrt(standing ** lean) + 1 for standing in range(2, amount + 1)]
    spare, counts = total - bound - (amount - 1), [1] * (amount - 1)
    while spare > 0:
        candidates = [i for i in range(amount - 1) if counts[i] < bound]
        pool, remaining = sum([loads[i] for i in candidates]), spare
        for i in candidates:
            more = min(bound - counts[i], max(1, remaining * loads[i] // pool), spare)
            counts[i] = counts[i] + more
            spare = spare - more
    return np.array([bound] + counts)


def uneven(rng, count, total, limit, skew):
    if count == 2:
        one = jax.random.randint(rng, (), max(1, total - limit), min(limit, total - 1) + 1)
        return jnp.stack([one, total - one])
    tallies = jnp.asarray(split_up(count, total, limit, skew), jnp.int32)
    pairs = (count - 1) // 2
    giver, taker = tallies[1:1 + 2 * pairs:2], tallies[2:2 + 2 * pairs:2]
    room = jnp.minimum(giver - 1, limit - taker)
    moved = jax.random.randint(jax.random.fold_in(rng, 1), (pairs,), 0, 1 << 20) % (room + 1)
    tallies = tallies.at[1:1 + 2 * pairs:2].set(giver - moved).at[2:2 + 2 * pairs:2].set(taker + moved)
    return tallies[jax.random.permutation(jax.random.fold_in(rng, 2), count)]


def noise(own_key, dims, width, bound, shards=(), kind=jnp.bfloat16):
    level = block_levels(own_key, dims, shards, -0.22, 0.18) if shards else 1.0
    entries = jax.random.normal(own_key, dims, jnp.float32) * width * level
    return jnp.minimum(jnp.maximum(entries, -bound), bound).astype(kind)


def setup_inputs(seed: int = 0) -> dict:
    streams_of = jax.random.split(jax.random.key(seed), 11)
    return {
        "queries": draw_queries(jax.random.fold_in(streams_of[10], 71), 0),
        "key_rows": draw_key_rows(jax.random.fold_in(streams_of[10], 71), 0),
        "values": noise(streams_of[2], (SEQUENCE_COUNT, SEQUENCE_LENGTH, KEY_VALUE_HEADS * HEAD_WIDTH), 1.0, 6.0, ((0, 8), (1, 4))),
        "outputs": noise(streams_of[3], (SEQUENCE_COUNT, SEQUENCE_LENGTH, QUERY_HEADS * HEAD_WIDTH), 0.5, 4.0, ((0, 8), (1, 4))),
        "out_grads": noise(streams_of[4], (SEQUENCE_COUNT, SEQUENCE_LENGTH, QUERY_HEADS * HEAD_WIDTH), 1.0, 6.0, ((0, 8), (1, 4))),
        "depths": draw_depths(jax.random.fold_in(streams_of[10], 71), 0),
        "subtree_end": draw_subtree_end(jax.random.fold_in(streams_of[10], 71), 0),
        "file_lengths": jax.vmap(lambda own: uneven(own, FILES, SEQUENCE_LENGTH, SEQUENCE_LENGTH * 3 // 4, 2))(jax.random.split(streams_of[7], SEQUENCE_COUNT)).reshape((SEQUENCE_COUNT, FILES)).astype(jnp.int32),
        "slopes": jnp.clip(jnp.exp(jax.random.uniform(streams_of[8], (QUERY_HEADS,), jnp.float32, math.log(0.02), math.log(0.5))), 0.02, 0.5),
        "ancestor_gain": jnp.clip(jax.random.uniform(streams_of[9], (QUERY_HEADS,), jnp.float32, 0.5, 3.0), 0.5, 3.0),
    }


masked_score = -1.0e30


def head_terms(query_h, key_h, value_h, output_h, grad_h, slope_h, gain_h, distance, ancestor, allowed):
    factor = HEAD_WIDTH ** -0.5
    scores = jnp.dot(query_h, key_h.T, preferred_element_type=jnp.float32) * factor
    scores = scores - slope_h * distance + gain_h * ancestor
    scores = jnp.where(allowed, scores, masked_score)
    row_top = jnp.max(scores, axis=1, keepdims=True)
    log_total = row_top + jnp.log(jnp.sum(jnp.exp(scores - row_top), axis=1, keepdims=True))
    probs = jnp.exp(scores - log_total)
    probs_b = probs.astype(jnp.bfloat16)
    row_delta = jnp.sum(grad_h.astype(jnp.float32) * output_h.astype(jnp.float32), axis=1, keepdims=True)
    dprobs = jnp.dot(grad_h, value_h.T, preferred_element_type=jnp.float32)
    dscores = probs * (dprobs - row_delta)
    dscores_b = dscores.astype(jnp.bfloat16)
    query_g = (jnp.dot(dscores_b, key_h, preferred_element_type=jnp.float32) * factor).astype(jnp.bfloat16)
    key_gradient = jnp.dot(dscores_b.T, query_h, preferred_element_type=jnp.float32) * factor
    value_gradient = jnp.dot(probs_b.T, grad_h, preferred_element_type=jnp.float32)
    slope_g = -jnp.sum(dscores * distance)
    gain_g = jnp.sum(dscores * ancestor)
    return query_g, key_gradient, value_gradient, jnp.stack([slope_g, gain_g])


def reference(queries, key_rows, values, outputs, out_grads, depths, subtree_end, file_lengths, slopes, ancestor_gain):
    positions = jnp.arange(SEQUENCE_LENGTH, dtype=jnp.int32)
    group_width = QUERY_HEADS // KEY_VALUE_HEADS

    def one_sequence(inputs):
        query_s, key_sequence, value_sequence, output_s, grad_s, depth_s, end_s, length_s = inputs
        bounds = jnp.cumsum(length_s)
        file_id = jnp.sum((positions[:, None] >= bounds[None, :]).astype(jnp.int32), axis=1)
        earlier = positions[None, :] <= positions[:, None]
        allowed = earlier & (file_id[:, None] == file_id[None, :])
        ancestor = (earlier & (positions[:, None] < end_s[None, :])).astype(jnp.float32)
        distance = jnp.abs(depth_s[:, None] - depth_s[None, :]).astype(jnp.float32)
        query_three = query_s.reshape(SEQUENCE_LENGTH, QUERY_HEADS, HEAD_WIDTH)
        output_three = output_s.reshape(SEQUENCE_LENGTH, QUERY_HEADS, HEAD_WIDTH)
        grad_three = grad_s.reshape(SEQUENCE_LENGTH, QUERY_HEADS, HEAD_WIDTH)
        key_triple = key_sequence.reshape(SEQUENCE_LENGTH, KEY_VALUE_HEADS, HEAD_WIDTH)
        value_triple = value_sequence.reshape(SEQUENCE_LENGTH, KEY_VALUE_HEADS, HEAD_WIDTH)

        def one_head(head_index):
            kv_index = head_index // group_width
            query_h = lax.dynamic_index_in_dim(query_three, head_index, 1, False)
            output_h = lax.dynamic_index_in_dim(output_three, head_index, 1, False)
            grad_h = lax.dynamic_index_in_dim(grad_three, head_index, 1, False)
            key_h = lax.dynamic_index_in_dim(key_triple, kv_index, 1, False)
            value_h = lax.dynamic_index_in_dim(value_triple, kv_index, 1, False)
            slope_h = lax.dynamic_index_in_dim(slopes, head_index, 0, False)
            gain_h = lax.dynamic_index_in_dim(ancestor_gain, head_index, 0, False)
            return head_terms(query_h, key_h, value_h, output_h, grad_h, slope_h, gain_h, distance, ancestor, allowed)

        query_g, key_gradient, value_gradient, bias_g = lax.map(one_head, jnp.arange(QUERY_HEADS, dtype=jnp.int32))
        query_out = jnp.transpose(query_g, (1, 0, 2)).reshape(SEQUENCE_LENGTH, QUERY_HEADS * HEAD_WIDTH)
        key_total_sum = jnp.sum(key_gradient.reshape(KEY_VALUE_HEADS, group_width, SEQUENCE_LENGTH, HEAD_WIDTH), axis=1)
        value_total_sum = jnp.sum(value_gradient.reshape(KEY_VALUE_HEADS, group_width, SEQUENCE_LENGTH, HEAD_WIDTH), axis=1)
        key_result = jnp.transpose(key_total_sum, (1, 0, 2)).reshape(SEQUENCE_LENGTH, KEY_VALUE_HEADS * HEAD_WIDTH).astype(jnp.bfloat16)
        value_result = jnp.transpose(value_total_sum, (1, 0, 2)).reshape(SEQUENCE_LENGTH, KEY_VALUE_HEADS * HEAD_WIDTH).astype(jnp.bfloat16)
        return query_out, key_result, value_result, bias_g

    results = lax.map(one_sequence, (queries, key_rows, values, outputs, out_grads, depths, subtree_end, file_lengths))
    return results[0], results[1], results[2], jnp.sum(results[3], axis=0)
```

```python
import functools

import jax
import jax.numpy as jnp
from jax import lax
from jax.experimental import pallas as pl
from jax.experimental.pallas import tpu as pltpu
from jax.sharding import PartitionSpec as P

WIDTH = 128
LOG2E = 1.4426950408889634
MASKED = -1e30
META_ROWS = 16
END_UNIT = 64

VMEM_LIMIT = 56 * 1024 * 1024


def dot_nt(a, b):
    return lax.dot_general(a, b, (((1,), (1,)), ((), ())), preferred_element_type=jnp.float32)


def dot_nn(a, b):
    return lax.dot_general(a, b, (((1,), (0,)), ((), ())), preferred_element_type=jnp.float32)


def pack_kernel(key_ref, value_ref, depth_ref, end_ref, message_ref):
    tokens, columns = key_ref.shape
    message_ref[0:tokens, 0:columns] = key_ref[...]
    message_ref[0:tokens, columns : 2 * columns] = value_ref[...]
    depth = depth_ref[...]
    end = end_ref[...]
    end_high = end // END_UNIT
    end_low = end - end_high * END_UNIT
    row = lax.broadcasted_iota(jnp.int32, (META_ROWS, tokens), 0)
    meta = jnp.where(row == 0, depth, jnp.where(row == 1, end_high, end_low))
    meta = meta.astype(jnp.float32).astype(jnp.bfloat16)
    message_ref[tokens : tokens + META_ROWS, 0:tokens] = meta
    message_ref[tokens : tokens + META_ROWS, tokens:] = jnp.zeros(
        (META_ROWS, 2 * columns - tokens), jnp.bfloat16
    )


def as_column(row):
    size = row.shape[1]
    return jnp.transpose(jnp.broadcast_to(row, (size, size)))


def main_kernel(
    blocks,
    heads_per_group,
    unroll_pairs,
    lengths_ref,
    slope_ref,
    gain_ref,
    depth_ref,
    end_ref,
    query_ref,
    output_ref,
    grad_ref,
    key_ref,
    value_ref,
    *refs,
):
    tokens = query_ref.shape[0]
    remote_key = refs[0 : blocks - 1]
    remote_value = refs[blocks - 1 : 2 * (blocks - 1)]
    remote_meta = refs[2 * (blocks - 1) : 3 * (blocks - 1)]
    rest = refs[3 * (blocks - 1) :]
    query_grad_ref = rest[0]
    key_grad_refs = rest[1 : 1 + blocks]
    value_grad_refs = rest[1 + blocks : 1 + 2 * blocks]
    bias_ref = rest[1 + 2 * blocks]
    distance_ref, ancestor_ref, slope_rows, gain_rows, key_acc, value_acc = rest[2 + 2 * blocks :]
    group = pl.program_id(0)
    factor = WIDTH**-0.5

    @pl.when(group == 0)
    def _():
        here = lax.axis_index("ctx")
        query_pos = here * tokens + lax.broadcasted_iota(jnp.int32, (tokens, tokens), 1)
        start = jnp.zeros((tokens, tokens), jnp.int32)
        bound = jnp.int32(0)
        for index in range(lengths_ref.shape[1]):
            bound = bound + lengths_ref[0, index]
            start = jnp.where(query_pos >= bound, bound, start)
        query_depth = jnp.broadcast_to(depth_ref[...].astype(jnp.float32), (tokens, tokens))
        for shift in range(blocks):
            key_pos = (here - shift) * tokens + lax.broadcasted_iota(
                jnp.int32, (tokens, tokens), 0
            )
            if shift == 0:
                key_depth = as_column(depth_ref[...].astype(jnp.float32))
                key_end = as_column(end_ref[...].astype(jnp.float32))
            else:
                meta = remote_meta[shift - 1][...].astype(jnp.float32)
                key_depth = as_column(meta[0:1])
                key_end = as_column(meta[1:2] * END_UNIT + meta[2:3])
            inside = query_pos.astype(jnp.float32) < key_end
            allowed = (key_pos <= query_pos) & (key_pos >= start) & (key_pos >= 0)
            rows = slice(shift * tokens, (shift + 1) * tokens)
            distance_ref[rows, :] = jnp.abs(query_depth - key_depth)
            ancestor_ref[rows, :] = jnp.where(allowed, jnp.where(inside, 1.0, 0.0), MASKED)

    keys = jnp.concatenate([key_ref[...]] + [r[...] for r in remote_key], axis=0)
    values = jnp.concatenate([value_ref[...]] + [r[...] for r in remote_value], axis=0)
    value_ext = jnp.concatenate([values, jnp.full(values.shape, -1.0, jnp.bfloat16)], axis=1)
    keys_across = jnp.transpose(keys)

    def columns_of(ref, head):
        if isinstance(head, int):
            return ref[:, head * WIDTH : (head + 1) * WIDTH]
        return ref[:, pl.ds(pl.multiple_of(head * WIDTH, WIDTH), WIDTH)]

    def pair_of_heads(pair, first):
        heads = (2 * pair, 2 * pair + 1)
        query_pair = jnp.concatenate([columns_of(query_ref, h) for h in heads], axis=0)
        grad_pair = jnp.concatenate([columns_of(grad_ref, h) for h in heads], axis=0)
        output_pair = jnp.concatenate([columns_of(output_ref, h) for h in heads], axis=0)
        grad_ext = jnp.concatenate([grad_pair, grad_pair * output_pair], axis=1)
        raw = dot_nt(keys, query_pair)
        centred = dot_nt(value_ext, grad_ext)
        probs_parts, dscore_parts = [], []
        for half in range(2):
            head = group * heads_per_group + heads[half]
            gain = gain_ref[head] * LOG2E
            slope = slope_ref[head] * LOG2E
            lanes = slice(half * tokens, (half + 1) * tokens)
            distance = distance_ref[...]
            ancestor = ancestor_ref[...]
            score = raw[:, lanes] * (factor * LOG2E) + gain * ancestor - slope * distance
            top = jnp.max(score, axis=0, keepdims=True)
            weight = jnp.exp2(score - top)
            total = jnp.sum(weight, axis=0, keepdims=True)
            probs = weight * (1.0 / total)
            dscore = probs * centred[:, lanes]
            slope_rows[pl.ds(head, 1), :] = -jnp.sum(dscore * distance, axis=0, keepdims=True)
            gain_rows[pl.ds(head, 1), :] = jnp.sum(dscore * ancestor, axis=0, keepdims=True)
            probs_parts.append(probs.astype(jnp.bfloat16))
            dscore_parts.append(dscore.astype(jnp.bfloat16))
        probs_b = jnp.concatenate(probs_parts, axis=1)
        dscore_b = jnp.concatenate(dscore_parts, axis=1)
        key_part = dot_nn(dscore_b, query_pair)
        value_part = dot_nn(probs_b, grad_pair)
        if first:
            key_acc[...] = key_part
            value_acc[...] = value_part
        else:
            key_acc[...] += key_part
            value_acc[...] += value_part
        query_across = dot_nn(keys_across, dscore_b) * factor
        query_pair_grad = jnp.transpose(query_across).astype(jnp.bfloat16)
        for half in range(2):
            rows = query_pair_grad[half * tokens : (half + 1) * tokens]
            if isinstance(pair, int):
                h = heads[half]
                query_grad_ref[:, h * WIDTH : (h + 1) * WIDTH] = rows
            else:
                at = pl.multiple_of(heads[half] * WIDTH, WIDTH)
                query_grad_ref[:, pl.ds(at, WIDTH)] = rows

    pairs = heads_per_group // 2
    if unroll_pairs:
        for pair in range(pairs):
            pair_of_heads(pair, pair == 0)
    else:
        key_acc[...] = jnp.zeros_like(key_acc)
        value_acc[...] = jnp.zeros_like(value_acc)

        @pl.loop(0, pairs)
        def _(pair):
            pair_of_heads(pair, False)

    for shift in range(blocks):
        rows = slice(shift * tokens, (shift + 1) * tokens)
        key_grad_refs[shift][...] = (key_acc[rows, :] * factor).astype(jnp.bfloat16)
        value_grad_refs[shift][...] = value_acc[rows, :].astype(jnp.bfloat16)

    @pl.when(group == pl.num_programs(0) - 1)
    def _():
        slope_sum = jnp.sum(slope_rows[...], axis=1, keepdims=True)
        gain_sum = jnp.sum(gain_rows[...], axis=1, keepdims=True)
        lane = lax.broadcasted_iota(jnp.int32, slope_rows.shape, 1)
        both = jnp.where(lane == 0, slope_sum, jnp.where(lane == 1, gain_sum, 0.0))
        local = bias_ref.shape[2]
        for part in range(bias_ref.shape[1]):
            rows = both[part * local : (part + 1) * local]
            bias_ref[:, part] = jnp.broadcast_to(rows[None], (bias_ref.shape[0],) + rows.shape)


def final_kernel(blocks, *refs):
    key_parts = refs[0:blocks]
    value_parts = refs[blocks : 2 * blocks]
    bias_parts = refs[2 * blocks]
    key_out, value_out, bias_out = refs[2 * blocks + 1 :]
    key_sum = key_parts[0][...].astype(jnp.float32)
    value_sum = value_parts[0][...].astype(jnp.float32)
    for shift in range(1, blocks):
        key_sum = key_sum + key_parts[shift][...].astype(jnp.float32)
        value_sum = value_sum + value_parts[shift][...].astype(jnp.float32)
    key_out[...] = key_sum.astype(jnp.bfloat16)
    value_out[...] = value_sum.astype(jnp.bfloat16)
    bias_out[...] = jnp.sum(bias_parts[...], axis=0)[:, 0:2]


def body(
    queries,
    key_rows,
    values,
    outputs,
    out_grads,
    depths,
    subtree_end,
    file_lengths,
    slopes,
    ancestor_gain,
):
    blocks = lax.axis_size("ctx")
    replicas = lax.axis_size("dp")
    tokens, width_all = queries.shape[1:]
    kv_width = key_rows.shape[2]
    heads_all = width_all // WIDTH
    kv_heads = kv_width // WIDTH
    heads_per_group = heads_all // kv_heads
    group_columns = heads_per_group * WIDTH
    local_heads = heads_all // blocks
    keys_seen = blocks * tokens
    bf16, f32 = jnp.bfloat16, jnp.float32
    vmem = pl.BlockSpec(memory_space=pltpu.VMEM)
    smem = pl.BlockSpec(memory_space=pltpu.SMEM)
    params = pltpu.CompilerParams(vmem_limit_bytes=VMEM_LIMIT)

    message = pl.pallas_call(
        pack_kernel,
        out_shape=jax.ShapeDtypeStruct((tokens + META_ROWS, 2 * kv_width), bf16),
        in_specs=[vmem] * 4,
        out_specs=vmem,
        compiler_params=params,
        name="pack",
    )(key_rows[0], values[0], depths, subtree_end)
    arrived = [
        lax.ppermute(message, "ctx", [(i, i + shift) for i in range(blocks - shift)])
        for shift in range(1, blocks)
    ]

    wide = pl.BlockSpec((tokens, group_columns), lambda g: (0, g))
    key_spec = pl.BlockSpec((tokens, WIDTH), lambda g: (0, g))
    value_spec = pl.BlockSpec((tokens, WIDTH), lambda g: (0, kv_heads + g))
    meta_spec = pl.BlockSpec((META_ROWS, tokens), lambda g: (tokens // META_ROWS, 0))
    row_spec = pl.BlockSpec((1, tokens), lambda g: (0, 0))
    bias_shape = (replicas, blocks, local_heads, WIDTH)
    bias_spec = pl.BlockSpec(bias_shape, lambda g: (0, 0, 0, 0))
    matmul_flops = 2 * tokens * keys_seen * WIDTH * heads_all
    results = pl.pallas_call(
        functools.partial(main_kernel, blocks, heads_per_group, blocks <= 4),
        grid=(kv_heads,),
        out_shape=[jax.ShapeDtypeStruct((tokens, width_all), bf16)]
        + [jax.ShapeDtypeStruct((tokens, kv_width), bf16)] * (2 * blocks)
        + [jax.ShapeDtypeStruct(bias_shape, f32)],
        in_specs=[smem, smem, smem, row_spec, row_spec, wide, wide, wide, key_spec, key_spec]
        + [key_spec] * (blocks - 1)
        + [value_spec] * (blocks - 1)
        + [meta_spec] * (blocks - 1),
        out_specs=[wide] + [key_spec] * (2 * blocks) + [bias_spec],
        scratch_shapes=[
            pltpu.VMEM((keys_seen, tokens), f32),
            pltpu.VMEM((keys_seen, tokens), f32),
            pltpu.VMEM((heads_all, tokens), f32),
            pltpu.VMEM((heads_all, tokens), f32),
            pltpu.VMEM((keys_seen, WIDTH), f32),
            pltpu.VMEM((keys_seen, WIDTH), f32),
        ],
        compiler_params=params,
        cost_estimate=pl.CostEstimate(
            flops=5 * matmul_flops,
            bytes_accessed=10 * tokens * width_all,
            transcendentals=tokens * keys_seen * heads_all,
        ),
        name="attend",
    )(
        file_lengths,
        slopes,
        ancestor_gain,
        depths,
        subtree_end,
        queries[0],
        outputs[0],
        out_grads[0],
        key_rows[0],
        values[0],
        *arrived,
        *arrived,
        *arrived,
    )
    query_grads = results[0]
    key_parts = list(results[1 : 1 + blocks])
    value_parts = list(results[1 + blocks : 1 + 2 * blocks])
    bias_parts = results[1 + 2 * blocks].reshape(replicas * blocks, local_heads, WIDTH)
    for shift in range(1, blocks):
        back = [(i + shift, i) for i in range(blocks - shift)]
        key_parts[shift] = lax.ppermute(key_parts[shift], "ctx", back)
        value_parts[shift] = lax.ppermute(value_parts[shift], "ctx", back)
    bias_parts = lax.all_to_all(bias_parts, ("dp", "ctx"), split_axis=0, concat_axis=0, tiled=True)

    key_grads, value_grads, bias_grads = pl.pallas_call(
        functools.partial(final_kernel, blocks),
        out_shape=[
            jax.ShapeDtypeStruct((tokens, kv_width), bf16),
            jax.ShapeDtypeStruct((tokens, kv_width), bf16),
            jax.ShapeDtypeStruct((local_heads, 2), f32),
        ],
        in_specs=[vmem] * (2 * blocks + 1),
        out_specs=[vmem] * 3,
        compiler_params=params,
        name="combine",
    )(*key_parts, *value_parts, bias_parts)
    return (query_grads[None], key_grads[None], value_grads[None], bias_grads)


def solution(mesh):
    in_specs = (
        P("dp", "ctx", None),
        P("dp", "ctx", None),
        P("dp", "ctx", None),
        P("dp", "ctx", None),
        P("dp", "ctx", None),
        P("dp", "ctx"),
        P("dp", "ctx"),
        P("dp", None),
        P(),
        P(),
    )
    out_specs = (P("dp", "ctx", None), P("dp", "ctx", None), P("dp", "ctx", None), P("ctx", None))
    return jax.shard_map(body, mesh=mesh, in_specs=in_specs, out_specs=out_specs, check_vma=False)
```

```python
import functools

import jax
import jax.numpy as jnp
from jax import lax
from jax.experimental import pallas as pl
from jax.experimental.pallas import tpu as pltpu
from jax.sharding import PartitionSpec as P

WIDTH = 128
LOG2E = 1.4426950408889634
MASKED = -1e30
META_ROWS = 16
END_UNIT = 64
CHUNKS = 2

VMEM_LIMIT = 32 * 1024 * 1024


def dot_nt(a, b):
    return lax.dot_general(a, b, (((1,), (1,)), ((), ())), preferred_element_type=jnp.float32)


def dot_nn(a, b):
    return lax.dot_general(a, b, (((1,), (0,)), ((), ())), preferred_element_type=jnp.float32)


def pack_kernel(key_ref, value_ref, depth_ref, end_ref, *message_refs):
    tokens = key_ref.shape[0]
    groups = key_ref.shape[1] // WIDTH // len(message_refs)
    for chunk, message_ref in enumerate(message_refs):
        for group in range(groups):
            source = slice((chunk * groups + group) * WIDTH, (chunk * groups + group + 1) * WIDTH)
            at = 2 * group * WIDTH
            message_ref[0:tokens, at : at + WIDTH] = key_ref[:, source]
            message_ref[0:tokens, at + WIDTH : at + 2 * WIDTH] = value_ref[:, source]
    depth = depth_ref[...]
    end = end_ref[...]
    end_high = end // END_UNIT
    end_low = end - end_high * END_UNIT
    row = lax.broadcasted_iota(jnp.int32, (META_ROWS, tokens), 0)
    meta = jnp.where(row == 0, depth, jnp.where(row == 1, end_high, end_low))
    meta = meta.astype(jnp.float32).astype(jnp.bfloat16)
    below = slice(tokens, tokens + META_ROWS)
    message_refs[0][below, 0:tokens] = meta
    message_refs[0][below, tokens:] = jnp.zeros(
        (META_ROWS, 2 * groups * WIDTH - tokens), jnp.bfloat16
    )


def as_column(row):
    size = row.shape[1]
    return jnp.transpose(jnp.broadcast_to(row, (size, size)))


def fold_rows(block):
    return jnp.sum(block.reshape(block.shape[0] // 8, 8, block.shape[1]), axis=0)


def main_kernel(
    blocks,
    heads_per_group,
    unroll_pairs,
    first_group,
    lengths_ref,
    slope_ref,
    gain_ref,
    depth_ref,
    end_ref,
    query_ref,
    output_ref,
    grad_ref,
    key_ref,
    value_ref,
    *refs,
):
    tokens = query_ref.shape[0]
    remote = refs[0 : blocks - 1]
    remote_meta = refs[blocks - 1 : 2 * (blocks - 1)]
    rest = refs[2 * (blocks - 1) :]
    if first_group:
        bias_before = rest[0]
        rest = rest[2 + blocks :]
    query_grad_ref = rest[0]
    part_refs = rest[1 : 1 + blocks]
    bias_ref = rest[1 + blocks]
    (
        distance_ref,
        ancestor_ref,
        slope_rows,
        gain_rows,
        key_acc,
        value_acc,
        weight_ref,
        probs_ref,
        dscore_ref,
    ) = rest[2 + blocks :]
    group = pl.program_id(0)
    factor = WIDTH**-0.5

    @pl.when(group == 0)
    def _():
        here = lax.axis_index("ctx")
        query_pos = here * tokens + lax.broadcasted_iota(jnp.int32, (tokens, tokens), 1)
        start = jnp.zeros((tokens, tokens), jnp.int32)
        bound = jnp.int32(0)
        for index in range(lengths_ref.shape[1]):
            bound = bound + lengths_ref[0, index]
            start = jnp.where(query_pos >= bound, bound, start)
        query_depth = jnp.broadcast_to(depth_ref[...].astype(jnp.float32), (tokens, tokens))
        for shift in range(blocks):
            key_pos = (here - shift) * tokens + lax.broadcasted_iota(
                jnp.int32, (tokens, tokens), 0
            )
            if shift == 0:
                key_depth = as_column(depth_ref[...].astype(jnp.float32))
                key_end = as_column(end_ref[...].astype(jnp.float32))
            else:
                meta = remote_meta[shift - 1][...].astype(jnp.float32)
                key_depth = as_column(meta[0:1])
                key_end = as_column(meta[1:2] * END_UNIT + meta[2:3])
            inside = query_pos.astype(jnp.float32) < key_end
            allowed = (key_pos <= query_pos) & (key_pos >= start) & (key_pos >= 0)
            rows = slice(shift * tokens, (shift + 1) * tokens)
            distance_ref[rows, :] = jnp.abs(query_depth - key_depth)
            ancestor_ref[rows, :] = jnp.where(allowed, jnp.where(inside, 1.0, 0.0), MASKED)

    keys = jnp.concatenate([key_ref[...]] + [r[:, 0:WIDTH] for r in remote], axis=0)
    values = jnp.concatenate([value_ref[...]] + [r[:, WIDTH:] for r in remote], axis=0)
    value_ext = jnp.concatenate([values, jnp.full(values.shape, -1.0, jnp.bfloat16)], axis=1)
    keys_across = jnp.transpose(keys)
    block_rows = [slice(shift * tokens, (shift + 1) * tokens) for shift in range(blocks)]

    def head_columns(ref, pair):
        parts = []
        for half in range(2):
            at = (2 * pair + half) * WIDTH
            if not isinstance(pair, int):
                at = pl.multiple_of(at, WIDTH)
            parts.append(ref[:, pl.ds(at, WIDTH)])
        return jnp.concatenate(parts, axis=0)

    def scores(pair, slot):
        query_pair = head_columns(query_ref, pair)
        grad_pair = head_columns(grad_ref, pair)
        output_pair = head_columns(output_ref, pair)
        grad_ext = jnp.concatenate([grad_pair, grad_pair * output_pair], axis=1)
        raw = dot_nt(keys, query_pair)
        scales = []
        for half in range(2):
            head = (first_group + group) * heads_per_group + 2 * pair + half
            gain = gain_ref[head] * LOG2E
            slope = slope_ref[head] * LOG2E
            lanes = slice(half * tokens, (half + 1) * tokens)
            tops, totals = [], []
            for rows in block_rows:
                score = raw[rows, lanes] * (factor * LOG2E) + (
                    gain * ancestor_ref[rows, :] - slope * distance_ref[rows, :]
                )
                top = jnp.max(score, axis=0, keepdims=True)
                weight = jnp.exp2(score - top)
                weight_ref[slot, rows, lanes] = weight
                tops.append(top)
                totals.append(jnp.sum(weight, axis=0, keepdims=True))
            top = functools.reduce(jnp.maximum, tops)
            shrink = [jnp.exp2(t - top) for t in tops]
            total = sum(a * b for a, b in zip(totals, shrink))
            inverse = 1.0 / total
            scales.append([s * inverse for s in shrink])
        centred = dot_nt(value_ext, grad_ext)
        for half in range(2):
            head = (first_group + group) * heads_per_group + 2 * pair + half
            lanes = slice(half * tokens, (half + 1) * tokens)
            slope_sum, gain_sum = 0.0, 0.0
            for rows, scale in zip(block_rows, scales[half]):
                probs = weight_ref[slot, rows, lanes] * scale
                dscore = probs * centred[rows, lanes]
                probs_ref[slot, rows, lanes] = probs.astype(jnp.bfloat16)
                dscore_ref[slot, rows, lanes] = dscore.astype(jnp.bfloat16)
                slope_sum = slope_sum + fold_rows(dscore * distance_ref[rows, :])
                gain_sum = gain_sum + fold_rows(dscore * ancestor_ref[rows, :])
            at = pl.ds(group * heads_per_group + 2 * pair + half, 1)
            slope_rows[at, :] = -jnp.sum(slope_sum, axis=0, keepdims=True)
            gain_rows[at, :] = jnp.sum(gain_sum, axis=0, keepdims=True)

    def gradients(pair, slot, first):
        query_pair = head_columns(query_ref, pair)
        grad_pair = head_columns(grad_ref, pair)
        dscore_b = dscore_ref[slot]
        key_part = dot_nn(dscore_b, query_pair)
        value_part = dot_nn(probs_ref[slot], grad_pair)
        if first:
            key_acc[...] = key_part
            value_acc[...] = value_part
        else:
            key_acc[...] += key_part
            value_acc[...] += value_part
        query_across = dot_nn(keys_across, dscore_b) * factor
        query_pair_grad = jnp.transpose(query_across).astype(jnp.bfloat16)
        for half in range(2):
            at = (2 * pair + half) * WIDTH
            if not isinstance(pair, int):
                at = pl.multiple_of(at, WIDTH)
            query_grad_ref[:, pl.ds(at, WIDTH)] = query_pair_grad[
                half * tokens : (half + 1) * tokens
            ]

    pairs = heads_per_group // 2
    if unroll_pairs:
        scores(0, 0)
        for pair in range(1, pairs):
            scores(pair, pair % 2)
            gradients(pair - 1, (pair - 1) % 2, pair == 1)
        gradients(pairs - 1, (pairs - 1) % 2, pairs == 1)
    else:
        key_acc[...] = jnp.zeros_like(key_acc)
        value_acc[...] = jnp.zeros_like(value_acc)

        @pl.loop(0, pairs)
        def _(pair):
            scores(pair, 0)
            gradients(pair, 0, False)

    for shift in range(blocks):
        rows = block_rows[shift]
        part_refs[shift][:, 0:WIDTH] = (key_acc[rows, :] * factor).astype(jnp.bfloat16)
        part_refs[shift][:, WIDTH:] = value_acc[rows, :].astype(jnp.bfloat16)

    @pl.when(group == pl.num_programs(0) - 1)
    def _():
        slope_sum = jnp.sum(slope_rows[...], axis=1, keepdims=True)
        gain_sum = jnp.sum(gain_rows[...], axis=1, keepdims=True)
        shape = slope_rows.shape
        lane = lax.broadcasted_iota(jnp.int32, shape, 1)
        row = lax.broadcasted_iota(jnp.int32, shape, 0)
        local = bias_ref.shape[3]
        for part in range(bias_ref.shape[1]):
            mine = lane == row - part * local + first_group * heads_per_group
            mine = mine & (lane < local) & (lane >= 0)
            for kind, column in ((0, slope_sum), (1, gain_sum)):
                line = jnp.sum(jnp.where(mine, column, 0.0), axis=0, keepdims=True)
                line = line[None, :, 0:local]
                if first_group:
                    line = line + bias_before[0:1, part, kind : kind + 1, :]
                bias_ref[:, part, kind : kind + 1, :] = jnp.broadcast_to(
                    line, (bias_ref.shape[0], 1, local)
                )


def final_kernel(blocks, *refs):
    parts = refs[0:blocks]
    bias_parts, key_out, value_out, bias_out = refs[blocks:]
    for group in range(key_out.shape[1] // WIDTH):
        to = slice(group * WIDTH, (group + 1) * WIDTH)
        for kind, out in enumerate((key_out, value_out)):
            at = (2 * group + kind) * WIDTH
            total = parts[0][:, at : at + WIDTH].astype(jnp.float32)
            for shift in range(1, blocks):
                total = total + parts[shift][:, at : at + WIDTH].astype(jnp.float32)
            out[:, to] = total.astype(jnp.bfloat16)
    bias_out[...] = jnp.sum(bias_parts[...], axis=0)


def body(
    queries,
    key_rows,
    values,
    outputs,
    out_grads,
    depths,
    subtree_end,
    file_lengths,
    slopes,
    ancestor_gain,
):
    blocks = lax.axis_size("ctx")
    replicas = lax.axis_size("dp")
    tokens, width_all = queries.shape[1:]
    kv_width = key_rows.shape[2]
    heads_all = width_all // WIDTH
    kv_heads = kv_width // WIDTH
    heads_per_group = heads_all // kv_heads
    group_columns = heads_per_group * WIDTH
    local_heads = heads_all // blocks
    keys_seen = blocks * tokens
    chunk_groups = kv_heads // CHUNKS
    bf16, f32 = jnp.bfloat16, jnp.float32
    vmem = pl.BlockSpec(memory_space=pltpu.VMEM)
    smem = pl.BlockSpec(memory_space=pltpu.SMEM)
    anywhere = pl.BlockSpec(memory_space=pl.ANY)
    params = pltpu.CompilerParams(vmem_limit_bytes=VMEM_LIMIT)

    messages = pl.pallas_call(
        pack_kernel,
        out_shape=[
            jax.ShapeDtypeStruct(
                (tokens + (META_ROWS if chunk == 0 else 0), 2 * chunk_groups * WIDTH), bf16
            )
            for chunk in range(CHUNKS)
        ],
        in_specs=[vmem] * 4,
        out_specs=[vmem] * CHUNKS,
        compiler_params=params,
        name="pack",
    )(key_rows[0], values[0], depths, subtree_end)
    arrived = [
        [
            lax.ppermute(message, "ctx", [(i, i + shift) for i in range(blocks - shift)])
            for shift in range(1, blocks)
        ]
        for message in messages
    ]

    bias_shape = (replicas, blocks, 2, local_heads)
    matmul_flops = 2 * tokens * keys_seen * WIDTH * heads_all
    out_shape = (
        [jax.ShapeDtypeStruct((tokens, width_all), bf16)]
        + [jax.ShapeDtypeStruct((tokens, 2 * kv_width), bf16)] * blocks
        + [jax.ShapeDtypeStruct(bias_shape, f32)]
    )
    results = None
    for chunk in range(CHUNKS):
        first = chunk * chunk_groups
        wide = pl.BlockSpec((tokens, group_columns), lambda g, first=first: (0, first + g))
        own_spec = pl.BlockSpec((tokens, WIDTH), lambda g, first=first: (0, first + g))
        remote_spec = pl.BlockSpec((tokens, 2 * WIDTH), lambda g: (0, g))
        part_spec = pl.BlockSpec((tokens, 2 * WIDTH), lambda g, first=first: (0, first + g))
        meta_spec = pl.BlockSpec((META_ROWS, tokens), lambda g: (tokens // META_ROWS, 0))
        row_spec = pl.BlockSpec((1, tokens), lambda g: (0, 0))
        bias_spec = pl.BlockSpec(bias_shape, lambda g: (0, 0, 0, 0))
        operands = [
            file_lengths,
            slopes,
            ancestor_gain,
            depths,
            subtree_end,
            queries[0],
            outputs[0],
            out_grads[0],
            key_rows[0],
            values[0],
            *arrived[chunk],
            *arrived[0],
        ]
        specs = [smem, smem, smem, row_spec, row_spec, wide, wide, wide, own_spec, own_spec]
        specs = specs + [remote_spec] * (blocks - 1) + [meta_spec] * (blocks - 1)
        aliases = {}
        if chunk:
            operands = operands + [results[1 + blocks]] + list(results[0 : 1 + blocks])
            specs = specs + [bias_spec] + [anywhere] * (1 + blocks)
            aliases = {len(operands) - 1 - blocks + i: i for i in range(1 + blocks)}
        results = pl.pallas_call(
            functools.partial(main_kernel, blocks, heads_per_group, blocks <= 4, first),
            grid=(chunk_groups,),
            out_shape=out_shape,
            in_specs=specs,
            out_specs=[wide] + [part_spec] * blocks + [bias_spec],
            scratch_shapes=[
                pltpu.VMEM((keys_seen, tokens), f32),
                pltpu.VMEM((keys_seen, tokens), f32),
                pltpu.VMEM((chunk_groups * heads_per_group, tokens), f32),
                pltpu.VMEM((chunk_groups * heads_per_group, tokens), f32),
                pltpu.VMEM((keys_seen, WIDTH), f32),
                pltpu.VMEM((keys_seen, WIDTH), f32),
                pltpu.VMEM((2, keys_seen, 2 * tokens), f32),
                pltpu.VMEM((2, keys_seen, 2 * tokens), bf16),
                pltpu.VMEM((2, keys_seen, 2 * tokens), bf16),
            ],
            input_output_aliases=aliases,
            compiler_params=params,
            cost_estimate=pl.CostEstimate(
                flops=5 * matmul_flops // CHUNKS,
                bytes_accessed=10 * tokens * width_all // CHUNKS,
                transcendentals=tokens * keys_seen * heads_all // CHUNKS,
            ),
            name=f"attend_{chunk}",
        )(*operands)
    query_grads = results[0]
    parts = list(results[1 : 1 + blocks])
    bias_parts = results[1 + blocks].reshape(replicas * blocks, 2, local_heads)
    for shift in range(1, blocks):
        back = [(i + shift, i) for i in range(blocks - shift)]
        parts[shift] = lax.ppermute(parts[shift], "ctx", back)
    bias_parts = lax.all_to_all(bias_parts, ("dp", "ctx"), split_axis=0, concat_axis=0, tiled=True)

    key_grads, value_grads, bias_grads = pl.pallas_call(
        functools.partial(final_kernel, blocks),
        out_shape=[
            jax.ShapeDtypeStruct((tokens, kv_width), bf16),
            jax.ShapeDtypeStruct((tokens, kv_width), bf16),
            jax.ShapeDtypeStruct((2, local_heads), f32),
        ],
        in_specs=[vmem] * (blocks + 1),
        out_specs=[vmem] * 3,
        compiler_params=params,
        name="combine",
    )(*parts, bias_parts)
    return (query_grads[None], key_grads[None], value_grads[None], bias_grads.T)


def solution(mesh):
    in_specs = (
        P("dp", "ctx", None),
        P("dp", "ctx", None),
        P("dp", "ctx", None),
        P("dp", "ctx", None),
        P("dp", "ctx", None),
        P("dp", "ctx"),
        P("dp", "ctx"),
        P("dp", None),
        P(),
        P(),
    )
    out_specs = (P("dp", "ctx", None), P("dp", "ctx", None), P("dp", "ctx", None), P("ctx", None))
    return jax.shard_map(body, mesh=mesh, in_specs=in_specs, out_specs=out_specs, check_vma=False)
```

```python
import functools

import jax
import jax.numpy as jnp
from jax import lax
from jax.experimental import pallas as pl
from jax.experimental.pallas import tpu as pltpu
from jax.sharding import PartitionSpec as P

WIDTH = 128
LOG2E = 1.4426950408889634
MASKED = -1e30
META_ROWS = 16
END_UNIT = 64
CHUNKS = 2
QUAD = 4

VMEM_LIMIT = 32 * 1024 * 1024


def dot_nt(a, b):
    return lax.dot_general(a, b, (((1,), (1,)), ((), ())), preferred_element_type=jnp.float32)


def dot_nn(a, b):
    return lax.dot_general(a, b, (((1,), (0,)), ((), ())), preferred_element_type=jnp.float32)


def pack_kernel(key_ref, value_ref, depth_ref, end_ref, *message_refs):
    tokens = key_ref.shape[0]
    groups = key_ref.shape[1] // WIDTH // len(message_refs)
    for chunk, message_ref in enumerate(message_refs):
        for group in range(groups):
            source = slice((chunk * groups + group) * WIDTH, (chunk * groups + group + 1) * WIDTH)
            at = 2 * group * WIDTH
            message_ref[0:tokens, at : at + WIDTH] = key_ref[:, source]
            message_ref[0:tokens, at + WIDTH : at + 2 * WIDTH] = value_ref[:, source]
    depth = depth_ref[...]
    end = end_ref[...]
    end_high = end // END_UNIT
    end_low = end - end_high * END_UNIT
    row = lax.broadcasted_iota(jnp.int32, (META_ROWS, tokens), 0)
    meta = jnp.where(row == 0, depth, jnp.where(row == 1, end_high, end_low))
    meta = meta.astype(jnp.float32).astype(jnp.bfloat16)
    below = slice(tokens, tokens + META_ROWS)
    message_refs[0][below, 0:tokens] = meta
    message_refs[0][below, tokens:] = jnp.zeros(
        (META_ROWS, 2 * groups * WIDTH - tokens), jnp.bfloat16
    )


def as_column(row):
    size = row.shape[1]
    return jnp.transpose(jnp.broadcast_to(row, (size, size)))


def dot_tn(a, b):
    return lax.dot_general(a, b, (((0,), (0,)), ((), ())), preferred_element_type=jnp.float32)


def fold_rows(block):
    return jnp.sum(block.reshape(block.shape[0] // 8, 8, block.shape[1]), axis=0)


def main_kernel(
    blocks,
    heads_per_group,
    groups,
    first_group,
    unroll,
    lengths_ref,
    slope_ref,
    gain_ref,
    depth_ref,
    end_ref,
    query_hbm,
    output_hbm,
    grad_hbm,
    key_hbm,
    value_hbm,
    *refs,
):
    tokens = query_hbm.shape[0]
    remote = refs[0 : blocks - 1]
    remote_meta = refs[blocks - 1 : 2 * (blocks - 1)]
    rest = refs[2 * (blocks - 1) :]
    if first_group:
        bias_before = rest[0]
        parts_before = rest[1 : 1 + blocks]
        rest = rest[2 + blocks :]
    query_grad_hbm = rest[0]
    part_refs = rest[1 : 1 + blocks]
    bias_ref = rest[1 + blocks]
    (
        query_ref,
        output_ref,
        grad_ref,
        key_ref,
        value_ref,
        query_grad_ref,
        distance_ref,
        ancestor_ref,
        slope_rows,
        gain_rows,
        key_acc,
        value_acc,
        weight_ref,
        probs_ref,
        dscore_ref,
        load_sems,
        store_sems,
    ) = rest[2 + blocks :]
    factor = WIDTH**-0.5
    group_columns = heads_per_group * WIDTH
    quads = heads_per_group // QUAD

    loads = []
    for group in range(groups):
        at = first_group + group
        wide = pl.ds(at * group_columns, group_columns)
        thin = pl.ds(at * WIDTH, WIDTH)
        pairs = [
            (query_hbm.at[:, wide], query_ref.at[group]),
            (key_hbm.at[:, thin], key_ref.at[group]),
            (output_hbm.at[:, wide], output_ref.at[group]),
            (grad_hbm.at[:, wide], grad_ref.at[group]),
            (value_hbm.at[:, thin], value_ref.at[group]),
        ]
        loads.append(
            [
                pltpu.make_async_copy(source, to, load_sems.at[group, i])
                for i, (source, to) in enumerate(pairs)
            ]
        )
        for load in loads[-1]:
            load.start()

    here = lax.axis_index("ctx")
    query_pos = here * tokens + lax.broadcasted_iota(jnp.int32, (tokens, tokens), 1)
    start = jnp.zeros((tokens, tokens), jnp.int32)
    bound = jnp.int32(0)
    for index in range(lengths_ref.shape[1]):
        bound = bound + lengths_ref[0, index]
        start = jnp.where(query_pos >= bound, bound, start)
    query_depth = jnp.broadcast_to(depth_ref[...].astype(jnp.float32), (tokens, tokens))
    for shift in range(blocks):
        key_pos = (here ^ shift) * tokens + lax.broadcasted_iota(jnp.int32, (tokens, tokens), 0)
        if shift == 0:
            key_depth = as_column(depth_ref[...].astype(jnp.float32))
            key_end = as_column(end_ref[...].astype(jnp.float32))
        else:
            meta = remote_meta[shift - 1][tokens : tokens + META_ROWS, 0:tokens]
            meta = meta.astype(jnp.float32)
            key_depth = as_column(meta[0:1])
            key_end = as_column(meta[1:2] * END_UNIT + meta[2:3])
        inside = query_pos.astype(jnp.float32) < key_end
        allowed = (key_pos <= query_pos) & (key_pos >= start)
        rows = slice(shift * tokens, (shift + 1) * tokens)
        distance_ref[rows, :] = jnp.abs(query_depth - key_depth)
        ancestor_ref[rows, :] = jnp.where(allowed, jnp.where(inside, 1.0, 0.0), MASKED)

    block_rows = [slice(shift * tokens, (shift + 1) * tokens) for shift in range(blocks)]

    def stacked(ref, group, first, count):
        heads = [first + i for i in range(count)]
        return jnp.concatenate([ref[group, :, h * WIDTH : (h + 1) * WIDTH] for h in heads], axis=0)

    def scores(group, keys, value_ext, first, slot, place):
        query_pair = stacked(query_ref, group, first, 2)
        grad_pair = stacked(grad_ref, group, first, 2)
        output_pair = stacked(output_ref, group, first, 2)
        grad_ext = jnp.concatenate([grad_pair, grad_pair * output_pair], axis=1)
        raw = dot_nt(keys, query_pair)
        scales = []
        for half in range(2):
            head = (first_group + group) * heads_per_group + first + half
            gain = gain_ref[head] * LOG2E
            slope = slope_ref[head] * LOG2E
            lanes = slice(half * tokens, (half + 1) * tokens)
            tops, totals = [], []
            for rows in block_rows:
                score = raw[rows, lanes] * (factor * LOG2E) + (
                    gain * ancestor_ref[rows, :] - slope * distance_ref[rows, :]
                )
                top = jnp.max(score, axis=0, keepdims=True)
                weight = jnp.exp2(score - top)
                weight_ref[slot, rows, lanes] = weight
                tops.append(top)
                totals.append(jnp.sum(weight, axis=0, keepdims=True))
            top = functools.reduce(jnp.maximum, tops)
            shrink = [jnp.exp2(t - top) for t in tops]
            total = sum(a * b for a, b in zip(totals, shrink))
            inverse = 1.0 / total
            scales.append([s * inverse for s in shrink])
        centred = dot_nt(value_ext, grad_ext)
        for half in range(2):
            lanes = slice(half * tokens, (half + 1) * tokens)
            to = slice((place + half) * tokens, (place + half + 1) * tokens)
            slope_sum, gain_sum = 0.0, 0.0
            for rows, scale in zip(block_rows, scales[half]):
                probs = weight_ref[slot, rows, lanes] * scale
                dscore = probs * centred[rows, lanes]
                probs_ref[slot, rows, to] = probs.astype(jnp.bfloat16)
                dscore_ref[slot, rows, to] = dscore.astype(jnp.bfloat16)
                slope_sum = slope_sum + fold_rows(dscore * distance_ref[rows, :])
                gain_sum = gain_sum + fold_rows(dscore * ancestor_ref[rows, :])
            at = group * heads_per_group + first + half
            slope_rows[at : at + 1, :] = -jnp.sum(slope_sum, axis=0, keepdims=True)
            gain_rows[at : at + 1, :] = jnp.sum(gain_sum, axis=0, keepdims=True)

    def gradients(group, keys, quad, slot):
        query_quad = stacked(query_ref, group, quad * QUAD, QUAD)
        grad_quad = stacked(grad_ref, group, quad * QUAD, QUAD)
        dscore_b = dscore_ref[slot]
        key_part = dot_nn(dscore_b, query_quad)
        value_part = dot_nn(probs_ref[slot], grad_quad)
        if quad == 0:
            key_acc[group] = key_part
            value_acc[group] = value_part
        else:
            key_acc[group] += key_part
            value_acc[group] += value_part
        query_part = (dot_tn(dscore_b, keys) * factor).astype(jnp.bfloat16)
        for i in range(QUAD):
            at = (quad * QUAD + i) * WIDTH
            query_grad_ref[group, :, at : at + WIDTH] = query_part[i * tokens : (i + 1) * tokens]
        if quad == quads - 1:
            for shift, rows in enumerate(block_rows):
                at = 2 * group * WIDTH
                if first_group:
                    at = at + parts_before[shift].shape[1]
                key_block = (key_acc[group, rows, :] * factor).astype(jnp.bfloat16)
                part_refs[shift][:, at : at + WIDTH] = key_block
                value_block = value_acc[group, rows, :].astype(jnp.bfloat16)
                part_refs[shift][:, at + WIDTH : at + 2 * WIDTH] = value_block

    stores = []
    for group in range(groups):
        wide = pl.ds((first_group + group) * group_columns, group_columns)
        stores.append(
            pltpu.make_async_copy(
                query_grad_ref.at[group], query_grad_hbm.at[:, wide], store_sems.at[group]
            )
        )
    waiting = None
    step = 0
    for group in range(groups):
        for load in loads[group]:
            load.wait()
        at = slice(2 * group * WIDTH, (2 * group + 1) * WIDTH)
        keys = jnp.concatenate([key_ref[group]] + [r[0:tokens, at] for r in remote], axis=0)
        at = slice((2 * group + 1) * WIDTH, (2 * group + 2) * WIDTH)
        values = jnp.concatenate([value_ref[group]] + [r[0:tokens, at] for r in remote], axis=0)
        value_ext = jnp.concatenate([values, jnp.full(values.shape, -1.0, jnp.bfloat16)], axis=1)
        for quad in range(quads):
            slot = step % 2
            for place in range(0, QUAD, 2):
                scores(group, keys, value_ext, quad * QUAD + place, slot, place)
            if waiting is not None:
                gradients(*waiting)
                if waiting[2] == quads - 1:
                    stores[waiting[0]].start()
            waiting = (group, keys, quad, slot)
            step += 1
    gradients(*waiting)
    stores[waiting[0]].start()

    if first_group:
        for shift in range(blocks):
            before = parts_before[shift]
            part_refs[shift][:, 0 : before.shape[1]] = before[...]
    slope_sum = jnp.sum(slope_rows[...], axis=1, keepdims=True)
    gain_sum = jnp.sum(gain_rows[...], axis=1, keepdims=True)
    shape = slope_rows.shape
    lane = lax.broadcasted_iota(jnp.int32, shape, 1)
    row = lax.broadcasted_iota(jnp.int32, shape, 0)
    replicas, parts, rows_here, local = bias_ref.shape
    local_heads = slope_ref.shape[0] // parts
    kind = lax.broadcasted_iota(jnp.int32, (rows_here, local), 0)
    for part in range(parts):
        mine = lane == row - part * local_heads + first_group * heads_per_group
        mine = mine & (lane < local_heads)
        slope_line = jnp.sum(jnp.where(mine, slope_sum, 0.0), axis=0, keepdims=True)
        gain_line = jnp.sum(jnp.where(mine, gain_sum, 0.0), axis=0, keepdims=True)
        tile = jnp.where(kind == 0, slope_line, jnp.where(kind == 1, gain_line, 0.0))
        if first_group:
            tile = tile + bias_before[0, part]
        bias_ref[:, part] = jnp.broadcast_to(tile[None], (replicas, rows_here, local))
    for store in stores:
        store.wait()


def final_kernel(blocks, *refs):
    parts = refs[0:blocks]
    bias_parts, key_out, value_out, bias_out = refs[blocks:]
    for group in range(key_out.shape[1] // WIDTH):
        to = slice(group * WIDTH, (group + 1) * WIDTH)
        for kind, out in enumerate((key_out, value_out)):
            at = (2 * group + kind) * WIDTH
            total = parts[0][:, at : at + WIDTH].astype(jnp.float32)
            for shift in range(1, blocks):
                total = total + parts[shift][:, at : at + WIDTH].astype(jnp.float32)
            out[:, to] = total.astype(jnp.bfloat16)
    bias_out[...] = jnp.sum(bias_parts[...], axis=0)[0:2, 0 : bias_out.shape[1]]


def gather_blocks(messages, blocks):
    if blocks != 4:
        return [
            [
                lax.ppermute(m, "ctx", [(i, i ^ s) for i in range(blocks) if i < i ^ s])
                for s in range(1, blocks)
            ]
            for m in messages
        ]
    turns = [turn % 2 for turn in range(len(messages))]
    x_pairs = [[(0, 1), (2, 3)], [(0, 1), (1, 0), (2, 3)]]
    along_x = [lax.ppermute(m, "ctx", x_pairs[t]) for m, t in zip(messages, turns)]
    along_y = [lax.ppermute(m, "ctx", [(0, 2), (1, 3)]) for m in messages]
    passed_on = [
        lax.ppermute(x, "ctx", [(0, 2), (1, 3)]) if t else lax.ppermute(y, "ctx", [(2, 3), (3, 2)])
        for x, y, t in zip(along_x, along_y, turns)
    ]
    return [list(three) for three in zip(along_x, along_y, passed_on)]


def body(
    queries,
    key_rows,
    values,
    outputs,
    out_grads,
    depths,
    subtree_end,
    file_lengths,
    slopes,
    ancestor_gain,
):
    blocks = lax.axis_size("ctx")
    replicas = lax.axis_size("dp")
    tokens, width_all = queries.shape[1:]
    kv_width = key_rows.shape[2]
    heads_all = width_all // WIDTH
    kv_heads = kv_width // WIDTH
    heads_per_group = heads_all // kv_heads
    group_columns = heads_per_group * WIDTH
    local_heads = heads_all // blocks
    keys_seen = blocks * tokens
    groups = kv_heads // CHUNKS
    bf16, f32 = jnp.bfloat16, jnp.float32
    vmem = pl.BlockSpec(memory_space=pltpu.VMEM)
    smem = pl.BlockSpec(memory_space=pltpu.SMEM)
    anywhere = pl.BlockSpec(memory_space=pl.ANY)
    params = pltpu.CompilerParams(vmem_limit_bytes=VMEM_LIMIT)

    def hold(array):
        return pltpu.with_memory_space_constraint(array, pltpu.HBM)

    key_held, value_held = hold(key_rows[0]), hold(values[0])
    depth_held, end_held = hold(depths), hold(subtree_end)
    messages = pl.pallas_call(
        pack_kernel,
        out_shape=[
            jax.ShapeDtypeStruct(
                (tokens + (META_ROWS if chunk == 0 else 0), 2 * groups * WIDTH), bf16
            )
            for chunk in range(CHUNKS)
        ],
        in_specs=[vmem] * 4,
        out_specs=[vmem] * CHUNKS,
        compiler_params=params,
        name="pack",
    )(key_held, value_held, depth_held, end_held)
    arrived = gather_blocks(messages, blocks)

    bias_shape = (replicas, blocks, 8, WIDTH)
    matmul_flops = 2 * tokens * keys_seen * WIDTH * heads_all
    results = None
    for chunk in range(CHUNKS):
        operands = [
            hold(file_lengths),
            hold(slopes),
            hold(ancestor_gain),
            depth_held,
            end_held,
            hold(queries[0]),
            hold(outputs[0]),
            hold(out_grads[0]),
            key_held,
            value_held,
            *arrived[chunk],
            *arrived[0],
        ]
        specs = [smem] * 3 + [vmem] * 2 + [anywhere] * 5 + [vmem] * (2 * blocks - 2)
        aliases = {}
        if chunk:
            operands = operands + [results[1 + blocks], *results[1 : 1 + blocks], results[0]]
            specs = specs + [vmem] * (1 + blocks) + [anywhere]
            aliases = {len(operands) - 1: 0}
        part_shape = (tokens, 2 * (chunk + 1) * groups * WIDTH)
        results = pl.pallas_call(
            functools.partial(
                main_kernel, blocks, heads_per_group, groups, chunk * groups, blocks <= 4
            ),
            out_shape=[jax.ShapeDtypeStruct((tokens, width_all), bf16)]
            + [jax.ShapeDtypeStruct(part_shape, bf16)] * blocks
            + [jax.ShapeDtypeStruct(bias_shape, f32)],
            in_specs=specs,
            out_specs=[anywhere] + [vmem] * (1 + blocks),
            scratch_shapes=[
                pltpu.VMEM((groups, tokens, group_columns), bf16),
                pltpu.VMEM((groups, tokens, group_columns), bf16),
                pltpu.VMEM((groups, tokens, group_columns), bf16),
                pltpu.VMEM((groups, tokens, WIDTH), bf16),
                pltpu.VMEM((groups, tokens, WIDTH), bf16),
                pltpu.VMEM((groups, tokens, group_columns), bf16),
                pltpu.VMEM((keys_seen, tokens), f32),
                pltpu.VMEM((keys_seen, tokens), f32),
                pltpu.VMEM((groups * heads_per_group, tokens), f32),
                pltpu.VMEM((groups * heads_per_group, tokens), f32),
                pltpu.VMEM((groups, keys_seen, WIDTH), f32),
                pltpu.VMEM((groups, keys_seen, WIDTH), f32),
                pltpu.VMEM((2, keys_seen, 2 * tokens), f32),
                pltpu.VMEM((2, keys_seen, QUAD * tokens), bf16),
                pltpu.VMEM((2, keys_seen, QUAD * tokens), bf16),
                pltpu.SemaphoreType.DMA((groups, 5)),
                pltpu.SemaphoreType.DMA((groups,)),
            ],
            input_output_aliases=aliases,
            compiler_params=params,
            cost_estimate=pl.CostEstimate(
                flops=5 * matmul_flops // CHUNKS,
                bytes_accessed=10 * tokens * width_all // CHUNKS,
                transcendentals=tokens * keys_seen * heads_all // CHUNKS,
            ),
            name=f"attend_{chunk}",
        )(*operands)
    query_grads = results[0]
    parts = list(results[1 : 1 + blocks])
    bias_parts = results[1 + blocks].reshape(replicas * blocks, 8, WIDTH)
    for shift in range(1, blocks):
        back = [(i, i ^ shift) for i in range(blocks) if i > i ^ shift]
        parts[shift] = lax.ppermute(parts[shift], "ctx", back)
    bias_parts = lax.all_to_all(bias_parts, ("dp", "ctx"), split_axis=0, concat_axis=0, tiled=True)

    key_grads, value_grads, bias_grads = pl.pallas_call(
        functools.partial(final_kernel, blocks),
        out_shape=[
            jax.ShapeDtypeStruct((tokens, kv_width), bf16),
            jax.ShapeDtypeStruct((tokens, kv_width), bf16),
            jax.ShapeDtypeStruct((2, local_heads), f32),
        ],
        in_specs=[vmem] * (blocks + 1),
        out_specs=[vmem] * 3,
        compiler_params=params,
        name="combine",
    )(*parts, bias_parts)
    return (query_grads[None], key_grads[None], value_grads[None], bias_grads.T)


def solution(mesh):
    in_specs = (
        P("dp", "ctx", None),
        P("dp", "ctx", None),
        P("dp", "ctx", None),
        P("dp", "ctx", None),
        P("dp", "ctx", None),
        P("dp", "ctx"),
        P("dp", "ctx"),
        P("dp", None),
        P(),
        P(),
    )
    out_specs = (P("dp", "ctx", None), P("dp", "ctx", None), P("dp", "ctx", None), P("ctx", None))
    return jax.shard_map(body, mesh=mesh, in_specs=in_specs, out_specs=out_specs, check_vma=False)
```

```python
import functools

import jax
import jax.numpy as jnp
from jax import lax
from jax.experimental import pallas as pl
from jax.experimental.pallas import tpu as pltpu
from jax.sharding import PartitionSpec as P

WIDTH = 128
LOG2E = 1.4426950408889634
MASKED = -1e30
META_ROWS = 16
END_UNIT = 64

VMEM_LIMIT = 40 * 1024 * 1024


def dot_nt(a, b):
    return lax.dot_general(a, b, (((1,), (1,)), ((), ())), preferred_element_type=jnp.float32)


def dot_nn(a, b):
    return lax.dot_general(a, b, (((1,), (0,)), ((), ())), preferred_element_type=jnp.float32)


def fold_rows(block):
    return jnp.sum(block.reshape(block.shape[0] // 8, 8, block.shape[1]), axis=0)


def as_column(row):
    size = row.shape[1]
    return jnp.transpose(jnp.broadcast_to(row, (size, size)))


def pack_kernel(key_ref, value_ref, depth_ref, end_ref, message_ref):
    tokens = key_ref.shape[0]
    groups = key_ref.shape[1] // WIDTH
    for kind, ref in enumerate((key_ref, value_ref)):
        for group in range(groups):
            at = (kind * groups + group) * tokens
            message_ref[at : at + tokens, :] = ref[:, group * WIDTH : (group + 1) * WIDTH]
    depth = depth_ref[...]
    end = end_ref[...]
    end_high = end // END_UNIT
    end_low = end - end_high * END_UNIT
    row = lax.broadcasted_iota(jnp.int32, (META_ROWS, tokens), 0)
    meta = jnp.where(row == 0, depth, jnp.where(row == 1, end_high, end_low))
    meta = meta.astype(jnp.float32).astype(jnp.bfloat16)
    message_ref[2 * groups * tokens : 2 * groups * tokens + META_ROWS, :] = meta


def main_kernel(
    blocks,
    heads_per_group,
    groups,
    lengths_ref,
    slope_ref,
    gain_ref,
    depth_ref,
    end_ref,
    query_hbm,
    output_hbm,
    grad_hbm,
    key_ref,
    value_ref,
    *refs,
):
    tokens = query_hbm.shape[0]
    remote = refs[0 : blocks - 1]
    query_grad_hbm = refs[blocks - 1]
    part_refs = refs[blocks : 2 * blocks]
    bias_hbm = refs[2 * blocks]
    (
        query_ref,
        output_ref,
        grad_ref,
        query_grad_ref,
        keys_ref,
        keys_across_ref,
        value_ext_ref,
        distance_ref,
        ancestor_ref,
        slope_rows,
        gain_rows,
        key_acc,
        value_acc,
        weight_ref,
        probs_ref,
        dscore_ref,
        bias_ref,
        load_sems,
        store_sems,
        bias_sem,
    ) = refs[2 * blocks + 1 :]
    factor = WIDTH**-0.5
    group_columns = heads_per_group * WIDTH
    pairs = heads_per_group // 2

    def load(group, index):
        wide = pl.ds(pl.multiple_of(group * group_columns, group_columns), group_columns)
        source = (query_hbm, output_hbm, grad_hbm)[index]
        to = (query_ref, output_ref, grad_ref)[index]
        return pltpu.make_async_copy(
            source.at[:, wide], to.at[group], load_sems.at[3 * group + index]
        )

    def store(group):
        wide = pl.ds(pl.multiple_of(group * group_columns, group_columns), group_columns)
        return pltpu.make_async_copy(
            query_grad_ref.at[group], query_grad_hbm.at[:, wide], store_sems.at[group]
        )

    for group in range(groups):
        for index in range(3):
            load(group, index).start()

    here = lax.axis_index("ctx")
    query_pos = here * tokens + lax.broadcasted_iota(jnp.int32, (tokens, tokens), 1)
    start = jnp.zeros((tokens, tokens), jnp.int32)
    bound = jnp.int32(0)
    for index in range(lengths_ref.shape[1]):
        bound = bound + lengths_ref[0, index]
        start = jnp.where(query_pos >= bound, bound, start)
    query_depth = jnp.broadcast_to(depth_ref[...].astype(jnp.float32), (tokens, tokens))
    block_rows = [slice(s * tokens, (s + 1) * tokens) for s in range(blocks)]
    for s, rows in enumerate(block_rows):
        key_pos = (here ^ s) * tokens + lax.broadcasted_iota(jnp.int32, (tokens, tokens), 0)
        if s == 0:
            key_depth = as_column(depth_ref[...].astype(jnp.float32))
            key_end = as_column(end_ref[...].astype(jnp.float32))
        else:
            below = slice(2 * groups * tokens, 2 * groups * tokens + META_ROWS)
            meta = remote[s - 1][below, :].astype(jnp.float32)
            key_depth = as_column(meta[0:1])
            key_end = as_column(meta[1:2] * END_UNIT + meta[2:3])
        inside = query_pos.astype(jnp.float32) < key_end
        allowed = (key_pos <= query_pos) & (key_pos >= start)
        distance_ref[rows, :] = jnp.abs(query_depth - key_depth)
        ancestor_ref[rows, :] = jnp.where(allowed, jnp.where(inside, 1.0, 0.0), MASKED)

    for group in range(groups):
        for s, rows in enumerate(block_rows):
            if s == 0:
                key = key_ref[:, group * WIDTH : (group + 1) * WIDTH]
                value = value_ref[:, group * WIDTH : (group + 1) * WIDTH]
            else:
                key = remote[s - 1][group * tokens : (group + 1) * tokens, :]
                at = (groups + group) * tokens
                value = remote[s - 1][at : at + tokens, :]
            keys_ref[group, rows, :] = key
            keys_across_ref[group, :, rows] = jnp.transpose(key)
            value_ext_ref[group, rows, 0:WIDTH] = value
            value_ext_ref[group, rows, WIDTH:] = jnp.full(value.shape, -1.0, jnp.bfloat16)
    key_acc[...] = jnp.zeros_like(key_acc)
    value_acc[...] = jnp.zeros_like(value_acc)

    def stacked(ref, step):
        group, pair = step // pairs, step % pairs
        at = pl.multiple_of(pair * 2 * WIDTH, 2 * WIDTH)
        both = ref[group, :, pl.ds(at, 2 * WIDTH)]
        return jnp.concatenate([both[:, 0:WIDTH], both[:, WIDTH:]], axis=0)

    def weigh(step, slot, raw, half):
        gain = gain_ref[2 * step + half] * LOG2E
        slope = slope_ref[2 * step + half] * LOG2E
        lanes = slice(half * tokens, (half + 1) * tokens)
        tops, totals = [], []
        for rows in block_rows:
            score = raw[rows, lanes] * (factor * LOG2E) + (
                gain * ancestor_ref[rows, :] - slope * distance_ref[rows, :]
            )
            top = jnp.max(score, axis=0, keepdims=True)
            weight = jnp.exp2(score - top)
            weight_ref[slot, rows, lanes] = weight
            tops.append(top)
            totals.append(jnp.sum(weight, axis=0, keepdims=True))
        top = functools.reduce(jnp.maximum, tops)
        shrink = [jnp.exp2(t - top) for t in tops]
        inverse = 1.0 / sum(a * b for a, b in zip(totals, shrink))
        return [s * inverse for s in shrink]

    def differentiate(step, slot, centred, scales, half):
        lanes = slice(half * tokens, (half + 1) * tokens)
        slope_sum, gain_sum = 0.0, 0.0
        for rows, scale in zip(block_rows, scales):
            probs = weight_ref[slot, rows, lanes] * scale
            dscore = probs * centred[rows, lanes]
            probs_ref[slot, rows, lanes] = probs.astype(jnp.bfloat16)
            dscore_ref[slot, rows, lanes] = dscore.astype(jnp.bfloat16)
            slope_sum = slope_sum + fold_rows(dscore * distance_ref[rows, :])
            gain_sum = gain_sum + fold_rows(dscore * ancestor_ref[rows, :])
        at = pl.ds(2 * step + half, 1)
        slope_rows[at, :] = -jnp.sum(slope_sum, axis=0, keepdims=True)
        gain_rows[at, :] = jnp.sum(gain_sum, axis=0, keepdims=True)

    def query_part(step, slot):
        group, pair = step // pairs, step % pairs
        across = dot_nn(keys_across_ref[group], dscore_ref[slot]) * factor
        rows = jnp.transpose(across.astype(jnp.bfloat16))
        at = pl.multiple_of(pair * 2 * WIDTH, 2 * WIDTH)
        both = jnp.concatenate([rows[0:tokens], rows[tokens:]], axis=1)
        query_grad_ref[group, :, pl.ds(at, 2 * WIDTH)] = both

    def advance(step, slot, now, before):
        other = 1 - slot
        if now:
            group = step // pairs
            query_pair = stacked(query_ref, step)
            grad_pair = stacked(grad_ref, step)
            grad_ext = jnp.concatenate(
                [grad_pair, grad_pair * stacked(output_ref, step)], axis=1
            )
            raw = dot_nt(keys_ref[group], query_pair)
        if before:
            last = step - 1
            last_group = last // pairs
            key_acc[last_group] += dot_nn(dscore_ref[other], stacked(query_ref, last))
        if now:
            scales = [weigh(step, slot, raw, 0)]
            centred = dot_nt(value_ext_ref[group], grad_ext)
            scales.append(weigh(step, slot, raw, 1))
        if before:
            value_acc[last_group] += dot_nn(probs_ref[other], stacked(grad_ref, last))
        if now:
            differentiate(step, slot, centred, scales[0], 0)
        if before:
            query_part(last, other)
        if now:
            differentiate(step, slot, centred, scales[1], 1)

    steps = groups * pairs
    for index in range(3):
        load(0, index).wait()
    advance(0, 0, True, False)

    @pl.loop(1, steps)
    def _(step):
        @pl.when(step % pairs == 0)
        def _():
            for index in range(3):
                load(step // pairs, index).wait()

        advance(step, step % 2, True, True)

        @pl.when(step % pairs == 0)
        def _():
            store(step // pairs - 1).start()

    advance(steps, steps % 2, False, True)
    store(groups - 1).start()

    for s, rows in enumerate(block_rows):
        for group in range(groups):
            at = group * tokens
            part_refs[s][at : at + tokens, :] = (key_acc[group, rows, :] * factor).astype(
                jnp.bfloat16
            )
            at = (groups + group) * tokens
            part_refs[s][at : at + tokens, :] = value_acc[group, rows, :].astype(jnp.bfloat16)
    slope_sum = jnp.sum(slope_rows[...], axis=1, keepdims=True)
    gain_sum = jnp.sum(gain_rows[...], axis=1, keepdims=True)
    shape = slope_rows.shape
    lane = lax.broadcasted_iota(jnp.int32, shape, 1)
    row = lax.broadcasted_iota(jnp.int32, shape, 0)
    replicas, parts, rows_here, local = bias_ref.shape
    local_heads = shape[0] // parts
    kind = lax.broadcasted_iota(jnp.int32, (rows_here, local), 0)
    for part in range(parts):
        mine = (lane == row - part * local_heads) & (lane < local_heads)
        slope_line = jnp.sum(jnp.where(mine, slope_sum, 0.0), axis=0, keepdims=True)
        gain_line = jnp.sum(jnp.where(mine, gain_sum, 0.0), axis=0, keepdims=True)
        tile = jnp.where(kind == 0, slope_line, jnp.where(kind == 1, gain_line, 0.0))
        bias_ref[:, part] = jnp.broadcast_to(tile[None], (replicas, rows_here, local))
    bias_copy = pltpu.make_async_copy(bias_ref, bias_hbm, bias_sem)
    bias_copy.start()
    for group in range(groups):
        store(group).wait()
    bias_copy.wait()


def final_kernel(blocks, *refs):
    parts = refs[0:blocks]
    bias_parts, key_out, value_out, bias_out = refs[blocks:]
    tokens = key_out.shape[0]
    groups = key_out.shape[1] // WIDTH
    for kind, out in enumerate((key_out, value_out)):
        for group in range(groups):
            at = (kind * groups + group) * tokens
            total = parts[0][at : at + tokens, :].astype(jnp.float32)
            for s in range(1, blocks):
                total = total + parts[s][at : at + tokens, :].astype(jnp.float32)
            out[:, group * WIDTH : (group + 1) * WIDTH] = total.astype(jnp.bfloat16)
    bias_out[...] = jnp.sum(bias_parts[...], axis=0)[0:2, 0 : bias_out.shape[1]]


def body(
    queries,
    key_rows,
    values,
    outputs,
    out_grads,
    depths,
    subtree_end,
    file_lengths,
    slopes,
    ancestor_gain,
):
    blocks = lax.axis_size("ctx")
    replicas = lax.axis_size("dp")
    tokens, width_all = queries.shape[1:]
    kv_width = key_rows.shape[2]
    heads_all = width_all // WIDTH
    groups = kv_width // WIDTH
    heads_per_group = heads_all // groups
    group_columns = heads_per_group * WIDTH
    local_heads = heads_all // blocks
    keys_seen = blocks * tokens
    bf16, f32 = jnp.bfloat16, jnp.float32
    vmem = pl.BlockSpec(memory_space=pltpu.VMEM)
    smem = pl.BlockSpec(memory_space=pltpu.SMEM)
    hbm = pl.BlockSpec(memory_space=pltpu.HBM)
    params = pltpu.CompilerParams(vmem_limit_bytes=VMEM_LIMIT)

    def hold(array):
        return pltpu.with_memory_space_constraint(array, pltpu.HBM)

    key_held, value_held = hold(key_rows[0]), hold(values[0])
    depth_held, end_held = hold(depths), hold(subtree_end)
    message_rows = 2 * groups * tokens
    message = pl.pallas_call(
        pack_kernel,
        out_shape=jax.ShapeDtypeStruct((message_rows + META_ROWS, WIDTH), bf16),
        in_specs=[vmem] * 4,
        out_specs=vmem,
        compiler_params=params,
        name="pack",
    )(key_held, value_held, depth_held, end_held)
    arrived = [
        lax.ppermute(message, "ctx", [(i, i ^ s) for i in range(blocks) if i < i ^ s])
        for s in range(1, blocks)
    ]

    bias_shape = (replicas, blocks, 8, WIDTH)
    matmul_flops = 2 * tokens * keys_seen * WIDTH * heads_all
    results = pl.pallas_call(
        functools.partial(main_kernel, blocks, heads_per_group, groups),
        out_shape=[jax.ShapeDtypeStruct((tokens, width_all), bf16)]
        + [jax.ShapeDtypeStruct((message_rows, WIDTH), bf16)] * blocks
        + [jax.ShapeDtypeStruct(bias_shape, f32)],
        in_specs=[smem] * 3 + [vmem] * 2 + [hbm] * 3 + [vmem] * (1 + blocks),
        out_specs=[hbm] + [vmem] * blocks + [hbm],
        scratch_shapes=[
            pltpu.VMEM((groups, tokens, group_columns), bf16),
            pltpu.VMEM((groups, tokens, group_columns), bf16),
            pltpu.VMEM((groups, tokens, group_columns), bf16),
            pltpu.VMEM((groups, tokens, group_columns), bf16),
            pltpu.VMEM((groups, keys_seen, WIDTH), bf16),
            pltpu.VMEM((groups, WIDTH, keys_seen), bf16),
            pltpu.VMEM((groups, keys_seen, 2 * WIDTH), bf16),
            pltpu.VMEM((keys_seen, tokens), f32),
            pltpu.VMEM((keys_seen, tokens), f32),
            pltpu.VMEM((heads_all, tokens), f32),
            pltpu.VMEM((heads_all, tokens), f32),
            pltpu.VMEM((groups, keys_seen, WIDTH), f32),
            pltpu.VMEM((groups, keys_seen, WIDTH), f32),
            pltpu.VMEM((2, keys_seen, 2 * tokens), f32),
            pltpu.VMEM((2, keys_seen, 2 * tokens), bf16),
            pltpu.VMEM((2, keys_seen, 2 * tokens), bf16),
            pltpu.VMEM(bias_shape, f32),
            pltpu.SemaphoreType.DMA((3 * groups,)),
            pltpu.SemaphoreType.DMA((groups,)),
            pltpu.SemaphoreType.DMA,
        ],
        compiler_params=params,
        cost_estimate=pl.CostEstimate(
            flops=5 * matmul_flops,
            bytes_accessed=10 * tokens * width_all,
            transcendentals=tokens * keys_seen * heads_all,
        ),
        name="attend",
    )(
        hold(file_lengths),
        hold(slopes),
        hold(ancestor_gain),
        depth_held,
        end_held,
        hold(queries[0]),
        hold(outputs[0]),
        hold(out_grads[0]),
        key_held,
        value_held,
        *arrived,
    )
    query_grads = results[0]
    parts = list(results[1 : 1 + blocks])
    bias_parts = results[1 + blocks].reshape(replicas * blocks, 8, WIDTH)
    for s in range(1, blocks):
        back = [(i, i ^ s) for i in range(blocks) if i > i ^ s]
        parts[s] = lax.ppermute(parts[s], "ctx", back)
    bias_parts = lax.all_to_all(bias_parts, ("dp", "ctx"), split_axis=0, concat_axis=0, tiled=True)

    key_grads, value_grads, bias_grads = pl.pallas_call(
        functools.partial(final_kernel, blocks),
        out_shape=[
            jax.ShapeDtypeStruct((tokens, kv_width), bf16),
            jax.ShapeDtypeStruct((tokens, kv_width), bf16),
            jax.ShapeDtypeStruct((2, local_heads), f32),
        ],
        in_specs=[vmem] * (blocks + 1),
        out_specs=[vmem] * 3,
        compiler_params=params,
        name="combine",
    )(*parts, bias_parts)
    return (query_grads[None], key_grads[None], value_grads[None], bias_grads.T)


def solution(mesh):
    in_specs = (
        P("dp", "ctx", None),
        P("dp", "ctx", None),
        P("dp", "ctx", None),
        P("dp", "ctx", None),
        P("dp", "ctx", None),
        P("dp", "ctx"),
        P("dp", "ctx"),
        P("dp", None),
        P(),
        P(),
    )
    out_specs = (P("dp", "ctx", None), P("dp", "ctx", None), P("dp", "ctx", None), P("ctx", None))
    return jax.shard_map(body, mesh=mesh, in_specs=in_specs, out_specs=out_specs, check_vma=False)
```

```python
import functools

import jax
import jax.numpy as jnp
from jax import lax
from jax.experimental import pallas as pl
from jax.experimental.pallas import tpu as pltpu
from jax.sharding import PartitionSpec as P

WIDTH = 128
LOG2E = 1.4426950408889634
MASKED = -1e30
META_ROWS = 16
END_UNIT = 64


def dot_nt(a, b):
    return lax.dot_general(a, b, (((1,), (1,)), ((), ())), preferred_element_type=jnp.float32)


def dot_nn(a, b):
    return lax.dot_general(a, b, (((1,), (0,)), ((), ())), preferred_element_type=jnp.float32)


def fold_rows(block):
    return jnp.sum(block.reshape(block.shape[0] // 8, 8, block.shape[1]), axis=0)


def as_column(row):
    size = row.shape[1]
    return jnp.transpose(jnp.broadcast_to(row, (size, size)))


def pack_kernel(key_ref, value_ref, depth_ref, end_ref, message_ref):
    tokens = key_ref.shape[0]
    groups = key_ref.shape[1] // WIDTH
    for kind, ref in enumerate((key_ref, value_ref)):
        for group in range(groups):
            at = (kind * groups + group) * tokens
            message_ref[at : at + tokens, :] = ref[:, group * WIDTH : (group + 1) * WIDTH]
    depth = depth_ref[...]
    end = end_ref[...]
    end_high = end // END_UNIT
    end_low = end - end_high * END_UNIT
    row = lax.broadcasted_iota(jnp.int32, (META_ROWS, tokens), 0)
    meta = jnp.where(row == 0, depth, jnp.where(row == 1, end_high, end_low))
    meta = meta.astype(jnp.float32).astype(jnp.bfloat16)
    message_ref[2 * groups * tokens : 2 * groups * tokens + META_ROWS, :] = meta


def main_kernel(
    blocks,
    heads_per_group,
    groups,
    lengths_ref,
    slope_ref,
    gain_ref,
    depth_ref,
    end_ref,
    query_hbm,
    output_hbm,
    grad_hbm,
    key_ref,
    value_ref,
    *refs,
):
    tokens = query_hbm.shape[0]
    remote = refs[0 : blocks - 1]
    query_grad_hbm = refs[blocks - 1]
    part_refs = refs[blocks : 2 * blocks]
    bias_hbm = refs[2 * blocks]
    (
        query_ref,
        output_ref,
        grad_ref,
        query_grad_ref,
        keys_ref,
        keys_across_ref,
        value_ext_ref,
        distance_ref,
        ancestor_ref,
        slope_rows,
        gain_rows,
        weight_ref,
        probs_ref,
        dscore_ref,
        bias_ref,
        load_sems,
        store_sems,
        bias_sem,
    ) = refs[2 * blocks + 1 :]
    factor = WIDTH**-0.5
    group_columns = heads_per_group * WIDTH
    pairs = heads_per_group // 2

    def load(group, index):
        wide = pl.ds(pl.multiple_of(group * group_columns, group_columns), group_columns)
        source = (query_hbm, output_hbm, grad_hbm)[index]
        to = (query_ref, output_ref, grad_ref)[index]
        return pltpu.make_async_copy(
            source.at[:, wide], to.at[group], load_sems.at[3 * group + index]
        )

    def store(group):
        wide = pl.ds(pl.multiple_of(group * group_columns, group_columns), group_columns)
        return pltpu.make_async_copy(
            query_grad_ref.at[group], query_grad_hbm.at[:, wide], store_sems.at[group]
        )

    for group in range(groups):
        for index in range(3):
            load(group, index).start()

    here = lax.axis_index("ctx")
    query_pos = here * tokens + lax.broadcasted_iota(jnp.int32, (tokens, tokens), 1)
    start = jnp.zeros((tokens, tokens), jnp.int32)
    bound = jnp.int32(0)
    for index in range(lengths_ref.shape[1]):
        bound = bound + lengths_ref[0, index]
        start = jnp.where(query_pos >= bound, bound, start)
    query_depth = jnp.broadcast_to(depth_ref[...].astype(jnp.float32), (tokens, tokens))
    block_rows = [slice(s * tokens, (s + 1) * tokens) for s in range(blocks)]
    for s, rows in enumerate(block_rows):
        key_pos = (here ^ s) * tokens + lax.broadcasted_iota(jnp.int32, (tokens, tokens), 0)
        if s == 0:
            key_depth = as_column(depth_ref[...].astype(jnp.float32))
            key_end = as_column(end_ref[...].astype(jnp.float32))
        else:
            below = slice(2 * groups * tokens, 2 * groups * tokens + META_ROWS)
            meta = remote[s - 1][below, :].astype(jnp.float32)
            key_depth = as_column(meta[0:1])
            key_end = as_column(meta[1:2] * END_UNIT + meta[2:3])
        inside = query_pos.astype(jnp.float32) < key_end
        allowed = (key_pos <= query_pos) & (key_pos >= start)
        distance_ref[rows, :] = jnp.abs(query_depth - key_depth)
        ancestor_ref[rows, :] = jnp.where(allowed, jnp.where(inside, 1.0, 0.0), MASKED)

    for group in range(groups):
        for s, rows in enumerate(block_rows):
            if s == 0:
                key = key_ref[:, group * WIDTH : (group + 1) * WIDTH]
                value = value_ref[:, group * WIDTH : (group + 1) * WIDTH]
            else:
                key = remote[s - 1][group * tokens : (group + 1) * tokens, :]
                at = (groups + group) * tokens
                value = remote[s - 1][at : at + tokens, :]
            keys_ref[group, rows, :] = key
            keys_across_ref[group, :, rows] = jnp.transpose(key)
            value_ext_ref[group, rows, 0:WIDTH] = value
            value_ext_ref[group, rows, WIDTH:] = jnp.full(value.shape, -1.0, jnp.bfloat16)

    def stacked(ref, group, first, count):
        heads = [slice((first + i) * WIDTH, (first + i + 1) * WIDTH) for i in range(count)]
        return jnp.concatenate([ref[group, :, h] for h in heads], axis=0)

    def weigh(group, pair, raw, half):
        head = group * heads_per_group + 2 * pair + half
        gain = gain_ref[head] * LOG2E
        slope = slope_ref[head] * LOG2E
        lanes = slice(half * tokens, (half + 1) * tokens)
        tops, totals = [], []
        for s, rows in enumerate(block_rows):
            score = raw[s][:, lanes] * (factor * LOG2E) + (
                gain * ancestor_ref[rows, :] - slope * distance_ref[rows, :]
            )
            top = jnp.max(score, axis=0, keepdims=True)
            weight = jnp.exp2(score - top)
            weight_ref[pair % 2, rows, lanes] = weight
            tops.append(top)
            totals.append(jnp.sum(weight, axis=0, keepdims=True))
        top = functools.reduce(jnp.maximum, tops)
        shrink = [jnp.exp2(t - top) for t in tops]
        inverse = 1.0 / sum(a * b for a, b in zip(totals, shrink))
        return [s * inverse for s in shrink]

    def differentiate(group, pair, slot, centred, scales, half):
        lanes = slice(half * tokens, (half + 1) * tokens)
        to = slice((2 * pair + half) * tokens, (2 * pair + half + 1) * tokens)
        slope_sum, gain_sum = 0.0, 0.0
        for s, rows in enumerate(block_rows):
            probs = weight_ref[pair % 2, rows, lanes] * scales[s]
            dscore = probs * centred[s][:, lanes]
            probs_ref[slot, rows, to] = probs.astype(jnp.bfloat16)
            dscore_ref[slot, rows, to] = dscore.astype(jnp.bfloat16)
            slope_sum = slope_sum + fold_rows(dscore * distance_ref[rows, :])
            gain_sum = gain_sum + fold_rows(dscore * ancestor_ref[rows, :])
        at = pl.ds(group * heads_per_group + 2 * pair + half, 1)
        slope_rows[at, :] = -jnp.sum(slope_sum, axis=0, keepdims=True)
        gain_rows[at, :] = jnp.sum(gain_sum, axis=0, keepdims=True)

    def put_part(group, kind, whole):
        at = pl.multiple_of((kind * groups + group) * tokens, tokens)
        for s, rows in enumerate(block_rows):
            part_refs[s][pl.ds(at, tokens), :] = whole[rows].astype(jnp.bfloat16)

    def key_part(group, slot):
        heads = stacked(query_ref, group, 0, heads_per_group)
        put_part(group, 0, dot_nn(dscore_ref[slot], heads) * factor)

    def value_part(group, slot):
        heads = stacked(grad_ref, group, 0, heads_per_group)
        put_part(group, 1, dot_nn(probs_ref[slot], heads))

    def query_part(group, slot, pair):
        lanes = slice(2 * pair * tokens, (2 * pair + 2) * tokens)
        across = dot_nn(keys_across_ref[group], dscore_ref[slot, :, lanes]) * factor
        rows = jnp.transpose(across.astype(jnp.bfloat16))
        for half in range(2):
            at = (2 * pair + half) * WIDTH
            query_grad_ref[group, :, at : at + WIDTH] = rows[half * tokens : (half + 1) * tokens]

    def products(ref, group, other):
        whole = dot_nt(ref[group], other)
        return [whole[rows] for rows in block_rows]

    def advance(group, slot, before, before_slot):
        for pair in range(pairs):
            if group is not None:
                query_pair = stacked(query_ref, group, 2 * pair, 2)
                grad_pair = stacked(grad_ref, group, 2 * pair, 2)
                output_pair = stacked(output_ref, group, 2 * pair, 2)
                grad_ext = jnp.concatenate([grad_pair, grad_pair * output_pair], axis=1)
                raw = products(keys_ref, group, query_pair)
                scales = [weigh(group, pair, raw, half) for half in range(2)]
            if pair == 0:
                key_part(before, before_slot)
            if pair == 1:
                value_part(before, before_slot)
            if group is not None:
                centred = products(value_ext_ref, group, grad_ext)
                for half in range(2):
                    differentiate(group, pair, slot, centred, scales[half], half)
            query_part(before, before_slot, pair)

    @pl.loop(0, groups // 2)
    def _(turn):
        first, second = 2 * turn, 2 * turn + 1
        for index in range(3):
            load(first, index).wait()
        before = jnp.maximum(first - 1, 0)
        advance(first, 0, before, 1)

        @pl.when(turn > 0)
        def _():
            store(before).start()

        for index in range(3):
            load(second, index).wait()
        advance(second, 1, first, 0)
        store(first).start()

    advance(None, None, groups - 1, 1)
    store(groups - 1).start()

    slope_sum = jnp.sum(slope_rows[...], axis=1, keepdims=True)
    gain_sum = jnp.sum(gain_rows[...], axis=1, keepdims=True)
    shape = slope_rows.shape
    lane = lax.broadcasted_iota(jnp.int32, shape, 1)
    row = lax.broadcasted_iota(jnp.int32, shape, 0)
    replicas, parts, rows_here, local = bias_ref.shape
    local_heads = shape[0] // parts
    kind = lax.broadcasted_iota(jnp.int32, (rows_here, local), 0)
    for part in range(parts):
        mine = (lane == row - part * local_heads) & (lane < local_heads)
        slope_line = jnp.sum(jnp.where(mine, slope_sum, 0.0), axis=0, keepdims=True)
        gain_line = jnp.sum(jnp.where(mine, gain_sum, 0.0), axis=0, keepdims=True)
        tile = jnp.where(kind == 0, slope_line, jnp.where(kind == 1, gain_line, 0.0))
        bias_ref[:, part] = jnp.broadcast_to(tile[None], (replicas, rows_here, local))
    bias_copy = pltpu.make_async_copy(bias_ref, bias_hbm, bias_sem)
    bias_copy.start()
    for group in range(groups):
        store(group).wait()
    bias_copy.wait()


def combine_kernel(blocks, *refs):
    parts = refs[0:blocks]
    key_out, value_out = refs[blocks:]
    tokens = key_out.shape[0]
    groups = key_out.shape[1] // WIDTH
    for kind, out in enumerate((key_out, value_out)):
        for group in range(groups):
            at = (kind * groups + group) * tokens
            total = parts[0][at : at + tokens, :].astype(jnp.float32)
            for s in range(1, blocks):
                total = total + parts[s][at : at + tokens, :].astype(jnp.float32)
            out[:, group * WIDTH : (group + 1) * WIDTH] = total.astype(jnp.bfloat16)


def bias_kernel(parts_ref, out_ref):
    out_ref[...] = jnp.sum(parts_ref[...], axis=0)[0:2, 0 : out_ref.shape[1]]


def body(
    queries,
    key_rows,
    values,
    outputs,
    out_grads,
    depths,
    subtree_end,
    file_lengths,
    slopes,
    ancestor_gain,
):
    blocks = lax.axis_size("ctx")
    replicas = lax.axis_size("dp")
    tokens, width_all = queries.shape[1:]
    kv_width = key_rows.shape[2]
    heads_all = width_all // WIDTH
    groups = kv_width // WIDTH
    heads_per_group = heads_all // groups
    group_columns = heads_per_group * WIDTH
    local_heads = heads_all // blocks
    keys_seen = blocks * tokens
    bf16, f32 = jnp.bfloat16, jnp.float32
    vmem = pl.BlockSpec(memory_space=pltpu.VMEM)
    smem = pl.BlockSpec(memory_space=pltpu.SMEM)
    hbm = pl.BlockSpec(memory_space=pltpu.HBM)
    params = pltpu.CompilerParams(vmem_limit_bytes=(40 if blocks <= 4 else 56) * 1024 * 1024)

    def hold(array):
        return pltpu.with_memory_space_constraint(array, pltpu.HBM)

    key_held, value_held = hold(key_rows[0]), hold(values[0])
    depth_held, end_held = hold(depths), hold(subtree_end)
    message_rows = 2 * groups * tokens
    message = pl.pallas_call(
        pack_kernel,
        out_shape=jax.ShapeDtypeStruct((message_rows + META_ROWS, WIDTH), bf16),
        in_specs=[vmem] * 4,
        out_specs=vmem,
        compiler_params=params,
        name="pack",
    )(key_held, value_held, depth_held, end_held)
    arrived = [
        lax.ppermute(message, "ctx", [(i, i ^ s) for i in range(blocks) if i < i ^ s])
        for s in range(1, blocks)
    ]

    bias_shape = (replicas, blocks, 8, WIDTH)
    matmul_flops = 2 * tokens * keys_seen * WIDTH * heads_all
    results = pl.pallas_call(
        functools.partial(main_kernel, blocks, heads_per_group, groups),
        out_shape=[jax.ShapeDtypeStruct((tokens, width_all), bf16)]
        + [jax.ShapeDtypeStruct((message_rows, WIDTH), bf16)] * blocks
        + [jax.ShapeDtypeStruct(bias_shape, f32)],
        in_specs=[smem] * 3 + [vmem] * 2 + [hbm] * 3 + [vmem] * (1 + blocks),
        out_specs=[hbm] + [vmem] * blocks + [hbm],
        scratch_shapes=[
            pltpu.VMEM((groups, tokens, group_columns), bf16),
            pltpu.VMEM((groups, tokens, group_columns), bf16),
            pltpu.VMEM((groups, tokens, group_columns), bf16),
            pltpu.VMEM((groups, tokens, group_columns), bf16),
            pltpu.VMEM((groups, keys_seen, WIDTH), bf16),
            pltpu.VMEM((groups, WIDTH, keys_seen), bf16),
            pltpu.VMEM((groups, keys_seen, 2 * WIDTH), bf16),
            pltpu.VMEM((keys_seen, tokens), f32),
            pltpu.VMEM((keys_seen, tokens), f32),
            pltpu.VMEM((heads_all, tokens), f32),
            pltpu.VMEM((heads_all, tokens), f32),
            pltpu.VMEM((2, keys_seen, 2 * tokens), f32),
            pltpu.VMEM((2, keys_seen, group_columns), bf16),
            pltpu.VMEM((2, keys_seen, group_columns), bf16),
            pltpu.VMEM(bias_shape, f32),
            pltpu.SemaphoreType.DMA((3 * groups,)),
            pltpu.SemaphoreType.DMA((groups,)),
            pltpu.SemaphoreType.DMA,
        ],
        compiler_params=params,
        cost_estimate=pl.CostEstimate(
            flops=5 * matmul_flops,
            bytes_accessed=10 * tokens * width_all,
            transcendentals=tokens * keys_seen * heads_all,
        ),
        name="attend",
    )(
        hold(file_lengths),
        hold(slopes),
        hold(ancestor_gain),
        depth_held,
        end_held,
        hold(queries[0]),
        hold(outputs[0]),
        hold(out_grads[0]),
        key_held,
        value_held,
        *arrived,
    )
    query_grads = results[0]
    parts = list(results[1 : 1 + blocks])
    bias_parts = results[1 + blocks].reshape(replicas * blocks, 8, WIDTH)
    for s in range(1, blocks):
        back = [(i, i ^ s) for i in range(blocks) if i > i ^ s]
        parts[s] = lax.ppermute(parts[s], "ctx", back)
    bias_parts = lax.all_to_all(bias_parts, ("dp", "ctx"), split_axis=0, concat_axis=0, tiled=True)

    key_grads, value_grads = pl.pallas_call(
        functools.partial(combine_kernel, blocks),
        out_shape=[jax.ShapeDtypeStruct((tokens, kv_width), bf16)] * 2,
        in_specs=[vmem] * blocks,
        out_specs=[vmem] * 2,
        compiler_params=params,
        cost_estimate=pl.CostEstimate(
            flops=2 * message_rows * WIDTH * blocks,
            bytes_accessed=2 * message_rows * WIDTH * (blocks + 1),
            transcendentals=0,
        ),
        name="combine",
    )(*parts)
    bias_grads = pl.pallas_call(
        bias_kernel,
        out_shape=jax.ShapeDtypeStruct((2, local_heads), f32),
        in_specs=[vmem],
        out_specs=vmem,
        compiler_params=params,
        name="bias",
    )(bias_parts)
    return (query_grads[None], key_grads[None], value_grads[None], bias_grads.T)


def solution(mesh):
    in_specs = (
        P("dp", "ctx", None),
        P("dp", "ctx", None),
        P("dp", "ctx", None),
        P("dp", "ctx", None),
        P("dp", "ctx", None),
        P("dp", "ctx"),
        P("dp", "ctx"),
        P("dp", None),
        P(),
        P(),
    )
    out_specs = (P("dp", "ctx", None), P("dp", "ctx", None), P("dp", "ctx", None), P("ctx", None))
    return jax.shard_map(body, mesh=mesh, in_specs=in_specs, out_specs=out_specs, check_vma=False)
```

```python
import functools

import jax
import jax.numpy as jnp
from jax import lax
from jax.experimental import pallas as pl
from jax.experimental.pallas import tpu as pltpu
from jax.sharding import PartitionSpec as P

WIDTH = 128
LOG2E = 1.4426950408889634
MASKED = -1e30
META_ROWS = 16
END_UNIT = 64
CHUNKS = 2


def dot_nt(a, b):
    return lax.dot_general(a, b, (((1,), (1,)), ((), ())), preferred_element_type=jnp.float32)


def dot_nn(a, b):
    return lax.dot_general(a, b, (((1,), (0,)), ((), ())), preferred_element_type=jnp.float32)


def fold_rows(block):
    return jnp.sum(block.reshape(block.shape[0] // 8, 8, block.shape[1]), axis=0)


def as_column(row):
    size = row.shape[1]
    return jnp.transpose(jnp.broadcast_to(row, (size, size)))


def pack_kernel(key_ref, value_ref, depth_ref, end_ref, *message_refs):
    tokens = key_ref.shape[0]
    groups = key_ref.shape[1] // WIDTH // len(message_refs)
    for chunk, message_ref in enumerate(message_refs):
        for kind, ref in enumerate((key_ref, value_ref)):
            for group in range(groups):
                at = (kind * groups + group) * tokens
                source = slice((chunk * groups + group) * WIDTH, (chunk * groups + group + 1) * WIDTH)
                message_ref[at : at + tokens, :] = ref[:, source]
    depth = depth_ref[...]
    end = end_ref[...]
    end_high = end // END_UNIT
    end_low = end - end_high * END_UNIT
    row = lax.broadcasted_iota(jnp.int32, (META_ROWS, tokens), 0)
    meta = jnp.where(row == 0, depth, jnp.where(row == 1, end_high, end_low))
    meta = meta.astype(jnp.float32).astype(jnp.bfloat16)
    message_refs[0][2 * groups * tokens : 2 * groups * tokens + META_ROWS, :] = meta


def fill_tables(
    blocks, groups, lengths_ref, depth_ref, end_ref, remote, distance_ref, ancestor_ref
):
    tokens = depth_ref.shape[1]
    here = lax.axis_index("ctx")
    query_pos = here * tokens + lax.broadcasted_iota(jnp.int32, (tokens, tokens), 1)
    start = jnp.zeros((tokens, tokens), jnp.int32)
    bound = jnp.int32(0)
    for index in range(lengths_ref.shape[1]):
        bound = bound + lengths_ref[0, index]
        start = jnp.where(query_pos >= bound, bound, start)
    query_depth = jnp.broadcast_to(depth_ref[...].astype(jnp.float32), (tokens, tokens))
    for s in range(blocks):
        rows = slice(s * tokens, (s + 1) * tokens)
        key_pos = (here ^ s) * tokens + lax.broadcasted_iota(jnp.int32, (tokens, tokens), 0)
        if s == 0:
            key_depth = as_column(depth_ref[...].astype(jnp.float32))
            key_end = as_column(end_ref[...].astype(jnp.float32))
        else:
            below = slice(2 * groups * tokens, 2 * groups * tokens + META_ROWS)
            meta = remote[s - 1][below, :].astype(jnp.float32)
            key_depth = as_column(meta[0:1])
            key_end = as_column(meta[1:2] * END_UNIT + meta[2:3])
        inside = query_pos.astype(jnp.float32) < key_end
        allowed = (key_pos <= query_pos) & (key_pos >= start)
        distance_ref[rows, :] = jnp.abs(query_depth - key_depth)
        ancestor_ref[rows, :] = jnp.where(allowed, jnp.where(inside, 1.0, 0.0), MASKED)


def main_kernel(blocks, heads_per_group, groups, chunk, last_chunk, *refs):
    refs = list(refs)
    take = lambda count: [refs.pop(0) for _ in range(count)]
    slope_ref, gain_ref, query_hbm, output_hbm, grad_hbm, key_ref, value_ref = take(7)
    remote = take(blocks - 1)
    if chunk == 0:
        lengths_ref, depth_ref, end_ref = take(3)
    else:
        distance_ref, ancestor_ref, sums_before = take(3)
        parts_before = take(blocks)
        take(1)
    (query_grad_hbm,) = take(1)
    part_refs = take(blocks)
    if chunk == 0:
        distance_ref, ancestor_ref = take(2)
    if last_chunk:
        (bias_ref,) = take(1)
        sums_ref = refs.pop()
    else:
        (sums_ref,) = take(1)
    (
        query_ref,
        output_ref,
        grad_ref,
        query_grad_ref,
        weight_ref,
        probs_ref,
        dscore_ref,
        load_sems,
        store_sems,
    ) = refs
    tokens = query_hbm.shape[0]
    factor = WIDTH**-0.5
    group_columns = heads_per_group * WIDTH
    pairs = heads_per_group // 2
    first_group = chunk * groups
    block_rows = [slice(s * tokens, (s + 1) * tokens) for s in range(blocks)]

    def load(group, index):
        wide = pl.ds((first_group + group) * group_columns, group_columns)
        source = (query_hbm, output_hbm, grad_hbm)[index]
        to = (query_ref, output_ref, grad_ref)[index]
        return pltpu.make_async_copy(
            source.at[:, wide], to.at[group], load_sems.at[3 * group + index]
        )

    def store(group):
        wide = pl.ds((first_group + group) * group_columns, group_columns)
        return pltpu.make_async_copy(
            query_grad_ref.at[group], query_grad_hbm.at[:, wide], store_sems.at[group]
        )

    for group in range(groups):
        for index in range(3):
            load(group, index).start()

    if chunk == 0:
        fill_tables(
            blocks, groups, lengths_ref, depth_ref, end_ref, remote, distance_ref, ancestor_ref
        )
    else:
        before = groups * chunk
        for s in range(blocks):
            for kind in range(2):
                part_refs[s][
                    kind * (before + groups) * tokens : (kind * (before + groups) + before) * tokens, :
                ] = parts_before[s][kind * before * tokens : (kind + 1) * before * tokens, :]

    def own_and_remote(ref, kind, group):
        own = ref[:, (first_group + group) * WIDTH : (first_group + group + 1) * WIDTH]
        at = (kind * groups + group) * tokens
        return jnp.concatenate([own] + [r[at : at + tokens, :] for r in remote], axis=0)

    def stacked(ref, group, first, count):
        heads = [slice((first + i) * WIDTH, (first + i + 1) * WIDTH) for i in range(count)]
        return jnp.concatenate([ref[group, :, h] for h in heads], axis=0)

    def weigh(group, pair, raw, half):
        head = (first_group + group) * heads_per_group + 2 * pair + half
        gain = gain_ref[head] * LOG2E
        slope = slope_ref[head] * LOG2E
        lanes = slice(half * tokens, (half + 1) * tokens)
        tops, totals = [], []
        for s, rows in enumerate(block_rows):
            score = raw[s][:, lanes] * (factor * LOG2E) + (
                gain * ancestor_ref[rows, :] - slope * distance_ref[rows, :]
            )
            top = jnp.max(score, axis=0, keepdims=True)
            weight = jnp.exp2(score - top)
            weight_ref[pair % 2, rows, lanes] = weight
            tops.append(top)
            totals.append(jnp.sum(weight, axis=0, keepdims=True))
        top = functools.reduce(jnp.maximum, tops)
        shrink = [jnp.exp2(t - top) for t in tops]
        inverse = 1.0 / sum(a * b for a, b in zip(totals, shrink))
        return [s * inverse for s in shrink]

    def differentiate(group, pair, slot, centred, scales, half):
        lanes = slice(half * tokens, (half + 1) * tokens)
        to = slice((2 * pair + half) * tokens, (2 * pair + half + 1) * tokens)
        slope_sum, gain_sum = 0.0, 0.0
        for s, rows in enumerate(block_rows):
            probs = weight_ref[pair % 2, rows, lanes] * scales[s]
            dscore = probs * centred[s][:, lanes]
            probs_ref[slot, rows, to] = probs.astype(jnp.bfloat16)
            dscore_ref[slot, rows, to] = dscore.astype(jnp.bfloat16)
            slope_sum = slope_sum + fold_rows(dscore * distance_ref[rows, :])
            gain_sum = gain_sum + fold_rows(dscore * ancestor_ref[rows, :])
        at = (first_group + group) * heads_per_group + 2 * pair + half
        sums_ref[0, at : at + 1, :] = -jnp.sum(slope_sum, axis=0, keepdims=True)
        sums_ref[1, at : at + 1, :] = jnp.sum(gain_sum, axis=0, keepdims=True)

    def put_part(group, kind, whole):
        at = (kind * (first_group + groups) + first_group + group) * tokens
        for s, rows in enumerate(block_rows):
            part_refs[s][at : at + tokens, :] = whole[rows].astype(jnp.bfloat16)

    def key_part(group, slot):
        heads = stacked(query_ref, group, 0, heads_per_group)
        put_part(group, 0, dot_nn(dscore_ref[slot], heads) * factor)

    def value_part(group, slot):
        heads = stacked(grad_ref, group, 0, heads_per_group)
        put_part(group, 1, dot_nn(probs_ref[slot], heads))

    def query_part(keys_across, group, slot, pair):
        lanes = slice(2 * pair * tokens, (2 * pair + 2) * tokens)
        across = dot_nn(keys_across, dscore_ref[slot, :, lanes]) * factor
        rows = jnp.transpose(across.astype(jnp.bfloat16))
        for half in range(2):
            at = (2 * pair + half) * WIDTH
            query_grad_ref[group, :, at : at + WIDTH] = rows[half * tokens : (half + 1) * tokens]

    def products(left, right):
        whole = dot_nt(left, right)
        return [whole[rows] for rows in block_rows]

    def advance(group, before):
        if group is not None:
            slot = group % 2
            keys = own_and_remote(key_ref, 0, group)
            values = own_and_remote(value_ref, 1, group)
            minus = jnp.full(values.shape, -1.0, jnp.bfloat16)
            value_ext = jnp.concatenate([values, minus], axis=1)
        if before is not None:
            before_slot = before % 2
            keys_across = jnp.transpose(own_and_remote(key_ref, 0, before))
        for pair in range(pairs):
            if group is not None:
                query_pair = stacked(query_ref, group, 2 * pair, 2)
                grad_pair = stacked(grad_ref, group, 2 * pair, 2)
                output_pair = stacked(output_ref, group, 2 * pair, 2)
                grad_ext = jnp.concatenate([grad_pair, grad_pair * output_pair], axis=1)
                raw = products(keys, query_pair)
                scales = [weigh(group, pair, raw, half) for half in range(2)]
            if before is not None and pair == 0:
                key_part(before, before_slot)
            if before is not None and pair == 1:
                value_part(before, before_slot)
            if group is not None:
                centred = products(value_ext, grad_ext)
                for half in range(2):
                    differentiate(group, pair, slot, centred, scales[half], half)
            if before is not None:
                query_part(keys_across, before, before_slot, pair)

    for group in range(groups):
        for index in range(3):
            load(group, index).wait()
        advance(group, group - 1 if group else None)
        if group:
            store(group - 1).start()
    advance(None, groups - 1)
    store(groups - 1).start()

    if last_chunk:
        heads = heads_per_group * first_group
        rows = [
            jnp.concatenate([sums_before[kind, 0:heads, :], sums_ref[kind, heads:, :]], axis=0)
            for kind in range(2)
        ]
        sums = [jnp.sum(r, axis=1, keepdims=True) for r in rows]
        shape = rows[0].shape
        diagonal = lax.broadcasted_iota(jnp.int32, shape, 0) == lax.broadcasted_iota(
            jnp.int32, shape, 1
        )
        lines = [
            jnp.sum(jnp.where(diagonal, column, 0.0), axis=0, keepdims=True) for column in sums
        ]
        row = lax.broadcasted_iota(jnp.int32, bias_ref.shape[1:], 0)
        tile = jnp.where(row == 0, lines[0], jnp.where(row == 1, lines[1], 0.0))
        bias_ref[...] = jnp.broadcast_to(tile[None], bias_ref.shape)
    for group in range(groups):
        store(group).wait()


def combine_kernel(blocks, *refs):
    parts = refs[0:blocks]
    key_out, value_out = refs[blocks:]
    tokens = key_out.shape[0]
    groups = key_out.shape[1] // WIDTH
    for kind, out in enumerate((key_out, value_out)):
        for group in range(groups):
            at = (kind * groups + group) * tokens
            total = parts[0][at : at + tokens, :].astype(jnp.float32)
            for s in range(1, blocks):
                total = total + parts[s][at : at + tokens, :].astype(jnp.float32)
            out[:, group * WIDTH : (group + 1) * WIDTH] = total.astype(jnp.bfloat16)


def spread_kernel(sums_ref, spread_ref):
    total = jnp.sum(sums_ref[...], axis=0)
    share = spread_ref.shape[2]
    for block in range(spread_ref.shape[0]):
        spread_ref[block] = total[:, block * share : (block + 1) * share]


def bias_kernel(parts_ref, out_ref):
    out_ref[...] = jnp.sum(parts_ref[...], axis=0)[0:2]


def body(
    queries,
    key_rows,
    values,
    outputs,
    out_grads,
    depths,
    subtree_end,
    file_lengths,
    slopes,
    ancestor_gain,
):
    blocks = lax.axis_size("ctx")
    replicas = lax.axis_size("dp")
    tokens, width_all = queries.shape[1:]
    kv_width = key_rows.shape[2]
    heads_all = width_all // WIDTH
    kv_heads = kv_width // WIDTH
    heads_per_group = heads_all // kv_heads
    group_columns = heads_per_group * WIDTH
    local_heads = heads_all // blocks
    keys_seen = blocks * tokens
    groups = kv_heads // CHUNKS
    bf16, f32 = jnp.bfloat16, jnp.float32
    vmem = pl.BlockSpec(memory_space=pltpu.VMEM)
    smem = pl.BlockSpec(memory_space=pltpu.SMEM)
    hbm = pl.BlockSpec(memory_space=pltpu.HBM)
    params = pltpu.CompilerParams(vmem_limit_bytes=(36 if blocks <= 4 else 48) * 1024 * 1024)

    def hold(array):
        return pltpu.with_memory_space_constraint(array, pltpu.HBM)

    def struct(shape, dtype):
        return jax.ShapeDtypeStruct(shape, dtype)

    key_held, value_held = hold(key_rows[0]), hold(values[0])
    depth_held, end_held = hold(depths), hold(subtree_end)
    chunk_rows = 2 * groups * tokens
    messages = pl.pallas_call(
        pack_kernel,
        out_shape=[
            struct((chunk_rows + (0 if chunk else META_ROWS), WIDTH), bf16)
            for chunk in range(CHUNKS)
        ],
        in_specs=[vmem] * 4,
        out_specs=[vmem] * CHUNKS,
        compiler_params=params,
        name="pack",
    )(key_held, value_held, depth_held, end_held)
    arrived = [
        [
            lax.ppermute(message, "ctx", [(i, i ^ s) for i in range(blocks) if i < i ^ s])
            for s in range(1, blocks)
        ]
        for message in messages
    ]

    matmul_flops = 2 * tokens * keys_seen * WIDTH * heads_all
    table = struct((keys_seen, tokens), f32)
    sums = struct((2, heads_all, tokens), f32)
    for chunk in range(CHUNKS):
        last_chunk = chunk == CHUNKS - 1
        operands = [
            hold(slopes),
            hold(ancestor_gain),
            hold(queries[0]),
            hold(outputs[0]),
            hold(out_grads[0]),
            key_held,
            value_held,
            *arrived[chunk],
        ]
        specs = [smem] * 2 + [hbm] * 3 + [vmem] * (1 + blocks)
        part = struct(((chunk + 1) * chunk_rows, WIDTH), bf16)
        out_shape = [struct((tokens, width_all), bf16)] + [part] * blocks
        aliases = {}
        if chunk == 0:
            operands = operands + [hold(file_lengths), depth_held, end_held]
            specs = specs + [smem, vmem, vmem]
            out_shape = out_shape + [table, table]
        else:
            operands = operands + [*tables, sums_before, *parts, query_grads]
            specs = specs + [vmem] * (3 + blocks) + [hbm]
            aliases = {len(operands) - 1: 0}
        out_shape = out_shape + [struct((replicas, 8, WIDTH), f32) if last_chunk else sums]
        scratch = [
            pltpu.VMEM((groups, tokens, group_columns), bf16),
            pltpu.VMEM((groups, tokens, group_columns), bf16),
            pltpu.VMEM((groups, tokens, group_columns), bf16),
            pltpu.VMEM((groups, tokens, group_columns), bf16),
            pltpu.VMEM((2, keys_seen, 2 * tokens), f32),
            pltpu.VMEM((2, keys_seen, group_columns), bf16),
            pltpu.VMEM((2, keys_seen, group_columns), bf16),
            pltpu.SemaphoreType.DMA((3 * groups,)),
            pltpu.SemaphoreType.DMA((groups,)),
        ]
        if last_chunk:
            scratch = scratch + [pltpu.VMEM(sums.shape, f32)]
        results = pl.pallas_call(
            functools.partial(main_kernel, blocks, heads_per_group, groups, chunk, last_chunk),
            out_shape=out_shape,
            in_specs=specs,
            out_specs=[hbm] + [vmem] * (len(out_shape) - 1),
            scratch_shapes=scratch,
            input_output_aliases=aliases,
            compiler_params=params,
            cost_estimate=pl.CostEstimate(
                flops=5 * matmul_flops // CHUNKS,
                bytes_accessed=10 * tokens * width_all // CHUNKS,
                transcendentals=tokens * keys_seen * heads_all // CHUNKS,
            ),
            name=f"attend_{chunk}",
        )(*operands)
        query_grads = results[0]
        parts = list(results[1 : 1 + blocks])
        if chunk == 0:
            tables = results[1 + blocks : 3 + blocks]
        sums_before = results[-1]

    for s in range(1, blocks):
        back = [(i, i ^ s) for i in range(blocks) if i > i ^ s]
        parts[s] = lax.ppermute(parts[s], "ctx", back)
    sums_of_all = lax.all_to_all(sums_before, "dp", split_axis=0, concat_axis=0, tiled=True)
    spread = pl.pallas_call(
        spread_kernel,
        out_shape=struct((blocks, 8, local_heads), f32),
        in_specs=[vmem],
        out_specs=vmem,
        compiler_params=params,
        name="spread",
    )(sums_of_all)
    bias_parts = lax.all_to_all(spread, "ctx", split_axis=0, concat_axis=0, tiled=True)
    bias_grads = pl.pallas_call(
        bias_kernel,
        out_shape=struct((2, local_heads), f32),
        in_specs=[vmem],
        out_specs=vmem,
        compiler_params=params,
        name="bias",
    )(bias_parts)
    key_grads, value_grads = pl.pallas_call(
        functools.partial(combine_kernel, blocks),
        out_shape=[struct((tokens, kv_width), bf16)] * 2,
        in_specs=[vmem] * blocks,
        out_specs=[vmem] * 2,
        compiler_params=params,
        name="combine",
    )(*parts)
    return (query_grads[None], key_grads[None], value_grads[None], bias_grads.T)


def solution(mesh):
    in_specs = (
        P("dp", "ctx", None),
        P("dp", "ctx", None),
        P("dp", "ctx", None),
        P("dp", "ctx", None),
        P("dp", "ctx", None),
        P("dp", "ctx"),
        P("dp", "ctx"),
        P("dp", None),
        P(),
        P(),
    )
    out_specs = (P("dp", "ctx", None), P("dp", "ctx", None), P("dp", "ctx", None), P("ctx", None))
    return jax.shard_map(body, mesh=mesh, in_specs=in_specs, out_specs=out_specs, check_vma=False)
```

```python
import functools

import jax
import jax.numpy as jnp
from jax import lax
from jax.experimental import pallas as pl
from jax.experimental.pallas import tpu as pltpu
from jax.sharding import PartitionSpec as P

WIDTH = 128
LOG2E = 1.4426950408889634
MASKED = -1e30
META_ROWS = 16
END_UNIT = 64


def dot_nt(a, b):
    return lax.dot_general(a, b, (((1,), (1,)), ((), ())), preferred_element_type=jnp.float32)


def dot_nn(a, b):
    return lax.dot_general(a, b, (((1,), (0,)), ((), ())), preferred_element_type=jnp.float32)


def fold_rows(block):
    return jnp.sum(block.reshape(block.shape[0] // 8, 8, block.shape[1]), axis=0)


def as_column(row):
    size = row.shape[1]
    return jnp.transpose(jnp.broadcast_to(row, (size, size)))


def pack_kernel(key_ref, value_ref, depth_ref, end_ref, message_ref):
    tokens = key_ref.shape[0]
    groups = key_ref.shape[1] // WIDTH
    for kind, ref in enumerate((key_ref, value_ref)):
        for group in range(groups):
            at = (kind * groups + group) * tokens
            message_ref[at : at + tokens, :] = ref[:, group * WIDTH : (group + 1) * WIDTH]
    depth = depth_ref[...]
    end = end_ref[...]
    end_high = end // END_UNIT
    end_low = end - end_high * END_UNIT
    row = lax.broadcasted_iota(jnp.int32, (META_ROWS, tokens), 0)
    meta = jnp.where(row == 0, depth, jnp.where(row == 1, end_high, end_low))
    meta = meta.astype(jnp.float32).astype(jnp.bfloat16)
    message_ref[2 * groups * tokens : 2 * groups * tokens + META_ROWS, :] = meta


def main_kernel(
    blocks,
    heads_per_group,
    groups,
    lengths_ref,
    slope_ref,
    gain_ref,
    depth_ref,
    end_ref,
    query_hbm,
    output_hbm,
    grad_hbm,
    key_ref,
    value_ref,
    *refs,
):
    tokens = query_hbm.shape[0]
    remote = refs[0 : blocks - 1]
    query_grad_hbm = refs[blocks - 1]
    part_refs = refs[blocks : 2 * blocks]
    bias_hbm = refs[2 * blocks]
    (
        query_ref,
        output_ref,
        grad_ref,
        query_grad_ref,
        distance_ref,
        ancestor_ref,
        slope_rows,
        gain_rows,
        key_acc,
        value_acc,
        weight_ref,
        probs_ref,
        dscore_ref,
        bias_ref,
        load_sems,
        store_sems,
        bias_sem,
    ) = refs[2 * blocks + 1 :]
    factor = WIDTH**-0.5
    group_columns = heads_per_group * WIDTH
    pairs = heads_per_group // 2

    def load(group, index):
        wide = pl.ds(pl.multiple_of(group * group_columns, group_columns), group_columns)
        source = (query_hbm, output_hbm, grad_hbm)[index]
        to = (query_ref, output_ref, grad_ref)[index]
        return pltpu.make_async_copy(
            source.at[:, wide], to.at[group], load_sems.at[3 * group + index]
        )

    def store(group):
        wide = pl.ds(pl.multiple_of(group * group_columns, group_columns), group_columns)
        return pltpu.make_async_copy(
            query_grad_ref.at[group], query_grad_hbm.at[:, wide], store_sems.at[group]
        )

    for group in range(groups):
        for index in range(3):
            load(group, index).start()

    here = lax.axis_index("ctx")
    query_pos = here * tokens + lax.broadcasted_iota(jnp.int32, (tokens, tokens), 1)
    start = jnp.zeros((tokens, tokens), jnp.int32)
    bound = jnp.int32(0)
    for index in range(lengths_ref.shape[1]):
        bound = bound + lengths_ref[0, index]
        start = jnp.where(query_pos >= bound, bound, start)
    query_depth = jnp.broadcast_to(depth_ref[...].astype(jnp.float32), (tokens, tokens))
    block_rows = [slice(s * tokens, (s + 1) * tokens) for s in range(blocks)]
    for s, rows in enumerate(block_rows):
        key_pos = (here ^ s) * tokens + lax.broadcasted_iota(jnp.int32, (tokens, tokens), 0)
        if s == 0:
            key_depth = as_column(depth_ref[...].astype(jnp.float32))
            key_end = as_column(end_ref[...].astype(jnp.float32))
        else:
            below = slice(2 * groups * tokens, 2 * groups * tokens + META_ROWS)
            meta = remote[s - 1][below, :].astype(jnp.float32)
            key_depth = as_column(meta[0:1])
            key_end = as_column(meta[1:2] * END_UNIT + meta[2:3])
        inside = query_pos.astype(jnp.float32) < key_end
        allowed = (key_pos <= query_pos) & (key_pos >= start)
        distance_ref[rows, :] = jnp.abs(query_depth - key_depth)
        ancestor_ref[rows, :] = jnp.where(allowed, jnp.where(inside, 1.0, 0.0), MASKED)

    def key_block(kind, group, s):
        if s == 0:
            at = pl.multiple_of(group * WIDTH, WIDTH)
            return (key_ref, value_ref)[kind][:, pl.ds(at, WIDTH)]
        at = pl.multiple_of((kind * groups + group) * tokens, tokens)
        return remote[s - 1][pl.ds(at, tokens), :]

    def all_blocks(kind, group):
        return jnp.concatenate([key_block(kind, group, s) for s in range(blocks)], axis=0)

    def stacked(ref, group, first, count):
        heads = [slice((first + i) * WIDTH, (first + i + 1) * WIDTH) for i in range(count)]
        return jnp.concatenate([ref[group, :, h] for h in heads], axis=0)

    def weigh(group, pair, raw, half):
        head = group * heads_per_group + 2 * pair + half
        gain = gain_ref[head] * LOG2E
        slope = slope_ref[head] * LOG2E
        lanes = slice(half * tokens, (half + 1) * tokens)
        tops, totals = [], []
        for s, rows in enumerate(block_rows):
            score = raw[s][:, lanes] * (factor * LOG2E) + (
                gain * ancestor_ref[rows, :] - slope * distance_ref[rows, :]
            )
            top = jnp.max(score, axis=0, keepdims=True)
            weight = jnp.exp2(score - top)
            weight_ref[pair % 2, rows, lanes] = weight
            tops.append(top)
            totals.append(jnp.sum(weight, axis=0, keepdims=True))
        top = functools.reduce(jnp.maximum, tops)
        shrink = [jnp.exp2(t - top) for t in tops]
        inverse = 1.0 / sum(a * b for a, b in zip(totals, shrink))
        return [s * inverse for s in shrink]

    def differentiate(group, pair, centred, scales, half):
        lanes = slice(half * tokens, (half + 1) * tokens)
        to = slice((2 * pair + half) * tokens, (2 * pair + half + 1) * tokens)
        slope_sum, gain_sum = 0.0, 0.0
        for s, rows in enumerate(block_rows):
            probs = weight_ref[pair % 2, rows, lanes] * scales[s]
            dscore = probs * centred[s][:, lanes]
            probs_ref[rows, to] = probs.astype(jnp.bfloat16)
            dscore_ref[rows, to] = dscore.astype(jnp.bfloat16)
            slope_sum = slope_sum + fold_rows(dscore * distance_ref[rows, :])
            gain_sum = gain_sum + fold_rows(dscore * ancestor_ref[rows, :])
        at = pl.ds(group * heads_per_group + 2 * pair + half, 1)
        slope_rows[at, :] = -jnp.sum(slope_sum, axis=0, keepdims=True)
        gain_rows[at, :] = jnp.sum(gain_sum, axis=0, keepdims=True)

    def put_part(group, kind, whole):
        at = pl.multiple_of((kind * groups + group) * tokens, tokens)
        for s, rows in enumerate(block_rows):
            part_refs[s][pl.ds(at, tokens), :] = whole[rows].astype(jnp.bfloat16)

    def key_part(group, first, count):
        heads = stacked(query_ref, group, first, count)
        lanes = slice(first * tokens, (first + count) * tokens)
        return dot_nn(dscore_ref[:, lanes], heads)

    def value_part(group, first, count):
        heads = stacked(grad_ref, group, first, count)
        lanes = slice(first * tokens, (first + count) * tokens)
        return dot_nn(probs_ref[:, lanes], heads)

    def query_part(keys_across, group, pair):
        lanes = slice(2 * pair * tokens, (2 * pair + 2) * tokens)
        across = dot_nn(keys_across, dscore_ref[:, lanes]) * factor
        rows = jnp.transpose(across.astype(jnp.bfloat16))
        for half in range(2):
            at = (2 * pair + half) * WIDTH
            query_grad_ref[group, :, at : at + WIDTH] = rows[half * tokens : (half + 1) * tokens]

    def products(left, right):
        whole = dot_nt(left, right)
        return [whole[rows] for rows in block_rows]

    @pl.loop(0, groups)
    def _(group):
        for index in range(3):
            load(group, index).wait()
        keys = all_blocks(0, group)
        values = all_blocks(1, group)
        value_ext = jnp.concatenate([values, jnp.full(values.shape, -1.0, jnp.bfloat16)], axis=1)
        keys_across = jnp.transpose(keys)
        half_heads = heads_per_group // 2
        for pair in range(pairs):
            query_pair = stacked(query_ref, group, 2 * pair, 2)
            grad_pair = stacked(grad_ref, group, 2 * pair, 2)
            output_pair = stacked(output_ref, group, 2 * pair, 2)
            grad_ext = jnp.concatenate([grad_pair, grad_pair * output_pair], axis=1)
            raw = products(keys, query_pair)
            if pair == pairs // 2:
                key_acc[...] = key_part(group, 0, half_heads)
            scales = [weigh(group, pair, raw, half) for half in range(2)]
            if pair == pairs // 2:
                value_acc[...] = value_part(group, 0, half_heads)
            if pair:
                query_part(keys_across, group, pair - 1)
            centred = products(value_ext, grad_ext)
            for half in range(2):
                differentiate(group, pair, centred, scales[half], half)
        key_whole = key_acc[...] + key_part(group, half_heads, half_heads)
        put_part(group, 0, key_whole * factor)
        put_part(group, 1, value_acc[...] + value_part(group, half_heads, half_heads))
        query_part(keys_across, group, pairs - 1)
        store(group).start()

    slope_sum = jnp.sum(slope_rows[...], axis=1, keepdims=True)
    gain_sum = jnp.sum(gain_rows[...], axis=1, keepdims=True)
    shape = slope_rows.shape
    lane = lax.broadcasted_iota(jnp.int32, shape, 1)
    row = lax.broadcasted_iota(jnp.int32, shape, 0)
    replicas, parts, rows_here, local = bias_ref.shape
    local_heads = shape[0] // parts
    kind = lax.broadcasted_iota(jnp.int32, (rows_here, local), 0)
    for part in range(parts):
        mine = (lane == row - part * local_heads) & (lane < local_heads)
        slope_line = jnp.sum(jnp.where(mine, slope_sum, 0.0), axis=0, keepdims=True)
        gain_line = jnp.sum(jnp.where(mine, gain_sum, 0.0), axis=0, keepdims=True)
        tile = jnp.where(kind == 0, slope_line, jnp.where(kind == 1, gain_line, 0.0))
        bias_ref[:, part] = jnp.broadcast_to(tile[None], (replicas, rows_here, local))
    bias_copy = pltpu.make_async_copy(bias_ref, bias_hbm, bias_sem)
    bias_copy.start()
    for group in range(groups):
        store(group).wait()
    bias_copy.wait()


def combine_kernel(blocks, *refs):
    parts = refs[0:blocks]
    key_out, value_out = refs[blocks:]
    tokens = key_out.shape[0]
    groups = key_out.shape[1] // WIDTH
    for kind, out in enumerate((key_out, value_out)):
        for group in range(groups):
            at = (kind * groups + group) * tokens
            total = parts[0][at : at + tokens, :].astype(jnp.float32)
            for s in range(1, blocks):
                total = total + parts[s][at : at + tokens, :].astype(jnp.float32)
            out[:, group * WIDTH : (group + 1) * WIDTH] = total.astype(jnp.bfloat16)


def bias_kernel(parts_ref, _, out_ref):
    out_ref[...] = jnp.sum(parts_ref[...], axis=0)[0:2, 0 : out_ref.shape[1]]


def body(
    queries,
    key_rows,
    values,
    outputs,
    out_grads,
    depths,
    subtree_end,
    file_lengths,
    slopes,
    ancestor_gain,
):
    blocks = lax.axis_size("ctx")
    replicas = lax.axis_size("dp")
    tokens, width_all = queries.shape[1:]
    kv_width = key_rows.shape[2]
    heads_all = width_all // WIDTH
    groups = kv_width // WIDTH
    heads_per_group = heads_all // groups
    group_columns = heads_per_group * WIDTH
    local_heads = heads_all // blocks
    keys_seen = blocks * tokens
    bf16, f32 = jnp.bfloat16, jnp.float32
    vmem = pl.BlockSpec(memory_space=pltpu.VMEM)
    smem = pl.BlockSpec(memory_space=pltpu.SMEM)
    hbm = pl.BlockSpec(memory_space=pltpu.HBM)
    params = pltpu.CompilerParams(vmem_limit_bytes=(40 if blocks <= 4 else 56) * 1024 * 1024)

    def hold(array):
        return pltpu.with_memory_space_constraint(array, pltpu.HBM)

    key_held, value_held = hold(key_rows[0]), hold(values[0])
    depth_held, end_held = hold(depths), hold(subtree_end)
    message_rows = 2 * groups * tokens
    message = pl.pallas_call(
        pack_kernel,
        out_shape=jax.ShapeDtypeStruct((message_rows + META_ROWS, WIDTH), bf16),
        in_specs=[vmem] * 4,
        out_specs=vmem,
        compiler_params=params,
        name="pack",
    )(key_held, value_held, depth_held, end_held)
    arrived = [
        lax.ppermute(message, "ctx", [(i, i ^ s) for i in range(blocks) if i < i ^ s])
        for s in range(1, blocks)
    ]

    bias_shape = (replicas, blocks, 8, WIDTH)
    matmul_flops = 2 * tokens * keys_seen * WIDTH * heads_all
    results = pl.pallas_call(
        functools.partial(main_kernel, blocks, heads_per_group, groups),
        out_shape=[jax.ShapeDtypeStruct((tokens, width_all), bf16)]
        + [jax.ShapeDtypeStruct((message_rows, WIDTH), bf16)] * blocks
        + [jax.ShapeDtypeStruct(bias_shape, f32)],
        in_specs=[smem] * 3 + [vmem] * 2 + [hbm] * 3 + [vmem] * (1 + blocks),
        out_specs=[hbm] + [vmem] * blocks + [hbm],
        scratch_shapes=[
            pltpu.VMEM((groups, tokens, group_columns), bf16),
            pltpu.VMEM((groups, tokens, group_columns), bf16),
            pltpu.VMEM((groups, tokens, group_columns), bf16),
            pltpu.VMEM((groups, tokens, group_columns), bf16),
            pltpu.VMEM((keys_seen, tokens), f32),
            pltpu.VMEM((keys_seen, tokens), f32),
            pltpu.VMEM((heads_all, tokens), f32),
            pltpu.VMEM((heads_all, tokens), f32),
            pltpu.VMEM((keys_seen, WIDTH), f32),
            pltpu.VMEM((keys_seen, WIDTH), f32),
            pltpu.VMEM((2, keys_seen, 2 * tokens), f32),
            pltpu.VMEM((keys_seen, group_columns), bf16),
            pltpu.VMEM((keys_seen, group_columns), bf16),
            pltpu.VMEM(bias_shape, f32),
            pltpu.SemaphoreType.DMA((3 * groups,)),
            pltpu.SemaphoreType.DMA((groups,)),
            pltpu.SemaphoreType.DMA,
        ],
        compiler_params=params,
        cost_estimate=pl.CostEstimate(
            flops=5 * matmul_flops,
            bytes_accessed=10 * tokens * width_all,
            transcendentals=tokens * keys_seen * heads_all,
        ),
        name="attend",
    )(
        hold(file_lengths),
        hold(slopes),
        hold(ancestor_gain),
        depth_held,
        end_held,
        hold(queries[0]),
        hold(outputs[0]),
        hold(out_grads[0]),
        key_held,
        value_held,
        *arrived,
    )
    query_grads = results[0]
    parts = list(results[1 : 1 + blocks])
    bias_parts = results[1 + blocks].reshape(replicas * blocks, 8, WIDTH)
    for s in range(1, blocks):
        back = [(i, i ^ s) for i in range(blocks) if i > i ^ s]
        parts[s] = lax.ppermute(parts[s], "ctx", back)
    bias_parts = lax.all_to_all(bias_parts, ("dp", "ctx"), split_axis=0, concat_axis=0, tiled=True)

    key_grads, value_grads = pl.pallas_call(
        functools.partial(combine_kernel, blocks),
        out_shape=[jax.ShapeDtypeStruct((tokens, kv_width), bf16)] * 2,
        in_specs=[vmem] * blocks,
        out_specs=[vmem] * 2,
        compiler_params=params,
        cost_estimate=pl.CostEstimate(
            flops=2 * message_rows * WIDTH * blocks,
            bytes_accessed=2 * message_rows * WIDTH * (blocks + 1),
            transcendentals=0,
        ),
        name="combine",
    )(*parts)
    bias_grads = pl.pallas_call(
        bias_kernel,
        out_shape=jax.ShapeDtypeStruct((2, local_heads), f32),
        in_specs=[vmem, hbm],
        out_specs=vmem,
        compiler_params=params,
        name="bias",
    )(bias_parts, key_grads)
    return (query_grads[None], key_grads[None], value_grads[None], bias_grads.T)


def solution(mesh):
    in_specs = (
        P("dp", "ctx", None),
        P("dp", "ctx", None),
        P("dp", "ctx", None),
        P("dp", "ctx", None),
        P("dp", "ctx", None),
        P("dp", "ctx"),
        P("dp", "ctx"),
        P("dp", None),
        P(),
        P(),
    )
    out_specs = (P("dp", "ctx", None), P("dp", "ctx", None), P("dp", "ctx", None), P("ctx", None))
    return jax.shard_map(body, mesh=mesh, in_specs=in_specs, out_specs=out_specs, check_vma=False)
```

```python
import functools

import jax
import jax.numpy as jnp
from jax import lax
from jax.experimental import pallas as pl
from jax.experimental.pallas import tpu as pltpu
from jax.sharding import PartitionSpec as P

WIDTH = 128
LOG2E = 1.4426950408889634
MASKED = -1e30
META_ROWS = 16
END_UNIT = 64


def dot_nt(a, b):
    return lax.dot_general(a, b, (((1,), (1,)), ((), ())), preferred_element_type=jnp.float32)


def dot_nn(a, b):
    return lax.dot_general(a, b, (((1,), (0,)), ((), ())), preferred_element_type=jnp.float32)


def fold_rows(block):
    return jnp.sum(block.reshape(block.shape[0] // 8, 8, block.shape[1]), axis=0)


def as_column(row):
    size = row.shape[1]
    return jnp.transpose(jnp.broadcast_to(row, (size, size)))


def pack_kernel(key_ref, value_ref, depth_ref, end_ref, key_message, value_message):
    tokens = key_ref.shape[0]
    groups = key_ref.shape[1] // WIDTH
    for group in range(groups):
        rows = slice(group * tokens, (group + 1) * tokens)
        columns = slice(group * WIDTH, (group + 1) * WIDTH)
        key_message[rows, :] = key_ref[:, columns]
        value_message[rows, :] = value_ref[:, columns]
    depth = depth_ref[...]
    end = end_ref[...]
    end_high = end // END_UNIT
    end_low = end - end_high * END_UNIT
    row = lax.broadcasted_iota(jnp.int32, (META_ROWS, tokens), 0)
    meta = jnp.where(row == 0, depth, jnp.where(row == 1, end_high, end_low))
    meta = meta.astype(jnp.float32).astype(jnp.bfloat16)
    key_message[groups * tokens : groups * tokens + META_ROWS, :] = meta


def fill_tables(groups, lengths_ref, depth_ref, end_ref, remote, distance_ref, ancestor_ref):
    tokens = depth_ref.shape[1]
    here = lax.axis_index("ctx")
    query_pos = here * tokens + lax.broadcasted_iota(jnp.int32, (tokens, tokens), 1)
    start = jnp.zeros((tokens, tokens), jnp.int32)
    bound = jnp.int32(0)
    for index in range(lengths_ref.shape[1]):
        bound = bound + lengths_ref[0, index]
        start = jnp.where(query_pos >= bound, bound, start)
    query_depth = jnp.broadcast_to(depth_ref[...].astype(jnp.float32), (tokens, tokens))
    for s in range(1 + len(remote)):
        rows = slice(s * tokens, (s + 1) * tokens)
        key_pos = (here ^ s) * tokens + lax.broadcasted_iota(jnp.int32, (tokens, tokens), 0)
        if s == 0:
            key_depth = as_column(depth_ref[...].astype(jnp.float32))
            key_end = as_column(end_ref[...].astype(jnp.float32))
        else:
            below = slice(groups * tokens, groups * tokens + META_ROWS)
            meta = remote[s - 1][below, :].astype(jnp.float32)
            key_depth = as_column(meta[0:1])
            key_end = as_column(meta[1:2] * END_UNIT + meta[2:3])
        inside = query_pos.astype(jnp.float32) < key_end
        allowed = (key_pos <= query_pos) & (key_pos >= start)
        distance_ref[rows, :] = jnp.abs(query_depth - key_depth)
        ancestor_ref[rows, :] = jnp.where(allowed, jnp.where(inside, 1.0, 0.0), MASKED)


def all_blocks(own_ref, remote, group):
    tokens = own_ref.shape[0]
    own = own_ref[:, pl.ds(pl.multiple_of(group * WIDTH, WIDTH), WIDTH)]
    at = pl.multiple_of(group * tokens, tokens)
    return jnp.concatenate([own] + [r[pl.ds(at, tokens), :] for r in remote], axis=0)


def stacked(ref, group, first, count):
    heads = [slice((first + i) * WIDTH, (first + i + 1) * WIDTH) for i in range(count)]
    return jnp.concatenate([ref[group, :, h] for h in heads], axis=0)


def group_columns(group, columns):
    return pl.ds(pl.multiple_of(group * columns, columns), columns)


def group_loads(group, sources, targets, sems):
    columns = targets[0].shape[2]
    return [
        pltpu.make_async_copy(
            source.at[:, group_columns(group, columns)],
            target.at[group],
            sems.at[len(sources) * group + index],
        )
        for index, (source, target) in enumerate(zip(sources, targets))
    ]


def put_part(part_refs, group, whole):
    tokens = whole.shape[0] // len(part_refs)
    at = pl.multiple_of(group * tokens, tokens)
    for s, part_ref in enumerate(part_refs):
        part = whole[s * tokens : (s + 1) * tokens].astype(jnp.bfloat16)
        part_ref[pl.ds(at, tokens), :] = part


def weigh_kernel(blocks, heads_per_group, groups, *refs):
    refs = list(refs)
    take = lambda count: [refs.pop(0) for _ in range(count)]
    lengths_ref, slope_ref, gain_ref, depth_ref, end_ref, query_hbm, grad_hbm, key_ref = take(8)
    remote = take(blocks - 1)
    probs_ref, distance_ref, ancestor_ref = take(3)
    part_refs = take(blocks)
    query_ref, grad_ref, weight_ref, value_acc, load_sems = refs
    tokens = query_hbm.shape[0]
    factor = WIDTH**-0.5
    pairs = heads_per_group // 2
    block_rows = [slice(s * tokens, (s + 1) * tokens) for s in range(blocks)]

    def loads(group):
        return group_loads(group, (query_hbm, grad_hbm), (query_ref, grad_ref), load_sems)

    for group in range(groups):
        for load in loads(group):
            load.start()
    fill_tables(groups, lengths_ref, depth_ref, end_ref, remote, distance_ref, ancestor_ref)

    def weigh(group, pair, raw, half):
        head = group * heads_per_group + 2 * pair + half
        gain = gain_ref[head] * LOG2E
        slope = slope_ref[head] * LOG2E
        lanes = slice(half * tokens, (half + 1) * tokens)
        tops, totals = [], []
        for rows in block_rows:
            score = raw[rows, lanes] * (factor * LOG2E) + (
                gain * ancestor_ref[rows, :] - slope * distance_ref[rows, :]
            )
            top = jnp.max(score, axis=0, keepdims=True)
            weight = jnp.exp2(score - top)
            weight_ref[pair % 2, rows, lanes] = weight
            tops.append(top)
            totals.append(jnp.sum(weight, axis=0, keepdims=True))
        top = functools.reduce(jnp.maximum, tops)
        shrink = [jnp.exp2(t - top) for t in tops]
        inverse = 1.0 / sum(a * b for a, b in zip(totals, shrink))
        return [s * inverse for s in shrink]

    def value_part(group, first, count):
        lanes = slice(first * tokens, (first + count) * tokens)
        return dot_nn(probs_ref[group, :, lanes], stacked(grad_ref, group, first, count))

    @pl.loop(0, groups)
    def _(group):
        for load in loads(group):
            load.wait()
        keys = all_blocks(key_ref, remote, group)
        half_heads = heads_per_group // 2
        for pair in range(pairs):
            raw = dot_nt(keys, stacked(query_ref, group, 2 * pair, 2))
            if pair == pairs // 2:
                value_acc[...] = value_part(group, 0, half_heads)
            scales = [weigh(group, pair, raw, half) for half in range(2)]
            for half in range(2):
                lanes = slice(half * tokens, (half + 1) * tokens)
                to = slice((2 * pair + half) * tokens, (2 * pair + half + 1) * tokens)
                for rows, scale in zip(block_rows, scales[half]):
                    probs = weight_ref[pair % 2, rows, lanes] * scale
                    probs_ref[group, rows, to] = probs.astype(jnp.bfloat16)
        put_part(part_refs, group, value_acc[...] + value_part(group, half_heads, half_heads))


def grad_kernel(blocks, heads_per_group, groups, *refs):
    refs = list(refs)
    take = lambda count: [refs.pop(0) for _ in range(count)]
    probs_ref, distance_ref, ancestor_ref = take(3)
    query_hbm, output_hbm, grad_hbm, key_ref, value_ref = take(5)
    remote_key = take(blocks - 1)
    remote_value = take(blocks - 1)
    (query_grad_hbm,) = take(1)
    part_refs = take(blocks)
    (bias_hbm,) = take(1)
    (
        query_ref,
        output_ref,
        grad_ref,
        query_grad_ref,
        dscore_ref,
        key_acc,
        slope_rows,
        gain_rows,
        bias_ref,
        load_sems,
        store_sems,
        bias_sem,
    ) = refs
    tokens = query_hbm.shape[0]
    factor = WIDTH**-0.5
    pairs = heads_per_group // 2
    block_rows = [slice(s * tokens, (s + 1) * tokens) for s in range(blocks)]

    def loads(group):
        sources = (query_hbm, output_hbm, grad_hbm)
        return group_loads(group, sources, (query_ref, output_ref, grad_ref), load_sems)

    def store(group):
        columns = group_columns(group, query_grad_ref.shape[2])
        return pltpu.make_async_copy(
            query_grad_ref.at[group], query_grad_hbm.at[:, columns], store_sems.at[group]
        )

    for group in range(groups):
        for load in loads(group):
            load.start()

    def differentiate(group, pair, centred, half):
        lanes = slice(half * tokens, (half + 1) * tokens)
        to = slice((2 * pair + half) * tokens, (2 * pair + half + 1) * tokens)
        slope_sum, gain_sum = 0.0, 0.0
        for rows in block_rows:
            probs = probs_ref[group, rows, to].astype(jnp.float32)
            dscore = probs * centred[rows, lanes]
            dscore_ref[rows, to] = dscore.astype(jnp.bfloat16)
            slope_sum = slope_sum + fold_rows(dscore * distance_ref[rows, :])
            gain_sum = gain_sum + fold_rows(dscore * ancestor_ref[rows, :])
        at = pl.ds(group * heads_per_group + 2 * pair + half, 1)
        slope_rows[at, :] = -jnp.sum(slope_sum, axis=0, keepdims=True)
        gain_rows[at, :] = jnp.sum(gain_sum, axis=0, keepdims=True)

    def key_part(group, first, count):
        lanes = slice(first * tokens, (first + count) * tokens)
        return dot_nn(dscore_ref[:, lanes], stacked(query_ref, group, first, count))

    def query_part(keys_across, group, pair):
        lanes = slice(2 * pair * tokens, (2 * pair + 2) * tokens)
        across = dot_nn(keys_across, dscore_ref[:, lanes]) * factor
        rows = jnp.transpose(across.astype(jnp.bfloat16))
        for half in range(2):
            at = (2 * pair + half) * WIDTH
            query_grad_ref[group, :, at : at + WIDTH] = rows[half * tokens : (half + 1) * tokens]

    @pl.loop(0, groups)
    def _(group):
        for load in loads(group):
            load.wait()
        values = all_blocks(value_ref, remote_value, group)
        value_ext = jnp.concatenate([values, jnp.full(values.shape, -1.0, jnp.bfloat16)], axis=1)
        keys_across = jnp.transpose(all_blocks(key_ref, remote_key, group))
        half_heads = heads_per_group // 2
        for pair in range(pairs):
            grad_pair = stacked(grad_ref, group, 2 * pair, 2)
            output_pair = stacked(output_ref, group, 2 * pair, 2)
            grad_ext = jnp.concatenate([grad_pair, grad_pair * output_pair], axis=1)
            centred = dot_nt(value_ext, grad_ext)
            if pair == pairs // 2:
                key_acc[...] = key_part(group, 0, half_heads)
            if pair:
                query_part(keys_across, group, pair - 1)
            for half in range(2):
                differentiate(group, pair, centred, half)
        key_whole = key_acc[...] + key_part(group, half_heads, half_heads)
        put_part(part_refs, group, key_whole * factor)
        query_part(keys_across, group, pairs - 1)
        store(group).start()

    slope_sum = jnp.sum(slope_rows[...], axis=1, keepdims=True)
    gain_sum = jnp.sum(gain_rows[...], axis=1, keepdims=True)
    shape = slope_rows.shape
    lane = lax.broadcasted_iota(jnp.int32, shape, 1)
    row = lax.broadcasted_iota(jnp.int32, shape, 0)
    replicas, parts, rows_here, local = bias_ref.shape
    local_heads = shape[0] // parts
    kind = lax.broadcasted_iota(jnp.int32, (rows_here, local), 0)
    for part in range(parts):
        mine = (lane == row - part * local_heads) & (lane < local_heads)
        slope_line = jnp.sum(jnp.where(mine, slope_sum, 0.0), axis=0, keepdims=True)
        gain_line = jnp.sum(jnp.where(mine, gain_sum, 0.0), axis=0, keepdims=True)
        tile = jnp.where(kind == 0, slope_line, jnp.where(kind == 1, gain_line, 0.0))
        bias_ref[:, part] = jnp.broadcast_to(tile[None], (replicas, rows_here, local))
    bias_copy = pltpu.make_async_copy(bias_ref, bias_hbm, bias_sem)
    bias_copy.start()
    for group in range(groups):
        store(group).wait()
    bias_copy.wait()


def combine_kernel(blocks, *refs):
    parts = refs[0:blocks]
    out = refs[blocks]
    tokens = out.shape[0]
    for group in range(out.shape[1] // WIDTH):
        rows = slice(group * tokens, (group + 1) * tokens)
        total = parts[0][rows, :].astype(jnp.float32)
        for s in range(1, blocks):
            total = total + parts[s][rows, :].astype(jnp.float32)
        out[:, group * WIDTH : (group + 1) * WIDTH] = total.astype(jnp.bfloat16)


def bias_kernel(parts_ref, _, __, out_ref):
    out_ref[...] = jnp.sum(parts_ref[...], axis=0)[0:2, 0 : out_ref.shape[1]]


def body(
    queries,
    key_rows,
    values,
    outputs,
    out_grads,
    depths,
    subtree_end,
    file_lengths,
    slopes,
    ancestor_gain,
):
    blocks = lax.axis_size("ctx")
    replicas = lax.axis_size("dp")
    tokens, width_all = queries.shape[1:]
    kv_width = key_rows.shape[2]
    heads_all = width_all // WIDTH
    groups = kv_width // WIDTH
    heads_per_group = heads_all // groups
    columns = heads_per_group * WIDTH
    local_heads = heads_all // blocks
    keys_seen = blocks * tokens
    part_rows = groups * tokens
    bf16, f32 = jnp.bfloat16, jnp.float32
    vmem = pl.BlockSpec(memory_space=pltpu.VMEM)
    smem = pl.BlockSpec(memory_space=pltpu.SMEM)
    hbm = pl.BlockSpec(memory_space=pltpu.HBM)
    params = pltpu.CompilerParams(vmem_limit_bytes=(24 if blocks <= 4 else 48) * 1024 * 1024)
    sem = pltpu.SemaphoreType.DMA

    def hold(array):
        return pltpu.with_memory_space_constraint(array, pltpu.HBM)

    def struct(*shape, dtype=bf16):
        return jax.ShapeDtypeStruct(shape, dtype)

    def cost(matmuls, exponentials):
        return pl.CostEstimate(
            flops=matmuls * 2 * tokens * keys_seen * WIDTH * heads_all,
            bytes_accessed=4 * tokens * width_all,
            transcendentals=exponentials * tokens * keys_seen * heads_all,
        )

    def gather(message):
        return [
            lax.ppermute(message, "ctx", [(i, i ^ s) for i in range(blocks) if i < i ^ s])
            for s in range(1, blocks)
        ]

    def give_back(parts):
        back = [[(i, i ^ s) for i in range(blocks) if i > i ^ s] for s in range(1, blocks)]
        return [parts[0]] + [lax.ppermute(p, "ctx", b) for p, b in zip(parts[1:], back)]

    def combine(parts, name):
        return pl.pallas_call(
            functools.partial(combine_kernel, blocks),
            out_shape=struct(tokens, kv_width),
            in_specs=[vmem] * blocks,
            out_specs=vmem,
            compiler_params=params,
            name=name,
        )(*parts)

    query_held, output_held, grad_held = hold(queries[0]), hold(outputs[0]), hold(out_grads[0])
    key_held, value_held = hold(key_rows[0]), hold(values[0])
    depth_held, end_held = hold(depths), hold(subtree_end)
    key_message, value_message = pl.pallas_call(
        pack_kernel,
        out_shape=[struct(part_rows + META_ROWS, WIDTH), struct(part_rows, WIDTH)],
        in_specs=[vmem] * 4,
        out_specs=[vmem] * 2,
        compiler_params=params,
        name="pack",
    )(key_held, value_held, depth_held, end_held)
    key_blocks = gather(key_message)
    value_blocks = gather(value_message)

    table = struct(keys_seen, tokens, dtype=f32)
    probs, distance, ancestor, *value_parts = pl.pallas_call(
        functools.partial(weigh_kernel, blocks, heads_per_group, groups),
        out_shape=[struct(groups, keys_seen, columns), table, table]
        + [struct(part_rows, WIDTH)] * blocks,
        in_specs=[smem] * 3 + [vmem] * 2 + [hbm] * 2 + [vmem] * blocks,
        out_specs=[vmem] * (3 + blocks),
        scratch_shapes=[
            pltpu.VMEM((groups, tokens, columns), bf16),
            pltpu.VMEM((groups, tokens, columns), bf16),
            pltpu.VMEM((2, keys_seen, 2 * tokens), f32),
            pltpu.VMEM((keys_seen, WIDTH), f32),
            sem((2 * groups,)),
        ],
        compiler_params=params,
        cost_estimate=cost(2, 1),
        name="weigh",
    )(
        hold(file_lengths),
        hold(slopes),
        hold(ancestor_gain),
        depth_held,
        end_held,
        query_held,
        grad_held,
        key_held,
        *key_blocks,
    )
    value_parts = give_back(value_parts)

    bias_shape = (replicas, blocks, 8, WIDTH)
    query_grads, *key_parts, bias_parts = pl.pallas_call(
        functools.partial(grad_kernel, blocks, heads_per_group, groups),
        out_shape=[struct(tokens, width_all)]
        + [struct(part_rows, WIDTH)] * blocks
        + [struct(*bias_shape, dtype=f32)],
        in_specs=[vmem] * 3 + [hbm] * 3 + [vmem] * (2 * blocks),
        out_specs=[hbm] + [vmem] * blocks + [hbm],
        scratch_shapes=[
            pltpu.VMEM((groups, tokens, columns), bf16),
            pltpu.VMEM((groups, tokens, columns), bf16),
            pltpu.VMEM((groups, tokens, columns), bf16),
            pltpu.VMEM((groups, tokens, columns), bf16),
            pltpu.VMEM((keys_seen, columns), bf16),
            pltpu.VMEM((keys_seen, WIDTH), f32),
            pltpu.VMEM((heads_all, tokens), f32),
            pltpu.VMEM((heads_all, tokens), f32),
            pltpu.VMEM(bias_shape, f32),
            sem((3 * groups,)),
            sem((groups,)),
            sem,
        ],
        compiler_params=params,
        cost_estimate=cost(3, 0),
        name="grad",
    )(
        probs,
        distance,
        ancestor,
        query_held,
        output_held,
        grad_held,
        key_held,
        value_held,
        *key_blocks,
        *value_blocks,
    )
    key_parts = give_back(key_parts)
    bias_parts = bias_parts.reshape(replicas * blocks, 8, WIDTH)
    bias_parts = lax.all_to_all(bias_parts, ("dp", "ctx"), split_axis=0, concat_axis=0, tiled=True)
    value_grads = combine(value_parts, "combine_values")
    key_grads = combine(key_parts, "combine_keys")
    bias_grads = pl.pallas_call(
        bias_kernel,
        out_shape=struct(2, local_heads, dtype=f32),
        in_specs=[vmem, hbm, hbm],
        out_specs=vmem,
        compiler_params=params,
        name="bias",
    )(bias_parts, hold(key_grads), hold(value_grads))
    return (query_grads[None], key_grads[None], value_grads[None], bias_grads.T)


def solution(mesh):
    in_specs = (
        P("dp", "ctx", None),
        P("dp", "ctx", None),
        P("dp", "ctx", None),
        P("dp", "ctx", None),
        P("dp", "ctx", None),
        P("dp", "ctx"),
        P("dp", "ctx"),
        P("dp", None),
        P(),
        P(),
    )
    out_specs = (P("dp", "ctx", None), P("dp", "ctx", None), P("dp", "ctx", None), P("ctx", None))
    return jax.shard_map(body, mesh=mesh, in_specs=in_specs, out_specs=out_specs, check_vma=False)
```

```python
import functools

import jax
import jax.numpy as jnp
from jax import lax
from jax.experimental import pallas as pl
from jax.experimental.pallas import tpu as pltpu
from jax.sharding import PartitionSpec as P

WIDTH = 128
LOG2E = 1.4426950408889634
MASKED = -1e30
META_ROWS = 16
END_UNIT = 64


def dot_nt(a, b):
    return lax.dot_general(a, b, (((1,), (1,)), ((), ())), preferred_element_type=jnp.float32)


def dot_nn(a, b):
    return lax.dot_general(a, b, (((1,), (0,)), ((), ())), preferred_element_type=jnp.float32)


def fold_rows(block):
    return jnp.sum(block.reshape(block.shape[0] // 8, 8, block.shape[1]), axis=0)


def as_column(row):
    size = row.shape[1]
    return jnp.transpose(jnp.broadcast_to(row, (size, size)))


def pack_kernel(key_ref, value_ref, depth_ref, end_ref, message_ref):
    tokens = key_ref.shape[0]
    groups = key_ref.shape[1] // WIDTH
    for kind, ref in enumerate((key_ref, value_ref)):
        for group in range(groups):
            at = (kind * groups + group) * tokens
            message_ref[at : at + tokens, :] = ref[:, group * WIDTH : (group + 1) * WIDTH]
    depth = depth_ref[...]
    end = end_ref[...]
    end_high = end // END_UNIT
    end_low = end - end_high * END_UNIT
    row = lax.broadcasted_iota(jnp.int32, (META_ROWS, tokens), 0)
    meta = jnp.where(row == 0, depth, jnp.where(row == 1, end_high, end_low))
    meta = meta.astype(jnp.float32).astype(jnp.bfloat16)
    message_ref[2 * groups * tokens : 2 * groups * tokens + META_ROWS, :] = meta


def fill_tables(groups, lengths_ref, depth_ref, end_ref, remote, distance_ref, ancestor_ref):
    tokens = depth_ref.shape[1]
    here = lax.axis_index("ctx")
    query_pos = here * tokens + lax.broadcasted_iota(jnp.int32, (tokens, tokens), 1)
    start = jnp.zeros((tokens, tokens), jnp.int32)
    bound = jnp.int32(0)
    for index in range(lengths_ref.shape[1]):
        bound = bound + lengths_ref[0, index]
        start = jnp.where(query_pos >= bound, bound, start)
    query_depth = jnp.broadcast_to(depth_ref[...].astype(jnp.float32), (tokens, tokens))
    for s in range(1 + len(remote)):
        rows = slice(s * tokens, (s + 1) * tokens)
        key_pos = (here ^ s) * tokens + lax.broadcasted_iota(jnp.int32, (tokens, tokens), 0)
        if s == 0:
            key_depth = as_column(depth_ref[...].astype(jnp.float32))
            key_end = as_column(end_ref[...].astype(jnp.float32))
        else:
            below = slice(2 * groups * tokens, 2 * groups * tokens + META_ROWS)
            meta = remote[s - 1][below, :].astype(jnp.float32)
            key_depth = as_column(meta[0:1])
            key_end = as_column(meta[1:2] * END_UNIT + meta[2:3])
        inside = query_pos.astype(jnp.float32) < key_end
        allowed = (key_pos <= query_pos) & (key_pos >= start)
        distance_ref[rows, :] = jnp.abs(query_depth - key_depth)
        ancestor_ref[rows, :] = jnp.where(allowed, jnp.where(inside, 1.0, 0.0), MASKED)


def all_blocks(own_ref, remote, kind, groups, group):
    tokens = own_ref.shape[0]
    own = own_ref[:, pl.ds(pl.multiple_of(group * WIDTH, WIDTH), WIDTH)]
    at = pl.multiple_of((kind * groups + group) * tokens, tokens)
    return jnp.concatenate([own] + [r[pl.ds(at, tokens), :] for r in remote], axis=0)


def stacked(ref, group, first, count):
    heads = [slice((first + i) * WIDTH, (first + i + 1) * WIDTH) for i in range(count)]
    return jnp.concatenate([ref[group, :, h] for h in heads], axis=0)


def group_columns(group, columns):
    return pl.ds(pl.multiple_of(group * columns, columns), columns)


def group_loads(group, sources, targets, sems):
    columns = targets[0].shape[2]
    return [
        pltpu.make_async_copy(
            source.at[:, group_columns(group, columns)],
            target.at[group],
            sems.at[len(sources) * group + index],
        )
        for index, (source, target) in enumerate(zip(sources, targets))
    ]


def score_kernel(blocks, heads_per_group, groups, *refs):
    refs = list(refs)
    take = lambda count: [refs.pop(0) for _ in range(count)]
    lengths_ref, slope_ref, gain_ref, depth_ref, end_ref = take(5)
    query_hbm, output_hbm, grad_hbm, key_ref, value_ref = take(5)
    remote = take(blocks - 1)
    dscore_ref, own_probs_ref, distance_ref, ancestor_ref = take(4)
    part_refs = take(blocks - 1)
    query_ref, output_ref, grad_ref, weight_ref, probs_ref, key_acc, value_acc, load_sems = refs
    tokens = query_hbm.shape[0]
    factor = WIDTH**-0.5
    pairs = heads_per_group // 2
    block_rows = [slice(s * tokens, (s + 1) * tokens) for s in range(blocks)]

    def loads(group):
        sources = (query_hbm, output_hbm, grad_hbm)
        return group_loads(group, sources, (query_ref, output_ref, grad_ref), load_sems)

    for group in range(groups):
        for load in loads(group):
            load.start()
    fill_tables(groups, lengths_ref, depth_ref, end_ref, remote, distance_ref, ancestor_ref)

    def weigh(group, pair, raw, half):
        head = group * heads_per_group + 2 * pair + half
        gain = gain_ref[head] * LOG2E
        slope = slope_ref[head] * LOG2E
        lanes = slice(half * tokens, (half + 1) * tokens)
        tops, totals = [], []
        for rows in block_rows:
            score = raw[rows, lanes] * (factor * LOG2E) + (
                gain * ancestor_ref[rows, :] - slope * distance_ref[rows, :]
            )
            top = jnp.max(score, axis=0, keepdims=True)
            weight = jnp.exp2(score - top)
            weight_ref[pair % 2, rows, lanes] = weight
            tops.append(top)
            totals.append(jnp.sum(weight, axis=0, keepdims=True))
        top = functools.reduce(jnp.maximum, tops)
        shrink = [jnp.exp2(t - top) for t in tops]
        inverse = 1.0 / sum(a * b for a, b in zip(totals, shrink))
        return [s * inverse for s in shrink]

    def differentiate(group, pair, centred, scales, half):
        lanes = slice(half * tokens, (half + 1) * tokens)
        to = slice((2 * pair + half) * tokens, (2 * pair + half + 1) * tokens)
        for s, (rows, scale) in enumerate(zip(block_rows, scales)):
            probs = weight_ref[pair % 2, rows, lanes] * scale
            dscore_ref[group, rows, to] = (probs * centred[rows, lanes]).astype(jnp.bfloat16)
            probs_b = probs.astype(jnp.bfloat16)
            if s == 0:
                own_probs_ref[group, :, to] = probs_b
            else:
                probs_ref[(s - 1) * tokens : s * tokens, to] = probs_b

    def key_part(group, first, count):
        lanes = slice(first * tokens, (first + count) * tokens)
        return dot_nn(dscore_ref[group, tokens:, lanes], stacked(query_ref, group, first, count))

    def value_part(group, first, count):
        lanes = slice(first * tokens, (first + count) * tokens)
        return dot_nn(probs_ref[:, lanes], stacked(grad_ref, group, first, count))

    def put_part(group, kind, whole):
        at = pl.multiple_of((kind * groups + group) * tokens, tokens)
        for s, part_ref in enumerate(part_refs):
            part = whole[s * tokens : (s + 1) * tokens].astype(jnp.bfloat16)
            part_ref[pl.ds(at, tokens), :] = part

    @pl.loop(0, groups)
    def _(group):
        for load in loads(group):
            load.wait()
        keys = all_blocks(key_ref, remote, 0, groups, group)
        values = all_blocks(value_ref, remote, 1, groups, group)
        value_ext = jnp.concatenate([values, jnp.full(values.shape, -1.0, jnp.bfloat16)], axis=1)
        half_heads = heads_per_group // 2
        for pair in range(pairs):
            query_pair = stacked(query_ref, group, 2 * pair, 2)
            grad_pair = stacked(grad_ref, group, 2 * pair, 2)
            output_pair = stacked(output_ref, group, 2 * pair, 2)
            grad_ext = jnp.concatenate([grad_pair, grad_pair * output_pair], axis=1)
            raw = dot_nt(keys, query_pair)
            if pair == pairs // 2:
                key_acc[...] = key_part(group, 0, half_heads)
            scales = [weigh(group, pair, raw, half) for half in range(2)]
            if pair == pairs // 2:
                value_acc[...] = value_part(group, 0, half_heads)
            centred = dot_nt(value_ext, grad_ext)
            for half in range(2):
                differentiate(group, pair, centred, scales[half], half)
        key_whole = key_acc[...] + key_part(group, half_heads, half_heads)
        put_part(group, 0, key_whole * factor)
        put_part(group, 1, value_acc[...] + value_part(group, half_heads, half_heads))


def local_kernel(blocks, heads_per_group, groups, *refs):
    refs = list(refs)
    take = lambda count: [refs.pop(0) for _ in range(count)]
    dscore_ref, own_probs_ref, distance_ref, ancestor_ref = take(4)
    query_hbm, grad_hbm, key_ref = take(3)
    remote = take(blocks - 1)
    query_grad_hbm, own_part_ref, bias_hbm = take(3)
    (
        query_ref,
        grad_ref,
        query_grad_ref,
        slope_rows,
        gain_rows,
        bias_ref,
        load_sems,
        store_sems,
        bias_sem,
    ) = refs
    tokens = query_hbm.shape[0]
    factor = WIDTH**-0.5
    pairs = heads_per_group // 2
    block_rows = [slice(s * tokens, (s + 1) * tokens) for s in range(blocks)]

    def loads(group):
        return group_loads(group, (query_hbm, grad_hbm), (query_ref, grad_ref), load_sems)

    def store(group):
        columns = group_columns(group, query_grad_ref.shape[2])
        return pltpu.make_async_copy(
            query_grad_ref.at[group], query_grad_hbm.at[:, columns], store_sems.at[group]
        )

    for group in range(groups):
        for load in loads(group):
            load.start()

    def sum_up(group, head):
        lanes = slice(head * tokens, (head + 1) * tokens)
        slope_sum, gain_sum = 0.0, 0.0
        for rows in block_rows:
            dscore = dscore_ref[group, rows, lanes].astype(jnp.float32)
            slope_sum = slope_sum + fold_rows(dscore * distance_ref[rows, :])
            gain_sum = gain_sum + fold_rows(dscore * ancestor_ref[rows, :])
        at = pl.ds(group * heads_per_group + head, 1)
        slope_rows[at, :] = -jnp.sum(slope_sum, axis=0, keepdims=True)
        gain_rows[at, :] = jnp.sum(gain_sum, axis=0, keepdims=True)

    @pl.loop(0, groups)
    def _(group):
        for load in loads(group):
            load.wait()
        keys_across = jnp.transpose(all_blocks(key_ref, remote, 0, groups, group))
        at = pl.multiple_of(group * tokens, tokens)
        own = dot_nn(dscore_ref[group, 0:tokens, :], stacked(query_ref, group, 0, heads_per_group))
        own_part_ref[pl.ds(at, tokens), :] = (own * factor).astype(jnp.bfloat16)
        for pair in range(pairs):
            lanes = slice(2 * pair * tokens, (2 * pair + 2) * tokens)
            across = dot_nn(keys_across, dscore_ref[group, :, lanes]) * factor
            for half in range(2):
                sum_up(group, 2 * pair + half)
            rows = jnp.transpose(across.astype(jnp.bfloat16))
            for half in range(2):
                to = slice((2 * pair + half) * WIDTH, (2 * pair + half + 1) * WIDTH)
                query_grad_ref[group, :, to] = rows[half * tokens : (half + 1) * tokens]
        at = pl.multiple_of((groups + group) * tokens, tokens)
        own = dot_nn(own_probs_ref[group], stacked(grad_ref, group, 0, heads_per_group))
        own_part_ref[pl.ds(at, tokens), :] = own.astype(jnp.bfloat16)
        store(group).start()

    slope_sum = jnp.sum(slope_rows[...], axis=1, keepdims=True)
    gain_sum = jnp.sum(gain_rows[...], axis=1, keepdims=True)
    shape = slope_rows.shape
    lane = lax.broadcasted_iota(jnp.int32, shape, 1)
    row = lax.broadcasted_iota(jnp.int32, shape, 0)
    replicas, parts, rows_here, local = bias_ref.shape
    local_heads = shape[0] // parts
    kind = lax.broadcasted_iota(jnp.int32, (rows_here, local), 0)
    for part in range(parts):
        mine = (lane == row - part * local_heads) & (lane < local_heads)
        slope_line = jnp.sum(jnp.where(mine, slope_sum, 0.0), axis=0, keepdims=True)
        gain_line = jnp.sum(jnp.where(mine, gain_sum, 0.0), axis=0, keepdims=True)
        tile = jnp.where(kind == 0, slope_line, jnp.where(kind == 1, gain_line, 0.0))
        bias_ref[:, part] = jnp.broadcast_to(tile[None], (replicas, rows_here, local))
    bias_copy = pltpu.make_async_copy(bias_ref, bias_hbm, bias_sem)
    bias_copy.start()
    for group in range(groups):
        store(group).wait()
    bias_copy.wait()


def combine_kernel(blocks, *refs):
    parts = refs[0:blocks]
    key_out, value_out = refs[blocks:]
    tokens = key_out.shape[0]
    groups = key_out.shape[1] // WIDTH
    for kind, out in enumerate((key_out, value_out)):
        for group in range(groups):
            at = (kind * groups + group) * tokens
            total = parts[0][at : at + tokens, :].astype(jnp.float32)
            for s in range(1, blocks):
                total = total + parts[s][at : at + tokens, :].astype(jnp.float32)
            out[:, group * WIDTH : (group + 1) * WIDTH] = total.astype(jnp.bfloat16)


def bias_kernel(parts_ref, _, out_ref):
    out_ref[...] = jnp.sum(parts_ref[...], axis=0)[0:2, 0 : out_ref.shape[1]]


def body(
    queries,
    key_rows,
    values,
    outputs,
    out_grads,
    depths,
    subtree_end,
    file_lengths,
    slopes,
    ancestor_gain,
):
    blocks = lax.axis_size("ctx")
    replicas = lax.axis_size("dp")
    tokens, width_all = queries.shape[1:]
    kv_width = key_rows.shape[2]
    heads_all = width_all // WIDTH
    groups = kv_width // WIDTH
    heads_per_group = heads_all // groups
    columns = heads_per_group * WIDTH
    local_heads = heads_all // blocks
    keys_seen = blocks * tokens
    message_rows = 2 * groups * tokens
    bf16, f32 = jnp.bfloat16, jnp.float32
    vmem = pl.BlockSpec(memory_space=pltpu.VMEM)
    smem = pl.BlockSpec(memory_space=pltpu.SMEM)
    hbm = pl.BlockSpec(memory_space=pltpu.HBM)
    params = pltpu.CompilerParams(vmem_limit_bytes=(24 if blocks <= 4 else 48) * 1024 * 1024)
    sem = pltpu.SemaphoreType.DMA

    def hold(array):
        return pltpu.with_memory_space_constraint(array, pltpu.HBM)

    def struct(*shape, dtype=bf16):
        return jax.ShapeDtypeStruct(shape, dtype)

    def cost(matmuls, exponentials):
        return pl.CostEstimate(
            flops=matmuls * 2 * tokens * keys_seen * WIDTH * heads_all,
            bytes_accessed=4 * tokens * width_all,
            transcendentals=exponentials * tokens * keys_seen * heads_all,
        )

    query_held, output_held, grad_held = hold(queries[0]), hold(outputs[0]), hold(out_grads[0])
    key_held, value_held = hold(key_rows[0]), hold(values[0])
    depth_held, end_held = hold(depths), hold(subtree_end)
    message = pl.pallas_call(
        pack_kernel,
        out_shape=struct(message_rows + META_ROWS, WIDTH),
        in_specs=[vmem] * 4,
        out_specs=vmem,
        compiler_params=params,
        name="pack",
    )(key_held, value_held, depth_held, end_held)
    arrived = [
        lax.ppermute(message, "ctx", [(i, i ^ s) for i in range(blocks) if i < i ^ s])
        for s in range(1, blocks)
    ]

    table = struct(keys_seen, tokens, dtype=f32)
    wide = pltpu.VMEM((groups, tokens, columns), bf16)
    dscore, own_probs, distance, ancestor, *parts = pl.pallas_call(
        functools.partial(score_kernel, blocks, heads_per_group, groups),
        out_shape=[
            struct(groups, keys_seen, columns),
            struct(groups, tokens, columns),
            table,
            table,
        ]
        + [struct(message_rows, WIDTH)] * (blocks - 1),
        in_specs=[smem] * 3 + [vmem] * 2 + [hbm] * 3 + [vmem] * (1 + blocks),
        out_specs=[vmem] * (3 + blocks),
        scratch_shapes=[
            wide,
            wide,
            wide,
            pltpu.VMEM((2, keys_seen, 2 * tokens), f32),
            pltpu.VMEM((keys_seen - tokens, columns), bf16),
            pltpu.VMEM((keys_seen - tokens, WIDTH), f32),
            pltpu.VMEM((keys_seen - tokens, WIDTH), f32),
            sem((3 * groups,)),
        ],
        compiler_params=params,
        cost_estimate=cost(4, 1),
        name="scores",
    )(
        hold(file_lengths),
        hold(slopes),
        hold(ancestor_gain),
        depth_held,
        end_held,
        query_held,
        output_held,
        grad_held,
        key_held,
        value_held,
        *arrived,
    )
    returned = []
    for s in reversed(range(1, blocks)):
        back = [(i, i ^ s) for i in range(blocks) if i > i ^ s]
        returned.append(lax.ppermute(parts[s - 1], "ctx", back))

    bias_shape = (replicas, blocks, 8, WIDTH)
    query_grads, own_part, bias_parts = pl.pallas_call(
        functools.partial(local_kernel, blocks, heads_per_group, groups),
        out_shape=[
            struct(tokens, width_all),
            struct(message_rows, WIDTH),
            struct(*bias_shape, dtype=f32),
        ],
        in_specs=[vmem] * 4 + [hbm] * 2 + [vmem] * blocks,
        out_specs=[hbm, vmem, hbm],
        scratch_shapes=[
            wide,
            wide,
            wide,
            pltpu.VMEM((heads_all, tokens), f32),
            pltpu.VMEM((heads_all, tokens), f32),
            pltpu.VMEM(bias_shape, f32),
            sem((2 * groups,)),
            sem((groups,)),
            sem,
        ],
        compiler_params=params,
        cost_estimate=cost(2, 0),
        name="local",
    )(dscore, own_probs, distance, ancestor, query_held, grad_held, key_held, *arrived)
    bias_parts = bias_parts.reshape(replicas * blocks, 8, WIDTH)
    bias_parts = lax.all_to_all(bias_parts, ("dp", "ctx"), split_axis=0, concat_axis=0, tiled=True)
    key_grads, value_grads = pl.pallas_call(
        functools.partial(combine_kernel, blocks),
        out_shape=[struct(tokens, kv_width)] * 2,
        in_specs=[vmem] * blocks,
        out_specs=[vmem] * 2,
        compiler_params=params,
        name="combine",
    )(own_part, *returned)
    bias_grads = pl.pallas_call(
        bias_kernel,
        out_shape=struct(2, local_heads, dtype=f32),
        in_specs=[vmem, hbm],
        out_specs=vmem,
        compiler_params=params,
        name="bias",
    )(bias_parts, hold(key_grads))
    return (query_grads[None], key_grads[None], value_grads[None], bias_grads.T)


def solution(mesh):
    in_specs = (
        P("dp", "ctx", None),
        P("dp", "ctx", None),
        P("dp", "ctx", None),
        P("dp", "ctx", None),
        P("dp", "ctx", None),
        P("dp", "ctx"),
        P("dp", "ctx"),
        P("dp", None),
        P(),
        P(),
    )
    out_specs = (P("dp", "ctx", None), P("dp", "ctx", None), P("dp", "ctx", None), P("ctx", None))
    return jax.shard_map(body, mesh=mesh, in_specs=in_specs, out_specs=out_specs, check_vma=False)
```

```python
import functools

import jax
import jax.numpy as jnp
from jax import lax
from jax.experimental import pallas as pl
from jax.experimental.pallas import tpu as pltpu
from jax.sharding import PartitionSpec as P

WIDTH = 128
LOG2E = 1.4426950408889634
MASKED = -1e30
META_ROWS = 16
END_UNIT = 64
CHUNKS = 2


def dot_nt(a, b):
    return lax.dot_general(a, b, (((1,), (1,)), ((), ())), preferred_element_type=jnp.float32)


def dot_nn(a, b):
    return lax.dot_general(a, b, (((1,), (0,)), ((), ())), preferred_element_type=jnp.float32)


def fold_rows(block):
    return jnp.sum(block.reshape(block.shape[0] // 8, 8, block.shape[1]), axis=0)


def as_column(row):
    size = row.shape[1]
    return jnp.transpose(jnp.broadcast_to(row, (size, size)))


def pack_kernel(key_ref, value_ref, depth_ref, end_ref, *message_refs):
    tokens = key_ref.shape[0]
    groups = key_ref.shape[1] // WIDTH // len(message_refs)
    for chunk, message_ref in enumerate(message_refs):
        for kind, ref in enumerate((key_ref, value_ref)):
            for group in range(groups):
                at = (kind * groups + group) * tokens
                source = slice((chunk * groups + group) * WIDTH, (chunk * groups + group + 1) * WIDTH)
                message_ref[at : at + tokens, :] = ref[:, source]
    depth = depth_ref[...]
    end = end_ref[...]
    end_high = end // END_UNIT
    end_low = end - end_high * END_UNIT
    row = lax.broadcasted_iota(jnp.int32, (META_ROWS, tokens), 0)
    meta = jnp.where(row == 0, depth, jnp.where(row == 1, end_high, end_low))
    meta = meta.astype(jnp.float32).astype(jnp.bfloat16)
    message_refs[0][2 * groups * tokens : 2 * groups * tokens + META_ROWS, :] = meta


def fill_tables(groups, lengths_ref, depth_ref, end_ref, remote, distance_ref, ancestor_ref):
    tokens = depth_ref.shape[1]
    here = lax.axis_index("ctx")
    query_pos = here * tokens + lax.broadcasted_iota(jnp.int32, (tokens, tokens), 1)
    start = jnp.zeros((tokens, tokens), jnp.int32)
    bound = jnp.int32(0)
    for index in range(lengths_ref.shape[1]):
        bound = bound + lengths_ref[0, index]
        start = jnp.where(query_pos >= bound, bound, start)
    query_depth = jnp.broadcast_to(depth_ref[...].astype(jnp.float32), (tokens, tokens))
    for s in range(1 + len(remote)):
        rows = slice(s * tokens, (s + 1) * tokens)
        key_pos = (here ^ s) * tokens + lax.broadcasted_iota(jnp.int32, (tokens, tokens), 0)
        if s == 0:
            key_depth = as_column(depth_ref[...].astype(jnp.float32))
            key_end = as_column(end_ref[...].astype(jnp.float32))
        else:
            below = slice(2 * groups * tokens, 2 * groups * tokens + META_ROWS)
            meta = remote[s - 1][below, :].astype(jnp.float32)
            key_depth = as_column(meta[0:1])
            key_end = as_column(meta[1:2] * END_UNIT + meta[2:3])
        inside = query_pos.astype(jnp.float32) < key_end
        allowed = (key_pos <= query_pos) & (key_pos >= start)
        distance_ref[rows, :] = jnp.abs(query_depth - key_depth)
        ancestor_ref[rows, :] = jnp.where(allowed, jnp.where(inside, 1.0, 0.0), MASKED)


def all_blocks(own_ref, remote, kind, first_group, groups, group):
    tokens = own_ref.shape[0]
    own = own_ref[:, pl.ds(pl.multiple_of((first_group + group) * WIDTH, WIDTH), WIDTH)]
    at = pl.multiple_of((kind * groups + group) * tokens, tokens)
    return jnp.concatenate([own] + [r[pl.ds(at, tokens), :] for r in remote], axis=0)


def stacked(ref, group, first, count):
    heads = [slice((first + i) * WIDTH, (first + i + 1) * WIDTH) for i in range(count)]
    return jnp.concatenate([ref[group, :, h] for h in heads], axis=0)


def query_part(keys_across, dscore, query_grad_ref, group, pair):
    tokens = query_grad_ref.shape[1]
    rows = jnp.transpose((dot_nn(keys_across, dscore) * WIDTH**-0.5).astype(jnp.bfloat16))
    for half in range(2):
        to = slice((2 * pair + half) * WIDTH, (2 * pair + half + 1) * WIDTH)
        query_grad_ref[group, :, to] = rows[half * tokens : (half + 1) * tokens]


def group_copy(whole_hbm, first_group, group, ref, sem, outward=False):
    columns = ref.shape[2]
    at = pl.multiple_of((first_group + group) * columns, columns)
    far, near = whole_hbm.at[:, pl.ds(at, columns)], ref.at[group]
    return pltpu.make_async_copy(*((near, far) if outward else (far, near)), sem.at[group])


def main_kernel(blocks, heads_per_group, groups, chunk, last_chunk, *refs):
    refs = list(refs)
    take = lambda count: [refs.pop(0) for _ in range(count)]
    slope_ref, gain_ref, query_hbm, output_hbm, grad_hbm, key_ref, value_ref = take(7)
    remote = take(blocks - 1)
    if chunk == 0:
        lengths_ref, depth_ref, end_ref = take(3)
    else:
        distance_ref, ancestor_ref, sums_before = take(3)
        parts_before = take(blocks)
    part_refs = take(blocks)
    if chunk == 0:
        distance_ref, ancestor_ref = take(2)
    if last_chunk:
        dscore_ref, bias_ref = take(2)
    else:
        query_grad_hbm, sums_ref = take(2)
    query_ref, output_ref, grad_ref, weight_ref, probs_ref, key_acc, value_acc = take(7)
    load_sems = take(3)
    if last_chunk:
        (sums_ref,) = refs
    else:
        dscore_ref, query_grad_ref, store_sem = refs
    tokens = query_hbm.shape[0]
    factor = WIDTH**-0.5
    pairs = heads_per_group // 2
    first_group = chunk * groups
    block_rows = [slice(s * tokens, (s + 1) * tokens) for s in range(blocks)]

    def loads(group):
        sources = (query_hbm, output_hbm, grad_hbm)
        targets = (query_ref, output_ref, grad_ref)
        return [
            group_copy(source, first_group, group, target, sem)
            for source, target, sem in zip(sources, targets, load_sems)
        ]

    def store(group):
        return group_copy(query_grad_hbm, first_group, group, query_grad_ref, store_sem, True)

    for group in range(groups):
        for load in loads(group):
            load.start()

    if chunk == 0:
        fill_tables(groups, lengths_ref, depth_ref, end_ref, remote, distance_ref, ancestor_ref)
    else:
        for s in range(blocks):
            for kind in range(2):
                size = first_group * tokens
                at = kind * (first_group + groups) * tokens
                part_refs[s][at : at + size, :] = parts_before[s][kind * size : (kind + 1) * size, :]

    def weigh(group, pair, raw, half):
        head = (first_group + group) * heads_per_group + 2 * pair + half
        gain = gain_ref[head] * LOG2E
        slope = slope_ref[head] * LOG2E
        lanes = slice(half * tokens, (half + 1) * tokens)
        tops, totals = [], []
        for rows in block_rows:
            score = raw[rows, lanes] * (factor * LOG2E) + (
                gain * ancestor_ref[rows, :] - slope * distance_ref[rows, :]
            )
            top = jnp.max(score, axis=0, keepdims=True)
            weight = jnp.exp2(score - top)
            weight_ref[pair % 2, rows, lanes] = weight
            tops.append(top)
            totals.append(jnp.sum(weight, axis=0, keepdims=True))
        top = functools.reduce(jnp.maximum, tops)
        shrink = [jnp.exp2(t - top) for t in tops]
        inverse = 1.0 / sum(a * b for a, b in zip(totals, shrink))
        return [s * inverse for s in shrink]

    def differentiate(group, pair, slot, centred, scales, half):
        lanes = slice(half * tokens, (half + 1) * tokens)
        to = slice((2 * pair + half) * tokens, (2 * pair + half + 1) * tokens)
        slope_sum, gain_sum = 0.0, 0.0
        for rows, scale in zip(block_rows, scales):
            probs = weight_ref[pair % 2, rows, lanes] * scale
            dscore = probs * centred[rows, lanes]
            probs_ref[rows, to] = probs.astype(jnp.bfloat16)
            dscore_ref[slot, rows, to] = dscore.astype(jnp.bfloat16)
            slope_sum = slope_sum + fold_rows(dscore * distance_ref[rows, :])
            gain_sum = gain_sum + fold_rows(dscore * ancestor_ref[rows, :])
        at = pl.ds((first_group + group) * heads_per_group + 2 * pair + half, 1)
        sums_ref[0, at, :] = -jnp.sum(slope_sum, axis=0, keepdims=True)
        sums_ref[1, at, :] = jnp.sum(gain_sum, axis=0, keepdims=True)

    def key_part(group, slot, first, count):
        lanes = slice(first * tokens, (first + count) * tokens)
        return dot_nn(dscore_ref[slot, :, lanes], stacked(query_ref, group, first, count))

    def value_part(group, first, count):
        lanes = slice(first * tokens, (first + count) * tokens)
        return dot_nn(probs_ref[:, lanes], stacked(grad_ref, group, first, count))

    def put_part(group, kind, whole):
        at = (kind * (first_group + groups) + first_group + group) * tokens
        for s, rows in enumerate(block_rows):
            to = pl.ds(pl.multiple_of(at, tokens), tokens)
            part_refs[s][to, :] = whole[rows].astype(jnp.bfloat16)

    @pl.loop(0, groups)
    def _(group):
        for load in loads(group):
            load.wait()
        slot = group if last_chunk else 0
        keys = all_blocks(key_ref, remote, 0, first_group, groups, group)
        values = all_blocks(value_ref, remote, 1, first_group, groups, group)
        value_ext = jnp.concatenate([values, jnp.full(values.shape, -1.0, jnp.bfloat16)], axis=1)
        keys_across = None if last_chunk else jnp.transpose(keys)

        def query_pair_part(pair):
            if not last_chunk:
                lanes = slice(2 * pair * tokens, (2 * pair + 2) * tokens)
                query_part(keys_across, dscore_ref[slot, :, lanes], query_grad_ref, group, pair)

        half_heads = heads_per_group // 2
        for pair in range(pairs):
            query_pair = stacked(query_ref, group, 2 * pair, 2)
            grad_pair = stacked(grad_ref, group, 2 * pair, 2)
            output_pair = stacked(output_ref, group, 2 * pair, 2)
            grad_ext = jnp.concatenate([grad_pair, grad_pair * output_pair], axis=1)
            raw = dot_nt(keys, query_pair)
            if pair == pairs // 2:
                key_acc[...] = key_part(group, slot, 0, half_heads)
            scales = [weigh(group, pair, raw, half) for half in range(2)]
            if pair == pairs // 2:
                value_acc[...] = value_part(group, 0, half_heads)
            if pair:
                query_pair_part(pair - 1)
            centred = dot_nt(value_ext, grad_ext)
            for half in range(2):
                differentiate(group, pair, slot, centred, scales[half], half)
        key_whole = key_acc[...] + key_part(group, slot, half_heads, half_heads)
        put_part(group, 0, key_whole * factor)
        put_part(group, 1, value_acc[...] + value_part(group, half_heads, half_heads))
        query_pair_part(pairs - 1)
        if not last_chunk:
            store(group).start()

    if last_chunk:
        heads = heads_per_group * first_group
        rows = [
            jnp.concatenate([sums_before[kind, 0:heads, :], sums_ref[kind, heads:, :]], axis=0)
            for kind in range(2)
        ]
        sums = [jnp.sum(r, axis=1, keepdims=True) for r in rows]
        shape = rows[0].shape
        diagonal = lax.broadcasted_iota(jnp.int32, shape, 0) == lax.broadcasted_iota(
            jnp.int32, shape, 1
        )
        lines = [
            jnp.sum(jnp.where(diagonal, column, 0.0), axis=0, keepdims=True) for column in sums
        ]
        row = lax.broadcasted_iota(jnp.int32, bias_ref.shape[1:], 0)
        tile = jnp.where(row == 0, lines[0], jnp.where(row == 1, lines[1], 0.0))
        bias_ref[...] = jnp.broadcast_to(tile[None], bias_ref.shape)
    else:
        for group in range(groups):
            store(group).wait()


def query_kernel(blocks, groups, first_group, *refs):
    dscore_ref, key_ref = refs[0:2]
    remote = refs[2 : 1 + blocks]
    _, query_grad_hbm, query_grad_ref, store_sem = refs[1 + blocks :]
    tokens = key_ref.shape[0]

    def store(group):
        return group_copy(query_grad_hbm, first_group, group, query_grad_ref, store_sem, True)

    @pl.loop(0, groups)
    def _(group):
        keys_across = jnp.transpose(all_blocks(key_ref, remote, 0, first_group, groups, group))
        for pair in range(query_grad_ref.shape[2] // WIDTH // 2):
            lanes = slice(2 * pair * tokens, (2 * pair + 2) * tokens)
            query_part(keys_across, dscore_ref[group, :, lanes], query_grad_ref, group, pair)
        store(group).start()

    for group in range(groups):
        store(group).wait()


def combine_kernel(blocks, *refs):
    parts = refs[0:blocks]
    key_out, value_out = refs[blocks:]
    tokens = key_out.shape[0]
    groups = key_out.shape[1] // WIDTH
    for kind, out in enumerate((key_out, value_out)):
        for group in range(groups):
            at = (kind * groups + group) * tokens
            total = parts[0][at : at + tokens, :].astype(jnp.float32)
            for s in range(1, blocks):
                total = total + parts[s][at : at + tokens, :].astype(jnp.float32)
            out[:, group * WIDTH : (group + 1) * WIDTH] = total.astype(jnp.bfloat16)


def spread_kernel(sums_ref, _, spread_ref):
    total = jnp.sum(sums_ref[...], axis=0)
    share = spread_ref.shape[2]
    for block in range(spread_ref.shape[0]):
        spread_ref[block] = total[:, block * share : (block + 1) * share]


def bias_kernel(parts_ref, _, out_ref):
    out_ref[...] = jnp.sum(parts_ref[...], axis=0)[0:2]


def body(
    queries,
    key_rows,
    values,
    outputs,
    out_grads,
    depths,
    subtree_end,
    file_lengths,
    slopes,
    ancestor_gain,
):
    blocks = lax.axis_size("ctx")
    replicas = lax.axis_size("dp")
    tokens, width_all = queries.shape[1:]
    kv_width = key_rows.shape[2]
    heads_all = width_all // WIDTH
    kv_heads = kv_width // WIDTH
    heads_per_group = heads_all // kv_heads
    group_columns = heads_per_group * WIDTH
    local_heads = heads_all // blocks
    keys_seen = blocks * tokens
    groups = kv_heads // CHUNKS
    bf16, f32 = jnp.bfloat16, jnp.float32
    vmem = pl.BlockSpec(memory_space=pltpu.VMEM)
    smem = pl.BlockSpec(memory_space=pltpu.SMEM)
    hbm = pl.BlockSpec(memory_space=pltpu.HBM)
    params = pltpu.CompilerParams(vmem_limit_bytes=(36 if blocks <= 4 else 48) * 1024 * 1024)

    def hold(array):
        return pltpu.with_memory_space_constraint(array, pltpu.HBM)

    def struct(shape, dtype):
        return jax.ShapeDtypeStruct(shape, dtype)

    key_held, value_held = hold(key_rows[0]), hold(values[0])
    depth_held, end_held = hold(depths), hold(subtree_end)
    chunk_rows = 2 * groups * tokens
    messages = pl.pallas_call(
        pack_kernel,
        out_shape=[
            struct((chunk_rows + (0 if chunk else META_ROWS), WIDTH), bf16)
            for chunk in range(CHUNKS)
        ],
        in_specs=[vmem] * 4,
        out_specs=[vmem] * CHUNKS,
        compiler_params=params,
        name="pack",
    )(key_held, value_held, depth_held, end_held)
    arrived = [
        [
            lax.ppermute(message, "ctx", [(i, i ^ s) for i in range(blocks) if i < i ^ s])
            for s in range(1, blocks)
        ]
        for message in messages
    ]

    matmul_flops = 2 * tokens * keys_seen * WIDTH * heads_all
    table = struct((keys_seen, tokens), f32)
    sums = struct((2, heads_all, tokens), f32)
    wide = pltpu.VMEM((groups, tokens, group_columns), bf16)
    group_sems = pltpu.SemaphoreType.DMA((groups,))
    for chunk in range(CHUNKS):
        last_chunk = chunk == CHUNKS - 1
        operands = [
            hold(slopes),
            hold(ancestor_gain),
            hold(queries[0]),
            hold(outputs[0]),
            hold(out_grads[0]),
            key_held,
            value_held,
            *arrived[chunk],
        ]
        specs = [smem] * 2 + [hbm] * 3 + [vmem] * (1 + blocks)
        out_shape = [struct(((chunk + 1) * chunk_rows, WIDTH), bf16)] * blocks
        if chunk == 0:
            operands = operands + [hold(file_lengths), depth_held, end_held]
            specs = specs + [smem, vmem, vmem]
            out_shape = out_shape + [table, table]
        else:
            operands = operands + [*tables, sums_before, *parts]
            specs = specs + [vmem] * (3 + blocks)
        out_specs = [vmem] * len(out_shape)
        scratch = [
            wide,
            wide,
            wide,
            pltpu.VMEM((2, keys_seen, 2 * tokens), f32),
            pltpu.VMEM((keys_seen, group_columns), bf16),
            pltpu.VMEM((keys_seen, WIDTH), f32),
            pltpu.VMEM((keys_seen, WIDTH), f32),
            group_sems,
            group_sems,
            group_sems,
        ]
        if last_chunk:
            out_shape = out_shape + [
                struct((groups, keys_seen, group_columns), bf16),
                struct((replicas, 8, WIDTH), f32),
            ]
            out_specs = out_specs + [vmem, vmem]
            scratch = scratch + [pltpu.VMEM(sums.shape, f32)]
        else:
            out_shape = out_shape + [struct((tokens, width_all), bf16), sums]
            out_specs = out_specs + [hbm, vmem]
            dscore_slot = pltpu.VMEM((1, keys_seen, group_columns), bf16)
            scratch = scratch + [dscore_slot, wide, group_sems]
        results = pl.pallas_call(
            functools.partial(main_kernel, blocks, heads_per_group, groups, chunk, last_chunk),
            out_shape=out_shape,
            in_specs=specs,
            out_specs=out_specs,
            scratch_shapes=scratch,
            compiler_params=params,
            cost_estimate=pl.CostEstimate(
                flops=5 * matmul_flops // CHUNKS,
                bytes_accessed=10 * tokens * width_all // CHUNKS,
                transcendentals=tokens * keys_seen * heads_all // CHUNKS,
            ),
            name=f"attend_{chunk}",
        )(*operands)
        parts = list(results[0:blocks])
        if chunk == 0:
            tables = results[blocks : 2 + blocks]
        if last_chunk:
            dscore, sums_here = results[-2:]
        else:
            query_grads, sums_before = results[-2:]

    returned = [parts[0]]
    for s in reversed(range(1, blocks)):
        back = [(i, i ^ s) for i in range(blocks) if i > i ^ s]
        returned.append(lax.ppermute(parts[s], "ctx", back))
    sums_of_all = lax.all_to_all(sums_here, "dp", split_axis=0, concat_axis=0, tiled=True)
    query_grads = pl.pallas_call(
        functools.partial(query_kernel, blocks, groups, (CHUNKS - 1) * groups),
        out_shape=struct((tokens, width_all), bf16),
        in_specs=[vmem] * (1 + blocks) + [hbm],
        out_specs=hbm,
        scratch_shapes=[wide, group_sems],
        input_output_aliases={1 + blocks: 0},
        compiler_params=params,
        cost_estimate=pl.CostEstimate(
            flops=matmul_flops // CHUNKS,
            bytes_accessed=2 * tokens * width_all // CHUNKS,
            transcendentals=0,
        ),
        name="query",
    )(dscore, key_held, *arrived[CHUNKS - 1], query_grads)
    spread = pl.pallas_call(
        spread_kernel,
        out_shape=struct((blocks, 8, local_heads), f32),
        in_specs=[vmem, hbm],
        out_specs=vmem,
        compiler_params=params,
        name="spread",
    )(sums_of_all, hold(query_grads))
    bias_parts = lax.all_to_all(spread, "ctx", split_axis=0, concat_axis=0, tiled=True)
    key_grads, value_grads = pl.pallas_call(
        functools.partial(combine_kernel, blocks),
        out_shape=[struct((tokens, kv_width), bf16)] * 2,
        in_specs=[vmem] * blocks,
        out_specs=[vmem] * 2,
        compiler_params=params,
        name="combine",
    )(*returned)
    bias_grads = pl.pallas_call(
        bias_kernel,
        out_shape=struct((2, local_heads), f32),
        in_specs=[vmem, hbm],
        out_specs=vmem,
        compiler_params=params,
        name="bias",
    )(bias_parts, hold(key_grads))
    return (query_grads[None], key_grads[None], value_grads[None], bias_grads.T)


def solution(mesh):
    in_specs = (
        P("dp", "ctx", None),
        P("dp", "ctx", None),
        P("dp", "ctx", None),
        P("dp", "ctx", None),
        P("dp", "ctx", None),
        P("dp", "ctx"),
        P("dp", "ctx"),
        P("dp", None),
        P(),
        P(),
    )
    out_specs = (P("dp", "ctx", None), P("dp", "ctx", None), P("dp", "ctx", None), P("ctx", None))
    return jax.shard_map(body, mesh=mesh, in_specs=in_specs, out_specs=out_specs, check_vma=False)
```

```python
import functools

import jax
import jax.numpy as jnp
from jax import lax
from jax.experimental import pallas as pl
from jax.experimental.pallas import tpu as pltpu
from jax.sharding import PartitionSpec as P

WIDTH = 128
LOG2E = 1.4426950408889634
MASKED = -1e30
META_ROWS = 16
END_UNIT = 64


def dot_nt(a, b):
    return lax.dot_general(a, b, (((1,), (1,)), ((), ())), preferred_element_type=jnp.float32)


def dot_nn(a, b):
    return lax.dot_general(a, b, (((1,), (0,)), ((), ())), preferred_element_type=jnp.float32)


def fold_rows(block):
    return jnp.sum(block.reshape(block.shape[0] // 8, 8, block.shape[1]), axis=0)


def as_column(row):
    size = row.shape[1]
    return jnp.transpose(jnp.broadcast_to(row, (size, size)))


def pack_kernel(key_ref, value_ref, depth_ref, end_ref, message_ref):
    tokens = key_ref.shape[0]
    groups = key_ref.shape[1] // WIDTH
    for kind, ref in enumerate((key_ref, value_ref)):
        for group in range(groups):
            at = (kind * groups + group) * tokens
            message_ref[at : at + tokens, :] = ref[:, group * WIDTH : (group + 1) * WIDTH]
    depth = depth_ref[...]
    end = end_ref[...]
    end_high = end // END_UNIT
    end_low = end - end_high * END_UNIT
    row = lax.broadcasted_iota(jnp.int32, (META_ROWS, tokens), 0)
    meta = jnp.where(row == 0, depth, jnp.where(row == 1, end_high, end_low))
    meta = meta.astype(jnp.float32).astype(jnp.bfloat16)
    message_ref[2 * groups * tokens : 2 * groups * tokens + META_ROWS, :] = meta


def fill_tables(groups, lengths_ref, depth_ref, end_ref, remote, distance_ref, ancestor_ref):
    tokens = depth_ref.shape[1]
    here = lax.axis_index("ctx")
    query_pos = here * tokens + lax.broadcasted_iota(jnp.int32, (tokens, tokens), 1)
    start = jnp.zeros((tokens, tokens), jnp.int32)
    bound = jnp.int32(0)
    for index in range(lengths_ref.shape[1]):
        bound = bound + lengths_ref[0, index]
        start = jnp.where(query_pos >= bound, bound, start)
    query_depth = jnp.broadcast_to(depth_ref[...].astype(jnp.float32), (tokens, tokens))
    for s in range(1 + len(remote)):
        rows = slice(s * tokens, (s + 1) * tokens)
        key_pos = (here ^ s) * tokens + lax.broadcasted_iota(jnp.int32, (tokens, tokens), 0)
        if s == 0:
            key_depth = as_column(depth_ref[...].astype(jnp.float32))
            key_end = as_column(end_ref[...].astype(jnp.float32))
        else:
            below = slice(2 * groups * tokens, 2 * groups * tokens + META_ROWS)
            meta = remote[s - 1][below, :].astype(jnp.float32)
            key_depth = as_column(meta[0:1])
            key_end = as_column(meta[1:2] * END_UNIT + meta[2:3])
        inside = query_pos.astype(jnp.float32) < key_end
        allowed = (key_pos <= query_pos) & (key_pos >= start)
        distance_ref[rows, :] = jnp.abs(query_depth - key_depth)
        ancestor_ref[rows, :] = jnp.where(allowed, jnp.where(inside, 1.0, 0.0), MASKED)


def all_blocks(own_ref, remote, kind, groups, group):
    tokens = own_ref.shape[0]
    own = own_ref[:, pl.ds(pl.multiple_of(group * WIDTH, WIDTH), WIDTH)]
    at = pl.multiple_of((kind * groups + group) * tokens, tokens)
    return jnp.concatenate([own] + [r[pl.ds(at, tokens), :] for r in remote], axis=0)


def stacked(ref, group, first, count):
    heads = [slice((first + i) * WIDTH, (first + i + 1) * WIDTH) for i in range(count)]
    return jnp.concatenate([ref[group, :, h] for h in heads], axis=0)


def group_columns(group, columns):
    return pl.ds(pl.multiple_of(group * columns, columns), columns)


def group_loads(group, sources, targets, sems):
    columns = targets[0].shape[2]
    return [
        pltpu.make_async_copy(
            source.at[:, group_columns(group, columns)],
            target.at[group],
            sems.at[len(sources) * group + index],
        )
        for index, (source, target) in enumerate(zip(sources, targets))
    ]


def score_kernel(blocks, heads_per_group, groups, *refs):
    refs = list(refs)
    take = lambda count: [refs.pop(0) for _ in range(count)]
    lengths_ref, slope_ref, gain_ref, depth_ref, end_ref = take(5)
    query_hbm, output_hbm, grad_hbm, key_ref, value_ref = take(5)
    remote = take(blocks - 1)
    dscore_ref, own_probs_ref = take(2)
    part_refs = take(blocks - 1)
    (bias_ref,) = take(1)
    query_ref, output_ref, grad_ref, weight_ref, probs_ref, key_acc, value_acc = take(7)
    distance_ref, ancestor_ref, slope_rows, gain_rows, load_sems = refs
    tokens = query_hbm.shape[0]
    factor = WIDTH**-0.5
    pairs = heads_per_group // 2
    block_rows = [slice(s * tokens, (s + 1) * tokens) for s in range(blocks)]

    def loads(group):
        sources = (query_hbm, output_hbm, grad_hbm)
        return group_loads(group, sources, (query_ref, output_ref, grad_ref), load_sems)

    for group in range(groups):
        for load in loads(group):
            load.start()
    fill_tables(groups, lengths_ref, depth_ref, end_ref, remote, distance_ref, ancestor_ref)

    def weigh(group, pair, raw, half):
        head = group * heads_per_group + 2 * pair + half
        gain = gain_ref[head] * LOG2E
        slope = slope_ref[head] * LOG2E
        lanes = slice(half * tokens, (half + 1) * tokens)
        tops, totals = [], []
        for rows in block_rows:
            score = raw[rows, lanes] * (factor * LOG2E) + (
                gain * ancestor_ref[rows, :] - slope * distance_ref[rows, :]
            )
            top = jnp.max(score, axis=0, keepdims=True)
            weight = jnp.exp2(score - top)
            weight_ref[pair % 2, rows, lanes] = weight
            tops.append(top)
            totals.append(jnp.sum(weight, axis=0, keepdims=True))
        top = functools.reduce(jnp.maximum, tops)
        shrink = [jnp.exp2(t - top) for t in tops]
        inverse = 1.0 / sum(a * b for a, b in zip(totals, shrink))
        return [s * inverse for s in shrink]

    def differentiate(group, pair, centred, scales, half):
        lanes = slice(half * tokens, (half + 1) * tokens)
        to = slice((2 * pair + half) * tokens, (2 * pair + half + 1) * tokens)
        slope_sum, gain_sum = 0.0, 0.0
        for s, (rows, scale) in enumerate(zip(block_rows, scales)):
            probs = weight_ref[pair % 2, rows, lanes] * scale
            dscore = probs * centred[rows, lanes]
            dscore_ref[group, rows, to] = dscore.astype(jnp.bfloat16)
            slope_sum = slope_sum + fold_rows(dscore * distance_ref[rows, :])
            gain_sum = gain_sum + fold_rows(dscore * ancestor_ref[rows, :])
            probs_b = probs.astype(jnp.bfloat16)
            if s == 0:
                own_probs_ref[group, :, to] = probs_b
            else:
                probs_ref[(s - 1) * tokens : s * tokens, to] = probs_b
        at = pl.ds(group * heads_per_group + 2 * pair + half, 1)
        slope_rows[at, :] = -jnp.sum(slope_sum, axis=0, keepdims=True)
        gain_rows[at, :] = jnp.sum(gain_sum, axis=0, keepdims=True)

    def key_part(group, first, count):
        lanes = slice(first * tokens, (first + count) * tokens)
        return dot_nn(dscore_ref[group, tokens:, lanes], stacked(query_ref, group, first, count))

    def value_part(group, first, count):
        lanes = slice(first * tokens, (first + count) * tokens)
        return dot_nn(probs_ref[:, lanes], stacked(grad_ref, group, first, count))

    def put_part(group, kind, whole):
        at = pl.multiple_of((kind * groups + group) * tokens, tokens)
        for s, part_ref in enumerate(part_refs):
            part = whole[s * tokens : (s + 1) * tokens].astype(jnp.bfloat16)
            part_ref[pl.ds(at, tokens), :] = part

    @pl.loop(0, groups)
    def _(group):
        for load in loads(group):
            load.wait()
        keys = all_blocks(key_ref, remote, 0, groups, group)
        values = all_blocks(value_ref, remote, 1, groups, group)
        value_ext = jnp.concatenate([values, jnp.full(values.shape, -1.0, jnp.bfloat16)], axis=1)
        half_heads = heads_per_group // 2
        for pair in range(pairs):
            query_pair = stacked(query_ref, group, 2 * pair, 2)
            grad_pair = stacked(grad_ref, group, 2 * pair, 2)
            output_pair = stacked(output_ref, group, 2 * pair, 2)
            grad_ext = jnp.concatenate([grad_pair, grad_pair * output_pair], axis=1)
            raw = dot_nt(keys, query_pair)
            if pair == pairs // 2:
                key_acc[...] = key_part(group, 0, half_heads)
            scales = [weigh(group, pair, raw, half) for half in range(2)]
            if pair == pairs // 2:
                value_acc[...] = value_part(group, 0, half_heads)
            centred = dot_nt(value_ext, grad_ext)
            for half in range(2):
                differentiate(group, pair, centred, scales[half], half)
        key_whole = key_acc[...] + key_part(group, half_heads, half_heads)
        put_part(group, 0, key_whole * factor)
        put_part(group, 1, value_acc[...] + value_part(group, half_heads, half_heads))

    slope_sum = jnp.sum(slope_rows[...], axis=1, keepdims=True)
    gain_sum = jnp.sum(gain_rows[...], axis=1, keepdims=True)
    shape = slope_rows.shape
    lane = lax.broadcasted_iota(jnp.int32, shape, 1)
    row = lax.broadcasted_iota(jnp.int32, shape, 0)
    replicas, parts, rows_here, local = bias_ref.shape
    local_heads = shape[0] // parts
    kind = lax.broadcasted_iota(jnp.int32, (rows_here, local), 0)
    for part in range(parts):
        mine = (lane == row - part * local_heads) & (lane < local_heads)
        slope_line = jnp.sum(jnp.where(mine, slope_sum, 0.0), axis=0, keepdims=True)
        gain_line = jnp.sum(jnp.where(mine, gain_sum, 0.0), axis=0, keepdims=True)
        tile = jnp.where(kind == 0, slope_line, jnp.where(kind == 1, gain_line, 0.0))
        bias_ref[:, part] = jnp.broadcast_to(tile[None], (replicas, rows_here, local))


def local_kernel(blocks, heads_per_group, groups, *refs):
    refs = list(refs)
    take = lambda count: [refs.pop(0) for _ in range(count)]
    dscore_ref, own_probs_ref = take(2)
    query_hbm, grad_hbm, key_ref = take(3)
    remote = take(blocks - 1)
    query_grad_hbm, own_part_ref = take(2)
    query_ref, grad_ref, query_grad_ref, load_sems, store_sems = refs
    tokens = query_hbm.shape[0]
    factor = WIDTH**-0.5
    pairs = heads_per_group // 2
    block_rows = [slice(s * tokens, (s + 1) * tokens) for s in range(blocks)]

    def loads(group):
        return group_loads(group, (query_hbm, grad_hbm), (query_ref, grad_ref), load_sems)

    def store(group):
        columns = group_columns(group, query_grad_ref.shape[2])
        return pltpu.make_async_copy(
            query_grad_ref.at[group], query_grad_hbm.at[:, columns], store_sems.at[group]
        )

    for group in range(groups):
        for load in loads(group):
            load.start()

    @pl.loop(0, groups)
    def _(group):
        for load in loads(group):
            load.wait()
        keys_across = jnp.transpose(all_blocks(key_ref, remote, 0, groups, group))
        at = pl.multiple_of(group * tokens, tokens)
        own = dot_nn(dscore_ref[group, 0:tokens, :], stacked(query_ref, group, 0, heads_per_group))
        own_part_ref[pl.ds(at, tokens), :] = (own * factor).astype(jnp.bfloat16)
        for pair in range(pairs):
            lanes = slice(2 * pair * tokens, (2 * pair + 2) * tokens)
            across = dot_nn(keys_across, dscore_ref[group, :, lanes]) * factor
            rows = jnp.transpose(across.astype(jnp.bfloat16))
            for half in range(2):
                to = slice((2 * pair + half) * WIDTH, (2 * pair + half + 1) * WIDTH)
                query_grad_ref[group, :, to] = rows[half * tokens : (half + 1) * tokens]
        at = pl.multiple_of((groups + group) * tokens, tokens)
        own = dot_nn(own_probs_ref[group], stacked(grad_ref, group, 0, heads_per_group))
        own_part_ref[pl.ds(at, tokens), :] = own.astype(jnp.bfloat16)
        store(group).start()

    for group in range(groups):
        store(group).wait()


def combine_kernel(blocks, *refs):
    parts = refs[0:blocks]
    key_out, value_out = refs[blocks:]
    tokens = key_out.shape[0]
    groups = key_out.shape[1] // WIDTH
    for kind, out in enumerate((key_out, value_out)):
        for group in range(groups):
            at = (kind * groups + group) * tokens
            total = parts[0][at : at + tokens, :].astype(jnp.float32)
            for s in range(1, blocks):
                total = total + parts[s][at : at + tokens, :].astype(jnp.float32)
            out[:, group * WIDTH : (group + 1) * WIDTH] = total.astype(jnp.bfloat16)


def bias_kernel(parts_ref, _, out_ref):
    out_ref[...] = jnp.sum(parts_ref[...], axis=0)[0:2, 0 : out_ref.shape[1]]


def body(
    queries,
    key_rows,
    values,
    outputs,
    out_grads,
    depths,
    subtree_end,
    file_lengths,
    slopes,
    ancestor_gain,
):
    blocks = lax.axis_size("ctx")
    replicas = lax.axis_size("dp")
    tokens, width_all = queries.shape[1:]
    kv_width = key_rows.shape[2]
    heads_all = width_all // WIDTH
    groups = kv_width // WIDTH
    heads_per_group = heads_all // groups
    columns = heads_per_group * WIDTH
    local_heads = heads_all // blocks
    keys_seen = blocks * tokens
    message_rows = 2 * groups * tokens
    bf16, f32 = jnp.bfloat16, jnp.float32
    vmem = pl.BlockSpec(memory_space=pltpu.VMEM)
    smem = pl.BlockSpec(memory_space=pltpu.SMEM)
    hbm = pl.BlockSpec(memory_space=pltpu.HBM)
    params = pltpu.CompilerParams(vmem_limit_bytes=(24 if blocks <= 4 else 48) * 1024 * 1024)
    sem = pltpu.SemaphoreType.DMA

    def hold(array):
        return pltpu.with_memory_space_constraint(array, pltpu.HBM)

    def struct(*shape, dtype=bf16):
        return jax.ShapeDtypeStruct(shape, dtype)

    def cost(matmuls, exponentials):
        return pl.CostEstimate(
            flops=matmuls * 2 * tokens * keys_seen * WIDTH * heads_all,
            bytes_accessed=4 * tokens * width_all,
            transcendentals=exponentials * tokens * keys_seen * heads_all,
        )

    query_held, output_held, grad_held = hold(queries[0]), hold(outputs[0]), hold(out_grads[0])
    key_held, value_held = hold(key_rows[0]), hold(values[0])
    depth_held, end_held = hold(depths), hold(subtree_end)
    message = pl.pallas_call(
        pack_kernel,
        out_shape=struct(message_rows + META_ROWS, WIDTH),
        in_specs=[vmem] * 4,
        out_specs=vmem,
        compiler_params=params,
        name="pack",
    )(key_held, value_held, depth_held, end_held)
    arrived = [
        lax.ppermute(message, "ctx", [(i, i ^ s) for i in range(blocks) if i < i ^ s])
        for s in range(1, blocks)
    ]

    wide = pltpu.VMEM((groups, tokens, columns), bf16)
    bias_shape = (replicas, blocks, 8, WIDTH)
    dscore, own_probs, *parts, bias_parts = pl.pallas_call(
        functools.partial(score_kernel, blocks, heads_per_group, groups),
        out_shape=[
            struct(groups, keys_seen, columns),
            struct(groups, tokens, columns),
        ]
        + [struct(message_rows, WIDTH)] * (blocks - 1)
        + [struct(*bias_shape, dtype=f32)],
        in_specs=[smem] * 3 + [vmem] * 2 + [hbm] * 3 + [vmem] * (1 + blocks),
        out_specs=[vmem] * (2 + blocks),
        scratch_shapes=[
            wide,
            wide,
            wide,
            pltpu.VMEM((2, keys_seen, 2 * tokens), f32),
            pltpu.VMEM((keys_seen - tokens, columns), bf16),
            pltpu.VMEM((keys_seen - tokens, WIDTH), f32),
            pltpu.VMEM((keys_seen - tokens, WIDTH), f32),
            pltpu.VMEM((keys_seen, tokens), f32),
            pltpu.VMEM((keys_seen, tokens), f32),
            pltpu.VMEM((heads_all, tokens), f32),
            pltpu.VMEM((heads_all, tokens), f32),
            sem((3 * groups,)),
        ],
        compiler_params=params,
        cost_estimate=cost(4, 1),
        name="scores",
    )(
        hold(file_lengths),
        hold(slopes),
        hold(ancestor_gain),
        depth_held,
        end_held,
        query_held,
        output_held,
        grad_held,
        key_held,
        value_held,
        *arrived,
    )
    returned = []
    for s in reversed(range(1, blocks)):
        back = [(i, i ^ s) for i in range(blocks) if i > i ^ s]
        returned.append(lax.ppermute(parts[s - 1], "ctx", back))

    bias_parts = bias_parts.reshape(replicas * blocks, 8, WIDTH)
    bias_parts = lax.all_to_all(bias_parts, ("dp", "ctx"), split_axis=0, concat_axis=0, tiled=True)
    query_grads, own_part = pl.pallas_call(
        functools.partial(local_kernel, blocks, heads_per_group, groups),
        out_shape=[struct(tokens, width_all), struct(message_rows, WIDTH)],
        in_specs=[vmem] * 2 + [hbm] * 2 + [vmem] * blocks,
        out_specs=[hbm, vmem],
        scratch_shapes=[wide, wide, wide, sem((2 * groups,)), sem((groups,))],
        compiler_params=params,
        cost_estimate=cost(2, 0),
        name="local",
    )(dscore, own_probs, query_held, grad_held, key_held, *arrived)
    key_grads, value_grads = pl.pallas_call(
        functools.partial(combine_kernel, blocks),
        out_shape=[struct(tokens, kv_width)] * 2,
        in_specs=[vmem] * blocks,
        out_specs=[vmem] * 2,
        compiler_params=params,
        name="combine",
    )(own_part, *returned)
    bias_grads = pl.pallas_call(
        bias_kernel,
        out_shape=struct(2, local_heads, dtype=f32),
        in_specs=[vmem, hbm],
        out_specs=vmem,
        compiler_params=params,
        name="bias",
    )(bias_parts, hold(key_grads))
    return (query_grads[None], key_grads[None], value_grads[None], bias_grads.T)


def solution(mesh):
    in_specs = (
        P("dp", "ctx", None),
        P("dp", "ctx", None),
        P("dp", "ctx", None),
        P("dp", "ctx", None),
        P("dp", "ctx", None),
        P("dp", "ctx"),
        P("dp", "ctx"),
        P("dp", None),
        P(),
        P(),
    )
    out_specs = (P("dp", "ctx", None), P("dp", "ctx", None), P("dp", "ctx", None), P("ctx", None))
    return jax.shard_map(body, mesh=mesh, in_specs=in_specs, out_specs=out_specs, check_vma=False)
```

```python
import functools

import jax
import jax.numpy as jnp
from jax import lax
from jax.experimental import pallas as pl
from jax.experimental.pallas import tpu as pltpu
from jax.sharding import PartitionSpec as P

WIDTH = 128
LOG2E = 1.4426950408889634
MASKED = -1e30
META_ROWS = 16
END_UNIT = 64


def dot_nt(a, b):
    return lax.dot_general(a, b, (((1,), (1,)), ((), ())), preferred_element_type=jnp.float32)


def dot_nn(a, b):
    return lax.dot_general(a, b, (((1,), (0,)), ((), ())), preferred_element_type=jnp.float32)


def fold_rows(block):
    return jnp.sum(block.reshape(block.shape[0] // 8, 8, block.shape[1]), axis=0)


def as_column(row):
    size = row.shape[1]
    return jnp.transpose(jnp.broadcast_to(row, (size, size)))


def pack_kernel(key_ref, value_ref, depth_ref, end_ref, message_ref):
    tokens = key_ref.shape[0]
    groups = key_ref.shape[1] // WIDTH
    for kind, ref in enumerate((key_ref, value_ref)):
        for group in range(groups):
            at = (kind * groups + group) * tokens
            message_ref[at : at + tokens, :] = ref[:, group * WIDTH : (group + 1) * WIDTH]
    depth = depth_ref[...]
    end = end_ref[...]
    end_high = end // END_UNIT
    end_low = end - end_high * END_UNIT
    row = lax.broadcasted_iota(jnp.int32, (META_ROWS, tokens), 0)
    meta = jnp.where(row == 0, depth, jnp.where(row == 1, end_high, end_low))
    meta = meta.astype(jnp.float32).astype(jnp.bfloat16)
    message_ref[2 * groups * tokens : 2 * groups * tokens + META_ROWS, :] = meta


def prepare_kernel(query_in, output_in, grad_in, query_out, grad_out, product_out):
    query_out[...] = query_in[...]
    grad_out[...] = grad_in[...]
    product_out[...] = grad_in[...] * output_in[...]


def main_kernel(
    blocks,
    heads_per_group,
    groups,
    lengths_ref,
    slope_ref,
    gain_ref,
    depth_ref,
    end_ref,
    query_ref,
    grad_ref,
    product_ref,
    key_ref,
    value_ref,
    *refs,
):
    tokens = query_ref.shape[0]
    remote = refs[0 : blocks - 1]
    query_grad_hbm = refs[blocks - 1]
    part_refs = refs[blocks : 2 * blocks]
    bias_hbm = refs[2 * blocks]
    (
        query_grad_ref,
        distance_ref,
        ancestor_ref,
        slope_rows,
        gain_rows,
        key_acc,
        value_acc,
        weight_ref,
        probs_ref,
        dscore_ref,
        bias_ref,
        store_sems,
        bias_sem,
    ) = refs[2 * blocks + 1 :]
    factor = WIDTH**-0.5
    group_columns = heads_per_group * WIDTH
    pairs = heads_per_group // 2

    def store(group):
        wide = pl.ds(pl.multiple_of(group * group_columns, group_columns), group_columns)
        return pltpu.make_async_copy(
            query_grad_ref.at[group], query_grad_hbm.at[:, wide], store_sems.at[group]
        )

    here = lax.axis_index("ctx")
    query_pos = here * tokens + lax.broadcasted_iota(jnp.int32, (tokens, tokens), 1)
    start = jnp.zeros((tokens, tokens), jnp.int32)
    bound = jnp.int32(0)
    for index in range(lengths_ref.shape[1]):
        bound = bound + lengths_ref[0, index]
        start = jnp.where(query_pos >= bound, bound, start)
    query_depth = jnp.broadcast_to(depth_ref[...].astype(jnp.float32), (tokens, tokens))
    block_rows = [slice(s * tokens, (s + 1) * tokens) for s in range(blocks)]
    for s, rows in enumerate(block_rows):
        key_pos = (here ^ s) * tokens + lax.broadcasted_iota(jnp.int32, (tokens, tokens), 0)
        if s == 0:
            key_depth = as_column(depth_ref[...].astype(jnp.float32))
            key_end = as_column(end_ref[...].astype(jnp.float32))
        else:
            below = slice(2 * groups * tokens, 2 * groups * tokens + META_ROWS)
            meta = remote[s - 1][below, :].astype(jnp.float32)
            key_depth = as_column(meta[0:1])
            key_end = as_column(meta[1:2] * END_UNIT + meta[2:3])
        inside = query_pos.astype(jnp.float32) < key_end
        allowed = (key_pos <= query_pos) & (key_pos >= start)
        distance_ref[rows, :] = jnp.abs(query_depth - key_depth)
        ancestor_ref[rows, :] = jnp.where(allowed, jnp.where(inside, 1.0, 0.0), MASKED)

    def key_block(kind, group, s):
        if s == 0:
            at = pl.multiple_of(group * WIDTH, WIDTH)
            return (key_ref, value_ref)[kind][:, pl.ds(at, WIDTH)]
        at = pl.multiple_of((kind * groups + group) * tokens, tokens)
        return remote[s - 1][pl.ds(at, tokens), :]

    def all_blocks(kind, group):
        return jnp.concatenate([key_block(kind, group, s) for s in range(blocks)], axis=0)

    def stacked(ref, group, first, count):
        at = pl.multiple_of(group * group_columns, group_columns) + first * WIDTH
        heads = [pl.ds(pl.multiple_of(at + i * WIDTH, WIDTH), WIDTH) for i in range(count)]
        return jnp.concatenate([ref[:, head] for head in heads], axis=0)

    def weigh(group, pair, raw, half):
        head = group * heads_per_group + 2 * pair + half
        gain = gain_ref[head] * LOG2E
        slope = slope_ref[head] * LOG2E
        lanes = slice(half * tokens, (half + 1) * tokens)
        tops, totals = [], []
        for s, rows in enumerate(block_rows):
            score = raw[s][:, lanes] * (factor * LOG2E) + (
                gain * ancestor_ref[rows, :] - slope * distance_ref[rows, :]
            )
            top = jnp.max(score, axis=0, keepdims=True)
            weight = jnp.exp2(score - top)
            weight_ref[pair % 2, rows, lanes] = weight
            tops.append(top)
            totals.append(jnp.sum(weight, axis=0, keepdims=True))
        top = functools.reduce(jnp.maximum, tops)
        shrink = [jnp.exp2(t - top) for t in tops]
        inverse = 1.0 / sum(a * b for a, b in zip(totals, shrink))
        return [s * inverse for s in shrink]

    def differentiate(group, pair, centred, scales, half):
        lanes = slice(half * tokens, (half + 1) * tokens)
        to = slice((2 * pair + half) * tokens, (2 * pair + half + 1) * tokens)
        slope_sum, gain_sum = 0.0, 0.0
        for s, rows in enumerate(block_rows):
            probs = weight_ref[pair % 2, rows, lanes] * scales[s]
            dscore = probs * centred[s][:, lanes]
            probs_ref[rows, to] = probs.astype(jnp.bfloat16)
            dscore_ref[rows, to] = dscore.astype(jnp.bfloat16)
            slope_sum = slope_sum + fold_rows(dscore * distance_ref[rows, :])
            gain_sum = gain_sum + fold_rows(dscore * ancestor_ref[rows, :])
        at = pl.ds(group * heads_per_group + 2 * pair + half, 1)
        slope_rows[at, :] = -jnp.sum(slope_sum, axis=0, keepdims=True)
        gain_rows[at, :] = jnp.sum(gain_sum, axis=0, keepdims=True)

    def put_part(group, kind, whole):
        at = pl.multiple_of((kind * groups + group) * tokens, tokens)
        for s, rows in enumerate(block_rows):
            part_refs[s][pl.ds(at, tokens), :] = whole[rows].astype(jnp.bfloat16)

    def key_part(group, first, count):
        heads = stacked(query_ref, group, first, count)
        lanes = slice(first * tokens, (first + count) * tokens)
        return dot_nn(dscore_ref[:, lanes], heads)

    def value_part(group, first, count):
        heads = stacked(grad_ref, group, first, count)
        lanes = slice(first * tokens, (first + count) * tokens)
        return dot_nn(probs_ref[:, lanes], heads)

    def query_part(keys_across, group, pair):
        lanes = slice(2 * pair * tokens, (2 * pair + 2) * tokens)
        across = dot_nn(keys_across, dscore_ref[:, lanes]) * factor
        rows = jnp.transpose(across.astype(jnp.bfloat16))
        for half in range(2):
            at = (2 * pair + half) * WIDTH
            query_grad_ref[group, :, at : at + WIDTH] = rows[half * tokens : (half + 1) * tokens]

    def products(left, right):
        whole = dot_nt(left, right)
        return [whole[rows] for rows in block_rows]

    @pl.loop(0, groups)
    def _(group):
        keys = all_blocks(0, group)
        values = all_blocks(1, group)
        value_ext = jnp.concatenate([values, jnp.full(values.shape, -1.0, jnp.bfloat16)], axis=1)
        keys_across = jnp.transpose(keys)
        half_heads = heads_per_group // 2
        for pair in range(pairs):
            query_pair = stacked(query_ref, group, 2 * pair, 2)
            grad_pair = stacked(grad_ref, group, 2 * pair, 2)
            product_pair = stacked(product_ref, group, 2 * pair, 2)
            grad_ext = jnp.concatenate([grad_pair, product_pair], axis=1)
            raw = products(keys, query_pair)
            if pair == pairs // 2:
                key_acc[...] = key_part(group, 0, half_heads)
            scales = [weigh(group, pair, raw, half) for half in range(2)]
            if pair == pairs // 2:
                value_acc[...] = value_part(group, 0, half_heads)
            if pair:
                query_part(keys_across, group, pair - 1)
            centred = products(value_ext, grad_ext)
            for half in range(2):
                differentiate(group, pair, centred, scales[half], half)
        key_whole = key_acc[...] + key_part(group, half_heads, half_heads)
        put_part(group, 0, key_whole * factor)
        put_part(group, 1, value_acc[...] + value_part(group, half_heads, half_heads))
        query_part(keys_across, group, pairs - 1)
        store(group).start()

    slope_sum = jnp.sum(slope_rows[...], axis=1, keepdims=True)
    gain_sum = jnp.sum(gain_rows[...], axis=1, keepdims=True)
    shape = slope_rows.shape
    lane = lax.broadcasted_iota(jnp.int32, shape, 1)
    row = lax.broadcasted_iota(jnp.int32, shape, 0)
    replicas, parts, rows_here, local = bias_ref.shape
    local_heads = shape[0] // parts
    kind = lax.broadcasted_iota(jnp.int32, (rows_here, local), 0)
    for part in range(parts):
        mine = (lane == row - part * local_heads) & (lane < local_heads)
        slope_line = jnp.sum(jnp.where(mine, slope_sum, 0.0), axis=0, keepdims=True)
        gain_line = jnp.sum(jnp.where(mine, gain_sum, 0.0), axis=0, keepdims=True)
        tile = jnp.where(kind == 0, slope_line, jnp.where(kind == 1, gain_line, 0.0))
        bias_ref[:, part] = jnp.broadcast_to(tile[None], (replicas, rows_here, local))
    bias_copy = pltpu.make_async_copy(bias_ref, bias_hbm, bias_sem)
    bias_copy.start()
    for group in range(groups):
        store(group).wait()
    bias_copy.wait()


def combine_kernel(blocks, *refs):
    parts = refs[0:blocks]
    key_out, value_out = refs[blocks:]
    tokens = key_out.shape[0]
    groups = key_out.shape[1] // WIDTH
    for kind, out in enumerate((key_out, value_out)):
        for group in range(groups):
            at = (kind * groups + group) * tokens
            total = parts[0][at : at + tokens, :].astype(jnp.float32)
            for s in range(1, blocks):
                total = total + parts[s][at : at + tokens, :].astype(jnp.float32)
            out[:, group * WIDTH : (group + 1) * WIDTH] = total.astype(jnp.bfloat16)


def bias_kernel(parts_ref, _, out_ref):
    out_ref[...] = jnp.sum(parts_ref[...], axis=0)[0:2, 0 : out_ref.shape[1]]


def body(
    queries,
    key_rows,
    values,
    outputs,
    out_grads,
    depths,
    subtree_end,
    file_lengths,
    slopes,
    ancestor_gain,
):
    blocks = lax.axis_size("ctx")
    replicas = lax.axis_size("dp")
    tokens, width_all = queries.shape[1:]
    kv_width = key_rows.shape[2]
    heads_all = width_all // WIDTH
    groups = kv_width // WIDTH
    heads_per_group = heads_all // groups
    group_columns = heads_per_group * WIDTH
    local_heads = heads_all // blocks
    keys_seen = blocks * tokens
    bf16, f32 = jnp.bfloat16, jnp.float32
    vmem = pl.BlockSpec(memory_space=pltpu.VMEM)
    smem = pl.BlockSpec(memory_space=pltpu.SMEM)
    hbm = pl.BlockSpec(memory_space=pltpu.HBM)
    params = pltpu.CompilerParams(vmem_limit_bytes=(24 if blocks <= 4 else 44) * 1024 * 1024)

    def hold(array):
        return pltpu.with_memory_space_constraint(array, pltpu.HBM)

    key_held, value_held = hold(key_rows[0]), hold(values[0])
    depth_held, end_held = hold(depths), hold(subtree_end)
    message_rows = 2 * groups * tokens
    message = pl.pallas_call(
        pack_kernel,
        out_shape=jax.ShapeDtypeStruct((message_rows + META_ROWS, WIDTH), bf16),
        in_specs=[vmem] * 4,
        out_specs=vmem,
        compiler_params=params,
        name="pack",
    )(key_held, value_held, depth_held, end_held)
    arrived = [
        lax.ppermute(message, "ctx", [(i, i ^ s) for i in range(blocks) if i < i ^ s])
        for s in range(1, blocks)
    ]

    prepared = pl.pallas_call(
        prepare_kernel,
        out_shape=[jax.ShapeDtypeStruct((tokens, width_all), bf16)] * 3,
        in_specs=[vmem] * 3,
        out_specs=[vmem] * 3,
        compiler_params=params,
        cost_estimate=pl.CostEstimate(
            flops=tokens * width_all, bytes_accessed=12 * tokens * width_all, transcendentals=0
        ),
        name="prepare",
    )(hold(queries[0]), hold(outputs[0]), hold(out_grads[0]))

    bias_shape = (replicas, blocks, 8, WIDTH)
    matmul_flops = 2 * tokens * keys_seen * WIDTH * heads_all
    results = pl.pallas_call(
        functools.partial(main_kernel, blocks, heads_per_group, groups),
        out_shape=[jax.ShapeDtypeStruct((tokens, width_all), bf16)]
        + [jax.ShapeDtypeStruct((message_rows, WIDTH), bf16)] * blocks
        + [jax.ShapeDtypeStruct(bias_shape, f32)],
        in_specs=[smem] * 3 + [vmem] * (6 + blocks),
        out_specs=[hbm] + [vmem] * blocks + [hbm],
        scratch_shapes=[
            pltpu.VMEM((groups, tokens, group_columns), bf16),
            pltpu.VMEM((keys_seen, tokens), f32),
            pltpu.VMEM((keys_seen, tokens), f32),
            pltpu.VMEM((heads_all, tokens), f32),
            pltpu.VMEM((heads_all, tokens), f32),
            pltpu.VMEM((keys_seen, WIDTH), f32),
            pltpu.VMEM((keys_seen, WIDTH), f32),
            pltpu.VMEM((2, keys_seen, 2 * tokens), f32),
            pltpu.VMEM((keys_seen, group_columns), bf16),
            pltpu.VMEM((keys_seen, group_columns), bf16),
            pltpu.VMEM(bias_shape, f32),
            pltpu.SemaphoreType.DMA((groups,)),
            pltpu.SemaphoreType.DMA,
        ],
        compiler_params=params,
        cost_estimate=pl.CostEstimate(
            flops=5 * matmul_flops,
            bytes_accessed=10 * tokens * width_all,
            transcendentals=tokens * keys_seen * heads_all,
        ),
        name="attend",
    )(
        hold(file_lengths),
        hold(slopes),
        hold(ancestor_gain),
        depth_held,
        end_held,
        *prepared,
        key_held,
        value_held,
        *arrived,
    )
    query_grads = results[0]
    parts = list(results[1 : 1 + blocks])
    bias_parts = results[1 + blocks].reshape(replicas * blocks, 8, WIDTH)
    for s in reversed(range(1, blocks)):
        back = [(i, i ^ s) for i in range(blocks) if i > i ^ s]
        parts[s] = lax.ppermute(parts[s], "ctx", back)
    bias_parts = lax.all_to_all(bias_parts, ("dp", "ctx"), split_axis=0, concat_axis=0, tiled=True)

    key_grads, value_grads = pl.pallas_call(
        functools.partial(combine_kernel, blocks),
        out_shape=[jax.ShapeDtypeStruct((tokens, kv_width), bf16)] * 2,
        in_specs=[vmem] * blocks,
        out_specs=[vmem] * 2,
        compiler_params=params,
        cost_estimate=pl.CostEstimate(
            flops=2 * message_rows * WIDTH * blocks,
            bytes_accessed=2 * message_rows * WIDTH * (blocks + 1),
            transcendentals=0,
        ),
        name="combine",
    )(parts[0], *reversed(parts[1:]))
    bias_grads = pl.pallas_call(
        bias_kernel,
        out_shape=jax.ShapeDtypeStruct((2, local_heads), f32),
        in_specs=[vmem, hbm],
        out_specs=vmem,
        compiler_params=params,
        name="bias",
    )(bias_parts, hold(key_grads))
    return (query_grads[None], key_grads[None], value_grads[None], bias_grads.T)


def solution(mesh):
    in_specs = (
        P("dp", "ctx", None),
        P("dp", "ctx", None),
        P("dp", "ctx", None),
        P("dp", "ctx", None),
        P("dp", "ctx", None),
        P("dp", "ctx"),
        P("dp", "ctx"),
        P("dp", None),
        P(),
        P(),
    )
    out_specs = (P("dp", "ctx", None), P("dp", "ctx", None), P("dp", "ctx", None), P("ctx", None))
    return jax.shard_map(body, mesh=mesh, in_specs=in_specs, out_specs=out_specs, check_vma=False)
```

```python
import functools

import jax
import jax.numpy as jnp
from jax import lax
from jax.experimental import pallas as pl
from jax.experimental.pallas import tpu as pltpu
from jax.sharding import PartitionSpec as P

WIDTH = 128
LOG2E = 1.4426950408889634
MASKED = -1e30
META_ROWS = 16
END_UNIT = 64


def dot_nt(a, b):
    return lax.dot_general(a, b, (((1,), (1,)), ((), ())), preferred_element_type=jnp.float32)


def dot_nn(a, b):
    return lax.dot_general(a, b, (((1,), (0,)), ((), ())), preferred_element_type=jnp.float32)


def fold_rows(block):
    return jnp.sum(block.reshape(block.shape[0] // 8, 8, block.shape[1]), axis=0)


def as_column(row):
    size = row.shape[1]
    return jnp.transpose(jnp.broadcast_to(row, (size, size)))


def pack_kernel(key_ref, value_ref, depth_ref, end_ref, message_ref):
    tokens = key_ref.shape[0]
    groups = key_ref.shape[1] // WIDTH
    for kind, ref in enumerate((key_ref, value_ref)):
        for group in range(groups):
            at = (kind * groups + group) * tokens
            message_ref[at : at + tokens, :] = ref[:, group * WIDTH : (group + 1) * WIDTH]
    depth = depth_ref[...]
    end = end_ref[...]
    end_high = end // END_UNIT
    end_low = end - end_high * END_UNIT
    row = lax.broadcasted_iota(jnp.int32, (META_ROWS, tokens), 0)
    meta = jnp.where(row == 0, depth, jnp.where(row == 1, end_high, end_low))
    meta = meta.astype(jnp.float32).astype(jnp.bfloat16)
    message_ref[2 * groups * tokens : 2 * groups * tokens + META_ROWS, :] = meta


def prepare_kernel(query_in, output_in, grad_in, query_out, grad_out, product_out):
    query_out[...] = query_in[...]
    grad_out[...] = grad_in[...]
    product_out[...] = grad_in[...] * output_in[...]


def main_kernel(
    blocks,
    heads_per_group,
    groups,
    lengths_ref,
    slope_ref,
    gain_ref,
    depth_ref,
    end_ref,
    query_ref,
    grad_ref,
    product_ref,
    key_ref,
    value_ref,
    *refs,
):
    tokens = query_ref.shape[0]
    remote = refs[0 : blocks - 1]
    query_grad_hbm = refs[blocks - 1]
    part_refs = refs[blocks : 2 * blocks]
    bias_hbm = refs[2 * blocks]
    (
        query_grad_ref,
        distance_ref,
        ancestor_ref,
        slope_rows,
        gain_rows,
        key_acc,
        value_acc,
        weight_ref,
        probs_ref,
        dscore_ref,
        bias_ref,
        store_sems,
        bias_sem,
    ) = refs[2 * blocks + 1 :]
    factor = WIDTH**-0.5
    group_columns = heads_per_group * WIDTH
    pairs = heads_per_group // 2

    def store(group):
        wide = pl.ds(pl.multiple_of(group * group_columns, group_columns), group_columns)
        return pltpu.make_async_copy(
            query_grad_ref.at[group], query_grad_hbm.at[:, wide], store_sems.at[group]
        )

    here = lax.axis_index("ctx")
    query_pos = here * tokens + lax.broadcasted_iota(jnp.int32, (tokens, tokens), 1)
    start = jnp.zeros((tokens, tokens), jnp.int32)
    bound = jnp.int32(0)
    for index in range(lengths_ref.shape[1]):
        bound = bound + lengths_ref[0, index]
        start = jnp.where(query_pos >= bound, bound, start)
    query_depth = jnp.broadcast_to(depth_ref[...].astype(jnp.float32), (tokens, tokens))
    block_rows = [slice(s * tokens, (s + 1) * tokens) for s in range(blocks)]
    for s, rows in enumerate(block_rows):
        key_pos = (here ^ s) * tokens + lax.broadcasted_iota(jnp.int32, (tokens, tokens), 0)
        if s == 0:
            key_depth = as_column(depth_ref[...].astype(jnp.float32))
            key_end = as_column(end_ref[...].astype(jnp.float32))
        else:
            below = slice(2 * groups * tokens, 2 * groups * tokens + META_ROWS)
            meta = remote[s - 1][below, :].astype(jnp.float32)
            key_depth = as_column(meta[0:1])
            key_end = as_column(meta[1:2] * END_UNIT + meta[2:3])
        inside = query_pos.astype(jnp.float32) < key_end
        allowed = (key_pos <= query_pos) & (key_pos >= start)
        distance_ref[rows, :] = jnp.abs(query_depth - key_depth)
        ancestor_ref[rows, :] = jnp.where(allowed, jnp.where(inside, 1.0, 0.0), MASKED)

    def key_block(kind, group, s):
        if s == 0:
            at = pl.multiple_of(group * WIDTH, WIDTH)
            return (key_ref, value_ref)[kind][:, pl.ds(at, WIDTH)]
        at = pl.multiple_of((kind * groups + group) * tokens, tokens)
        return remote[s - 1][pl.ds(at, tokens), :]

    def all_blocks(kind, group):
        return jnp.concatenate([key_block(kind, group, s) for s in range(blocks)], axis=0)

    def stacked(ref, group, first, count):
        at = pl.multiple_of(group * group_columns, group_columns) + first * WIDTH
        heads = [pl.ds(pl.multiple_of(at + i * WIDTH, WIDTH), WIDTH) for i in range(count)]
        return jnp.concatenate([ref[:, head] for head in heads], axis=0)

    def weigh(group, pair, raw, half):
        head = group * heads_per_group + 2 * pair + half
        gain = gain_ref[head] * LOG2E
        slope = slope_ref[head] * LOG2E
        lanes = slice(half * tokens, (half + 1) * tokens)
        tops, totals = [], []
        for s, rows in enumerate(block_rows):
            score = raw[s][:, lanes] * (factor * LOG2E) + (
                gain * ancestor_ref[rows, :] - slope * distance_ref[rows, :]
            )
            top = jnp.max(score, axis=0, keepdims=True)
            weight = jnp.exp2(score - top)
            weight_ref[pair % 2, rows, lanes] = weight
            tops.append(top)
            totals.append(jnp.sum(weight, axis=0, keepdims=True))
        top = functools.reduce(jnp.maximum, tops)
        shrink = [jnp.exp2(t - top) for t in tops]
        inverse = 1.0 / sum(a * b for a, b in zip(totals, shrink))
        return [s * inverse for s in shrink]

    def differentiate(group, pair, centred, scales, half):
        lanes = slice(half * tokens, (half + 1) * tokens)
        to = slice((2 * pair + half) * tokens, (2 * pair + half + 1) * tokens)
        slope_sum, gain_sum = 0.0, 0.0
        for s, rows in enumerate(block_rows):
            probs = weight_ref[pair % 2, rows, lanes] * scales[s]
            dscore = probs * centred[s][:, lanes]
            probs_ref[rows, to] = probs.astype(jnp.bfloat16)
            dscore_ref[rows, to] = dscore.astype(jnp.bfloat16)
            slope_sum = slope_sum + fold_rows(dscore * distance_ref[rows, :])
            gain_sum = gain_sum + fold_rows(dscore * ancestor_ref[rows, :])
        at = pl.ds(group * heads_per_group + 2 * pair + half, 1)
        slope_rows[at, :] = -jnp.sum(slope_sum, axis=0, keepdims=True)
        gain_rows[at, :] = jnp.sum(gain_sum, axis=0, keepdims=True)

    def put_part(group, kind, whole):
        at = pl.multiple_of((kind * groups + group) * tokens, tokens)
        for s, rows in enumerate(block_rows):
            part_refs[s][pl.ds(at, tokens), :] = whole[rows].astype(jnp.bfloat16)

    def key_part(group, first, count):
        heads = stacked(query_ref, group, first, count)
        lanes = slice(first * tokens, (first + count) * tokens)
        return dot_nn(dscore_ref[:, lanes], heads)

    def value_part(group, first, count):
        heads = stacked(grad_ref, group, first, count)
        lanes = slice(first * tokens, (first + count) * tokens)
        return dot_nn(probs_ref[:, lanes], heads)

    def query_part(keys_across, group, pair):
        lanes = slice(2 * pair * tokens, (2 * pair + 2) * tokens)
        across = dot_nn(keys_across, dscore_ref[:, lanes]) * factor
        rows = jnp.transpose(across.astype(jnp.bfloat16))
        for half in range(2):
            at = (2 * pair + half) * WIDTH
            query_grad_ref[group, :, at : at + WIDTH] = rows[half * tokens : (half + 1) * tokens]

    def products(left, right):
        whole = dot_nt(left, right)
        return [whole[rows] for rows in block_rows]

    @pl.loop(0, groups)
    def _(group):
        keys = all_blocks(0, group)
        values = all_blocks(1, group)
        value_ext = jnp.concatenate([values, jnp.full(values.shape, -1.0, jnp.bfloat16)], axis=1)
        keys_across = jnp.transpose(keys)
        half_heads = heads_per_group // 2
        for pair in range(pairs):
            query_pair = stacked(query_ref, group, 2 * pair, 2)
            grad_pair = stacked(grad_ref, group, 2 * pair, 2)
            product_pair = stacked(product_ref, group, 2 * pair, 2)
            grad_ext = jnp.concatenate([grad_pair, product_pair], axis=1)
            raw = products(keys, query_pair)
            if pair == pairs // 2:
                key_acc[...] = key_part(group, 0, half_heads)
            scales = [weigh(group, pair, raw, half) for half in range(2)]
            if pair == pairs // 2:
                value_acc[...] = value_part(group, 0, half_heads)
            if pair:
                query_part(keys_across, group, pair - 1)
            centred = products(value_ext, grad_ext)
            for half in range(2):
                differentiate(group, pair, centred, scales[half], half)
        key_whole = key_acc[...] + key_part(group, half_heads, half_heads)
        put_part(group, 0, key_whole * factor)
        put_part(group, 1, value_acc[...] + value_part(group, half_heads, half_heads))
        query_part(keys_across, group, pairs - 1)
        store(group).start()

    slope_sum = jnp.sum(slope_rows[...], axis=1, keepdims=True)
    gain_sum = jnp.sum(gain_rows[...], axis=1, keepdims=True)
    shape = slope_rows.shape
    lane = lax.broadcasted_iota(jnp.int32, shape, 1)
    row = lax.broadcasted_iota(jnp.int32, shape, 0)
    replicas, parts, rows_here, local = bias_ref.shape
    local_heads = shape[0] // parts
    kind = lax.broadcasted_iota(jnp.int32, (rows_here, local), 0)
    for part in range(parts):
        mine = (lane == row - part * local_heads) & (lane < local_heads)
        slope_line = jnp.sum(jnp.where(mine, slope_sum, 0.0), axis=0, keepdims=True)
        gain_line = jnp.sum(jnp.where(mine, gain_sum, 0.0), axis=0, keepdims=True)
        tile = jnp.where(kind == 0, slope_line, jnp.where(kind == 1, gain_line, 0.0))
        bias_ref[:, part] = jnp.broadcast_to(tile[None], (replicas, rows_here, local))
    bias_copy = pltpu.make_async_copy(bias_ref, bias_hbm, bias_sem)
    bias_copy.start()
    for group in range(groups):
        store(group).wait()
    bias_copy.wait()


def add_kernel(mine_ref, theirs_ref, next_ref, sum_ref, next_out):
    total = mine_ref[...].astype(jnp.float32) + theirs_ref[...].astype(jnp.float32)
    sum_ref[...] = total.astype(jnp.bfloat16)
    next_out[...] = next_ref[...]


def combine_kernel(blocks, *refs):
    parts = refs[0:blocks]
    key_out, value_out = refs[blocks:]
    tokens = key_out.shape[0]
    groups = key_out.shape[1] // WIDTH
    for kind, out in enumerate((key_out, value_out)):
        for group in range(groups):
            at = (kind * groups + group) * tokens
            total = parts[0][at : at + tokens, :].astype(jnp.float32)
            for s in range(1, blocks):
                total = total + parts[s][at : at + tokens, :].astype(jnp.float32)
            out[:, group * WIDTH : (group + 1) * WIDTH] = total.astype(jnp.bfloat16)


def bias_kernel(parts_ref, _, out_ref):
    out_ref[...] = jnp.sum(parts_ref[...], axis=0)[0:2, 0 : out_ref.shape[1]]


def body(
    queries,
    key_rows,
    values,
    outputs,
    out_grads,
    depths,
    subtree_end,
    file_lengths,
    slopes,
    ancestor_gain,
):
    blocks = lax.axis_size("ctx")
    replicas = lax.axis_size("dp")
    tokens, width_all = queries.shape[1:]
    kv_width = key_rows.shape[2]
    heads_all = width_all // WIDTH
    groups = kv_width // WIDTH
    heads_per_group = heads_all // groups
    group_columns = heads_per_group * WIDTH
    local_heads = heads_all // blocks
    keys_seen = blocks * tokens
    bf16, f32 = jnp.bfloat16, jnp.float32
    vmem = pl.BlockSpec(memory_space=pltpu.VMEM)
    smem = pl.BlockSpec(memory_space=pltpu.SMEM)
    hbm = pl.BlockSpec(memory_space=pltpu.HBM)
    params = pltpu.CompilerParams(vmem_limit_bytes=(24 if blocks <= 4 else 44) * 1024 * 1024)

    def hold(array):
        return pltpu.with_memory_space_constraint(array, pltpu.HBM)

    key_held, value_held = hold(key_rows[0]), hold(values[0])
    depth_held, end_held = hold(depths), hold(subtree_end)
    message_rows = 2 * groups * tokens
    message = pl.pallas_call(
        pack_kernel,
        out_shape=jax.ShapeDtypeStruct((message_rows + META_ROWS, WIDTH), bf16),
        in_specs=[vmem] * 4,
        out_specs=vmem,
        compiler_params=params,
        name="pack",
    )(key_held, value_held, depth_held, end_held)
    if blocks == 4:
        along_y = lax.ppermute(message, "ctx", [(0, 2), (1, 3)])
        along_x = lax.ppermute(message, "ctx", [(0, 1), (2, 3)])
        across = lax.ppermute(along_y, "ctx", [(2, 3), (3, 2)])
        arrived = [along_x, along_y, across]
    else:
        arrived = [
            lax.ppermute(message, "ctx", [(i, i ^ s) for i in range(blocks) if i < i ^ s])
            for s in range(1, blocks)
        ]

    prepared = pl.pallas_call(
        prepare_kernel,
        out_shape=[jax.ShapeDtypeStruct((tokens, width_all), bf16)] * 3,
        in_specs=[vmem] * 3,
        out_specs=[vmem] * 3,
        compiler_params=params,
        cost_estimate=pl.CostEstimate(
            flops=tokens * width_all, bytes_accessed=12 * tokens * width_all, transcendentals=0
        ),
        name="prepare",
    )(hold(queries[0]), hold(outputs[0]), hold(out_grads[0]))

    bias_shape = (replicas, blocks, 8, WIDTH)
    matmul_flops = 2 * tokens * keys_seen * WIDTH * heads_all
    results = pl.pallas_call(
        functools.partial(main_kernel, blocks, heads_per_group, groups),
        out_shape=[jax.ShapeDtypeStruct((tokens, width_all), bf16)]
        + [jax.ShapeDtypeStruct((message_rows, WIDTH), bf16)] * blocks
        + [jax.ShapeDtypeStruct(bias_shape, f32)],
        in_specs=[smem] * 3 + [vmem] * (6 + blocks),
        out_specs=[hbm] + [vmem] * blocks + [hbm],
        scratch_shapes=[
            pltpu.VMEM((groups, tokens, group_columns), bf16),
            pltpu.VMEM((keys_seen, tokens), f32),
            pltpu.VMEM((keys_seen, tokens), f32),
            pltpu.VMEM((heads_all, tokens), f32),
            pltpu.VMEM((heads_all, tokens), f32),
            pltpu.VMEM((keys_seen, WIDTH), f32),
            pltpu.VMEM((keys_seen, WIDTH), f32),
            pltpu.VMEM((2, keys_seen, 2 * tokens), f32),
            pltpu.VMEM((keys_seen, group_columns), bf16),
            pltpu.VMEM((keys_seen, group_columns), bf16),
            pltpu.VMEM(bias_shape, f32),
            pltpu.SemaphoreType.DMA((groups,)),
            pltpu.SemaphoreType.DMA,
        ],
        compiler_params=params,
        cost_estimate=pl.CostEstimate(
            flops=5 * matmul_flops,
            bytes_accessed=10 * tokens * width_all,
            transcendentals=tokens * keys_seen * heads_all,
        ),
        name="attend",
    )(
        hold(file_lengths),
        hold(slopes),
        hold(ancestor_gain),
        depth_held,
        end_held,
        *prepared,
        key_held,
        value_held,
        *arrived,
    )
    query_grads = results[0]
    parts = list(results[1 : 1 + blocks])
    bias_parts = results[1 + blocks].reshape(replicas * blocks, 8, WIDTH)
    if blocks == 4:
        across = lax.ppermute(parts[3], "ctx", [(3, 2), (2, 3)])
        along_y, along_x = pl.pallas_call(
            add_kernel,
            out_shape=[jax.ShapeDtypeStruct(parts[0].shape, bf16)] * 2,
            in_specs=[vmem] * 3,
            out_specs=[vmem] * 2,
            compiler_params=params,
            name="add",
        )(parts[2], across, parts[1])
        along_y = lax.ppermute(along_y, "ctx", [(2, 0), (3, 1)])
        along_x = lax.ppermute(along_x, "ctx", [(1, 0), (3, 2)])
        parts = [parts[0], along_y, along_x]
    else:
        for s in range(1, blocks):
            back = [(i, i ^ s) for i in range(blocks) if i > i ^ s]
            parts[s] = lax.ppermute(parts[s], "ctx", back)
    bias_parts = lax.all_to_all(bias_parts, ("dp", "ctx"), split_axis=0, concat_axis=0, tiled=True)

    key_grads, value_grads = pl.pallas_call(
        functools.partial(combine_kernel, len(parts)),
        out_shape=[jax.ShapeDtypeStruct((tokens, kv_width), bf16)] * 2,
        in_specs=[vmem] * len(parts),
        out_specs=[vmem] * 2,
        compiler_params=params,
        cost_estimate=pl.CostEstimate(
            flops=2 * message_rows * WIDTH * blocks,
            bytes_accessed=2 * message_rows * WIDTH * (blocks + 1),
            transcendentals=0,
        ),
        name="combine",
    )(*parts)
    bias_grads = pl.pallas_call(
        bias_kernel,
        out_shape=jax.ShapeDtypeStruct((2, local_heads), f32),
        in_specs=[vmem, hbm],
        out_specs=vmem,
        compiler_params=params,
        name="bias",
    )(bias_parts, hold(key_grads))
    return (query_grads[None], key_grads[None], value_grads[None], bias_grads.T)


def solution(mesh):
    in_specs = (
        P("dp", "ctx", None),
        P("dp", "ctx", None),
        P("dp", "ctx", None),
        P("dp", "ctx", None),
        P("dp", "ctx", None),
        P("dp", "ctx"),
        P("dp", "ctx"),
        P("dp", None),
        P(),
        P(),
    )
    out_specs = (P("dp", "ctx", None), P("dp", "ctx", None), P("dp", "ctx", None), P("ctx", None))
    return jax.shard_map(body, mesh=mesh, in_specs=in_specs, out_specs=out_specs, check_vma=False)
```

```python
import functools

import jax
import jax.numpy as jnp
from jax import lax
from jax.experimental import pallas as pl
from jax.experimental.pallas import tpu as pltpu
from jax.sharding import PartitionSpec as P

WIDTH = 128
LOG2E = 1.4426950408889634
MASKED = -1e30
META_ROWS = 16
END_UNIT = 64


def dot_nt(a, b):
    return lax.dot_general(a, b, (((1,), (1,)), ((), ())), preferred_element_type=jnp.float32)


def dot_nn(a, b):
    return lax.dot_general(a, b, (((1,), (0,)), ((), ())), preferred_element_type=jnp.float32)


def fold_rows(block):
    return jnp.sum(block.reshape(block.shape[0] // 8, 8, block.shape[1]), axis=0)


def as_column(row):
    size = row.shape[1]
    return jnp.transpose(jnp.broadcast_to(row, (size, size)))


def pack_kernel(key_ref, value_ref, depth_ref, end_ref, message_ref):
    tokens = key_ref.shape[0]
    groups = key_ref.shape[1] // WIDTH
    for kind, ref in enumerate((key_ref, value_ref)):
        for group in range(groups):
            at = (kind * groups + group) * tokens
            message_ref[at : at + tokens, :] = ref[:, group * WIDTH : (group + 1) * WIDTH]
    depth = depth_ref[...]
    end = end_ref[...]
    end_high = end // END_UNIT
    end_low = end - end_high * END_UNIT
    row = lax.broadcasted_iota(jnp.int32, (META_ROWS, tokens), 0)
    meta = jnp.where(row == 0, depth, jnp.where(row == 1, end_high, end_low))
    meta = meta.astype(jnp.float32).astype(jnp.bfloat16)
    message_ref[2 * groups * tokens : 2 * groups * tokens + META_ROWS, :] = meta


def prepare_kernel(query_in, output_in, grad_in, query_out, grad_out, product_out):
    query_out[...] = query_in[...]
    grad_out[...] = grad_in[...]
    product_out[...] = grad_in[...] * output_in[...]


def main_kernel(
    blocks,
    heads_per_group,
    groups,
    lengths_ref,
    slope_ref,
    gain_ref,
    depth_ref,
    end_ref,
    query_ref,
    grad_ref,
    product_ref,
    key_ref,
    value_ref,
    *refs,
):
    tokens = query_ref.shape[0]
    remote = refs[0 : blocks - 1]
    query_grad_hbm = refs[blocks - 1]
    part_refs = refs[blocks : 2 * blocks]
    bias_ref = refs[2 * blocks]
    (
        query_grad_ref,
        distance_ref,
        ancestor_ref,
        slope_rows,
        gain_rows,
        key_acc,
        value_acc,
        weight_ref,
        probs_ref,
        dscore_ref,
        store_sems,
    ) = refs[2 * blocks + 1 :]
    factor = WIDTH**-0.5
    group_columns = heads_per_group * WIDTH
    pairs = heads_per_group // 2

    def store(group):
        wide = pl.ds(pl.multiple_of(group * group_columns, group_columns), group_columns)
        return pltpu.make_async_copy(
            query_grad_ref.at[group], query_grad_hbm.at[:, wide], store_sems.at[group]
        )

    here = lax.axis_index("ctx")
    query_pos = here * tokens + lax.broadcasted_iota(jnp.int32, (tokens, tokens), 1)
    start = jnp.zeros((tokens, tokens), jnp.int32)
    bound = jnp.int32(0)
    for index in range(lengths_ref.shape[1]):
        bound = bound + lengths_ref[0, index]
        start = jnp.where(query_pos >= bound, bound, start)
    query_depth = jnp.broadcast_to(depth_ref[...].astype(jnp.float32), (tokens, tokens))
    block_rows = [slice(s * tokens, (s + 1) * tokens) for s in range(blocks)]
    for s, rows in enumerate(block_rows):
        key_pos = (here ^ s) * tokens + lax.broadcasted_iota(jnp.int32, (tokens, tokens), 0)
        if s == 0:
            key_depth = as_column(depth_ref[...].astype(jnp.float32))
            key_end = as_column(end_ref[...].astype(jnp.float32))
        else:
            below = slice(2 * groups * tokens, 2 * groups * tokens + META_ROWS)
            meta = remote[s - 1][below, :].astype(jnp.float32)
            key_depth = as_column(meta[0:1])
            key_end = as_column(meta[1:2] * END_UNIT + meta[2:3])
        inside = query_pos.astype(jnp.float32) < key_end
        allowed = (key_pos <= query_pos) & (key_pos >= start)
        distance_ref[rows, :] = jnp.abs(query_depth - key_depth)
        ancestor_ref[rows, :] = jnp.where(allowed, jnp.where(inside, 1.0, 0.0), MASKED)

    def key_block(kind, group, s):
        if s == 0:
            at = pl.multiple_of(group * WIDTH, WIDTH)
            return (key_ref, value_ref)[kind][:, pl.ds(at, WIDTH)]
        at = pl.multiple_of((kind * groups + group) * tokens, tokens)
        return remote[s - 1][pl.ds(at, tokens), :]

    def all_blocks(kind, group):
        return jnp.concatenate([key_block(kind, group, s) for s in range(blocks)], axis=0)

    def stacked(ref, group, first, count):
        at = pl.multiple_of(group * group_columns, group_columns) + first * WIDTH
        heads = [pl.ds(pl.multiple_of(at + i * WIDTH, WIDTH), WIDTH) for i in range(count)]
        return jnp.concatenate([ref[:, head] for head in heads], axis=0)

    def weigh(group, pair, raw, half):
        head = group * heads_per_group + 2 * pair + half
        gain = gain_ref[head] * LOG2E
        slope = slope_ref[head] * LOG2E
        lanes = slice(half * tokens, (half + 1) * tokens)
        tops, totals = [], []
        for s, rows in enumerate(block_rows):
            score = raw[s][:, lanes] * (factor * LOG2E) + (
                gain * ancestor_ref[rows, :] - slope * distance_ref[rows, :]
            )
            top = jnp.max(score, axis=0, keepdims=True)
            weight = jnp.exp2(score - top)
            weight_ref[pair % 2, rows, lanes] = weight
            tops.append(top)
            totals.append(jnp.sum(weight, axis=0, keepdims=True))
        top = functools.reduce(jnp.maximum, tops)
        shrink = [jnp.exp2(t - top) for t in tops]
        inverse = 1.0 / sum(a * b for a, b in zip(totals, shrink))
        return [s * inverse for s in shrink]

    def differentiate(group, pair, centred, scales, half):
        lanes = slice(half * tokens, (half + 1) * tokens)
        to = slice((2 * pair + half) * tokens, (2 * pair + half + 1) * tokens)
        slope_sum, gain_sum = 0.0, 0.0
        for s, rows in enumerate(block_rows):
            probs = weight_ref[pair % 2, rows, lanes] * scales[s]
            dscore = probs * centred[s][:, lanes]
            probs_ref[rows, to] = probs.astype(jnp.bfloat16)
            dscore_ref[rows, to] = dscore.astype(jnp.bfloat16)
            slope_sum = slope_sum + fold_rows(dscore * distance_ref[rows, :])
            gain_sum = gain_sum + fold_rows(dscore * ancestor_ref[rows, :])
        at = pl.ds(group * heads_per_group + 2 * pair + half, 1)
        slope_rows[at, :] = -jnp.sum(slope_sum, axis=0, keepdims=True)
        gain_rows[at, :] = jnp.sum(gain_sum, axis=0, keepdims=True)

    def put_part(group, kind, whole):
        at = pl.multiple_of((kind * groups + group) * tokens, tokens)
        for s, rows in enumerate(block_rows):
            part_refs[s][pl.ds(at, tokens), :] = whole[rows].astype(jnp.bfloat16)

    def key_part(group, first, count):
        heads = stacked(query_ref, group, first, count)
        lanes = slice(first * tokens, (first + count) * tokens)
        return dot_nn(dscore_ref[:, lanes], heads)

    def value_part(group, first, count):
        heads = stacked(grad_ref, group, first, count)
        lanes = slice(first * tokens, (first + count) * tokens)
        return dot_nn(probs_ref[:, lanes], heads)

    def query_part(keys_across, group, pair):
        lanes = slice(2 * pair * tokens, (2 * pair + 2) * tokens)
        across = dot_nn(keys_across, dscore_ref[:, lanes]) * factor
        rows = jnp.transpose(across.astype(jnp.bfloat16))
        for half in range(2):
            at = (2 * pair + half) * WIDTH
            query_grad_ref[group, :, at : at + WIDTH] = rows[half * tokens : (half + 1) * tokens]

    def products(left, right):
        whole = dot_nt(left, right)
        return [whole[rows] for rows in block_rows]

    @pl.loop(0, groups)
    def _(group):
        keys = all_blocks(0, group)
        values = all_blocks(1, group)
        value_ext = jnp.concatenate([values, jnp.full(values.shape, -1.0, jnp.bfloat16)], axis=1)
        keys_across = jnp.transpose(keys)
        half_heads = heads_per_group // 2
        for pair in range(pairs):
            query_pair = stacked(query_ref, group, 2 * pair, 2)
            grad_pair = stacked(grad_ref, group, 2 * pair, 2)
            product_pair = stacked(product_ref, group, 2 * pair, 2)
            grad_ext = jnp.concatenate([grad_pair, product_pair], axis=1)
            raw = products(keys, query_pair)
            if pair == pairs // 2:
                key_acc[...] = key_part(group, 0, half_heads)
            scales = [weigh(group, pair, raw, half) for half in range(2)]
            if pair == pairs // 2:
                value_acc[...] = value_part(group, 0, half_heads)
            if pair:
                query_part(keys_across, group, pair - 1)
            centred = products(value_ext, grad_ext)
            for half in range(2):
                differentiate(group, pair, centred, scales[half], half)
        key_whole = key_acc[...] + key_part(group, half_heads, half_heads)
        put_part(group, 0, key_whole * factor)
        put_part(group, 1, value_acc[...] + value_part(group, half_heads, half_heads))
        query_part(keys_across, group, pairs - 1)
        store(group).start()

    shape = slope_rows.shape
    diagonal = lax.broadcasted_iota(jnp.int32, shape, 0) == lax.broadcasted_iota(
        jnp.int32, shape, 1
    )
    lines = []
    for rows in (slope_rows, gain_rows):
        column = jnp.sum(rows[...], axis=1, keepdims=True)
        lines.append(jnp.sum(jnp.where(diagonal, column, 0.0), axis=0, keepdims=True))
    row = lax.broadcasted_iota(jnp.int32, bias_ref.shape, 0)
    bias_ref[...] = jnp.where(row == 0, lines[0], jnp.where(row == 1, lines[1], 0.0))
    for group in range(groups):
        store(group).wait()


def combine_kernel(blocks, *refs):
    parts = refs[0:blocks]
    bias_ref, key_out, value_out, bias_out = refs[blocks:]
    tokens = key_out.shape[0]
    groups = key_out.shape[1] // WIDTH
    for kind, out in enumerate((key_out, value_out)):
        for group in range(groups):
            at = (kind * groups + group) * tokens
            total = parts[0][at : at + tokens, :].astype(jnp.float32)
            for s in range(1, blocks):
                total = total + parts[s][at : at + tokens, :].astype(jnp.float32)
            out[:, group * WIDTH : (group + 1) * WIDTH] = total.astype(jnp.bfloat16)
    here = lax.axis_index("ctx")
    share = bias_out.shape[1]
    mine = bias_ref[0:2, 0:share]
    for block in range(1, blocks):
        other = bias_ref[0:2, block * share : (block + 1) * share]
        mine = jnp.where(here == block, other, mine)
    bias_out[...] = mine


def body(
    queries,
    key_rows,
    values,
    outputs,
    out_grads,
    depths,
    subtree_end,
    file_lengths,
    slopes,
    ancestor_gain,
):
    blocks = lax.axis_size("ctx")
    replicas = lax.axis_size("dp")
    tokens, width_all = queries.shape[1:]
    kv_width = key_rows.shape[2]
    heads_all = width_all // WIDTH
    groups = kv_width // WIDTH
    heads_per_group = heads_all // groups
    group_columns = heads_per_group * WIDTH
    local_heads = heads_all // blocks
    keys_seen = blocks * tokens
    bf16, f32 = jnp.bfloat16, jnp.float32
    vmem = pl.BlockSpec(memory_space=pltpu.VMEM)
    smem = pl.BlockSpec(memory_space=pltpu.SMEM)
    hbm = pl.BlockSpec(memory_space=pltpu.HBM)
    params = pltpu.CompilerParams(vmem_limit_bytes=(24 if blocks <= 4 else 44) * 1024 * 1024)

    def hold(array):
        return pltpu.with_memory_space_constraint(array, pltpu.HBM)

    key_held, value_held = hold(key_rows[0]), hold(values[0])
    depth_held, end_held = hold(depths), hold(subtree_end)
    message_rows = 2 * groups * tokens
    message = pl.pallas_call(
        pack_kernel,
        out_shape=jax.ShapeDtypeStruct((message_rows + META_ROWS, WIDTH), bf16),
        in_specs=[vmem] * 4,
        out_specs=vmem,
        compiler_params=params,
        name="pack",
    )(key_held, value_held, depth_held, end_held)
    arrived = [
        lax.ppermute(message, "ctx", [(i, i ^ s) for i in range(blocks) if i < i ^ s])
        for s in range(1, blocks)
    ]

    prepared = pl.pallas_call(
        prepare_kernel,
        out_shape=[jax.ShapeDtypeStruct((tokens, width_all), bf16)] * 3,
        in_specs=[vmem] * 3,
        out_specs=[vmem] * 3,
        compiler_params=params,
        cost_estimate=pl.CostEstimate(
            flops=tokens * width_all, bytes_accessed=12 * tokens * width_all, transcendentals=0
        ),
        name="prepare",
    )(hold(queries[0]), hold(outputs[0]), hold(out_grads[0]))

    bias_shape = (8, WIDTH)
    matmul_flops = 2 * tokens * keys_seen * WIDTH * heads_all
    results = pl.pallas_call(
        functools.partial(main_kernel, blocks, heads_per_group, groups),
        out_shape=[jax.ShapeDtypeStruct((tokens, width_all), bf16)]
        + [jax.ShapeDtypeStruct((message_rows, WIDTH), bf16)] * blocks
        + [jax.ShapeDtypeStruct(bias_shape, f32)],
        in_specs=[smem] * 3 + [vmem] * (6 + blocks),
        out_specs=[hbm] + [vmem] * (blocks + 1),
        scratch_shapes=[
            pltpu.VMEM((groups, tokens, group_columns), bf16),
            pltpu.VMEM((keys_seen, tokens), f32),
            pltpu.VMEM((keys_seen, tokens), f32),
            pltpu.VMEM((heads_all, tokens), f32),
            pltpu.VMEM((heads_all, tokens), f32),
            pltpu.VMEM((keys_seen, WIDTH), f32),
            pltpu.VMEM((keys_seen, WIDTH), f32),
            pltpu.VMEM((2, keys_seen, 2 * tokens), f32),
            pltpu.VMEM((keys_seen, group_columns), bf16),
            pltpu.VMEM((keys_seen, group_columns), bf16),
            pltpu.SemaphoreType.DMA((groups,)),
        ],
        compiler_params=params,
        cost_estimate=pl.CostEstimate(
            flops=5 * matmul_flops,
            bytes_accessed=10 * tokens * width_all,
            transcendentals=tokens * keys_seen * heads_all,
        ),
        name="attend",
    )(
        hold(file_lengths),
        hold(slopes),
        hold(ancestor_gain),
        depth_held,
        end_held,
        *prepared,
        key_held,
        value_held,
        *arrived,
    )
    query_grads = results[0]
    parts = list(results[1 : 1 + blocks])
    bias = results[1 + blocks]
    for s in range(1, blocks):
        back = [(i, i ^ s) for i in range(blocks) if i > i ^ s]
        parts[s] = lax.ppermute(parts[s], "ctx", back)
    for axis, size in (("ctx", blocks), ("dp", replicas)):
        bit = 1
        while bit < size:
            bias = bias + lax.ppermute(bias, axis, [(i, i ^ bit) for i in range(size)])
            bit = 2 * bit

    key_grads, value_grads, bias_grads = pl.pallas_call(
        functools.partial(combine_kernel, blocks),
        out_shape=[jax.ShapeDtypeStruct((tokens, kv_width), bf16)] * 2
        + [jax.ShapeDtypeStruct((2, local_heads), f32)],
        in_specs=[vmem] * (blocks + 1),
        out_specs=[vmem] * 3,
        compiler_params=params,
        cost_estimate=pl.CostEstimate(
            flops=2 * message_rows * WIDTH * blocks,
            bytes_accessed=2 * message_rows * WIDTH * (blocks + 1),
            transcendentals=0,
        ),
        name="combine",
    )(*parts, bias)
    return (query_grads[None], key_grads[None], value_grads[None], bias_grads.T)


def solution(mesh):
    in_specs = (
        P("dp", "ctx", None),
        P("dp", "ctx", None),
        P("dp", "ctx", None),
        P("dp", "ctx", None),
        P("dp", "ctx", None),
        P("dp", "ctx"),
        P("dp", "ctx"),
        P("dp", None),
        P(),
        P(),
    )
    out_specs = (P("dp", "ctx", None), P("dp", "ctx", None), P("dp", "ctx", None), P("ctx", None))
    return jax.shard_map(body, mesh=mesh, in_specs=in_specs, out_specs=out_specs, check_vma=False)
```

```python
import functools

import jax
import jax.numpy as jnp
from jax import lax
from jax.experimental import pallas as pl
from jax.experimental.pallas import tpu as pltpu
from jax.sharding import PartitionSpec as P

WIDTH = 128
LOG2E = 1.4426950408889634
MASKED = -1e30
META_ROWS = 16
END_UNIT = 64


def dot_nt(a, b):
    return lax.dot_general(a, b, (((1,), (1,)), ((), ())), preferred_element_type=jnp.float32)


def dot_nn(a, b):
    return lax.dot_general(a, b, (((1,), (0,)), ((), ())), preferred_element_type=jnp.float32)


def fold_rows(block):
    return jnp.sum(block.reshape(block.shape[0] // 8, 8, block.shape[1]), axis=0)


def as_column(row):
    size = row.shape[1]
    return jnp.transpose(jnp.broadcast_to(row, (size, size)))


def pack_kernel(key_ref, value_ref, depth_ref, end_ref, message_ref):
    tokens = key_ref.shape[0]
    groups = key_ref.shape[1] // WIDTH
    for kind, ref in enumerate((key_ref, value_ref)):
        for group in range(groups):
            at = (kind * groups + group) * tokens
            message_ref[at : at + tokens, :] = ref[:, group * WIDTH : (group + 1) * WIDTH]
    depth = depth_ref[...]
    end = end_ref[...]
    end_high = end // END_UNIT
    end_low = end - end_high * END_UNIT
    row = lax.broadcasted_iota(jnp.int32, (META_ROWS, tokens), 0)
    meta = jnp.where(row == 0, depth, jnp.where(row == 1, end_high, end_low))
    meta = meta.astype(jnp.float32).astype(jnp.bfloat16)
    message_ref[2 * groups * tokens : 2 * groups * tokens + META_ROWS, :] = meta


def prepare_kernel(query_in, output_in, grad_in, query_out, grad_out, product_out):
    query_out[...] = query_in[...]
    grad_out[...] = grad_in[...]
    product_out[...] = grad_in[...] * output_in[...]


def main_kernel(
    blocks,
    heads_per_group,
    groups,
    shifts,
    lengths_ref,
    slope_ref,
    gain_ref,
    depth_ref,
    end_ref,
    query_ref,
    grad_ref,
    product_ref,
    key_ref,
    value_ref,
    *refs,
):
    tokens = query_ref.shape[0]
    remote = [refs[shifts.index(s)] for s in range(1, blocks)]
    query_grad_hbm = refs[blocks - 1]
    part_refs = refs[blocks : 2 * blocks]
    bias_hbm = refs[2 * blocks]
    (
        query_grad_ref,
        distance_ref,
        ancestor_ref,
        slope_rows,
        gain_rows,
        key_acc,
        value_acc,
        weight_ref,
        probs_ref,
        dscore_ref,
        bias_ref,
        store_sems,
        bias_sem,
    ) = refs[2 * blocks + 1 :]
    factor = WIDTH**-0.5
    group_columns = heads_per_group * WIDTH
    pairs = heads_per_group // 2

    def store(group):
        wide = pl.ds(pl.multiple_of(group * group_columns, group_columns), group_columns)
        return pltpu.make_async_copy(
            query_grad_ref.at[group], query_grad_hbm.at[:, wide], store_sems.at[group]
        )

    here = lax.axis_index("ctx")
    query_pos = here * tokens + lax.broadcasted_iota(jnp.int32, (tokens, tokens), 1)
    start = jnp.zeros((tokens, tokens), jnp.int32)
    bound = jnp.int32(0)
    for index in range(lengths_ref.shape[1]):
        bound = bound + lengths_ref[0, index]
        start = jnp.where(query_pos >= bound, bound, start)
    query_depth = jnp.broadcast_to(depth_ref[...].astype(jnp.float32), (tokens, tokens))
    block_rows = [slice(s * tokens, (s + 1) * tokens) for s in range(blocks)]
    for s, rows in enumerate(block_rows):
        key_pos = (here ^ s) * tokens + lax.broadcasted_iota(jnp.int32, (tokens, tokens), 0)
        if s == 0:
            key_depth = as_column(depth_ref[...].astype(jnp.float32))
            key_end = as_column(end_ref[...].astype(jnp.float32))
        else:
            below = slice(2 * groups * tokens, 2 * groups * tokens + META_ROWS)
            meta = remote[s - 1][below, :].astype(jnp.float32)
            key_depth = as_column(meta[0:1])
            key_end = as_column(meta[1:2] * END_UNIT + meta[2:3])
        inside = query_pos.astype(jnp.float32) < key_end
        allowed = (key_pos <= query_pos) & (key_pos >= start)
        distance_ref[rows, :] = jnp.abs(query_depth - key_depth)
        ancestor_ref[rows, :] = jnp.where(allowed, jnp.where(inside, 1.0, 0.0), MASKED)

    def key_block(kind, group, s):
        if s == 0:
            at = pl.multiple_of(group * WIDTH, WIDTH)
            return (key_ref, value_ref)[kind][:, pl.ds(at, WIDTH)]
        at = pl.multiple_of((kind * groups + group) * tokens, tokens)
        return remote[s - 1][pl.ds(at, tokens), :]

    def all_blocks(kind, group):
        return jnp.concatenate([key_block(kind, group, s) for s in range(blocks)], axis=0)

    def stacked(ref, group, first, count):
        at = pl.multiple_of(group * group_columns, group_columns) + first * WIDTH
        heads = [pl.ds(pl.multiple_of(at + i * WIDTH, WIDTH), WIDTH) for i in range(count)]
        return jnp.concatenate([ref[:, head] for head in heads], axis=0)

    def weigh(group, pair, raw, half):
        head = group * heads_per_group + 2 * pair + half
        gain = gain_ref[head] * LOG2E
        slope = slope_ref[head] * LOG2E
        lanes = slice(half * tokens, (half + 1) * tokens)
        tops, totals = [], []
        for s, rows in enumerate(block_rows):
            score = raw[s][:, lanes] * (factor * LOG2E) + (
                gain * ancestor_ref[rows, :] - slope * distance_ref[rows, :]
            )
            top = jnp.max(score, axis=0, keepdims=True)
            weight = jnp.exp2(score - top)
            weight_ref[pair % 2, rows, lanes] = weight
            tops.append(top)
            totals.append(jnp.sum(weight, axis=0, keepdims=True))
        top = functools.reduce(jnp.maximum, tops)
        shrink = [jnp.exp2(t - top) for t in tops]
        inverse = 1.0 / sum(a * b for a, b in zip(totals, shrink))
        return [s * inverse for s in shrink]

    def differentiate(group, pair, centred, scales, half):
        lanes = slice(half * tokens, (half + 1) * tokens)
        to = slice((2 * pair + half) * tokens, (2 * pair + half + 1) * tokens)
        slope_sum, gain_sum = 0.0, 0.0
        for s, rows in enumerate(block_rows):
            probs = weight_ref[pair % 2, rows, lanes] * scales[s]
            dscore = probs * centred[s][:, lanes]
            probs_ref[rows, to] = probs.astype(jnp.bfloat16)
            dscore_ref[rows, to] = dscore.astype(jnp.bfloat16)
            slope_sum = slope_sum + fold_rows(dscore * distance_ref[rows, :])
            gain_sum = gain_sum + fold_rows(dscore * ancestor_ref[rows, :])
        at = pl.ds(group * heads_per_group + 2 * pair + half, 1)
        slope_rows[at, :] = -jnp.sum(slope_sum, axis=0, keepdims=True)
        gain_rows[at, :] = jnp.sum(gain_sum, axis=0, keepdims=True)

    def put_part(group, kind, whole):
        at = pl.multiple_of((kind * groups + group) * tokens, tokens)
        for s, rows in enumerate(block_rows):
            part_refs[s][pl.ds(at, tokens), :] = whole[rows].astype(jnp.bfloat16)

    def key_part(group, first, count):
        heads = stacked(query_ref, group, first, count)
        lanes = slice(first * tokens, (first + count) * tokens)
        return dot_nn(dscore_ref[:, lanes], heads)

    def value_part(group, first, count):
        heads = stacked(grad_ref, group, first, count)
        lanes = slice(first * tokens, (first + count) * tokens)
        return dot_nn(probs_ref[:, lanes], heads)

    def query_part(keys_across, group, pair):
        lanes = slice(2 * pair * tokens, (2 * pair + 2) * tokens)
        across = dot_nn(keys_across, dscore_ref[:, lanes]) * factor
        rows = jnp.transpose(across.astype(jnp.bfloat16))
        for half in range(2):
            at = (2 * pair + half) * WIDTH
            query_grad_ref[group, :, at : at + WIDTH] = rows[half * tokens : (half + 1) * tokens]

    def products(left, right):
        whole = dot_nt(left, right)
        return [whole[rows] for rows in block_rows]

    @pl.loop(0, groups)
    def _(group):
        keys = all_blocks(0, group)
        values = all_blocks(1, group)
        value_ext = jnp.concatenate([values, jnp.full(values.shape, -1.0, jnp.bfloat16)], axis=1)
        keys_across = jnp.transpose(keys)
        half_heads = heads_per_group // 2
        for pair in range(pairs):
            query_pair = stacked(query_ref, group, 2 * pair, 2)
            grad_pair = stacked(grad_ref, group, 2 * pair, 2)
            product_pair = stacked(product_ref, group, 2 * pair, 2)
            grad_ext = jnp.concatenate([grad_pair, product_pair], axis=1)
            raw = products(keys, query_pair)
            if pair == pairs // 2:
                key_acc[...] = key_part(group, 0, half_heads)
            scales = [weigh(group, pair, raw, half) for half in range(2)]
            if pair == pairs // 2:
                value_acc[...] = value_part(group, 0, half_heads)
            if pair:
                query_part(keys_across, group, pair - 1)
            centred = products(value_ext, grad_ext)
            for half in range(2):
                differentiate(group, pair, centred, scales[half], half)
        key_whole = key_acc[...] + key_part(group, half_heads, half_heads)
        put_part(group, 0, key_whole * factor)
        put_part(group, 1, value_acc[...] + value_part(group, half_heads, half_heads))
        query_part(keys_across, group, pairs - 1)
        store(group).start()

    slope_sum = jnp.sum(slope_rows[...], axis=1, keepdims=True)
    gain_sum = jnp.sum(gain_rows[...], axis=1, keepdims=True)
    shape = slope_rows.shape
    lane = lax.broadcasted_iota(jnp.int32, shape, 1)
    row = lax.broadcasted_iota(jnp.int32, shape, 0)
    replicas, parts, rows_here, local = bias_ref.shape
    local_heads = shape[0] // parts
    kind = lax.broadcasted_iota(jnp.int32, (rows_here, local), 0)
    for part in range(parts):
        mine = (lane == row - part * local_heads) & (lane < local_heads)
        slope_line = jnp.sum(jnp.where(mine, slope_sum, 0.0), axis=0, keepdims=True)
        gain_line = jnp.sum(jnp.where(mine, gain_sum, 0.0), axis=0, keepdims=True)
        tile = jnp.where(kind == 0, slope_line, jnp.where(kind == 1, gain_line, 0.0))
        bias_ref[:, part] = jnp.broadcast_to(tile[None], (replicas, rows_here, local))
    bias_copy = pltpu.make_async_copy(bias_ref, bias_hbm, bias_sem)
    bias_copy.start()
    for group in range(groups):
        store(group).wait()
    bias_copy.wait()


def combine_kernel(blocks, *refs):
    parts = refs[0:blocks]
    key_out, value_out = refs[blocks:]
    tokens = key_out.shape[0]
    groups = key_out.shape[1] // WIDTH
    for kind, out in enumerate((key_out, value_out)):
        for group in range(groups):
            at = (kind * groups + group) * tokens
            total = parts[0][at : at + tokens, :].astype(jnp.float32)
            for s in range(1, blocks):
                total = total + parts[s][at : at + tokens, :].astype(jnp.float32)
            out[:, group * WIDTH : (group + 1) * WIDTH] = total.astype(jnp.bfloat16)


def bias_kernel(parts_ref, _, out_ref):
    out_ref[...] = jnp.sum(parts_ref[...], axis=0)[0:2, 0 : out_ref.shape[1]]


def body(
    queries,
    key_rows,
    values,
    outputs,
    out_grads,
    depths,
    subtree_end,
    file_lengths,
    slopes,
    ancestor_gain,
):
    blocks = lax.axis_size("ctx")
    replicas = lax.axis_size("dp")
    tokens, width_all = queries.shape[1:]
    kv_width = key_rows.shape[2]
    heads_all = width_all // WIDTH
    groups = kv_width // WIDTH
    heads_per_group = heads_all // groups
    group_columns = heads_per_group * WIDTH
    local_heads = heads_all // blocks
    keys_seen = blocks * tokens
    bf16, f32 = jnp.bfloat16, jnp.float32
    vmem = pl.BlockSpec(memory_space=pltpu.VMEM)
    smem = pl.BlockSpec(memory_space=pltpu.SMEM)
    hbm = pl.BlockSpec(memory_space=pltpu.HBM)
    params = pltpu.CompilerParams(vmem_limit_bytes=(24 if blocks <= 4 else 44) * 1024 * 1024)

    def hold(array):
        return pltpu.with_memory_space_constraint(array, pltpu.HBM)

    key_held, value_held = hold(key_rows[0]), hold(values[0])
    depth_held, end_held = hold(depths), hold(subtree_end)
    message_rows = 2 * groups * tokens
    message = pl.pallas_call(
        pack_kernel,
        out_shape=jax.ShapeDtypeStruct((message_rows + META_ROWS, WIDTH), bf16),
        in_specs=[vmem] * 4,
        out_specs=vmem,
        compiler_params=params,
        name="pack",
    )(key_held, value_held, depth_held, end_held)
    shifts = [s for s in range(1, blocks) if s != 2] + [2]
    arrived = [
        lax.ppermute(message, "ctx", [(i, i ^ s) for i in range(blocks) if i < i ^ s])
        for s in shifts
    ]

    prepared = pl.pallas_call(
        prepare_kernel,
        out_shape=[jax.ShapeDtypeStruct((tokens, width_all), bf16)] * 3,
        in_specs=[vmem] * 3,
        out_specs=[vmem] * 3,
        compiler_params=params,
        cost_estimate=pl.CostEstimate(
            flops=tokens * width_all, bytes_accessed=12 * tokens * width_all, transcendentals=0
        ),
        name="prepare",
    )(hold(queries[0]), hold(outputs[0]), hold(out_grads[0]))

    bias_shape = (replicas, blocks, 8, WIDTH)
    matmul_flops = 2 * tokens * keys_seen * WIDTH * heads_all
    results = pl.pallas_call(
        functools.partial(main_kernel, blocks, heads_per_group, groups, shifts),
        out_shape=[jax.ShapeDtypeStruct((tokens, width_all), bf16)]
        + [jax.ShapeDtypeStruct((message_rows, WIDTH), bf16)] * blocks
        + [jax.ShapeDtypeStruct(bias_shape, f32)],
        in_specs=[smem] * 3 + [vmem] * (6 + blocks),
        out_specs=[hbm] + [vmem] * blocks + [hbm],
        scratch_shapes=[
            pltpu.VMEM((groups, tokens, group_columns), bf16),
            pltpu.VMEM((keys_seen, tokens), f32),
            pltpu.VMEM((keys_seen, tokens), f32),
            pltpu.VMEM((heads_all, tokens), f32),
            pltpu.VMEM((heads_all, tokens), f32),
            pltpu.VMEM((keys_seen, WIDTH), f32),
            pltpu.VMEM((keys_seen, WIDTH), f32),
            pltpu.VMEM((2, keys_seen, 2 * tokens), f32),
            pltpu.VMEM((keys_seen, group_columns), bf16),
            pltpu.VMEM((keys_seen, group_columns), bf16),
            pltpu.VMEM(bias_shape, f32),
            pltpu.SemaphoreType.DMA((groups,)),
            pltpu.SemaphoreType.DMA,
        ],
        compiler_params=params,
        cost_estimate=pl.CostEstimate(
            flops=5 * matmul_flops,
            bytes_accessed=10 * tokens * width_all,
            transcendentals=tokens * keys_seen * heads_all,
        ),
        name="attend",
    )(
        hold(file_lengths),
        hold(slopes),
        hold(ancestor_gain),
        depth_held,
        end_held,
        *prepared,
        key_held,
        value_held,
        *arrived,
    )
    query_grads = results[0]
    parts = list(results[1 : 1 + blocks])
    bias_parts = results[1 + blocks].reshape(replicas * blocks, 8, WIDTH)
    for s in [2] + [s for s in range(1, blocks) if s != 2]:
        back = [(i, i ^ s) for i in range(blocks) if i > i ^ s]
        parts[s] = lax.ppermute(parts[s], "ctx", back)
    bias_parts = lax.all_to_all(bias_parts, ("dp", "ctx"), split_axis=0, concat_axis=0, tiled=True)

    key_grads, value_grads = pl.pallas_call(
        functools.partial(combine_kernel, blocks),
        out_shape=[jax.ShapeDtypeStruct((tokens, kv_width), bf16)] * 2,
        in_specs=[vmem] * blocks,
        out_specs=[vmem] * 2,
        compiler_params=params,
        cost_estimate=pl.CostEstimate(
            flops=2 * message_rows * WIDTH * blocks,
            bytes_accessed=2 * message_rows * WIDTH * (blocks + 1),
            transcendentals=0,
        ),
        name="combine",
    )(parts[0], parts[2], parts[1], *parts[3:])
    bias_grads = pl.pallas_call(
        bias_kernel,
        out_shape=jax.ShapeDtypeStruct((2, local_heads), f32),
        in_specs=[vmem, hbm],
        out_specs=vmem,
        compiler_params=params,
        name="bias",
    )(bias_parts, hold(key_grads))
    return (query_grads[None], key_grads[None], value_grads[None], bias_grads.T)


def solution(mesh):
    in_specs = (
        P("dp", "ctx", None),
        P("dp", "ctx", None),
        P("dp", "ctx", None),
        P("dp", "ctx", None),
        P("dp", "ctx", None),
        P("dp", "ctx"),
        P("dp", "ctx"),
        P("dp", None),
        P(),
        P(),
    )
    out_specs = (P("dp", "ctx", None), P("dp", "ctx", None), P("dp", "ctx", None), P("ctx", None))
    return jax.shard_map(body, mesh=mesh, in_specs=in_specs, out_specs=out_specs, check_vma=False)
```

```python
import functools

import jax
import jax.numpy as jnp
from jax import lax
from jax.experimental import pallas as pl
from jax.experimental.pallas import tpu as pltpu
from jax.sharding import PartitionSpec as P

WIDTH = 128
LOG2E = 1.4426950408889634
MASKED = -1e30
META_ROWS = 16
END_UNIT = 64


def dot_nt(a, b):
    return lax.dot_general(a, b, (((1,), (1,)), ((), ())), preferred_element_type=jnp.float32)


def dot_nn(a, b):
    return lax.dot_general(a, b, (((1,), (0,)), ((), ())), preferred_element_type=jnp.float32)


def fold_rows(block):
    return jnp.sum(block.reshape(block.shape[0] // 8, 8, block.shape[1]), axis=0)


def as_column(row):
    size = row.shape[1]
    return jnp.transpose(jnp.broadcast_to(row, (size, size)))


def pack_kernel(key_ref, value_ref, depth_ref, end_ref, message_ref):
    tokens = key_ref.shape[0]
    groups = key_ref.shape[1] // WIDTH
    for kind, ref in enumerate((key_ref, value_ref)):
        for group in range(groups):
            at = (kind * groups + group) * tokens
            message_ref[at : at + tokens, :] = ref[:, group * WIDTH : (group + 1) * WIDTH]
    depth = depth_ref[...]
    end = end_ref[...]
    end_high = end // END_UNIT
    end_low = end - end_high * END_UNIT
    row = lax.broadcasted_iota(jnp.int32, (META_ROWS, tokens), 0)
    meta = jnp.where(row == 0, depth, jnp.where(row == 1, end_high, end_low))
    meta = meta.astype(jnp.float32).astype(jnp.bfloat16)
    message_ref[2 * groups * tokens : 2 * groups * tokens + META_ROWS, :] = meta


def prepare_kernel(query_in, output_in, grad_in, query_out, grad_out, product_out):
    query_out[...] = query_in[...]
    grad_out[...] = grad_in[...]
    product_out[...] = grad_in[...] * output_in[...]


def main_kernel(
    blocks,
    heads_per_group,
    groups,
    shifts,
    lengths_ref,
    slope_ref,
    gain_ref,
    depth_ref,
    end_ref,
    query_ref,
    grad_ref,
    product_ref,
    key_ref,
    value_ref,
    *refs,
):
    tokens = query_ref.shape[0]
    remote = [refs[shifts.index(s)] for s in range(1, blocks)]
    query_grad_hbm = refs[blocks - 1]
    part_refs = refs[blocks : 2 * blocks]
    bias_hbm = refs[2 * blocks]
    (
        query_grad_ref,
        distance_ref,
        ancestor_ref,
        slope_rows,
        gain_rows,
        key_acc,
        value_acc,
        weight_ref,
        probs_ref,
        dscore_ref,
        bias_ref,
        store_sems,
        bias_sem,
    ) = refs[2 * blocks + 1 :]
    factor = WIDTH**-0.5
    group_columns = heads_per_group * WIDTH
    pairs = heads_per_group // 2

    def store(group):
        wide = pl.ds(pl.multiple_of(group * group_columns, group_columns), group_columns)
        return pltpu.make_async_copy(
            query_grad_ref.at[group], query_grad_hbm.at[:, wide], store_sems.at[group]
        )

    here = lax.axis_index("ctx")
    query_pos = here * tokens + lax.broadcasted_iota(jnp.int32, (tokens, tokens), 1)
    start = jnp.zeros((tokens, tokens), jnp.int32)
    bound = jnp.int32(0)
    for index in range(lengths_ref.shape[1]):
        bound = bound + lengths_ref[0, index]
        start = jnp.where(query_pos >= bound, bound, start)
    query_depth = jnp.broadcast_to(depth_ref[...].astype(jnp.float32), (tokens, tokens))
    block_rows = [slice(s * tokens, (s + 1) * tokens) for s in range(blocks)]
    for s, rows in enumerate(block_rows):
        key_pos = (here ^ s) * tokens + lax.broadcasted_iota(jnp.int32, (tokens, tokens), 0)
        if s == 0:
            key_depth = as_column(depth_ref[...].astype(jnp.float32))
            key_end = as_column(end_ref[...].astype(jnp.float32))
        else:
            below = slice(2 * groups * tokens, 2 * groups * tokens + META_ROWS)
            meta = remote[s - 1][below, :].astype(jnp.float32)
            key_depth = as_column(meta[0:1])
            key_end = as_column(meta[1:2] * END_UNIT + meta[2:3])
        inside = query_pos.astype(jnp.float32) < key_end
        allowed = (key_pos <= query_pos) & (key_pos >= start)
        distance_ref[rows, :] = jnp.abs(query_depth - key_depth)
        ancestor_ref[rows, :] = jnp.where(allowed, jnp.where(inside, 1.0, 0.0), MASKED)

    def key_block(kind, group, s):
        if s == 0:
            at = pl.multiple_of(group * WIDTH, WIDTH)
            return (key_ref, value_ref)[kind][:, pl.ds(at, WIDTH)]
        at = pl.multiple_of((kind * groups + group) * tokens, tokens)
        return remote[s - 1][pl.ds(at, tokens), :]

    def all_blocks(kind, group):
        return jnp.concatenate([key_block(kind, group, s) for s in range(blocks)], axis=0)

    def stacked(ref, group, first, count):
        at = pl.multiple_of(group * group_columns, group_columns) + first * WIDTH
        heads = [pl.ds(pl.multiple_of(at + i * WIDTH, WIDTH), WIDTH) for i in range(count)]
        return jnp.concatenate([ref[:, head] for head in heads], axis=0)

    def weigh(group, pair, raw, half):
        head = group * heads_per_group + 2 * pair + half
        gain = gain_ref[head] * LOG2E
        slope = slope_ref[head] * LOG2E
        lanes = slice(half * tokens, (half + 1) * tokens)
        tops, totals = [], []
        for s, rows in enumerate(block_rows):
            score = raw[s][:, lanes] * (factor * LOG2E) + (
                gain * ancestor_ref[rows, :] - slope * distance_ref[rows, :]
            )
            top = jnp.max(score, axis=0, keepdims=True)
            weight = jnp.exp2(score - top)
            weight_ref[pair % 2, rows, lanes] = weight
            tops.append(top)
            totals.append(jnp.sum(weight, axis=0, keepdims=True))
        top = functools.reduce(jnp.maximum, tops)
        shrink = [jnp.exp2(t - top) for t in tops]
        inverse = 1.0 / sum(a * b for a, b in zip(totals, shrink))
        return [s * inverse for s in shrink]

    def differentiate(group, pair, centred, scales, half):
        lanes = slice(half * tokens, (half + 1) * tokens)
        to = slice((2 * pair + half) * tokens, (2 * pair + half + 1) * tokens)
        slope_sum, gain_sum = 0.0, 0.0
        for s, rows in enumerate(block_rows):
            probs = weight_ref[pair % 2, rows, lanes] * scales[s]
            dscore = probs * centred[s][:, lanes]
            probs_ref[rows, to] = probs.astype(jnp.bfloat16)
            dscore_ref[rows, to] = dscore.astype(jnp.bfloat16)
            slope_sum = slope_sum + fold_rows(dscore * distance_ref[rows, :])
            gain_sum = gain_sum + fold_rows(dscore * ancestor_ref[rows, :])
        at = pl.ds(group * heads_per_group + 2 * pair + half, 1)
        slope_rows[at, :] = -jnp.sum(slope_sum, axis=0, keepdims=True)
        gain_rows[at, :] = jnp.sum(gain_sum, axis=0, keepdims=True)

    def put_part(group, kind, whole):
        at = pl.multiple_of((kind * groups + group) * tokens, tokens)
        for s, rows in enumerate(block_rows):
            part_refs[s][pl.ds(at, tokens), :] = whole[rows].astype(jnp.bfloat16)

    def key_part(group, first, count):
        heads = stacked(query_ref, group, first, count)
        lanes = slice(first * tokens, (first + count) * tokens)
        return dot_nn(dscore_ref[:, lanes], heads)

    def value_part(group, first, count):
        heads = stacked(grad_ref, group, first, count)
        lanes = slice(first * tokens, (first + count) * tokens)
        return dot_nn(probs_ref[:, lanes], heads)

    def query_part(keys_across, group, pair):
        lanes = slice(2 * pair * tokens, (2 * pair + 2) * tokens)
        across = dot_nn(keys_across, dscore_ref[:, lanes]) * factor
        rows = jnp.transpose(across.astype(jnp.bfloat16))
        for half in range(2):
            at = (2 * pair + half) * WIDTH
            query_grad_ref[group, :, at : at + WIDTH] = rows[half * tokens : (half + 1) * tokens]

    def products(left, right):
        whole = dot_nt(left, right)
        return [whole[rows] for rows in block_rows]

    @pl.loop(0, groups)
    def _(group):
        keys = all_blocks(0, group)
        values = all_blocks(1, group)
        value_ext = jnp.concatenate([values, jnp.full(values.shape, -1.0, jnp.bfloat16)], axis=1)
        keys_across = jnp.transpose(keys)
        half_heads = heads_per_group // 2
        for pair in range(pairs):
            query_pair = stacked(query_ref, group, 2 * pair, 2)
            grad_pair = stacked(grad_ref, group, 2 * pair, 2)
            product_pair = stacked(product_ref, group, 2 * pair, 2)
            grad_ext = jnp.concatenate([grad_pair, product_pair], axis=1)
            raw = products(keys, query_pair)
            if pair == pairs // 2:
                key_acc[...] = key_part(group, 0, half_heads)
            scales = [weigh(group, pair, raw, half) for half in range(2)]
            if pair == pairs // 2:
                value_acc[...] = value_part(group, 0, half_heads)
            if pair:
                query_part(keys_across, group, pair - 1)
            centred = products(value_ext, grad_ext)
            for half in range(2):
                differentiate(group, pair, centred, scales[half], half)
        query_part(keys_across, group, pairs - 1)
        store(group).start()
        key_whole = key_acc[...] + key_part(group, half_heads, half_heads)
        put_part(group, 0, key_whole * factor)
        put_part(group, 1, value_acc[...] + value_part(group, half_heads, half_heads))

    slope_sum = jnp.sum(slope_rows[...], axis=1, keepdims=True)
    gain_sum = jnp.sum(gain_rows[...], axis=1, keepdims=True)
    shape = slope_rows.shape
    lane = lax.broadcasted_iota(jnp.int32, shape, 1)
    row = lax.broadcasted_iota(jnp.int32, shape, 0)
    replicas, parts, rows_here, local = bias_ref.shape
    local_heads = shape[0] // parts
    kind = lax.broadcasted_iota(jnp.int32, (rows_here, local), 0)
    for part in range(parts):
        mine = (lane == row - part * local_heads) & (lane < local_heads)
        slope_line = jnp.sum(jnp.where(mine, slope_sum, 0.0), axis=0, keepdims=True)
        gain_line = jnp.sum(jnp.where(mine, gain_sum, 0.0), axis=0, keepdims=True)
        tile = jnp.where(kind == 0, slope_line, jnp.where(kind == 1, gain_line, 0.0))
        bias_ref[:, part] = jnp.broadcast_to(tile[None], (replicas, rows_here, local))
    bias_copy = pltpu.make_async_copy(bias_ref, bias_hbm, bias_sem)
    bias_copy.start()
    for group in range(groups):
        store(group).wait()
    bias_copy.wait()


def combine_kernel(blocks, *refs):
    parts = refs[0:blocks]
    key_out, value_out = refs[blocks:]
    tokens = key_out.shape[0]
    groups = key_out.shape[1] // WIDTH
    for kind, out in enumerate((key_out, value_out)):
        for group in range(groups):
            at = (kind * groups + group) * tokens
            total = parts[0][at : at + tokens, :].astype(jnp.float32)
            for s in range(1, blocks):
                total = total + parts[s][at : at + tokens, :].astype(jnp.float32)
            out[:, group * WIDTH : (group + 1) * WIDTH] = total.astype(jnp.bfloat16)


def bias_kernel(parts_ref, _, out_ref):
    out_ref[...] = jnp.sum(parts_ref[...], axis=0)[0:2, 0 : out_ref.shape[1]]


def body(
    queries,
    key_rows,
    values,
    outputs,
    out_grads,
    depths,
    subtree_end,
    file_lengths,
    slopes,
    ancestor_gain,
):
    blocks = lax.axis_size("ctx")
    replicas = lax.axis_size("dp")
    tokens, width_all = queries.shape[1:]
    kv_width = key_rows.shape[2]
    heads_all = width_all // WIDTH
    groups = kv_width // WIDTH
    heads_per_group = heads_all // groups
    group_columns = heads_per_group * WIDTH
    local_heads = heads_all // blocks
    keys_seen = blocks * tokens
    bf16, f32 = jnp.bfloat16, jnp.float32
    vmem = pl.BlockSpec(memory_space=pltpu.VMEM)
    smem = pl.BlockSpec(memory_space=pltpu.SMEM)
    hbm = pl.BlockSpec(memory_space=pltpu.HBM)
    params = pltpu.CompilerParams(vmem_limit_bytes=(24 if blocks <= 4 else 44) * 1024 * 1024)

    def hold(array):
        return pltpu.with_memory_space_constraint(array, pltpu.HBM)

    key_held, value_held = hold(key_rows[0]), hold(values[0])
    depth_held, end_held = hold(depths), hold(subtree_end)
    message_rows = 2 * groups * tokens
    message = pl.pallas_call(
        pack_kernel,
        out_shape=jax.ShapeDtypeStruct((message_rows + META_ROWS, WIDTH), bf16),
        in_specs=[vmem] * 4,
        out_specs=vmem,
        compiler_params=params,
        name="pack",
    )(key_held, value_held, depth_held, end_held)
    shifts = list(range(1, blocks))
    arrived = [
        lax.ppermute(message, "ctx", [(i, i ^ s) for i in range(blocks) if i < i ^ s])
        for s in shifts
    ]

    prepared = pl.pallas_call(
        prepare_kernel,
        out_shape=[jax.ShapeDtypeStruct((tokens, width_all), bf16)] * 3,
        in_specs=[vmem] * 3,
        out_specs=[vmem] * 3,
        compiler_params=params,
        cost_estimate=pl.CostEstimate(
            flops=tokens * width_all, bytes_accessed=12 * tokens * width_all, transcendentals=0
        ),
        name="prepare",
    )(hold(queries[0]), hold(outputs[0]), hold(out_grads[0]))

    bias_shape = (replicas, blocks, 8, WIDTH)
    matmul_flops = 2 * tokens * keys_seen * WIDTH * heads_all
    results = pl.pallas_call(
        functools.partial(main_kernel, blocks, heads_per_group, groups, shifts),
        out_shape=[jax.ShapeDtypeStruct((tokens, width_all), bf16)]
        + [jax.ShapeDtypeStruct((message_rows, WIDTH), bf16)] * blocks
        + [jax.ShapeDtypeStruct(bias_shape, f32)],
        in_specs=[smem] * 3 + [vmem] * (6 + blocks),
        out_specs=[hbm] + [vmem] * blocks + [hbm],
        scratch_shapes=[
            pltpu.VMEM((groups, tokens, group_columns), bf16),
            pltpu.VMEM((keys_seen, tokens), f32),
            pltpu.VMEM((keys_seen, tokens), f32),
            pltpu.VMEM((heads_all, tokens), f32),
            pltpu.VMEM((heads_all, tokens), f32),
            pltpu.VMEM((keys_seen, WIDTH), f32),
            pltpu.VMEM((keys_seen, WIDTH), f32),
            pltpu.VMEM((2, keys_seen, 2 * tokens), f32),
            pltpu.VMEM((keys_seen, group_columns), bf16),
            pltpu.VMEM((keys_seen, group_columns), bf16),
            pltpu.VMEM(bias_shape, f32),
            pltpu.SemaphoreType.DMA((groups,)),
            pltpu.SemaphoreType.DMA,
        ],
        compiler_params=params,
        cost_estimate=pl.CostEstimate(
            flops=5 * matmul_flops,
            bytes_accessed=10 * tokens * width_all,
            transcendentals=tokens * keys_seen * heads_all,
        ),
        name="attend",
    )(
        hold(file_lengths),
        hold(slopes),
        hold(ancestor_gain),
        depth_held,
        end_held,
        *prepared,
        key_held,
        value_held,
        *arrived,
    )
    query_grads = results[0]
    parts = list(results[1 : 1 + blocks])
    bias_parts = results[1 + blocks].reshape(replicas * blocks, 8, WIDTH)
    for s in [2] + [s for s in range(1, blocks) if s != 2]:
        back = [(i, i ^ s) for i in range(blocks) if i > i ^ s]
        parts[s] = lax.ppermute(parts[s], "ctx", back)
    bias_parts = lax.all_to_all(bias_parts, ("dp", "ctx"), split_axis=0, concat_axis=0, tiled=True)

    key_grads, value_grads = pl.pallas_call(
        functools.partial(combine_kernel, blocks),
        out_shape=[jax.ShapeDtypeStruct((tokens, kv_width), bf16)] * 2,
        in_specs=[vmem] * blocks,
        out_specs=[vmem] * 2,
        compiler_params=params,
        cost_estimate=pl.CostEstimate(
            flops=2 * message_rows * WIDTH * blocks,
            bytes_accessed=2 * message_rows * WIDTH * (blocks + 1),
            transcendentals=0,
        ),
        name="combine",
    )(parts[0], parts[2], parts[1], *parts[3:])
    bias_grads = pl.pallas_call(
        bias_kernel,
        out_shape=jax.ShapeDtypeStruct((2, local_heads), f32),
        in_specs=[vmem, hbm],
        out_specs=vmem,
        compiler_params=params,
        name="bias",
    )(bias_parts, hold(key_grads))
    return (query_grads[None], key_grads[None], value_grads[None], bias_grads.T)


def solution(mesh):
    in_specs = (
        P("dp", "ctx", None),
        P("dp", "ctx", None),
        P("dp", "ctx", None),
        P("dp", "ctx", None),
        P("dp", "ctx", None),
        P("dp", "ctx"),
        P("dp", "ctx"),
        P("dp", None),
        P(),
        P(),
    )
    out_specs = (P("dp", "ctx", None), P("dp", "ctx", None), P("dp", "ctx", None), P("ctx", None))
    return jax.shard_map(body, mesh=mesh, in_specs=in_specs, out_specs=out_specs, check_vma=False)
```

```python
import functools

import jax
import jax.numpy as jnp
from jax import lax
from jax.experimental import pallas as pl
from jax.experimental.pallas import tpu as pltpu
from jax.sharding import PartitionSpec as P

WIDTH = 128
LOG2E = 1.4426950408889634
MASKED = -1e30
META_ROWS = 16
END_UNIT = 64


def dot_nt(a, b):
    return lax.dot_general(a, b, (((1,), (1,)), ((), ())), preferred_element_type=jnp.float32)


def dot_nn(a, b):
    return lax.dot_general(a, b, (((1,), (0,)), ((), ())), preferred_element_type=jnp.float32)


def fold_rows(block):
    return jnp.sum(block.reshape(block.shape[0] // 8, 8, block.shape[1]), axis=0)


def as_column(row):
    size = row.shape[1]
    return jnp.transpose(jnp.broadcast_to(row, (size, size)))


def pack_kernel(blocks, key_hbm, value_hbm, depth_hbm, end_hbm, message_ref, depth_ref, end_ref, sems):
    tokens, columns = key_hbm.shape
    groups = columns // WIDTH

    @pl.when(lax.axis_index("ctx") != blocks - 1)
    def _():
        copies = [
            pltpu.make_async_copy(depth_hbm, depth_ref, sems.at[0]),
            pltpu.make_async_copy(end_hbm, end_ref, sems.at[1]),
        ]
        for kind, hbm in enumerate((key_hbm, value_hbm)):
            for group in range(groups):
                index = kind * groups + group
                copies.append(
                    pltpu.make_async_copy(
                        hbm.at[:, group * WIDTH : (group + 1) * WIDTH],
                        message_ref.at[index * tokens : (index + 1) * tokens, :],
                        sems.at[2 + index],
                    )
                )
        for copy in copies:
            copy.start()
        copies[0].wait()
        copies[1].wait()
        end = end_ref[...]
        end_high = end // END_UNIT
        end_low = end - end_high * END_UNIT
        row = lax.broadcasted_iota(jnp.int32, (META_ROWS, tokens), 0)
        meta = jnp.where(row == 0, depth_ref[...], jnp.where(row == 1, end_high, end_low))
        meta = meta.astype(jnp.float32).astype(jnp.bfloat16)
        message_ref[2 * groups * tokens : 2 * groups * tokens + META_ROWS, :] = meta
        for copy in copies[2:]:
            copy.wait()


def table(lengths_ref, depth_ref, s, key_depth, key_end):
    shape = key_depth.shape
    here = lax.axis_index("ctx")
    query_pos = here * shape[1] + lax.broadcasted_iota(jnp.int32, shape, 1)
    key_pos = (here ^ s) * shape[0] + lax.broadcasted_iota(jnp.int32, shape, 0)
    start = jnp.zeros(shape, jnp.int32)
    bound = jnp.int32(0)
    for index in range(lengths_ref.shape[1]):
        bound = bound + lengths_ref[0, index]
        start = jnp.where(query_pos >= bound, bound, start)
    inside = query_pos.astype(jnp.float32) < key_end
    allowed = (key_pos <= query_pos) & (key_pos >= start)
    distance = jnp.abs(depth_ref[...].astype(jnp.float32) - key_depth)
    return distance, jnp.where(allowed, jnp.where(inside, 1.0, 0.0), MASKED)


def prepare_kernel(
    heads_per_group,
    groups,
    lengths_ref,
    slope_ref,
    gain_ref,
    depth_ref,
    end_ref,
    query_in,
    output_in,
    grad_in,
    key_ref,
    value_ref,
    query_out,
    grad_out,
    product_out,
    distance_ref,
    ancestor_ref,
    weight_ref,
    dscore_ref,
    rows_ref,
):
    tokens = query_in.shape[0]
    factor = WIDTH**-0.5
    query_out[...] = query_in[...]
    grad_out[...] = grad_in[...]
    product_out[...] = grad_in[...] * output_in[...]
    distance, ancestor = table(
        lengths_ref,
        depth_ref,
        0,
        as_column(depth_ref[...].astype(jnp.float32)),
        as_column(end_ref[...].astype(jnp.float32)),
    )
    distance_ref[...] = distance
    ancestor_ref[...] = ancestor

    @pl.loop(0, groups)
    def _(group):
        own = pl.ds(pl.multiple_of(group * WIDTH, WIDTH), WIDTH)
        key, value = key_ref[:, own], value_ref[:, own]
        value_ext = jnp.concatenate([value, jnp.full(value.shape, -1.0, jnp.bfloat16)], axis=1)
        for pair in range(heads_per_group // 2):
            first = group * heads_per_group + 2 * pair
            both = pl.ds(pl.multiple_of(first * WIDTH, 2 * WIDTH), 2 * WIDTH)

            def stack(array):
                return jnp.concatenate([array[:, 0:WIDTH], array[:, WIDTH:]], axis=0)

            grad = grad_in[:, both]
            grad_ext = jnp.concatenate([stack(grad), stack(grad * output_in[:, both])], axis=1)
            raw = dot_nt(key, stack(query_in[:, both]))
            centred = dot_nt(value_ext, grad_ext)
            for half in range(2):
                head = first + half
                gain = gain_ref[head] * LOG2E
                slope = slope_ref[head] * LOG2E
                lanes = slice(half * tokens, (half + 1) * tokens)
                distance, ancestor = distance_ref[...], ancestor_ref[...]
                score = raw[:, lanes] * (factor * LOG2E) + (gain * ancestor - slope * distance)
                top = jnp.max(score, axis=0, keepdims=True)
                weight = jnp.exp2(score - top)
                dscore = weight * centred[:, lanes]
                to = pl.ds(pl.multiple_of(head * tokens, tokens), tokens)
                weight_ref[:, to] = weight
                dscore_ref[:, to] = dscore
                at = pl.ds(head, 1)
                rows_ref[0, at, :] = top
                rows_ref[1, at, :] = jnp.sum(weight, axis=0, keepdims=True)
                rows_ref[2, at, :] = jnp.sum(dscore * distance, axis=0, keepdims=True)
                rows_ref[3, at, :] = jnp.sum(dscore * ancestor, axis=0, keepdims=True)


def main_kernel(
    blocks,
    heads_per_group,
    groups,
    shifts,
    lengths_ref,
    slope_ref,
    gain_ref,
    depth_ref,
    query_ref,
    grad_ref,
    product_ref,
    own_weight_ref,
    own_dscore_ref,
    own_rows_ref,
    key_ref,
    *refs,
):
    tokens = query_ref.shape[0]
    remote = [refs[shifts.index(s)] for s in range(1, blocks)]
    query_grad_hbm = refs[blocks - 1]
    part_refs = refs[blocks : 2 * blocks]
    bias_hbm = refs[2 * blocks]
    (
        query_grad_ref,
        distance_ref,
        ancestor_ref,
        slope_rows,
        gain_rows,
        key_acc,
        value_acc,
        weight_ref,
        probs_ref,
        dscore_ref,
        bias_ref,
        store_sems,
        bias_sem,
    ) = refs[2 * blocks + 1 :]
    factor = WIDTH**-0.5
    group_columns = heads_per_group * WIDTH
    pairs = heads_per_group // 2

    def store(group):
        wide = pl.ds(pl.multiple_of(group * group_columns, group_columns), group_columns)
        return pltpu.make_async_copy(
            query_grad_ref.at[group], query_grad_hbm.at[:, wide], store_sems.at[group]
        )

    block_rows = [slice(s * tokens, (s + 1) * tokens) for s in range(blocks)]
    remote_rows = block_rows[:-1]
    below = slice(2 * groups * tokens, 2 * groups * tokens + META_ROWS)
    for s in range(1, blocks):
        meta = remote[s - 1][below, :].astype(jnp.float32)
        distance, ancestor = table(
            lengths_ref,
            depth_ref,
            s,
            as_column(meta[0:1]),
            as_column(meta[1:2] * END_UNIT + meta[2:3]),
        )
        distance_ref[remote_rows[s - 1], :] = distance
        ancestor_ref[remote_rows[s - 1], :] = ancestor

    def remote_blocks(kind, group):
        at = pl.multiple_of((kind * groups + group) * tokens, tokens)
        return jnp.concatenate([r[pl.ds(at, tokens), :] for r in remote], axis=0)

    def stacked(ref, group, first, count):
        at = pl.multiple_of(group * group_columns, group_columns) + first * WIDTH
        heads = [pl.ds(pl.multiple_of(at + i * WIDTH, WIDTH), WIDTH) for i in range(count)]
        return jnp.concatenate([ref[:, head] for head in heads], axis=0)

    def weigh(group, pair, raw, half):
        head = group * heads_per_group + 2 * pair + half
        gain = gain_ref[head] * LOG2E
        slope = slope_ref[head] * LOG2E
        lanes = slice(half * tokens, (half + 1) * tokens)
        tops, totals = [own_rows_ref[0, pl.ds(head, 1), :]], [own_rows_ref[1, pl.ds(head, 1), :]]
        for rows in remote_rows:
            score = raw[rows, lanes] * (factor * LOG2E) + (
                gain * ancestor_ref[rows, :] - slope * distance_ref[rows, :]
            )
            top = jnp.max(score, axis=0, keepdims=True)
            weight = jnp.exp2(score - top)
            weight_ref[pair % 2, rows, lanes] = weight
            tops.append(top)
            totals.append(jnp.sum(weight, axis=0, keepdims=True))
        top = functools.reduce(jnp.maximum, tops)
        shrink = [jnp.exp2(t - top) for t in tops]
        inverse = 1.0 / sum(a * b for a, b in zip(totals, shrink))
        return [s * inverse for s in shrink]

    def differentiate(group, pair, centred, scales, half):
        lanes = slice(half * tokens, (half + 1) * tokens)
        to = slice((2 * pair + half) * tokens, (2 * pair + half + 1) * tokens)
        head = group * heads_per_group + 2 * pair + half
        own = pl.ds(pl.multiple_of(head * tokens, tokens), tokens)
        own_rows = block_rows[0]
        probs_ref[own_rows, to] = (own_weight_ref[:, own] * scales[0]).astype(jnp.bfloat16)
        dscore_ref[own_rows, to] = (own_dscore_ref[:, own] * scales[0]).astype(jnp.bfloat16)
        slope_sum, gain_sum = 0.0, 0.0
        for s, rows in enumerate(remote_rows, 1):
            probs = weight_ref[pair % 2, rows, lanes] * scales[s]
            dscore = probs * centred[rows, lanes]
            probs_ref[block_rows[s], to] = probs.astype(jnp.bfloat16)
            dscore_ref[block_rows[s], to] = dscore.astype(jnp.bfloat16)
            slope_sum = slope_sum + fold_rows(dscore * distance_ref[rows, :])
            gain_sum = gain_sum + fold_rows(dscore * ancestor_ref[rows, :])
        at = pl.ds(head, 1)
        slope_rows[at, :] = -(
            jnp.sum(slope_sum, axis=0, keepdims=True) + own_rows_ref[2, at, :] * scales[0]
        )
        gain_rows[at, :] = (
            jnp.sum(gain_sum, axis=0, keepdims=True) + own_rows_ref[3, at, :] * scales[0]
        )

    def put_part(group, kind, whole):
        at = pl.multiple_of((kind * groups + group) * tokens, tokens)
        for s, rows in enumerate(block_rows):
            part_refs[s][pl.ds(at, tokens), :] = whole[rows].astype(jnp.bfloat16)

    def key_part(group, first, count):
        heads = stacked(query_ref, group, first, count)
        lanes = slice(first * tokens, (first + count) * tokens)
        return dot_nn(dscore_ref[:, lanes], heads)

    def value_part(group, first, count):
        heads = stacked(grad_ref, group, first, count)
        lanes = slice(first * tokens, (first + count) * tokens)
        return dot_nn(probs_ref[:, lanes], heads)

    def query_part(keys_across, group, pair):
        lanes = slice(2 * pair * tokens, (2 * pair + 2) * tokens)
        across = dot_nn(keys_across, dscore_ref[:, lanes]) * factor
        rows = jnp.transpose(across.astype(jnp.bfloat16))
        for half in range(2):
            at = (2 * pair + half) * WIDTH
            query_grad_ref[group, :, at : at + WIDTH] = rows[half * tokens : (half + 1) * tokens]

    @pl.loop(0, groups)
    def _(group):
        keys = remote_blocks(0, group)
        values = remote_blocks(1, group)
        value_ext = jnp.concatenate([values, jnp.full(values.shape, -1.0, jnp.bfloat16)], axis=1)
        own_key = key_ref[:, pl.ds(pl.multiple_of(group * WIDTH, WIDTH), WIDTH)]
        keys_across = jnp.transpose(jnp.concatenate([own_key, keys], axis=0))
        half_heads = heads_per_group // 2
        for pair in range(pairs):
            query_pair = stacked(query_ref, group, 2 * pair, 2)
            grad_pair = stacked(grad_ref, group, 2 * pair, 2)
            product_pair = stacked(product_ref, group, 2 * pair, 2)
            grad_ext = jnp.concatenate([grad_pair, product_pair], axis=1)
            raw = dot_nt(keys, query_pair)
            if pair == pairs // 2:
                key_acc[...] = key_part(group, 0, half_heads)
            scales = [weigh(group, pair, raw, half) for half in range(2)]
            if pair == pairs // 2:
                value_acc[...] = value_part(group, 0, half_heads)
            if pair:
                query_part(keys_across, group, pair - 1)
            centred = dot_nt(value_ext, grad_ext)
            for half in range(2):
                differentiate(group, pair, centred, scales[half], half)
        key_whole = key_acc[...] + key_part(group, half_heads, half_heads)
        put_part(group, 0, key_whole * factor)
        put_part(group, 1, value_acc[...] + value_part(group, half_heads, half_heads))
        query_part(keys_across, group, pairs - 1)
        store(group).start()

    slope_sum = jnp.sum(slope_rows[...], axis=1, keepdims=True)
    gain_sum = jnp.sum(gain_rows[...], axis=1, keepdims=True)
    shape = slope_rows.shape
    lane = lax.broadcasted_iota(jnp.int32, shape, 1)
    row = lax.broadcasted_iota(jnp.int32, shape, 0)
    replicas, parts, rows_here, local = bias_ref.shape
    local_heads = shape[0] // parts
    kind = lax.broadcasted_iota(jnp.int32, (rows_here, local), 0)
    for part in range(parts):
        mine = (lane == row - part * local_heads) & (lane < local_heads)
        slope_line = jnp.sum(jnp.where(mine, slope_sum, 0.0), axis=0, keepdims=True)
        gain_line = jnp.sum(jnp.where(mine, gain_sum, 0.0), axis=0, keepdims=True)
        tile = jnp.where(kind == 0, slope_line, jnp.where(kind == 1, gain_line, 0.0))
        bias_ref[:, part] = jnp.broadcast_to(tile[None], (replicas, rows_here, local))
    bias_copy = pltpu.make_async_copy(bias_ref, bias_hbm, bias_sem)
    bias_copy.start()
    for group in range(groups):
        store(group).wait()
    bias_copy.wait()


def combine_kernel(blocks, *refs):
    parts = refs[0:blocks]
    key_out, value_out = refs[blocks:]
    tokens = key_out.shape[0]
    groups = key_out.shape[1] // WIDTH
    for kind, out in enumerate((key_out, value_out)):
        for group in range(groups):
            at = (kind * groups + group) * tokens
            total = parts[0][at : at + tokens, :].astype(jnp.float32)
            for s in range(1, blocks):
                total = total + parts[s][at : at + tokens, :].astype(jnp.float32)
            out[:, group * WIDTH : (group + 1) * WIDTH] = total.astype(jnp.bfloat16)


def bias_kernel(parts_ref, _, out_ref):
    out_ref[...] = jnp.sum(parts_ref[...], axis=0)[0:2, 0 : out_ref.shape[1]]


def body(
    queries,
    key_rows,
    values,
    outputs,
    out_grads,
    depths,
    subtree_end,
    file_lengths,
    slopes,
    ancestor_gain,
):
    blocks = lax.axis_size("ctx")
    replicas = lax.axis_size("dp")
    tokens, width_all = queries.shape[1:]
    kv_width = key_rows.shape[2]
    heads_all = width_all // WIDTH
    groups = kv_width // WIDTH
    heads_per_group = heads_all // groups
    group_columns = heads_per_group * WIDTH
    local_heads = heads_all // blocks
    keys_seen = blocks * tokens
    bf16, f32 = jnp.bfloat16, jnp.float32
    vmem = pl.BlockSpec(memory_space=pltpu.VMEM)
    smem = pl.BlockSpec(memory_space=pltpu.SMEM)
    hbm = pl.BlockSpec(memory_space=pltpu.HBM)
    params = pltpu.CompilerParams(vmem_limit_bytes=(24 if blocks <= 4 else 44) * 1024 * 1024)

    def hold(array):
        return pltpu.with_memory_space_constraint(array, pltpu.HBM)

    key_held, value_held = hold(key_rows[0]), hold(values[0])
    depth_held, end_held = hold(depths), hold(subtree_end)
    message_rows = 2 * groups * tokens
    message = pl.pallas_call(
        functools.partial(pack_kernel, blocks),
        out_shape=jax.ShapeDtypeStruct((message_rows + META_ROWS, WIDTH), bf16),
        in_specs=[hbm] * 4,
        out_specs=vmem,
        scratch_shapes=[
            pltpu.VMEM((1, tokens), jnp.int32),
            pltpu.VMEM((1, tokens), jnp.int32),
            pltpu.SemaphoreType.DMA((2 + 2 * groups,)),
        ],
        compiler_params=params,
        name="pack",
    )(key_held, value_held, depth_held, end_held)
    shifts = list(range(1, blocks))
    arrived = [
        lax.ppermute(message, "ctx", [(i, i ^ s) for i in range(blocks) if i < i ^ s])
        for s in shifts
    ]

    lengths_held, slope_held, gain_held = hold(file_lengths), hold(slopes), hold(ancestor_gain)
    own_table = jax.ShapeDtypeStruct((tokens, tokens), f32)
    own_scores = jax.ShapeDtypeStruct((tokens, heads_all * tokens), f32)
    query_here, grad_here, product_here, _, _, own_weight, own_dscore, own_rows = pl.pallas_call(
        functools.partial(prepare_kernel, heads_per_group, groups),
        out_shape=[jax.ShapeDtypeStruct((tokens, width_all), bf16)] * 3
        + [own_table, own_table, own_scores, own_scores]
        + [jax.ShapeDtypeStruct((4, heads_all, tokens), f32)],
        in_specs=[smem] * 3 + [vmem] * 7,
        out_specs=[vmem] * 8,
        compiler_params=params,
        cost_estimate=pl.CostEstimate(
            flops=4 * tokens * tokens * width_all,
            bytes_accessed=12 * tokens * width_all,
            transcendentals=tokens * tokens * heads_all,
        ),
        name="prepare",
    )(
        lengths_held,
        slope_held,
        gain_held,
        depth_held,
        end_held,
        hold(queries[0]),
        hold(outputs[0]),
        hold(out_grads[0]),
        key_held,
        value_held,
    )

    bias_shape = (replicas, blocks, 8, WIDTH)
    matmul_flops = 2 * tokens * keys_seen * WIDTH * heads_all
    results = pl.pallas_call(
        functools.partial(main_kernel, blocks, heads_per_group, groups, shifts),
        out_shape=[jax.ShapeDtypeStruct((tokens, width_all), bf16)]
        + [jax.ShapeDtypeStruct((message_rows, WIDTH), bf16)] * blocks
        + [jax.ShapeDtypeStruct(bias_shape, f32)],
        in_specs=[smem] * 3 + [vmem] * (7 + blocks),
        out_specs=[hbm] + [vmem] * blocks + [hbm],
        scratch_shapes=[
            pltpu.VMEM((groups, tokens, group_columns), bf16),
            pltpu.VMEM((keys_seen - tokens, tokens), f32),
            pltpu.VMEM((keys_seen - tokens, tokens), f32),
            pltpu.VMEM((heads_all, tokens), f32),
            pltpu.VMEM((heads_all, tokens), f32),
            pltpu.VMEM((keys_seen, WIDTH), f32),
            pltpu.VMEM((keys_seen, WIDTH), f32),
            pltpu.VMEM((2, keys_seen - tokens, 2 * tokens), f32),
            pltpu.VMEM((keys_seen, group_columns), bf16),
            pltpu.VMEM((keys_seen, group_columns), bf16),
            pltpu.VMEM(bias_shape, f32),
            pltpu.SemaphoreType.DMA((groups,)),
            pltpu.SemaphoreType.DMA,
        ],
        compiler_params=params,
        cost_estimate=pl.CostEstimate(
            flops=5 * matmul_flops,
            bytes_accessed=10 * tokens * width_all,
            transcendentals=tokens * keys_seen * heads_all,
        ),
        name="attend",
    )(
        lengths_held,
        slope_held,
        gain_held,
        depth_held,
        query_here,
        grad_here,
        product_here,
        own_weight,
        own_dscore,
        own_rows,
        key_held,
        *arrived,
    )
    query_grads = results[0]
    parts = list(results[1 : 1 + blocks])
    bias_parts = results[1 + blocks].reshape(replicas * blocks, 8, WIDTH)
    for s in [2] + [s for s in range(1, blocks) if s != 2]:
        back = [(i, i ^ s) for i in range(blocks) if i > i ^ s]
        parts[s] = lax.ppermute(parts[s], "ctx", back)
    bias_parts = lax.all_to_all(bias_parts, ("dp", "ctx"), split_axis=0, concat_axis=0, tiled=True)

    key_grads, value_grads = pl.pallas_call(
        functools.partial(combine_kernel, blocks),
        out_shape=[jax.ShapeDtypeStruct((tokens, kv_width), bf16)] * 2,
        in_specs=[vmem] * blocks,
        out_specs=[vmem] * 2,
        compiler_params=params,
        cost_estimate=pl.CostEstimate(
            flops=2 * message_rows * WIDTH * blocks,
            bytes_accessed=2 * message_rows * WIDTH * (blocks + 1),
            transcendentals=0,
        ),
        name="combine",
    )(parts[0], parts[2], parts[1], *parts[3:])
    bias_grads = pl.pallas_call(
        bias_kernel,
        out_shape=jax.ShapeDtypeStruct((2, local_heads), f32),
        in_specs=[vmem, hbm],
        out_specs=vmem,
        compiler_params=params,
        name="bias",
    )(bias_parts, hold(key_grads))
    return (query_grads[None], key_grads[None], value_grads[None], bias_grads.T)


def solution(mesh):
    in_specs = (
        P("dp", "ctx", None),
        P("dp", "ctx", None),
        P("dp", "ctx", None),
        P("dp", "ctx", None),
        P("dp", "ctx", None),
        P("dp", "ctx"),
        P("dp", "ctx"),
        P("dp", None),
        P(),
        P(),
    )
    out_specs = (P("dp", "ctx", None), P("dp", "ctx", None), P("dp", "ctx", None), P("ctx", None))
    return jax.shard_map(body, mesh=mesh, in_specs=in_specs, out_specs=out_specs, check_vma=False)
```

```python
import functools

import jax
import jax.numpy as jnp
from jax import lax
from jax.experimental import pallas as pl
from jax.experimental.pallas import tpu as pltpu
from jax.sharding import PartitionSpec as P

WIDTH = 128
LOG2E = 1.4426950408889634
MASKED = -1e30
META_ROWS = 16
END_UNIT = 64


def dot_nt(a, b):
    return lax.dot_general(a, b, (((1,), (1,)), ((), ())), preferred_element_type=jnp.float32)


def dot_nn(a, b):
    return lax.dot_general(a, b, (((1,), (0,)), ((), ())), preferred_element_type=jnp.float32)


def fold_rows(block):
    return jnp.sum(block.reshape(block.shape[0] // 8, 8, block.shape[1]), axis=0)


def as_column(row):
    size = row.shape[1]
    return jnp.transpose(jnp.broadcast_to(row, (size, size)))


def pack_kernel(blocks, key_hbm, value_hbm, depth_hbm, end_hbm, message_ref, depth_ref, end_ref, sems):
    tokens, columns = key_hbm.shape
    groups = columns // WIDTH

    @pl.when(lax.axis_index("ctx") != blocks - 1)
    def _():
        copies = [
            pltpu.make_async_copy(depth_hbm, depth_ref, sems.at[0]),
            pltpu.make_async_copy(end_hbm, end_ref, sems.at[1]),
        ]
        for kind, hbm in enumerate((key_hbm, value_hbm)):
            for group in range(groups):
                index = kind * groups + group
                copies.append(
                    pltpu.make_async_copy(
                        hbm.at[:, group * WIDTH : (group + 1) * WIDTH],
                        message_ref.at[index * tokens : (index + 1) * tokens, :],
                        sems.at[2 + index],
                    )
                )
        for copy in copies:
            copy.start()
        copies[0].wait()
        copies[1].wait()
        end = end_ref[...]
        end_high = end // END_UNIT
        end_low = end - end_high * END_UNIT
        row = lax.broadcasted_iota(jnp.int32, (META_ROWS, tokens), 0)
        meta = jnp.where(row == 0, depth_ref[...], jnp.where(row == 1, end_high, end_low))
        meta = meta.astype(jnp.float32).astype(jnp.bfloat16)
        message_ref[2 * groups * tokens : 2 * groups * tokens + META_ROWS, :] = meta
        for copy in copies[2:]:
            copy.wait()


def table(lengths_ref, depth_ref, s, key_depth, key_end):
    shape = key_depth.shape
    here = lax.axis_index("ctx")
    query_pos = here * shape[1] + lax.broadcasted_iota(jnp.int32, shape, 1)
    key_pos = (here ^ s) * shape[0] + lax.broadcasted_iota(jnp.int32, shape, 0)
    start = jnp.zeros(shape, jnp.int32)
    bound = jnp.int32(0)
    for index in range(lengths_ref.shape[1]):
        bound = bound + lengths_ref[0, index]
        start = jnp.where(query_pos >= bound, bound, start)
    inside = query_pos.astype(jnp.float32) < key_end
    allowed = (key_pos <= query_pos) & (key_pos >= start)
    distance = jnp.abs(depth_ref[...].astype(jnp.float32) - key_depth)
    return distance, jnp.where(allowed, jnp.where(inside, 1.0, 0.0), MASKED)


def prepare_kernel(
    heads_per_group,
    groups,
    lengths_ref,
    slope_ref,
    gain_ref,
    depth_ref,
    end_ref,
    query_in,
    output_in,
    grad_in,
    key_ref,
    value_ref,
    query_out,
    grad_out,
    product_out,
    distance_ref,
    ancestor_ref,
    weight_ref,
    dscore_ref,
    rows_ref,
):
    tokens = query_in.shape[0]
    factor = WIDTH**-0.5
    query_out[...] = query_in[...]
    grad_out[...] = grad_in[...]
    product_out[...] = grad_in[...] * output_in[...]
    distance, ancestor = table(
        lengths_ref,
        depth_ref,
        0,
        as_column(depth_ref[...].astype(jnp.float32)),
        as_column(end_ref[...].astype(jnp.float32)),
    )
    distance_ref[...] = distance
    ancestor_ref[...] = ancestor

    @pl.loop(0, groups)
    def _(group):
        own = pl.ds(pl.multiple_of(group * WIDTH, WIDTH), WIDTH)
        key, value = key_ref[:, own], value_ref[:, own]
        value_ext = jnp.concatenate([value, jnp.full(value.shape, -1.0, jnp.bfloat16)], axis=1)
        for pair in range(heads_per_group // 2):
            first = group * heads_per_group + 2 * pair
            both = pl.ds(pl.multiple_of(first * WIDTH, 2 * WIDTH), 2 * WIDTH)

            def stack(array):
                return jnp.concatenate([array[:, 0:WIDTH], array[:, WIDTH:]], axis=0)

            grad = grad_in[:, both]
            grad_ext = jnp.concatenate([stack(grad), stack(grad * output_in[:, both])], axis=1)
            raw = dot_nt(key, stack(query_in[:, both]))
            centred = dot_nt(value_ext, grad_ext)
            for half in range(2):
                head = first + half
                gain = gain_ref[head] * LOG2E
                slope = slope_ref[head] * LOG2E
                lanes = slice(half * tokens, (half + 1) * tokens)
                distance, ancestor = distance_ref[...], ancestor_ref[...]
                score = raw[:, lanes] * (factor * LOG2E) + (gain * ancestor - slope * distance)
                top = jnp.max(score, axis=0, keepdims=True)
                weight = jnp.exp2(score - top)
                dscore = weight * centred[:, lanes]
                to = pl.ds(pl.multiple_of(head * tokens, tokens), tokens)
                weight_ref[:, to] = weight
                dscore_ref[:, to] = dscore
                at = pl.ds(head, 1)
                rows_ref[0, at, :] = top
                rows_ref[1, at, :] = jnp.sum(weight, axis=0, keepdims=True)
                rows_ref[2, at, :] = jnp.sum(dscore * distance, axis=0, keepdims=True)
                rows_ref[3, at, :] = jnp.sum(dscore * ancestor, axis=0, keepdims=True)


def main_kernel(
    blocks,
    heads_per_group,
    groups,
    shifts,
    lengths_ref,
    slope_ref,
    gain_ref,
    depth_ref,
    query_ref,
    grad_ref,
    product_ref,
    own_weight_ref,
    own_dscore_ref,
    own_rows_ref,
    key_ref,
    *refs,
):
    tokens = query_ref.shape[0]
    remote = [refs[shifts.index(s)] for s in range(1, blocks)]
    query_grad_hbm = refs[blocks - 1]
    part_refs = refs[blocks : 2 * blocks]
    bias_hbm = refs[2 * blocks]
    (
        query_grad_ref,
        distance_ref,
        ancestor_ref,
        slope_rows,
        gain_rows,
        key_acc,
        value_acc,
        weight_ref,
        probs_ref,
        dscore_ref,
        bias_ref,
        store_sems,
        bias_sem,
    ) = refs[2 * blocks + 1 :]
    factor = WIDTH**-0.5
    group_columns = heads_per_group * WIDTH
    pairs = heads_per_group // 2

    def store(group):
        wide = pl.ds(pl.multiple_of(group * group_columns, group_columns), group_columns)
        return pltpu.make_async_copy(
            query_grad_ref.at[group], query_grad_hbm.at[:, wide], store_sems.at[group]
        )

    block_rows = [slice(s * tokens, (s + 1) * tokens) for s in range(blocks)]
    remote_rows = block_rows[:-1]
    below = slice(2 * groups * tokens, 2 * groups * tokens + META_ROWS)
    for s in range(1, blocks):
        meta = remote[s - 1][below, :].astype(jnp.float32)
        distance, ancestor = table(
            lengths_ref,
            depth_ref,
            s,
            as_column(meta[0:1]),
            as_column(meta[1:2] * END_UNIT + meta[2:3]),
        )
        distance_ref[remote_rows[s - 1], :] = distance
        ancestor_ref[remote_rows[s - 1], :] = ancestor

    def remote_blocks(kind, group):
        at = pl.multiple_of((kind * groups + group) * tokens, tokens)
        return jnp.concatenate([r[pl.ds(at, tokens), :] for r in remote], axis=0)

    def stacked(ref, group, first, count):
        at = pl.multiple_of(group * group_columns, group_columns) + first * WIDTH
        heads = [pl.ds(pl.multiple_of(at + i * WIDTH, WIDTH), WIDTH) for i in range(count)]
        return jnp.concatenate([ref[:, head] for head in heads], axis=0)

    def weigh(group, pair, raw, half):
        head = group * heads_per_group + 2 * pair + half
        gain = gain_ref[head] * LOG2E
        slope = slope_ref[head] * LOG2E
        lanes = slice(half * tokens, (half + 1) * tokens)
        tops, totals = [own_rows_ref[0, pl.ds(head, 1), :]], [own_rows_ref[1, pl.ds(head, 1), :]]
        for rows in remote_rows:
            score = raw[rows, lanes] * (factor * LOG2E) + (
                gain * ancestor_ref[rows, :] - slope * distance_ref[rows, :]
            )
            top = jnp.max(score, axis=0, keepdims=True)
            weight = jnp.exp2(score - top)
            weight_ref[pair % 2, rows, lanes] = weight
            tops.append(top)
            totals.append(jnp.sum(weight, axis=0, keepdims=True))
        top = functools.reduce(jnp.maximum, tops)
        shrink = [jnp.exp2(t - top) for t in tops]
        inverse = 1.0 / sum(a * b for a, b in zip(totals, shrink))
        return [s * inverse for s in shrink]

    def differentiate(group, pair, centred, scales, half):
        lanes = slice(half * tokens, (half + 1) * tokens)
        to = slice((2 * pair + half) * tokens, (2 * pair + half + 1) * tokens)
        head = group * heads_per_group + 2 * pair + half
        own = pl.ds(pl.multiple_of(head * tokens, tokens), tokens)
        own_rows = block_rows[0]
        probs_ref[own_rows, to] = (own_weight_ref[:, own] * scales[0]).astype(jnp.bfloat16)
        dscore_ref[own_rows, to] = (own_dscore_ref[:, own] * scales[0]).astype(jnp.bfloat16)
        slope_sum, gain_sum = 0.0, 0.0
        for s, rows in enumerate(remote_rows, 1):
            probs = weight_ref[pair % 2, rows, lanes] * scales[s]
            dscore = probs * centred[rows, lanes]
            probs_ref[block_rows[s], to] = probs.astype(jnp.bfloat16)
            dscore_ref[block_rows[s], to] = dscore.astype(jnp.bfloat16)
            slope_sum = slope_sum + fold_rows(dscore * distance_ref[rows, :])
            gain_sum = gain_sum + fold_rows(dscore * ancestor_ref[rows, :])
        at = pl.ds(head, 1)
        slope_rows[at, :] = -(
            jnp.sum(slope_sum, axis=0, keepdims=True) + own_rows_ref[2, at, :] * scales[0]
        )
        gain_rows[at, :] = (
            jnp.sum(gain_sum, axis=0, keepdims=True) + own_rows_ref[3, at, :] * scales[0]
        )

    def put_part(group, kind, whole):
        at = pl.multiple_of((kind * groups + group) * tokens, tokens)
        for s, rows in enumerate(block_rows):
            part_refs[s][pl.ds(at, tokens), :] = whole[rows].astype(jnp.bfloat16)

    def key_part(group, first, count):
        heads = stacked(query_ref, group, first, count)
        lanes = slice(first * tokens, (first + count) * tokens)
        return dot_nn(dscore_ref[:, lanes], heads)

    def value_part(group, first, count):
        heads = stacked(grad_ref, group, first, count)
        lanes = slice(first * tokens, (first + count) * tokens)
        return dot_nn(probs_ref[:, lanes], heads)

    def query_part(keys_across, group, pair):
        lanes = slice(2 * pair * tokens, (2 * pair + 2) * tokens)
        across = dot_nn(keys_across, dscore_ref[:, lanes]) * factor
        rows = jnp.transpose(across.astype(jnp.bfloat16))
        for half in range(2):
            at = (2 * pair + half) * WIDTH
            query_grad_ref[group, :, at : at + WIDTH] = rows[half * tokens : (half + 1) * tokens]

    @pl.loop(0, groups)
    def _(group):
        keys = remote_blocks(0, group)
        values = remote_blocks(1, group)
        value_ext = jnp.concatenate([values, jnp.full(values.shape, -1.0, jnp.bfloat16)], axis=1)
        own_key = key_ref[:, pl.ds(pl.multiple_of(group * WIDTH, WIDTH), WIDTH)]
        keys_across = jnp.transpose(jnp.concatenate([own_key, keys], axis=0))
        half_heads = heads_per_group // 2
        for pair in range(pairs):
            query_pair = stacked(query_ref, group, 2 * pair, 2)
            grad_pair = stacked(grad_ref, group, 2 * pair, 2)
            product_pair = stacked(product_ref, group, 2 * pair, 2)
            grad_ext = jnp.concatenate([grad_pair, product_pair], axis=1)
            raw = dot_nt(keys, query_pair)
            if pair == pairs // 2:
                key_acc[...] = key_part(group, 0, half_heads)
            scales = [weigh(group, pair, raw, half) for half in range(2)]
            if pair == pairs // 2:
                value_acc[...] = value_part(group, 0, half_heads)
            if pair:
                query_part(keys_across, group, pair - 1)
            centred = dot_nt(value_ext, grad_ext)
            for half in range(2):
                differentiate(group, pair, centred, scales[half], half)
        key_whole = key_acc[...] + key_part(group, half_heads, half_heads)
        put_part(group, 0, key_whole * factor)
        put_part(group, 1, value_acc[...] + value_part(group, half_heads, half_heads))
        query_part(keys_across, group, pairs - 1)
        store(group).start()

    slope_sum = jnp.sum(slope_rows[...], axis=1, keepdims=True)
    gain_sum = jnp.sum(gain_rows[...], axis=1, keepdims=True)
    shape = slope_rows.shape
    lane = lax.broadcasted_iota(jnp.int32, shape, 1)
    row = lax.broadcasted_iota(jnp.int32, shape, 0)
    replicas, parts, rows_here, local = bias_ref.shape
    local_heads = shape[0] // parts
    kind = lax.broadcasted_iota(jnp.int32, (rows_here, local), 0)
    for part in range(parts):
        mine = (lane == row - part * local_heads) & (lane < local_heads)
        slope_line = jnp.sum(jnp.where(mine, slope_sum, 0.0), axis=0, keepdims=True)
        gain_line = jnp.sum(jnp.where(mine, gain_sum, 0.0), axis=0, keepdims=True)
        tile = jnp.where(kind == 0, slope_line, jnp.where(kind == 1, gain_line, 0.0))
        bias_ref[:, part] = jnp.broadcast_to(tile[None], (replicas, rows_here, local))
    bias_copy = pltpu.make_async_copy(bias_ref, bias_hbm, bias_sem)
    bias_copy.start()
    for group in range(groups):
        store(group).wait()
    bias_copy.wait()


def gather_parts_kernel(*refs):
    total = refs[0][...].astype(jnp.float32)
    for part in refs[1:-1]:
        total = total + part[...].astype(jnp.float32)
    refs[-1][...] = total


def combine_kernel(sum_ref, part_ref, bias_parts, key_out, value_out, bias_out):
    tokens = key_out.shape[0]
    groups = key_out.shape[1] // WIDTH
    for kind, out in enumerate((key_out, value_out)):
        for group in range(groups):
            at = (kind * groups + group) * tokens
            rows = slice(at, at + tokens)
            total = sum_ref[rows, :] + part_ref[rows, :].astype(jnp.float32)
            out[:, group * WIDTH : (group + 1) * WIDTH] = total.astype(jnp.bfloat16)
    bias_out[...] = jnp.sum(bias_parts[...], axis=0)[0:2, 0 : bias_out.shape[1]]


def body(
    queries,
    key_rows,
    values,
    outputs,
    out_grads,
    depths,
    subtree_end,
    file_lengths,
    slopes,
    ancestor_gain,
):
    blocks = lax.axis_size("ctx")
    replicas = lax.axis_size("dp")
    tokens, width_all = queries.shape[1:]
    kv_width = key_rows.shape[2]
    heads_all = width_all // WIDTH
    groups = kv_width // WIDTH
    heads_per_group = heads_all // groups
    group_columns = heads_per_group * WIDTH
    local_heads = heads_all // blocks
    keys_seen = blocks * tokens
    bf16, f32 = jnp.bfloat16, jnp.float32
    vmem = pl.BlockSpec(memory_space=pltpu.VMEM)
    smem = pl.BlockSpec(memory_space=pltpu.SMEM)
    hbm = pl.BlockSpec(memory_space=pltpu.HBM)
    params = pltpu.CompilerParams(vmem_limit_bytes=(24 if blocks <= 4 else 44) * 1024 * 1024)

    def hold(array):
        return pltpu.with_memory_space_constraint(array, pltpu.HBM)

    key_held, value_held = hold(key_rows[0]), hold(values[0])
    depth_held, end_held = hold(depths), hold(subtree_end)
    message_rows = 2 * groups * tokens
    message = pl.pallas_call(
        functools.partial(pack_kernel, blocks),
        out_shape=jax.ShapeDtypeStruct((message_rows + META_ROWS, WIDTH), bf16),
        in_specs=[hbm] * 4,
        out_specs=vmem,
        scratch_shapes=[
            pltpu.VMEM((1, tokens), jnp.int32),
            pltpu.VMEM((1, tokens), jnp.int32),
            pltpu.SemaphoreType.DMA((2 + 2 * groups,)),
        ],
        compiler_params=params,
        name="pack",
    )(key_held, value_held, depth_held, end_held)
    shifts = [s for s in range(blocks - 1, 0, -1) if s != 2] + [2]
    arrived = [
        lax.ppermute(message, "ctx", [(i, i ^ s) for i in range(blocks) if i < i ^ s])
        for s in shifts
    ]

    lengths_held, slope_held, gain_held = hold(file_lengths), hold(slopes), hold(ancestor_gain)
    own_table = jax.ShapeDtypeStruct((tokens, tokens), f32)
    own_scores = jax.ShapeDtypeStruct((tokens, heads_all * tokens), f32)
    query_here, grad_here, product_here, _, _, own_weight, own_dscore, own_rows = pl.pallas_call(
        functools.partial(prepare_kernel, heads_per_group, groups),
        out_shape=[jax.ShapeDtypeStruct((tokens, width_all), bf16)] * 3
        + [own_table, own_table, own_scores, own_scores]
        + [jax.ShapeDtypeStruct((4, heads_all, tokens), f32)],
        in_specs=[smem] * 3 + [vmem] * 7,
        out_specs=[vmem] * 8,
        compiler_params=params,
        cost_estimate=pl.CostEstimate(
            flops=4 * tokens * tokens * width_all,
            bytes_accessed=12 * tokens * width_all,
            transcendentals=tokens * tokens * heads_all,
        ),
        name="prepare",
    )(
        lengths_held,
        slope_held,
        gain_held,
        depth_held,
        end_held,
        hold(queries[0]),
        hold(outputs[0]),
        hold(out_grads[0]),
        key_held,
        value_held,
    )

    bias_shape = (replicas, blocks, 8, WIDTH)
    matmul_flops = 2 * tokens * keys_seen * WIDTH * heads_all
    results = pl.pallas_call(
        functools.partial(main_kernel, blocks, heads_per_group, groups, shifts),
        out_shape=[jax.ShapeDtypeStruct((tokens, width_all), bf16)]
        + [jax.ShapeDtypeStruct((message_rows, WIDTH), bf16)] * blocks
        + [jax.ShapeDtypeStruct(bias_shape, f32)],
        in_specs=[smem] * 3 + [vmem] * (7 + blocks),
        out_specs=[hbm] + [vmem] * blocks + [hbm],
        scratch_shapes=[
            pltpu.VMEM((groups, tokens, group_columns), bf16),
            pltpu.VMEM((keys_seen - tokens, tokens), f32),
            pltpu.VMEM((keys_seen - tokens, tokens), f32),
            pltpu.VMEM((heads_all, tokens), f32),
            pltpu.VMEM((heads_all, tokens), f32),
            pltpu.VMEM((keys_seen, WIDTH), f32),
            pltpu.VMEM((keys_seen, WIDTH), f32),
            pltpu.VMEM((2, keys_seen - tokens, 2 * tokens), f32),
            pltpu.VMEM((keys_seen, group_columns), bf16),
            pltpu.VMEM((keys_seen, group_columns), bf16),
            pltpu.VMEM(bias_shape, f32),
            pltpu.SemaphoreType.DMA((groups,)),
            pltpu.SemaphoreType.DMA,
        ],
        compiler_params=params,
        cost_estimate=pl.CostEstimate(
            flops=5 * matmul_flops,
            bytes_accessed=10 * tokens * width_all,
            transcendentals=tokens * keys_seen * heads_all,
        ),
        name="attend",
    )(
        lengths_held,
        slope_held,
        gain_held,
        depth_held,
        query_here,
        grad_here,
        product_here,
        own_weight,
        own_dscore,
        own_rows,
        key_held,
        *arrived,
    )
    query_grads = results[0]
    parts = list(results[1 : 1 + blocks])
    bias_parts = results[1 + blocks].reshape(replicas * blocks, 8, WIDTH)
    for s in [2] + [s for s in range(1, blocks) if s != 2]:
        back = [(i, i ^ s) for i in range(blocks) if i > i ^ s]
        parts[s] = lax.ppermute(parts[s], "ctx", back)
    bias_parts = lax.all_to_all(bias_parts, ("dp", "ctx"), split_axis=0, concat_axis=0, tiled=True)

    early = [parts[0], parts[2], parts[1], *parts[3:-1]] if blocks > 3 else parts[:-1]
    parts_sum = pl.pallas_call(
        gather_parts_kernel,
        out_shape=jax.ShapeDtypeStruct((message_rows, WIDTH), f32),
        in_specs=[vmem] * len(early),
        out_specs=vmem,
        compiler_params=params,
        cost_estimate=pl.CostEstimate(
            flops=2 * message_rows * WIDTH * blocks,
            bytes_accessed=2 * message_rows * WIDTH * (blocks + 1),
            transcendentals=0,
        ),
        name="sum_parts",
    )(*early)
    key_grads, value_grads, bias_grads = pl.pallas_call(
        combine_kernel,
        out_shape=[jax.ShapeDtypeStruct((tokens, kv_width), bf16)] * 2
        + [jax.ShapeDtypeStruct((2, local_heads), f32)],
        in_specs=[vmem] * 3,
        out_specs=[vmem] * 3,
        compiler_params=params,
        name="combine",
    )(parts_sum, parts[-1], bias_parts)
    return (query_grads[None], key_grads[None], value_grads[None], bias_grads.T)


def solution(mesh):
    in_specs = (
        P("dp", "ctx", None),
        P("dp", "ctx", None),
        P("dp", "ctx", None),
        P("dp", "ctx", None),
        P("dp", "ctx", None),
        P("dp", "ctx"),
        P("dp", "ctx"),
        P("dp", None),
        P(),
        P(),
    )
    out_specs = (P("dp", "ctx", None), P("dp", "ctx", None), P("dp", "ctx", None), P("ctx", None))
    return jax.shard_map(body, mesh=mesh, in_specs=in_specs, out_specs=out_specs, check_vma=False)
```

```python
import functools

import jax
import jax.numpy as jnp
from jax import lax
from jax.experimental import pallas as pl
from jax.experimental.pallas import tpu as pltpu
from jax.sharding import PartitionSpec as P

WIDTH = 128
LOG2E = 1.4426950408889634
MASKED = -1e30
META_ROWS = 16
END_UNIT = 64


def dot_nt(a, b):
    return lax.dot_general(a, b, (((1,), (1,)), ((), ())), preferred_element_type=jnp.float32)


def dot_nn(a, b):
    return lax.dot_general(a, b, (((1,), (0,)), ((), ())), preferred_element_type=jnp.float32)


def fold_rows(block):
    return jnp.sum(block.reshape(block.shape[0] // 8, 8, block.shape[1]), axis=0)


def as_column(row):
    size = row.shape[1]
    return jnp.transpose(jnp.broadcast_to(row, (size, size)))


def pack_kernel(blocks, key_hbm, value_hbm, depth_hbm, end_hbm, message_ref, depth_ref, end_ref, sems):
    tokens, columns = key_hbm.shape
    groups = columns // WIDTH

    @pl.when(lax.axis_index("ctx") != blocks - 1)
    def _():
        copies = [
            pltpu.make_async_copy(depth_hbm, depth_ref, sems.at[0]),
            pltpu.make_async_copy(end_hbm, end_ref, sems.at[1]),
        ]
        for kind, hbm in enumerate((key_hbm, value_hbm)):
            for group in range(groups):
                index = kind * groups + group
                copies.append(
                    pltpu.make_async_copy(
                        hbm.at[:, group * WIDTH : (group + 1) * WIDTH],
                        message_ref.at[index * tokens : (index + 1) * tokens, :],
                        sems.at[2 + index],
                    )
                )
        for copy in copies:
            copy.start()
        copies[0].wait()
        copies[1].wait()
        end = end_ref[...]
        end_high = end // END_UNIT
        end_low = end - end_high * END_UNIT
        row = lax.broadcasted_iota(jnp.int32, (META_ROWS, tokens), 0)
        meta = jnp.where(row == 0, depth_ref[...], jnp.where(row == 1, end_high, end_low))
        meta = meta.astype(jnp.float32).astype(jnp.bfloat16)
        message_ref[2 * groups * tokens : 2 * groups * tokens + META_ROWS, :] = meta
        for copy in copies[2:]:
            copy.wait()


def table(lengths_ref, depth_ref, s, key_depth, key_end):
    shape = key_depth.shape
    here = lax.axis_index("ctx")
    query_pos = here * shape[1] + lax.broadcasted_iota(jnp.int32, shape, 1)
    key_pos = (here ^ s) * shape[0] + lax.broadcasted_iota(jnp.int32, shape, 0)
    start = jnp.zeros(shape, jnp.int32)
    bound = jnp.int32(0)
    for index in range(lengths_ref.shape[1]):
        bound = bound + lengths_ref[0, index]
        start = jnp.where(query_pos >= bound, bound, start)
    inside = query_pos.astype(jnp.float32) < key_end
    allowed = (key_pos <= query_pos) & (key_pos >= start)
    distance = jnp.abs(depth_ref[...].astype(jnp.float32) - key_depth)
    return distance, jnp.where(allowed, jnp.where(inside, 1.0, 0.0), MASKED)


def prepare_kernel(
    heads_per_group,
    groups,
    lengths_ref,
    slope_ref,
    gain_ref,
    depth_ref,
    end_ref,
    query_in,
    output_in,
    grad_in,
    key_ref,
    value_ref,
    query_out,
    grad_out,
    product_out,
    distance_ref,
    ancestor_ref,
    weight_ref,
    dscore_ref,
    rows_ref,
):
    tokens = query_in.shape[0]
    factor = WIDTH**-0.5
    query_out[...] = query_in[...]
    grad_out[...] = grad_in[...]
    product_out[...] = grad_in[...] * output_in[...]
    distance, ancestor = table(
        lengths_ref,
        depth_ref,
        0,
        as_column(depth_ref[...].astype(jnp.float32)),
        as_column(end_ref[...].astype(jnp.float32)),
    )
    distance_ref[...] = distance
    ancestor_ref[...] = ancestor

    @pl.loop(0, groups)
    def _(group):
        own = pl.ds(pl.multiple_of(group * WIDTH, WIDTH), WIDTH)
        key, value = key_ref[:, own], value_ref[:, own]
        value_ext = jnp.concatenate([value, jnp.full(value.shape, -1.0, jnp.bfloat16)], axis=1)
        for pair in range(heads_per_group // 2):
            first = group * heads_per_group + 2 * pair
            both = pl.ds(pl.multiple_of(first * WIDTH, 2 * WIDTH), 2 * WIDTH)

            def stack(array):
                return jnp.concatenate([array[:, 0:WIDTH], array[:, WIDTH:]], axis=0)

            grad = grad_in[:, both]
            grad_ext = jnp.concatenate([stack(grad), stack(grad * output_in[:, both])], axis=1)
            raw = dot_nt(key, stack(query_in[:, both]))
            centred = dot_nt(value_ext, grad_ext)
            for half in range(2):
                head = first + half
                gain = gain_ref[head] * LOG2E
                slope = slope_ref[head] * LOG2E
                lanes = slice(half * tokens, (half + 1) * tokens)
                distance, ancestor = distance_ref[...], ancestor_ref[...]
                score = raw[:, lanes] * (factor * LOG2E) + (gain * ancestor - slope * distance)
                top = jnp.max(score, axis=0, keepdims=True)
                weight = jnp.exp2(score - top)
                dscore = weight * centred[:, lanes]
                to = pl.ds(pl.multiple_of(head * tokens, tokens), tokens)
                weight_ref[:, to] = weight
                dscore_ref[:, to] = dscore
                at = pl.ds(head, 1)
                rows_ref[0, at, :] = top
                rows_ref[1, at, :] = jnp.sum(weight, axis=0, keepdims=True)
                rows_ref[2, at, :] = jnp.sum(dscore * distance, axis=0, keepdims=True)
                rows_ref[3, at, :] = jnp.sum(dscore * ancestor, axis=0, keepdims=True)


def main_kernel(
    blocks,
    heads_per_group,
    groups,
    shifts,
    lengths_ref,
    slope_ref,
    gain_ref,
    depth_ref,
    query_ref,
    grad_ref,
    product_ref,
    own_weight_ref,
    own_dscore_ref,
    own_rows_ref,
    key_ref,
    *refs,
):
    tokens = query_ref.shape[0]
    remote = [refs[shifts.index(s)] for s in range(1, blocks)]
    query_grad_hbm = refs[blocks - 1]
    part_refs = refs[blocks : 2 * blocks]
    bias_hbm = refs[2 * blocks]
    (
        query_grad_ref,
        distance_ref,
        ancestor_ref,
        slope_rows,
        gain_rows,
        key_acc,
        value_acc,
        weight_ref,
        probs_ref,
        dscore_ref,
        bias_ref,
        store_sems,
        bias_sem,
    ) = refs[2 * blocks + 1 :]
    factor = WIDTH**-0.5
    group_columns = heads_per_group * WIDTH
    pairs = heads_per_group // 2

    def store(group):
        wide = pl.ds(pl.multiple_of(group * group_columns, group_columns), group_columns)
        return pltpu.make_async_copy(
            query_grad_ref.at[group], query_grad_hbm.at[:, wide], store_sems.at[group]
        )

    block_rows = [slice(s * tokens, (s + 1) * tokens) for s in range(blocks)]
    remote_rows = block_rows[:-1]
    below = slice(2 * groups * tokens, 2 * groups * tokens + META_ROWS)
    for s in range(1, blocks):
        meta = remote[s - 1][below, :].astype(jnp.float32)
        distance, ancestor = table(
            lengths_ref,
            depth_ref,
            s,
            as_column(meta[0:1]),
            as_column(meta[1:2] * END_UNIT + meta[2:3]),
        )
        distance_ref[remote_rows[s - 1], :] = distance
        ancestor_ref[remote_rows[s - 1], :] = ancestor

    def remote_blocks(kind, group):
        at = pl.multiple_of((kind * groups + group) * tokens, tokens)
        return jnp.concatenate([r[pl.ds(at, tokens), :] for r in remote], axis=0)

    def stacked(ref, group, first, count):
        at = pl.multiple_of(group * group_columns, group_columns) + first * WIDTH
        heads = [pl.ds(pl.multiple_of(at + i * WIDTH, WIDTH), WIDTH) for i in range(count)]
        return jnp.concatenate([ref[:, head] for head in heads], axis=0)

    def weigh(group, pair, raw, half):
        head = group * heads_per_group + 2 * pair + half
        gain = gain_ref[head] * LOG2E
        slope = slope_ref[head] * LOG2E
        lanes = slice(half * tokens, (half + 1) * tokens)
        tops, totals = [own_rows_ref[0, pl.ds(head, 1), :]], [own_rows_ref[1, pl.ds(head, 1), :]]
        for rows in remote_rows:
            score = raw[rows, lanes] * (factor * LOG2E) + (
                gain * ancestor_ref[rows, :] - slope * distance_ref[rows, :]
            )
            top = jnp.max(score, axis=0, keepdims=True)
            weight = jnp.exp2(score - top)
            weight_ref[pair % 2, rows, lanes] = weight
            tops.append(top)
            totals.append(jnp.sum(weight, axis=0, keepdims=True))
        top = functools.reduce(jnp.maximum, tops)
        shrink = [jnp.exp2(t - top) for t in tops]
        inverse = 1.0 / sum(a * b for a, b in zip(totals, shrink))
        return [s * inverse for s in shrink]

    def differentiate(group, pair, centred, scales, half):
        lanes = slice(half * tokens, (half + 1) * tokens)
        to = slice((2 * pair + half) * tokens, (2 * pair + half + 1) * tokens)
        head = group * heads_per_group + 2 * pair + half
        own = pl.ds(pl.multiple_of(head * tokens, tokens), tokens)
        own_rows = block_rows[0]
        probs_ref[own_rows, to] = (own_weight_ref[:, own] * scales[0]).astype(jnp.bfloat16)
        dscore_ref[own_rows, to] = (own_dscore_ref[:, own] * scales[0]).astype(jnp.bfloat16)
        slope_sum, gain_sum = 0.0, 0.0
        for s, rows in enumerate(remote_rows, 1):
            probs = weight_ref[pair % 2, rows, lanes] * scales[s]
            dscore = probs * centred[rows, lanes]
            probs_ref[block_rows[s], to] = probs.astype(jnp.bfloat16)
            dscore_ref[block_rows[s], to] = dscore.astype(jnp.bfloat16)
            slope_sum = slope_sum + fold_rows(dscore * distance_ref[rows, :])
            gain_sum = gain_sum + fold_rows(dscore * ancestor_ref[rows, :])
        at = pl.ds(head, 1)
        slope_rows[at, :] = -(
            jnp.sum(slope_sum, axis=0, keepdims=True) + own_rows_ref[2, at, :] * scales[0]
        )
        gain_rows[at, :] = (
            jnp.sum(gain_sum, axis=0, keepdims=True) + own_rows_ref[3, at, :] * scales[0]
        )

    def put_part(group, kind, whole):
        at = pl.multiple_of((kind * groups + group) * tokens, tokens)
        for s, rows in enumerate(block_rows):
            part_refs[s][pl.ds(at, tokens), :] = whole[rows].astype(jnp.bfloat16)

    def key_part(group, first, count):
        heads = stacked(query_ref, group, first, count)
        lanes = slice(first * tokens, (first + count) * tokens)
        return dot_nn(dscore_ref[:, lanes], heads)

    def value_part(group, first, count):
        heads = stacked(grad_ref, group, first, count)
        lanes = slice(first * tokens, (first + count) * tokens)
        return dot_nn(probs_ref[:, lanes], heads)

    def query_part(keys_across, group, pair):
        lanes = slice(2 * pair * tokens, (2 * pair + 2) * tokens)
        across = dot_nn(keys_across, dscore_ref[:, lanes]) * factor
        rows = jnp.transpose(across.astype(jnp.bfloat16))
        for half in range(2):
            at = (2 * pair + half) * WIDTH
            query_grad_ref[group, :, at : at + WIDTH] = rows[half * tokens : (half + 1) * tokens]

    @pl.loop(0, groups)
    def _(group):
        keys = remote_blocks(0, group)
        values = remote_blocks(1, group)
        value_ext = jnp.concatenate([values, jnp.full(values.shape, -1.0, jnp.bfloat16)], axis=1)
        own_key = key_ref[:, pl.ds(pl.multiple_of(group * WIDTH, WIDTH), WIDTH)]
        keys_across = jnp.transpose(jnp.concatenate([own_key, keys], axis=0))
        half_heads = heads_per_group // 2
        for pair in range(pairs):
            query_pair = stacked(query_ref, group, 2 * pair, 2)
            grad_pair = stacked(grad_ref, group, 2 * pair, 2)
            product_pair = stacked(product_ref, group, 2 * pair, 2)
            grad_ext = jnp.concatenate([grad_pair, product_pair], axis=1)
            raw = dot_nt(keys, query_pair)
            if pair == pairs // 2:
                key_acc[...] = key_part(group, 0, half_heads)
            scales = [weigh(group, pair, raw, half) for half in range(2)]
            if pair == pairs // 2:
                value_acc[...] = value_part(group, 0, half_heads)
            if pair:
                query_part(keys_across, group, pair - 1)
            centred = dot_nt(value_ext, grad_ext)
            for half in range(2):
                differentiate(group, pair, centred, scales[half], half)
        key_whole = key_acc[...] + key_part(group, half_heads, half_heads)
        put_part(group, 0, key_whole * factor)
        put_part(group, 1, value_acc[...] + value_part(group, half_heads, half_heads))
        query_part(keys_across, group, pairs - 1)
        store(group).start()

    slope_sum = jnp.sum(slope_rows[...], axis=1, keepdims=True)
    gain_sum = jnp.sum(gain_rows[...], axis=1, keepdims=True)
    shape = slope_rows.shape
    lane = lax.broadcasted_iota(jnp.int32, shape, 1)
    row = lax.broadcasted_iota(jnp.int32, shape, 0)
    replicas, parts, rows_here, local = bias_ref.shape
    local_heads = shape[0] // parts
    kind = lax.broadcasted_iota(jnp.int32, (rows_here, local), 0)
    for part in range(parts):
        mine = (lane == row - part * local_heads) & (lane < local_heads)
        slope_line = jnp.sum(jnp.where(mine, slope_sum, 0.0), axis=0, keepdims=True)
        gain_line = jnp.sum(jnp.where(mine, gain_sum, 0.0), axis=0, keepdims=True)
        tile = jnp.where(kind == 0, slope_line, jnp.where(kind == 1, gain_line, 0.0))
        bias_ref[:, part] = jnp.broadcast_to(tile[None], (replicas, rows_here, local))
    bias_copy = pltpu.make_async_copy(bias_ref, bias_hbm, bias_sem)
    bias_copy.start()
    for group in range(groups):
        store(group).wait()
    bias_copy.wait()


def gather_parts_kernel(*refs):
    total = refs[0][...].astype(jnp.float32)
    for part in refs[1:-1]:
        total = total + part[...].astype(jnp.float32)
    refs[-1][...] = total


def combine_kernel(sum_ref, part_ref, bias_parts, key_out, value_out, bias_out):
    tokens = key_out.shape[0]
    groups = key_out.shape[1] // WIDTH
    for kind, out in enumerate((key_out, value_out)):
        for group in range(groups):
            at = (kind * groups + group) * tokens
            rows = slice(at, at + tokens)
            total = sum_ref[rows, :] + part_ref[rows, :].astype(jnp.float32)
            out[:, group * WIDTH : (group + 1) * WIDTH] = total.astype(jnp.bfloat16)
    bias_out[...] = jnp.sum(bias_parts[...], axis=0)[0:2, 0 : bias_out.shape[1]]


def body(
    queries,
    key_rows,
    values,
    outputs,
    out_grads,
    depths,
    subtree_end,
    file_lengths,
    slopes,
    ancestor_gain,
):
    blocks = lax.axis_size("ctx")
    replicas = lax.axis_size("dp")
    tokens, width_all = queries.shape[1:]
    kv_width = key_rows.shape[2]
    heads_all = width_all // WIDTH
    groups = kv_width // WIDTH
    heads_per_group = heads_all // groups
    group_columns = heads_per_group * WIDTH
    local_heads = heads_all // blocks
    keys_seen = blocks * tokens
    bf16, f32 = jnp.bfloat16, jnp.float32
    vmem = pl.BlockSpec(memory_space=pltpu.VMEM)
    smem = pl.BlockSpec(memory_space=pltpu.SMEM)
    hbm = pl.BlockSpec(memory_space=pltpu.HBM)
    params = pltpu.CompilerParams(vmem_limit_bytes=(24 if blocks <= 4 else 44) * 1024 * 1024)

    def hold(array):
        return pltpu.with_memory_space_constraint(array, pltpu.HBM)

    key_held, value_held = hold(key_rows[0]), hold(values[0])
    depth_held, end_held = hold(depths), hold(subtree_end)
    message_rows = 2 * groups * tokens
    message = pl.pallas_call(
        functools.partial(pack_kernel, blocks),
        out_shape=jax.ShapeDtypeStruct((message_rows + META_ROWS, WIDTH), bf16),
        in_specs=[hbm] * 4,
        out_specs=vmem,
        scratch_shapes=[
            pltpu.VMEM((1, tokens), jnp.int32),
            pltpu.VMEM((1, tokens), jnp.int32),
            pltpu.SemaphoreType.DMA((2 + 2 * groups,)),
        ],
        compiler_params=params,
        name="pack",
    )(key_held, value_held, depth_held, end_held)
    shifts = list(range(1, blocks))
    arrived = [
        lax.ppermute(message, "ctx", [(i, i ^ s) for i in range(blocks) if i < i ^ s])
        for s in shifts
    ]

    lengths_held, slope_held, gain_held = hold(file_lengths), hold(slopes), hold(ancestor_gain)
    own_table = jax.ShapeDtypeStruct((tokens, tokens), f32)
    own_scores = jax.ShapeDtypeStruct((tokens, heads_all * tokens), f32)
    query_here, grad_here, product_here, _, _, own_weight, own_dscore, own_rows = pl.pallas_call(
        functools.partial(prepare_kernel, heads_per_group, groups),
        out_shape=[jax.ShapeDtypeStruct((tokens, width_all), bf16)] * 3
        + [own_table, own_table, own_scores, own_scores]
        + [jax.ShapeDtypeStruct((4, heads_all, tokens), f32)],
        in_specs=[smem] * 3 + [vmem] * 7,
        out_specs=[vmem] * 8,
        compiler_params=params,
        cost_estimate=pl.CostEstimate(
            flops=4 * tokens * tokens * width_all,
            bytes_accessed=12 * tokens * width_all,
            transcendentals=tokens * tokens * heads_all,
        ),
        name="prepare",
    )(
        lengths_held,
        slope_held,
        gain_held,
        depth_held,
        end_held,
        hold(queries[0]),
        hold(outputs[0]),
        hold(out_grads[0]),
        key_held,
        value_held,
    )

    bias_shape = (replicas, blocks, 8, WIDTH)
    matmul_flops = 2 * tokens * keys_seen * WIDTH * heads_all
    results = pl.pallas_call(
        functools.partial(main_kernel, blocks, heads_per_group, groups, shifts),
        out_shape=[jax.ShapeDtypeStruct((tokens, width_all), bf16)]
        + [jax.ShapeDtypeStruct((message_rows, WIDTH), bf16)] * blocks
        + [jax.ShapeDtypeStruct(bias_shape, f32)],
        in_specs=[smem] * 3 + [vmem] * (7 + blocks),
        out_specs=[hbm] + [vmem] * blocks + [hbm],
        scratch_shapes=[
            pltpu.VMEM((groups, tokens, group_columns), bf16),
            pltpu.VMEM((keys_seen - tokens, tokens), f32),
            pltpu.VMEM((keys_seen - tokens, tokens), f32),
            pltpu.VMEM((heads_all, tokens), f32),
            pltpu.VMEM((heads_all, tokens), f32),
            pltpu.VMEM((keys_seen, WIDTH), f32),
            pltpu.VMEM((keys_seen, WIDTH), f32),
            pltpu.VMEM((2, keys_seen - tokens, 2 * tokens), f32),
            pltpu.VMEM((keys_seen, group_columns), bf16),
            pltpu.VMEM((keys_seen, group_columns), bf16),
            pltpu.VMEM(bias_shape, f32),
            pltpu.SemaphoreType.DMA((groups,)),
            pltpu.SemaphoreType.DMA,
        ],
        compiler_params=params,
        cost_estimate=pl.CostEstimate(
            flops=5 * matmul_flops,
            bytes_accessed=10 * tokens * width_all,
            transcendentals=tokens * keys_seen * heads_all,
        ),
        name="attend",
    )(
        lengths_held,
        slope_held,
        gain_held,
        depth_held,
        query_here,
        grad_here,
        product_here,
        own_weight,
        own_dscore,
        own_rows,
        key_held,
        *arrived,
    )
    query_grads = results[0]
    parts = list(results[1 : 1 + blocks])
    bias_parts = results[1 + blocks].reshape(replicas * blocks, 8, WIDTH)
    for s in [2] + [s for s in range(1, blocks) if s != 2]:
        back = [(i, i ^ s) for i in range(blocks) if i > i ^ s]
        parts[s] = lax.ppermute(parts[s], "ctx", back)
    bias_parts = lax.all_to_all(bias_parts, ("dp", "ctx"), split_axis=0, concat_axis=0, tiled=True)

    early = [parts[0], parts[2], parts[1], *parts[3:-1]] if blocks > 3 else parts[:-1]
    parts_sum = pl.pallas_call(
        gather_parts_kernel,
        out_shape=jax.ShapeDtypeStruct((message_rows, WIDTH), f32),
        in_specs=[vmem] * len(early),
        out_specs=vmem,
        compiler_params=params,
        cost_estimate=pl.CostEstimate(
            flops=2 * message_rows * WIDTH * blocks,
            bytes_accessed=2 * message_rows * WIDTH * (blocks + 1),
            transcendentals=0,
        ),
        name="sum_parts",
    )(*early)
    key_grads, value_grads, bias_grads = pl.pallas_call(
        combine_kernel,
        out_shape=[jax.ShapeDtypeStruct((tokens, kv_width), bf16)] * 2
        + [jax.ShapeDtypeStruct((2, local_heads), f32)],
        in_specs=[vmem] * 3,
        out_specs=[vmem] * 3,
        compiler_params=params,
        name="combine",
    )(parts_sum, parts[-1], bias_parts)
    return (query_grads[None], key_grads[None], value_grads[None], bias_grads.T)


def solution(mesh):
    in_specs = (
        P("dp", "ctx", None),
        P("dp", "ctx", None),
        P("dp", "ctx", None),
        P("dp", "ctx", None),
        P("dp", "ctx", None),
        P("dp", "ctx"),
        P("dp", "ctx"),
        P("dp", None),
        P(),
        P(),
    )
    out_specs = (P("dp", "ctx", None), P("dp", "ctx", None), P("dp", "ctx", None), P("ctx", None))
    return jax.shard_map(body, mesh=mesh, in_specs=in_specs, out_specs=out_specs, check_vma=False)
```

```python
import functools

import jax
import jax.numpy as jnp
from jax import lax
from jax.experimental import pallas as pl
from jax.experimental.pallas import tpu as pltpu
from jax.sharding import PartitionSpec as P

WIDTH = 128
LOG2E = 1.4426950408889634
MASKED = -1e30
META_ROWS = 16
END_UNIT = 64


def dot_nt(a, b):
    return lax.dot_general(a, b, (((1,), (1,)), ((), ())), preferred_element_type=jnp.float32)


def dot_nn(a, b):
    return lax.dot_general(a, b, (((1,), (0,)), ((), ())), preferred_element_type=jnp.float32)


def fold_rows(block):
    return jnp.sum(block.reshape(block.shape[0] // 8, 8, block.shape[1]), axis=0)


def as_column(row):
    size = row.shape[1]
    return jnp.transpose(jnp.broadcast_to(row, (size, size)))


def pack_kernel(blocks, key_hbm, value_hbm, depth_hbm, end_hbm, message_ref, depth_ref, end_ref, sems):
    tokens, columns = key_hbm.shape
    groups = columns // WIDTH

    @pl.when(lax.axis_index("ctx") != blocks - 1)
    def _():
        copies = [
            pltpu.make_async_copy(depth_hbm, depth_ref, sems.at[0]),
            pltpu.make_async_copy(end_hbm, end_ref, sems.at[1]),
        ]
        for kind, hbm in enumerate((key_hbm, value_hbm)):
            for group in range(groups):
                index = kind * groups + group
                copies.append(
                    pltpu.make_async_copy(
                        hbm.at[:, group * WIDTH : (group + 1) * WIDTH],
                        message_ref.at[index * tokens : (index + 1) * tokens, :],
                        sems.at[2 + index],
                    )
                )
        for copy in copies:
            copy.start()
        copies[0].wait()
        copies[1].wait()
        end = end_ref[...]
        end_high = end // END_UNIT
        end_low = end - end_high * END_UNIT
        row = lax.broadcasted_iota(jnp.int32, (META_ROWS, tokens), 0)
        meta = jnp.where(row == 0, depth_ref[...], jnp.where(row == 1, end_high, end_low))
        meta = meta.astype(jnp.float32).astype(jnp.bfloat16)
        message_ref[2 * groups * tokens : 2 * groups * tokens + META_ROWS, :] = meta
        for copy in copies[2:]:
            copy.wait()


def table(lengths_ref, depth_ref, s, key_depth, key_end):
    shape = key_depth.shape
    here = lax.axis_index("ctx")
    query_pos = here * shape[1] + lax.broadcasted_iota(jnp.int32, shape, 1)
    key_pos = (here ^ s) * shape[0] + lax.broadcasted_iota(jnp.int32, shape, 0)
    start = jnp.zeros(shape, jnp.int32)
    bound = jnp.int32(0)
    for index in range(lengths_ref.shape[1]):
        bound = bound + lengths_ref[0, index]
        start = jnp.where(query_pos >= bound, bound, start)
    inside = query_pos.astype(jnp.float32) < key_end
    allowed = (key_pos <= query_pos) & (key_pos >= start)
    distance = jnp.abs(depth_ref[...].astype(jnp.float32) - key_depth)
    return distance, jnp.where(allowed, jnp.where(inside, 1.0, 0.0), MASKED)


def prepare_kernel(
    heads_per_group,
    groups,
    lengths_ref,
    slope_ref,
    gain_ref,
    depth_ref,
    end_ref,
    query_in,
    output_in,
    grad_in,
    key_ref,
    value_ref,
    query_out,
    grad_out,
    product_out,
    distance_ref,
    ancestor_ref,
    weight_ref,
    dscore_ref,
    rows_ref,
):
    tokens = query_in.shape[0]
    factor = WIDTH**-0.5
    query_out[...] = query_in[...]
    grad_out[...] = grad_in[...]
    product_out[...] = grad_in[...] * output_in[...]
    distance, ancestor = table(
        lengths_ref,
        depth_ref,
        0,
        as_column(depth_ref[...].astype(jnp.float32)),
        as_column(end_ref[...].astype(jnp.float32)),
    )
    distance_ref[...] = distance
    ancestor_ref[...] = ancestor

    @pl.loop(0, groups)
    def _(group):
        own = pl.ds(pl.multiple_of(group * WIDTH, WIDTH), WIDTH)
        key, value = key_ref[:, own], value_ref[:, own]
        value_ext = jnp.concatenate([value, jnp.full(value.shape, -1.0, jnp.bfloat16)], axis=1)
        for pair in range(heads_per_group // 2):
            first = group * heads_per_group + 2 * pair
            both = pl.ds(pl.multiple_of(first * WIDTH, 2 * WIDTH), 2 * WIDTH)

            def stack(array):
                return jnp.concatenate([array[:, 0:WIDTH], array[:, WIDTH:]], axis=0)

            grad = grad_in[:, both]
            grad_ext = jnp.concatenate([stack(grad), stack(grad * output_in[:, both])], axis=1)
            raw = dot_nt(key, stack(query_in[:, both]))
            centred = dot_nt(value_ext, grad_ext)
            for half in range(2):
                head = first + half
                gain = gain_ref[head] * LOG2E
                slope = slope_ref[head] * LOG2E
                lanes = slice(half * tokens, (half + 1) * tokens)
                distance, ancestor = distance_ref[...], ancestor_ref[...]
                score = raw[:, lanes] * (factor * LOG2E) + (gain * ancestor - slope * distance)
                top = jnp.max(score, axis=0, keepdims=True)
                weight = jnp.exp2(score - top)
                dscore = weight * centred[:, lanes]
                to = pl.ds(pl.multiple_of(head * tokens, tokens), tokens)
                weight_ref[:, to] = weight
                dscore_ref[:, to] = dscore
                at = pl.ds(head, 1)
                rows_ref[0, at, :] = top
                rows_ref[1, at, :] = jnp.sum(weight, axis=0, keepdims=True)
                rows_ref[2, at, :] = jnp.sum(dscore * distance, axis=0, keepdims=True)
                rows_ref[3, at, :] = jnp.sum(dscore * ancestor, axis=0, keepdims=True)


def main_kernel(
    blocks,
    heads_per_group,
    groups,
    shifts,
    lengths_ref,
    slope_ref,
    gain_ref,
    depth_ref,
    query_ref,
    grad_ref,
    product_ref,
    own_weight_ref,
    own_dscore_ref,
    own_rows_ref,
    key_ref,
    *refs,
):
    tokens = query_ref.shape[0]
    remote = [refs[shifts.index(s)] for s in range(1, blocks)]
    query_grad_hbm = refs[blocks - 1]
    part_refs = refs[blocks : 2 * blocks]
    bias_hbm = refs[2 * blocks]
    (
        query_grad_ref,
        distance_ref,
        ancestor_ref,
        slope_rows,
        gain_rows,
        key_acc,
        value_acc,
        weight_ref,
        probs_ref,
        dscore_ref,
        bias_ref,
        store_sems,
        bias_sem,
    ) = refs[2 * blocks + 1 :]
    factor = WIDTH**-0.5
    group_columns = heads_per_group * WIDTH
    pairs = heads_per_group // 2

    def store(group):
        wide = pl.ds(pl.multiple_of(group * group_columns, group_columns), group_columns)
        return pltpu.make_async_copy(
            query_grad_ref.at[group], query_grad_hbm.at[:, wide], store_sems.at[group]
        )

    block_rows = [slice(s * tokens, (s + 1) * tokens) for s in range(blocks)]
    remote_rows = block_rows[:-1]
    below = slice(2 * groups * tokens, 2 * groups * tokens + META_ROWS)
    for s in range(1, blocks):
        meta = remote[s - 1][below, :].astype(jnp.float32)
        distance, ancestor = table(
            lengths_ref,
            depth_ref,
            s,
            as_column(meta[0:1]),
            as_column(meta[1:2] * END_UNIT + meta[2:3]),
        )
        distance_ref[remote_rows[s - 1], :] = distance
        ancestor_ref[remote_rows[s - 1], :] = ancestor

    def remote_blocks(kind, group):
        at = pl.multiple_of((kind * groups + group) * tokens, tokens)
        return jnp.concatenate([r[pl.ds(at, tokens), :] for r in remote], axis=0)

    def stacked(ref, group, first, count):
        at = pl.multiple_of(group * group_columns, group_columns) + first * WIDTH
        heads = [pl.ds(pl.multiple_of(at + i * WIDTH, WIDTH), WIDTH) for i in range(count)]
        return jnp.concatenate([ref[:, head] for head in heads], axis=0)

    def weigh(group, pair, raw, half):
        head = group * heads_per_group + 2 * pair + half
        gain = gain_ref[head] * LOG2E
        slope = slope_ref[head] * LOG2E
        lanes = slice(half * tokens, (half + 1) * tokens)
        tops, totals = [own_rows_ref[0, pl.ds(head, 1), :]], [own_rows_ref[1, pl.ds(head, 1), :]]
        for rows in remote_rows:
            score = raw[rows, lanes] * (factor * LOG2E) + (
                gain * ancestor_ref[rows, :] - slope * distance_ref[rows, :]
            )
            top = jnp.max(score, axis=0, keepdims=True)
            weight = jnp.exp2(score - top)
            weight_ref[pair % 2, rows, lanes] = weight
            tops.append(top)
            totals.append(jnp.sum(weight, axis=0, keepdims=True))
        top = functools.reduce(jnp.maximum, tops)
        shrink = [jnp.exp2(t - top) for t in tops]
        inverse = 1.0 / sum(a * b for a, b in zip(totals, shrink))
        return [s * inverse for s in shrink]

    def differentiate(group, pair, centred, scales, half):
        lanes = slice(half * tokens, (half + 1) * tokens)
        to = slice((2 * pair + half) * tokens, (2 * pair + half + 1) * tokens)
        head = group * heads_per_group + 2 * pair + half
        own = pl.ds(pl.multiple_of(head * tokens, tokens), tokens)
        own_rows = block_rows[0]
        probs_ref[own_rows, to] = (own_weight_ref[:, own] * scales[0]).astype(jnp.bfloat16)
        dscore_ref[own_rows, to] = (own_dscore_ref[:, own] * scales[0]).astype(jnp.bfloat16)
        slope_sum, gain_sum = 0.0, 0.0
        for s, rows in enumerate(remote_rows, 1):
            probs = weight_ref[pair % 2, rows, lanes] * scales[s]
            dscore = probs * centred[rows, lanes]
            probs_ref[block_rows[s], to] = probs.astype(jnp.bfloat16)
            dscore_ref[block_rows[s], to] = dscore.astype(jnp.bfloat16)
            slope_sum = slope_sum + fold_rows(dscore * distance_ref[rows, :])
            gain_sum = gain_sum + fold_rows(dscore * ancestor_ref[rows, :])
        at = pl.ds(head, 1)
        slope_rows[at, :] = -(
            jnp.sum(slope_sum, axis=0, keepdims=True) + own_rows_ref[2, at, :] * scales[0]
        )
        gain_rows[at, :] = (
            jnp.sum(gain_sum, axis=0, keepdims=True) + own_rows_ref[3, at, :] * scales[0]
        )

    def put_part(group, kind, whole):
        at = pl.multiple_of((kind * groups + group) * tokens, tokens)
        for s, rows in enumerate(block_rows):
            part_refs[s][pl.ds(at, tokens), :] = whole[rows].astype(jnp.bfloat16)

    def key_part(group, first, count):
        heads = stacked(query_ref, group, first, count)
        lanes = slice(first * tokens, (first + count) * tokens)
        return dot_nn(dscore_ref[:, lanes], heads)

    def value_part(group, first, count):
        heads = stacked(grad_ref, group, first, count)
        lanes = slice(first * tokens, (first + count) * tokens)
        return dot_nn(probs_ref[:, lanes], heads)

    def query_part(keys_across, group, pair):
        lanes = slice(2 * pair * tokens, (2 * pair + 2) * tokens)
        across = dot_nn(keys_across, dscore_ref[:, lanes]) * factor
        rows = jnp.transpose(across.astype(jnp.bfloat16))
        for half in range(2):
            at = (2 * pair + half) * WIDTH
            query_grad_ref[group, :, at : at + WIDTH] = rows[half * tokens : (half + 1) * tokens]

    @pl.loop(0, groups)
    def _(group):
        keys = remote_blocks(0, group)
        values = remote_blocks(1, group)
        value_ext = jnp.concatenate([values, jnp.full(values.shape, -1.0, jnp.bfloat16)], axis=1)
        own_key = key_ref[:, pl.ds(pl.multiple_of(group * WIDTH, WIDTH), WIDTH)]
        keys_across = jnp.transpose(jnp.concatenate([own_key, keys], axis=0))
        half_heads = heads_per_group // 2
        raws = [dot_nt(keys, stacked(query_ref, group, 0, 2))]
        for pair in range(pairs):
            grad_pair = stacked(grad_ref, group, 2 * pair, 2)
            product_pair = stacked(product_ref, group, 2 * pair, 2)
            grad_ext = jnp.concatenate([grad_pair, product_pair], axis=1)
            raw = raws.pop(0)
            if pair + 1 < pairs:
                raws.append(dot_nt(keys, stacked(query_ref, group, 2 * pair + 2, 2)))
            if pair:
                part = key_part(group, 2 * pair - 2, 2)
                key_acc[...] = part if pair == 1 else key_acc[...] + part
            scales = [weigh(group, pair, raw, half) for half in range(2)]
            if pair:
                part = value_part(group, 2 * pair - 2, 2)
                value_acc[...] = part if pair == 1 else value_acc[...] + part
            if pair:
                query_part(keys_across, group, pair - 1)
            centred = dot_nt(value_ext, grad_ext)
            for half in range(2):
                differentiate(group, pair, centred, scales[half], half)
        key_whole = key_acc[...] + key_part(group, heads_per_group - 2, 2)
        put_part(group, 0, key_whole * factor)
        put_part(group, 1, value_acc[...] + value_part(group, heads_per_group - 2, 2))
        query_part(keys_across, group, pairs - 1)
        store(group).start()

    slope_sum = jnp.sum(slope_rows[...], axis=1, keepdims=True)
    gain_sum = jnp.sum(gain_rows[...], axis=1, keepdims=True)
    shape = slope_rows.shape
    lane = lax.broadcasted_iota(jnp.int32, shape, 1)
    row = lax.broadcasted_iota(jnp.int32, shape, 0)
    replicas, parts, rows_here, local = bias_ref.shape
    local_heads = shape[0] // parts
    kind = lax.broadcasted_iota(jnp.int32, (rows_here, local), 0)
    for part in range(parts):
        mine = (lane == row - part * local_heads) & (lane < local_heads)
        slope_line = jnp.sum(jnp.where(mine, slope_sum, 0.0), axis=0, keepdims=True)
        gain_line = jnp.sum(jnp.where(mine, gain_sum, 0.0), axis=0, keepdims=True)
        tile = jnp.where(kind == 0, slope_line, jnp.where(kind == 1, gain_line, 0.0))
        bias_ref[:, part] = jnp.broadcast_to(tile[None], (replicas, rows_here, local))
    bias_copy = pltpu.make_async_copy(bias_ref, bias_hbm, bias_sem)
    bias_copy.start()
    for group in range(groups):
        store(group).wait()
    bias_copy.wait()


def gather_parts_kernel(*refs):
    total = refs[0][...].astype(jnp.float32)
    for part in refs[1:-1]:
        total = total + part[...].astype(jnp.float32)
    refs[-1][...] = total


def combine_kernel(sum_ref, part_ref, bias_parts, key_out, value_out, bias_out):
    tokens = key_out.shape[0]
    groups = key_out.shape[1] // WIDTH
    for kind, out in enumerate((key_out, value_out)):
        for group in range(groups):
            at = (kind * groups + group) * tokens
            rows = slice(at, at + tokens)
            total = sum_ref[rows, :] + part_ref[rows, :].astype(jnp.float32)
            out[:, group * WIDTH : (group + 1) * WIDTH] = total.astype(jnp.bfloat16)
    bias_out[...] = jnp.sum(bias_parts[...], axis=0)[0:2, 0 : bias_out.shape[1]]


def body(
    queries,
    key_rows,
    values,
    outputs,
    out_grads,
    depths,
    subtree_end,
    file_lengths,
    slopes,
    ancestor_gain,
):
    blocks = lax.axis_size("ctx")
    replicas = lax.axis_size("dp")
    tokens, width_all = queries.shape[1:]
    kv_width = key_rows.shape[2]
    heads_all = width_all // WIDTH
    groups = kv_width // WIDTH
    heads_per_group = heads_all // groups
    group_columns = heads_per_group * WIDTH
    local_heads = heads_all // blocks
    keys_seen = blocks * tokens
    bf16, f32 = jnp.bfloat16, jnp.float32
    vmem = pl.BlockSpec(memory_space=pltpu.VMEM)
    smem = pl.BlockSpec(memory_space=pltpu.SMEM)
    hbm = pl.BlockSpec(memory_space=pltpu.HBM)
    params = pltpu.CompilerParams(vmem_limit_bytes=(24 if blocks <= 4 else 44) * 1024 * 1024)

    def hold(array):
        return pltpu.with_memory_space_constraint(array, pltpu.HBM)

    key_held, value_held = hold(key_rows[0]), hold(values[0])
    depth_held, end_held = hold(depths), hold(subtree_end)
    message_rows = 2 * groups * tokens
    message = pl.pallas_call(
        functools.partial(pack_kernel, blocks),
        out_shape=jax.ShapeDtypeStruct((message_rows + META_ROWS, WIDTH), bf16),
        in_specs=[hbm] * 4,
        out_specs=vmem,
        scratch_shapes=[
            pltpu.VMEM((1, tokens), jnp.int32),
            pltpu.VMEM((1, tokens), jnp.int32),
            pltpu.SemaphoreType.DMA((2 + 2 * groups,)),
        ],
        compiler_params=params,
        name="pack",
    )(key_held, value_held, depth_held, end_held)
    shifts = list(range(1, blocks))
    arrived = [
        lax.ppermute(message, "ctx", [(i, i ^ s) for i in range(blocks) if i < i ^ s])
        for s in shifts
    ]

    lengths_held, slope_held, gain_held = hold(file_lengths), hold(slopes), hold(ancestor_gain)
    own_table = jax.ShapeDtypeStruct((tokens, tokens), f32)
    own_scores = jax.ShapeDtypeStruct((tokens, heads_all * tokens), f32)
    query_here, grad_here, product_here, _, _, own_weight, own_dscore, own_rows = pl.pallas_call(
        functools.partial(prepare_kernel, heads_per_group, groups),
        out_shape=[jax.ShapeDtypeStruct((tokens, width_all), bf16)] * 3
        + [own_table, own_table, own_scores, own_scores]
        + [jax.ShapeDtypeStruct((4, heads_all, tokens), f32)],
        in_specs=[smem] * 3 + [vmem] * 7,
        out_specs=[vmem] * 8,
        compiler_params=params,
        cost_estimate=pl.CostEstimate(
            flops=4 * tokens * tokens * width_all,
            bytes_accessed=12 * tokens * width_all,
            transcendentals=tokens * tokens * heads_all,
        ),
        name="prepare",
    )(
        lengths_held,
        slope_held,
        gain_held,
        depth_held,
        end_held,
        hold(queries[0]),
        hold(outputs[0]),
        hold(out_grads[0]),
        key_held,
        value_held,
    )

    bias_shape = (replicas, blocks, 8, WIDTH)
    matmul_flops = 2 * tokens * keys_seen * WIDTH * heads_all
    results = pl.pallas_call(
        functools.partial(main_kernel, blocks, heads_per_group, groups, shifts),
        out_shape=[jax.ShapeDtypeStruct((tokens, width_all), bf16)]
        + [jax.ShapeDtypeStruct((message_rows, WIDTH), bf16)] * blocks
        + [jax.ShapeDtypeStruct(bias_shape, f32)],
        in_specs=[smem] * 3 + [vmem] * (7 + blocks),
        out_specs=[hbm] + [vmem] * blocks + [hbm],
        scratch_shapes=[
            pltpu.VMEM((groups, tokens, group_columns), bf16),
            pltpu.VMEM((keys_seen - tokens, tokens), f32),
            pltpu.VMEM((keys_seen - tokens, tokens), f32),
            pltpu.VMEM((heads_all, tokens), f32),
            pltpu.VMEM((heads_all, tokens), f32),
            pltpu.VMEM((keys_seen, WIDTH), f32),
            pltpu.VMEM((keys_seen, WIDTH), f32),
            pltpu.VMEM((2, keys_seen - tokens, 2 * tokens), f32),
            pltpu.VMEM((keys_seen, group_columns), bf16),
            pltpu.VMEM((keys_seen, group_columns), bf16),
            pltpu.VMEM(bias_shape, f32),
            pltpu.SemaphoreType.DMA((groups,)),
            pltpu.SemaphoreType.DMA,
        ],
        compiler_params=params,
        cost_estimate=pl.CostEstimate(
            flops=5 * matmul_flops,
            bytes_accessed=10 * tokens * width_all,
            transcendentals=tokens * keys_seen * heads_all,
        ),
        name="attend",
    )(
        lengths_held,
        slope_held,
        gain_held,
        depth_held,
        query_here,
        grad_here,
        product_here,
        own_weight,
        own_dscore,
        own_rows,
        key_held,
        *arrived,
    )
    query_grads = results[0]
    parts = list(results[1 : 1 + blocks])
    bias_parts = results[1 + blocks].reshape(replicas * blocks, 8, WIDTH)
    for s in [2] + [s for s in range(1, blocks) if s != 2]:
        back = [(i, i ^ s) for i in range(blocks) if i > i ^ s]
        parts[s] = lax.ppermute(parts[s], "ctx", back)
    bias_parts = lax.all_to_all(bias_parts, ("dp", "ctx"), split_axis=0, concat_axis=0, tiled=True)

    early = [parts[0], parts[2], parts[1], *parts[3:-1]] if blocks > 3 else parts[:-1]
    parts_sum = pl.pallas_call(
        gather_parts_kernel,
        out_shape=jax.ShapeDtypeStruct((message_rows, WIDTH), f32),
        in_specs=[vmem] * len(early),
        out_specs=vmem,
        compiler_params=params,
        cost_estimate=pl.CostEstimate(
            flops=2 * message_rows * WIDTH * blocks,
            bytes_accessed=2 * message_rows * WIDTH * (blocks + 1),
            transcendentals=0,
        ),
        name="sum_parts",
    )(*early)
    key_grads, value_grads, bias_grads = pl.pallas_call(
        combine_kernel,
        out_shape=[jax.ShapeDtypeStruct((tokens, kv_width), bf16)] * 2
        + [jax.ShapeDtypeStruct((2, local_heads), f32)],
        in_specs=[vmem] * 3,
        out_specs=[vmem] * 3,
        compiler_params=params,
        name="combine",
    )(parts_sum, parts[-1], bias_parts)
    return (query_grads[None], key_grads[None], value_grads[None], bias_grads.T)


def solution(mesh):
    in_specs = (
        P("dp", "ctx", None),
        P("dp", "ctx", None),
        P("dp", "ctx", None),
        P("dp", "ctx", None),
        P("dp", "ctx", None),
        P("dp", "ctx"),
        P("dp", "ctx"),
        P("dp", None),
        P(),
        P(),
    )
    out_specs = (P("dp", "ctx", None), P("dp", "ctx", None), P("dp", "ctx", None), P("ctx", None))
    return jax.shard_map(body, mesh=mesh, in_specs=in_specs, out_specs=out_specs, check_vma=False)
```

```python
import functools

import jax
import jax.numpy as jnp
from jax import lax
from jax.experimental import pallas as pl
from jax.experimental.pallas import tpu as pltpu
from jax.sharding import PartitionSpec as P

WIDTH = 128
LOG2E = 1.4426950408889634
MASKED = -1e30
META_ROWS = 16
END_UNIT = 64


def dot_nt(a, b):
    return lax.dot_general(a, b, (((1,), (1,)), ((), ())), preferred_element_type=jnp.float32)


def dot_nn(a, b):
    return lax.dot_general(a, b, (((1,), (0,)), ((), ())), preferred_element_type=jnp.float32)


def fold_rows(block):
    return jnp.sum(block.reshape(block.shape[0] // 8, 8, block.shape[1]), axis=0)


def as_column(row):
    size = row.shape[1]
    return jnp.transpose(jnp.broadcast_to(row, (size, size)))


def pack_kernel(blocks, key_hbm, value_hbm, depth_hbm, end_hbm, message_ref, depth_ref, end_ref, sems):
    tokens, columns = key_hbm.shape
    groups = columns // WIDTH

    @pl.when(lax.axis_index("ctx") != blocks - 1)
    def _():
        copies = [
            pltpu.make_async_copy(depth_hbm, depth_ref, sems.at[0]),
            pltpu.make_async_copy(end_hbm, end_ref, sems.at[1]),
        ]
        for kind, hbm in enumerate((key_hbm, value_hbm)):
            for group in range(groups):
                index = kind * groups + group
                copies.append(
                    pltpu.make_async_copy(
                        hbm.at[:, group * WIDTH : (group + 1) * WIDTH],
                        message_ref.at[index * tokens : (index + 1) * tokens, :],
                        sems.at[2 + index],
                    )
                )
        for copy in copies:
            copy.start()
        copies[0].wait()
        copies[1].wait()
        end = end_ref[...]
        end_high = end // END_UNIT
        end_low = end - end_high * END_UNIT
        row = lax.broadcasted_iota(jnp.int32, (META_ROWS, tokens), 0)
        meta = jnp.where(row == 0, depth_ref[...], jnp.where(row == 1, end_high, end_low))
        meta = meta.astype(jnp.float32).astype(jnp.bfloat16)
        message_ref[2 * groups * tokens : 2 * groups * tokens + META_ROWS, :] = meta
        for copy in copies[2:]:
            copy.wait()


def table(lengths_ref, depth_ref, s, key_depth, key_end):
    shape = key_depth.shape
    here = lax.axis_index("ctx")
    query_pos = here * shape[1] + lax.broadcasted_iota(jnp.int32, shape, 1)
    key_pos = (here ^ s) * shape[0] + lax.broadcasted_iota(jnp.int32, shape, 0)
    start = jnp.zeros(shape, jnp.int32)
    bound = jnp.int32(0)
    for index in range(lengths_ref.shape[1]):
        bound = bound + lengths_ref[0, index]
        start = jnp.where(query_pos >= bound, bound, start)
    inside = query_pos.astype(jnp.float32) < key_end
    allowed = (key_pos <= query_pos) & (key_pos >= start)
    distance = jnp.abs(depth_ref[...].astype(jnp.float32) - key_depth)
    return distance, jnp.where(allowed, jnp.where(inside, 1.0, 0.0), MASKED)


def prepare_kernel(
    heads_per_group,
    groups,
    lengths_ref,
    slope_ref,
    gain_ref,
    depth_ref,
    end_ref,
    query_in,
    output_in,
    grad_in,
    key_ref,
    value_ref,
    query_out,
    grad_out,
    product_out,
    distance_ref,
    ancestor_ref,
    weight_ref,
    dscore_ref,
    rows_ref,
):
    tokens = query_in.shape[0]
    factor = WIDTH**-0.5
    query_out[...] = query_in[...]
    grad_out[...] = grad_in[...]
    product_out[...] = grad_in[...] * output_in[...]
    distance, ancestor = table(
        lengths_ref,
        depth_ref,
        0,
        as_column(depth_ref[...].astype(jnp.float32)),
        as_column(end_ref[...].astype(jnp.float32)),
    )
    distance_ref[...] = distance
    ancestor_ref[...] = ancestor

    @pl.loop(0, groups)
    def _(group):
        own = pl.ds(pl.multiple_of(group * WIDTH, WIDTH), WIDTH)
        key, value = key_ref[:, own], value_ref[:, own]
        value_ext = jnp.concatenate([value, jnp.full(value.shape, -1.0, jnp.bfloat16)], axis=1)
        for pair in range(heads_per_group // 2):
            first = group * heads_per_group + 2 * pair
            both = pl.ds(pl.multiple_of(first * WIDTH, 2 * WIDTH), 2 * WIDTH)

            def stack(array):
                return jnp.concatenate([array[:, 0:WIDTH], array[:, WIDTH:]], axis=0)

            grad = grad_in[:, both]
            grad_ext = jnp.concatenate([stack(grad), stack(grad * output_in[:, both])], axis=1)
            raw = dot_nt(key, stack(query_in[:, both]))
            centred = dot_nt(value_ext, grad_ext)
            for half in range(2):
                head = first + half
                gain = gain_ref[head] * LOG2E
                slope = slope_ref[head] * LOG2E
                lanes = slice(half * tokens, (half + 1) * tokens)
                distance, ancestor = distance_ref[...], ancestor_ref[...]
                score = raw[:, lanes] * (factor * LOG2E) + (gain * ancestor - slope * distance)
                top = jnp.max(score, axis=0, keepdims=True)
                weight = jnp.exp2(score - top)
                dscore = weight * centred[:, lanes]
                to = pl.ds(pl.multiple_of(head * tokens, tokens), tokens)
                weight_ref[:, to] = weight
                dscore_ref[:, to] = dscore
                at = pl.ds(head, 1)
                rows_ref[0, at, :] = top
                rows_ref[1, at, :] = jnp.sum(weight, axis=0, keepdims=True)
                rows_ref[2, at, :] = jnp.sum(dscore * distance, axis=0, keepdims=True)
                rows_ref[3, at, :] = jnp.sum(dscore * ancestor, axis=0, keepdims=True)


def main_kernel(
    blocks,
    heads_per_group,
    groups,
    shifts,
    lengths_ref,
    slope_ref,
    gain_ref,
    depth_ref,
    query_ref,
    grad_ref,
    product_ref,
    own_weight_ref,
    own_dscore_ref,
    own_rows_ref,
    key_ref,
    *refs,
):
    tokens = query_ref.shape[0]
    remote = [refs[shifts.index(s)] for s in range(1, blocks)]
    query_grad_hbm = refs[blocks - 1]
    part_refs = refs[blocks : 2 * blocks]
    bias_ref = refs[2 * blocks]
    (
        query_grad_ref,
        distance_ref,
        ancestor_ref,
        slope_rows,
        gain_rows,
        key_acc,
        value_acc,
        weight_ref,
        probs_ref,
        dscore_ref,
        store_sems,
    ) = refs[2 * blocks + 1 :]
    factor = WIDTH**-0.5
    group_columns = heads_per_group * WIDTH
    pairs = heads_per_group // 2

    def store(group, pair):
        inside = slice(2 * pair * WIDTH, (2 * pair + 2) * WIDTH)
        at = pl.multiple_of(group * group_columns, group_columns) + 2 * pair * WIDTH
        wide = pl.ds(pl.multiple_of(at, 2 * WIDTH), 2 * WIDTH)
        return pltpu.make_async_copy(
            query_grad_ref.at[group, :, inside],
            query_grad_hbm.at[:, wide],
            store_sems.at[group, pair],
        )

    block_rows = [slice(s * tokens, (s + 1) * tokens) for s in range(blocks)]
    remote_rows = block_rows[:-1]
    below = slice(2 * groups * tokens, 2 * groups * tokens + META_ROWS)
    for s in range(1, blocks):
        meta = remote[s - 1][below, :].astype(jnp.float32)
        distance, ancestor = table(
            lengths_ref,
            depth_ref,
            s,
            as_column(meta[0:1]),
            as_column(meta[1:2] * END_UNIT + meta[2:3]),
        )
        distance_ref[remote_rows[s - 1], :] = distance
        ancestor_ref[remote_rows[s - 1], :] = ancestor

    def remote_blocks(kind, group):
        at = pl.multiple_of((kind * groups + group) * tokens, tokens)
        return jnp.concatenate([r[pl.ds(at, tokens), :] for r in remote], axis=0)

    def stacked(ref, group, first, count):
        at = pl.multiple_of(group * group_columns, group_columns) + first * WIDTH
        heads = [pl.ds(pl.multiple_of(at + i * WIDTH, WIDTH), WIDTH) for i in range(count)]
        return jnp.concatenate([ref[:, head] for head in heads], axis=0)

    def weigh(group, pair, raw, half):
        head = group * heads_per_group + 2 * pair + half
        gain = gain_ref[head] * LOG2E
        slope = slope_ref[head] * LOG2E
        lanes = slice(half * tokens, (half + 1) * tokens)
        tops, totals = [own_rows_ref[0, pl.ds(head, 1), :]], [own_rows_ref[1, pl.ds(head, 1), :]]
        for rows in remote_rows:
            score = raw[rows, lanes] * (factor * LOG2E) + (
                gain * ancestor_ref[rows, :] - slope * distance_ref[rows, :]
            )
            top = jnp.max(score, axis=0, keepdims=True)
            weight = jnp.exp2(score - top)
            weight_ref[pair % 2, rows, lanes] = weight
            tops.append(top)
            totals.append(jnp.sum(weight, axis=0, keepdims=True))
        top = functools.reduce(jnp.maximum, tops)
        shrink = [jnp.exp2(t - top) for t in tops]
        inverse = 1.0 / sum(a * b for a, b in zip(totals, shrink))
        return [s * inverse for s in shrink]

    def differentiate(group, pair, centred, scales, half):
        lanes = slice(half * tokens, (half + 1) * tokens)
        to = slice((2 * pair + half) * tokens, (2 * pair + half + 1) * tokens)
        head = group * heads_per_group + 2 * pair + half
        own = pl.ds(pl.multiple_of(head * tokens, tokens), tokens)
        own_rows = block_rows[0]
        probs_ref[own_rows, to] = (own_weight_ref[:, own] * scales[0]).astype(jnp.bfloat16)
        dscore_ref[own_rows, to] = (own_dscore_ref[:, own] * scales[0]).astype(jnp.bfloat16)
        slope_sum, gain_sum = 0.0, 0.0
        for s, rows in enumerate(remote_rows, 1):
            probs = weight_ref[pair % 2, rows, lanes] * scales[s]
            dscore = probs * centred[rows, lanes]
            probs_ref[block_rows[s], to] = probs.astype(jnp.bfloat16)
            dscore_ref[block_rows[s], to] = dscore.astype(jnp.bfloat16)
            slope_sum = slope_sum + fold_rows(dscore * distance_ref[rows, :])
            gain_sum = gain_sum + fold_rows(dscore * ancestor_ref[rows, :])
        at = pl.ds(head, 1)
        slope_rows[at, :] = -(
            jnp.sum(slope_sum, axis=0, keepdims=True) + own_rows_ref[2, at, :] * scales[0]
        )
        gain_rows[at, :] = (
            jnp.sum(gain_sum, axis=0, keepdims=True) + own_rows_ref[3, at, :] * scales[0]
        )

    def put_part(group, kind, whole):
        at = pl.multiple_of((kind * groups + group) * tokens, tokens)
        for s, rows in enumerate(block_rows):
            part_refs[s][pl.ds(at, tokens), :] = whole[rows].astype(jnp.bfloat16)

    def key_part(group, first, count):
        heads = stacked(query_ref, group, first, count)
        lanes = slice(first * tokens, (first + count) * tokens)
        return dot_nn(dscore_ref[:, lanes], heads)

    def value_part(group, first, count):
        heads = stacked(grad_ref, group, first, count)
        lanes = slice(first * tokens, (first + count) * tokens)
        return dot_nn(probs_ref[:, lanes], heads)

    def query_part(keys_across, group, pair):
        lanes = slice(2 * pair * tokens, (2 * pair + 2) * tokens)
        across = dot_nn(keys_across, dscore_ref[:, lanes]) * factor
        rows = jnp.transpose(across.astype(jnp.bfloat16))
        for half in range(2):
            at = (2 * pair + half) * WIDTH
            query_grad_ref[group, :, at : at + WIDTH] = rows[half * tokens : (half + 1) * tokens]
        store(group, pair).start()

    @pl.loop(0, groups)
    def _(group):
        keys = remote_blocks(0, group)
        values = remote_blocks(1, group)
        value_ext = jnp.concatenate([values, jnp.full(values.shape, -1.0, jnp.bfloat16)], axis=1)
        own_key = key_ref[:, pl.ds(pl.multiple_of(group * WIDTH, WIDTH), WIDTH)]
        keys_across = jnp.transpose(jnp.concatenate([own_key, keys], axis=0))
        half_heads = heads_per_group // 2
        raws = [dot_nt(keys, stacked(query_ref, group, 0, 2))]
        for pair in range(pairs):
            grad_pair = stacked(grad_ref, group, 2 * pair, 2)
            product_pair = stacked(product_ref, group, 2 * pair, 2)
            grad_ext = jnp.concatenate([grad_pair, product_pair], axis=1)
            raw = raws.pop(0)
            if pair + 1 < pairs:
                raws.append(dot_nt(keys, stacked(query_ref, group, 2 * pair + 2, 2)))
            if pair:
                part = key_part(group, 2 * pair - 2, 2)
                key_acc[...] = part if pair == 1 else key_acc[...] + part
            scales = [weigh(group, pair, raw, half) for half in range(2)]
            if pair:
                part = value_part(group, 2 * pair - 2, 2)
                value_acc[...] = part if pair == 1 else value_acc[...] + part
            if pair:
                query_part(keys_across, group, pair - 1)
            centred = dot_nt(value_ext, grad_ext)
            for half in range(2):
                differentiate(group, pair, centred, scales[half], half)
        key_whole = key_acc[...] + key_part(group, heads_per_group - 2, 2)
        put_part(group, 0, key_whole * factor)
        put_part(group, 1, value_acc[...] + value_part(group, heads_per_group - 2, 2))
        query_part(keys_across, group, pairs - 1)

    slope_sum = jnp.sum(slope_rows[...], axis=1, keepdims=True)
    gain_sum = jnp.sum(gain_rows[...], axis=1, keepdims=True)
    shape = slope_rows.shape
    lane = lax.broadcasted_iota(jnp.int32, shape, 1)
    row = lax.broadcasted_iota(jnp.int32, shape, 0)
    replicas, parts, rows_here, local = bias_ref.shape
    local_heads = shape[0] // parts
    kind = lax.broadcasted_iota(jnp.int32, (rows_here, local), 0)
    for part in range(parts):
        mine = (lane == row - part * local_heads) & (lane < local_heads)
        slope_line = jnp.sum(jnp.where(mine, slope_sum, 0.0), axis=0, keepdims=True)
        gain_line = jnp.sum(jnp.where(mine, gain_sum, 0.0), axis=0, keepdims=True)
        tile = jnp.where(kind == 0, slope_line, jnp.where(kind == 1, gain_line, 0.0))
        bias_ref[:, part] = jnp.broadcast_to(tile[None], (replicas, rows_here, local))
    for group in range(groups):
        for pair in range(pairs):
            store(group, pair).wait()


def gather_parts_kernel(*refs):
    total = refs[0][...].astype(jnp.float32)
    for part in refs[1:-1]:
        total = total + part[...].astype(jnp.float32)
    refs[-1][...] = total


def combine_kernel(sum_ref, part_ref, bias_parts, key_out, value_out, bias_out):
    tokens = key_out.shape[0]
    groups = key_out.shape[1] // WIDTH
    for kind, out in enumerate((key_out, value_out)):
        for group in range(groups):
            at = (kind * groups + group) * tokens
            rows = slice(at, at + tokens)
            total = sum_ref[rows, :] + part_ref[rows, :].astype(jnp.float32)
            out[:, group * WIDTH : (group + 1) * WIDTH] = total.astype(jnp.bfloat16)
    bias_out[...] = jnp.sum(bias_parts[...], axis=0)[0:2, 0 : bias_out.shape[1]]


def body(
    queries,
    key_rows,
    values,
    outputs,
    out_grads,
    depths,
    subtree_end,
    file_lengths,
    slopes,
    ancestor_gain,
):
    blocks = lax.axis_size("ctx")
    replicas = lax.axis_size("dp")
    tokens, width_all = queries.shape[1:]
    kv_width = key_rows.shape[2]
    heads_all = width_all // WIDTH
    groups = kv_width // WIDTH
    heads_per_group = heads_all // groups
    group_columns = heads_per_group * WIDTH
    local_heads = heads_all // blocks
    keys_seen = blocks * tokens
    bf16, f32 = jnp.bfloat16, jnp.float32
    vmem = pl.BlockSpec(memory_space=pltpu.VMEM)
    smem = pl.BlockSpec(memory_space=pltpu.SMEM)
    hbm = pl.BlockSpec(memory_space=pltpu.HBM)
    params = pltpu.CompilerParams(vmem_limit_bytes=(24 if blocks <= 4 else 44) * 1024 * 1024)

    def hold(array):
        return pltpu.with_memory_space_constraint(array, pltpu.HBM)

    key_held, value_held = hold(key_rows[0]), hold(values[0])
    depth_held, end_held = hold(depths), hold(subtree_end)
    message_rows = 2 * groups * tokens
    message = pl.pallas_call(
        functools.partial(pack_kernel, blocks),
        out_shape=jax.ShapeDtypeStruct((message_rows + META_ROWS, WIDTH), bf16),
        in_specs=[hbm] * 4,
        out_specs=vmem,
        scratch_shapes=[
            pltpu.VMEM((1, tokens), jnp.int32),
            pltpu.VMEM((1, tokens), jnp.int32),
            pltpu.SemaphoreType.DMA((2 + 2 * groups,)),
        ],
        compiler_params=params,
        name="pack",
    )(key_held, value_held, depth_held, end_held)
    shifts = list(range(1, blocks))
    arrived = [
        lax.ppermute(message, "ctx", [(i, i ^ s) for i in range(blocks) if i < i ^ s])
        for s in shifts
    ]

    lengths_held, slope_held, gain_held = hold(file_lengths), hold(slopes), hold(ancestor_gain)
    own_table = jax.ShapeDtypeStruct((tokens, tokens), f32)
    own_scores = jax.ShapeDtypeStruct((tokens, heads_all * tokens), f32)
    query_here, grad_here, product_here, _, _, own_weight, own_dscore, own_rows = pl.pallas_call(
        functools.partial(prepare_kernel, heads_per_group, groups),
        out_shape=[jax.ShapeDtypeStruct((tokens, width_all), bf16)] * 3
        + [own_table, own_table, own_scores, own_scores]
        + [jax.ShapeDtypeStruct((4, heads_all, tokens), f32)],
        in_specs=[smem] * 3 + [vmem] * 7,
        out_specs=[vmem] * 8,
        compiler_params=params,
        cost_estimate=pl.CostEstimate(
            flops=4 * tokens * tokens * width_all,
            bytes_accessed=12 * tokens * width_all,
            transcendentals=tokens * tokens * heads_all,
        ),
        name="prepare",
    )(
        lengths_held,
        slope_held,
        gain_held,
        depth_held,
        end_held,
        hold(queries[0]),
        hold(outputs[0]),
        hold(out_grads[0]),
        key_held,
        value_held,
    )

    bias_shape = (replicas, blocks, 8, WIDTH)
    matmul_flops = 2 * tokens * keys_seen * WIDTH * heads_all
    results = pl.pallas_call(
        functools.partial(main_kernel, blocks, heads_per_group, groups, shifts),
        out_shape=[jax.ShapeDtypeStruct((tokens, width_all), bf16)]
        + [jax.ShapeDtypeStruct((message_rows, WIDTH), bf16)] * blocks
        + [jax.ShapeDtypeStruct(bias_shape, f32)],
        in_specs=[smem] * 3 + [vmem] * (7 + blocks),
        out_specs=[hbm] + [vmem] * (blocks + 1),
        scratch_shapes=[
            pltpu.VMEM((groups, tokens, group_columns), bf16),
            pltpu.VMEM((keys_seen - tokens, tokens), f32),
            pltpu.VMEM((keys_seen - tokens, tokens), f32),
            pltpu.VMEM((heads_all, tokens), f32),
            pltpu.VMEM((heads_all, tokens), f32),
            pltpu.VMEM((keys_seen, WIDTH), f32),
            pltpu.VMEM((keys_seen, WIDTH), f32),
            pltpu.VMEM((2, keys_seen - tokens, 2 * tokens), f32),
            pltpu.VMEM((keys_seen, group_columns), bf16),
            pltpu.VMEM((keys_seen, group_columns), bf16),
            pltpu.SemaphoreType.DMA((groups, heads_per_group // 2)),
        ],
        compiler_params=params,
        cost_estimate=pl.CostEstimate(
            flops=5 * matmul_flops,
            bytes_accessed=10 * tokens * width_all,
            transcendentals=tokens * keys_seen * heads_all,
        ),
        name="attend",
    )(
        lengths_held,
        slope_held,
        gain_held,
        depth_held,
        query_here,
        grad_here,
        product_here,
        own_weight,
        own_dscore,
        own_rows,
        key_held,
        *arrived,
    )
    query_grads = results[0]
    parts = list(results[1 : 1 + blocks])
    bias_parts = results[1 + blocks].reshape(replicas * blocks, 8, WIDTH)
    for s in [2] + [s for s in range(1, blocks) if s != 2]:
        back = [(i, i ^ s) for i in range(blocks) if i > i ^ s]
        parts[s] = lax.ppermute(parts[s], "ctx", back)
    bias_parts = lax.all_to_all(bias_parts, ("dp", "ctx"), split_axis=0, concat_axis=0, tiled=True)

    early = [parts[0], parts[2], parts[1], *parts[3:-1]] if blocks > 3 else parts[:-1]
    parts_sum = pl.pallas_call(
        gather_parts_kernel,
        out_shape=jax.ShapeDtypeStruct((message_rows, WIDTH), f32),
        in_specs=[vmem] * len(early),
        out_specs=vmem,
        compiler_params=params,
        cost_estimate=pl.CostEstimate(
            flops=2 * message_rows * WIDTH * blocks,
            bytes_accessed=2 * message_rows * WIDTH * (blocks + 1),
            transcendentals=0,
        ),
        name="sum_parts",
    )(*early)
    key_grads, value_grads, bias_grads = pl.pallas_call(
        combine_kernel,
        out_shape=[jax.ShapeDtypeStruct((tokens, kv_width), bf16)] * 2
        + [jax.ShapeDtypeStruct((2, local_heads), f32)],
        in_specs=[vmem] * 3,
        out_specs=[vmem] * 3,
        compiler_params=params,
        name="combine",
    )(parts_sum, parts[-1], bias_parts)
    return (query_grads[None], key_grads[None], value_grads[None], bias_grads.T)


def solution(mesh):
    in_specs = (
        P("dp", "ctx", None),
        P("dp", "ctx", None),
        P("dp", "ctx", None),
        P("dp", "ctx", None),
        P("dp", "ctx", None),
        P("dp", "ctx"),
        P("dp", "ctx"),
        P("dp", None),
        P(),
        P(),
    )
    out_specs = (P("dp", "ctx", None), P("dp", "ctx", None), P("dp", "ctx", None), P("ctx", None))
    return jax.shard_map(body, mesh=mesh, in_specs=in_specs, out_specs=out_specs, check_vma=False)
```

```python
import functools

import jax
import jax.numpy as jnp
from jax import lax
from jax.experimental import pallas as pl
from jax.experimental.pallas import tpu as pltpu
from jax.sharding import PartitionSpec as P

WIDTH = 128
LOG2E = 1.4426950408889634
MASKED = -1e30
META_ROWS = 16
END_UNIT = 64


def dot_nt(a, b):
    return lax.dot_general(a, b, (((1,), (1,)), ((), ())), preferred_element_type=jnp.float32)


def dot_nn(a, b):
    return lax.dot_general(a, b, (((1,), (0,)), ((), ())), preferred_element_type=jnp.float32)


def fold_rows(block):
    return jnp.sum(block.reshape(block.shape[0] // 8, 8, block.shape[1]), axis=0)


def as_column(row):
    size = row.shape[1]
    return jnp.transpose(jnp.broadcast_to(row, (size, size)))


def pack_kernel(blocks, key_hbm, value_hbm, depth_hbm, end_hbm, message_ref, depth_ref, end_ref, sems):
    tokens, columns = key_hbm.shape
    groups = columns // WIDTH

    @pl.when(lax.axis_index("ctx") != blocks - 1)
    def _():
        copies = [
            pltpu.make_async_copy(depth_hbm, depth_ref, sems.at[0]),
            pltpu.make_async_copy(end_hbm, end_ref, sems.at[1]),
        ]
        for kind, hbm in enumerate((key_hbm, value_hbm)):
            for group in range(groups):
                index = kind * groups + group
                copies.append(
                    pltpu.make_async_copy(
                        hbm.at[:, group * WIDTH : (group + 1) * WIDTH],
                        message_ref.at[index * tokens : (index + 1) * tokens, :],
                        sems.at[2 + index],
                    )
                )
        for copy in copies:
            copy.start()
        copies[0].wait()
        copies[1].wait()
        end = end_ref[...]
        end_high = end // END_UNIT
        end_low = end - end_high * END_UNIT
        row = lax.broadcasted_iota(jnp.int32, (META_ROWS, tokens), 0)
        meta = jnp.where(row == 0, depth_ref[...], jnp.where(row == 1, end_high, end_low))
        meta = meta.astype(jnp.float32).astype(jnp.bfloat16)
        message_ref[2 * groups * tokens : 2 * groups * tokens + META_ROWS, :] = meta
        for copy in copies[2:]:
            copy.wait()


def table(lengths_ref, depth_ref, s, key_depth, key_end):
    shape = key_depth.shape
    here = lax.axis_index("ctx")
    query_pos = here * shape[1] + lax.broadcasted_iota(jnp.int32, shape, 1)
    key_pos = (here ^ s) * shape[0] + lax.broadcasted_iota(jnp.int32, shape, 0)
    start = jnp.zeros(shape, jnp.int32)
    bound = jnp.int32(0)
    for index in range(lengths_ref.shape[1]):
        bound = bound + lengths_ref[0, index]
        start = jnp.where(query_pos >= bound, bound, start)
    inside = query_pos.astype(jnp.float32) < key_end
    allowed = (key_pos <= query_pos) & (key_pos >= start)
    distance = jnp.abs(depth_ref[...].astype(jnp.float32) - key_depth)
    return distance, jnp.where(allowed, jnp.where(inside, 1.0, 0.0), MASKED)


def prepare_kernel(
    heads_per_group,
    groups,
    lengths_ref,
    slope_ref,
    gain_ref,
    depth_ref,
    end_ref,
    query_in,
    output_in,
    grad_in,
    key_ref,
    value_ref,
    query_out,
    grad_out,
    product_out,
    distance_ref,
    ancestor_ref,
    weight_ref,
    dscore_ref,
    rows_ref,
):
    tokens = query_in.shape[0]
    factor = WIDTH**-0.5
    query_out[...] = query_in[...]
    grad_out[...] = grad_in[...]
    product_out[...] = grad_in[...] * output_in[...]
    distance, ancestor = table(
        lengths_ref,
        depth_ref,
        0,
        as_column(depth_ref[...].astype(jnp.float32)),
        as_column(end_ref[...].astype(jnp.float32)),
    )
    distance_ref[...] = distance
    ancestor_ref[...] = ancestor

    @pl.loop(0, groups)
    def _(group):
        own = pl.ds(pl.multiple_of(group * WIDTH, WIDTH), WIDTH)
        key, value = key_ref[:, own], value_ref[:, own]
        value_ext = jnp.concatenate([value, jnp.full(value.shape, -1.0, jnp.bfloat16)], axis=1)
        for pair in range(heads_per_group // 2):
            first = group * heads_per_group + 2 * pair
            both = pl.ds(pl.multiple_of(first * WIDTH, 2 * WIDTH), 2 * WIDTH)

            def stack(array):
                return jnp.concatenate([array[:, 0:WIDTH], array[:, WIDTH:]], axis=0)

            grad = grad_in[:, both]
            grad_ext = jnp.concatenate([stack(grad), stack(grad * output_in[:, both])], axis=1)
            raw = dot_nt(key, stack(query_in[:, both]))
            centred = dot_nt(value_ext, grad_ext)
            for half in range(2):
                head = first + half
                gain = gain_ref[head] * LOG2E
                slope = slope_ref[head] * LOG2E
                lanes = slice(half * tokens, (half + 1) * tokens)
                distance, ancestor = distance_ref[...], ancestor_ref[...]
                score = raw[:, lanes] * (factor * LOG2E) + (gain * ancestor - slope * distance)
                top = jnp.max(score, axis=0, keepdims=True)
                weight = jnp.exp2(score - top)
                dscore = weight * centred[:, lanes]
                to = pl.ds(pl.multiple_of(head * tokens, tokens), tokens)
                weight_ref[:, to] = weight
                dscore_ref[:, to] = dscore
                at = pl.ds(head, 1)
                rows_ref[0, at, :] = top
                rows_ref[1, at, :] = jnp.sum(weight, axis=0, keepdims=True)
                rows_ref[2, at, :] = jnp.sum(dscore * distance, axis=0, keepdims=True)
                rows_ref[3, at, :] = jnp.sum(dscore * ancestor, axis=0, keepdims=True)


def main_kernel(
    blocks,
    heads_per_group,
    groups,
    shifts,
    lengths_ref,
    slope_ref,
    gain_ref,
    depth_ref,
    query_ref,
    grad_ref,
    product_ref,
    own_weight_ref,
    own_dscore_ref,
    own_rows_ref,
    key_ref,
    *refs,
):
    tokens = query_ref.shape[0]
    remote = [refs[shifts.index(s)] for s in range(1, blocks)]
    query_grad_hbm = refs[blocks - 1]
    part_refs = refs[blocks : 2 * blocks]
    bias_ref = refs[2 * blocks]
    (
        query_grad_ref,
        distance_ref,
        ancestor_ref,
        slope_rows,
        gain_rows,
        key_acc,
        value_acc,
        weight_ref,
        probs_ref,
        dscore_ref,
        store_sems,
    ) = refs[2 * blocks + 1 :]
    factor = WIDTH**-0.5
    group_columns = heads_per_group * WIDTH
    pairs = heads_per_group // 2

    def store(group):
        wide = pl.ds(pl.multiple_of(group * group_columns, group_columns), group_columns)
        return pltpu.make_async_copy(
            query_grad_ref.at[group], query_grad_hbm.at[:, wide], store_sems.at[group]
        )

    block_rows = [slice(s * tokens, (s + 1) * tokens) for s in range(blocks)]
    remote_rows = block_rows[:-1]
    below = slice(2 * groups * tokens, 2 * groups * tokens + META_ROWS)
    for s in range(1, blocks):
        meta = remote[s - 1][below, :].astype(jnp.float32)
        distance, ancestor = table(
            lengths_ref,
            depth_ref,
            s,
            as_column(meta[0:1]),
            as_column(meta[1:2] * END_UNIT + meta[2:3]),
        )
        distance_ref[remote_rows[s - 1], :] = distance
        ancestor_ref[remote_rows[s - 1], :] = ancestor

    def remote_blocks(kind, group):
        at = pl.multiple_of((kind * groups + group) * tokens, tokens)
        return jnp.concatenate([r[pl.ds(at, tokens), :] for r in remote], axis=0)

    def stacked(ref, group, first, count):
        at = pl.multiple_of(group * group_columns, group_columns) + first * WIDTH
        heads = [pl.ds(pl.multiple_of(at + i * WIDTH, WIDTH), WIDTH) for i in range(count)]
        return jnp.concatenate([ref[:, head] for head in heads], axis=0)

    def weigh(group, pair, raw, half):
        head = group * heads_per_group + 2 * pair + half
        gain = gain_ref[head] * LOG2E
        slope = slope_ref[head] * LOG2E
        lanes = slice(half * tokens, (half + 1) * tokens)
        tops, totals = [own_rows_ref[0, pl.ds(head, 1), :]], [own_rows_ref[1, pl.ds(head, 1), :]]
        for rows in remote_rows:
            score = raw[rows, lanes] * (factor * LOG2E) + (
                gain * ancestor_ref[rows, :] - slope * distance_ref[rows, :]
            )
            top = jnp.max(score, axis=0, keepdims=True)
            weight = jnp.exp2(score - top)
            weight_ref[pair % 2, rows, lanes] = weight
            tops.append(top)
            totals.append(jnp.sum(weight, axis=0, keepdims=True))
        top = functools.reduce(jnp.maximum, tops)
        shrink = [jnp.exp2(t - top) for t in tops]
        inverse = 1.0 / sum(a * b for a, b in zip(totals, shrink))
        return [s * inverse for s in shrink]

    def differentiate(group, pair, centred, scales, half):
        lanes = slice(half * tokens, (half + 1) * tokens)
        to = slice((2 * pair + half) * tokens, (2 * pair + half + 1) * tokens)
        head = group * heads_per_group + 2 * pair + half
        own = pl.ds(pl.multiple_of(head * tokens, tokens), tokens)
        own_rows = block_rows[0]
        probs_ref[own_rows, to] = (own_weight_ref[:, own] * scales[0]).astype(jnp.bfloat16)
        dscore_ref[own_rows, to] = (own_dscore_ref[:, own] * scales[0]).astype(jnp.bfloat16)
        slope_sum, gain_sum = 0.0, 0.0
        for s, rows in enumerate(remote_rows, 1):
            probs = weight_ref[pair % 2, rows, lanes] * scales[s]
            dscore = probs * centred[rows, lanes]
            probs_ref[block_rows[s], to] = probs.astype(jnp.bfloat16)
            dscore_ref[block_rows[s], to] = dscore.astype(jnp.bfloat16)
            slope_sum = slope_sum + fold_rows(dscore * distance_ref[rows, :])
            gain_sum = gain_sum + fold_rows(dscore * ancestor_ref[rows, :])
        at = pl.ds(head, 1)
        slope_rows[at, :] = -(
            jnp.sum(slope_sum, axis=0, keepdims=True) + own_rows_ref[2, at, :] * scales[0]
        )
        gain_rows[at, :] = (
            jnp.sum(gain_sum, axis=0, keepdims=True) + own_rows_ref[3, at, :] * scales[0]
        )

    def put_part(group, kind, whole):
        at = pl.multiple_of((kind * groups + group) * tokens, tokens)
        for s, rows in enumerate(block_rows):
            part_refs[s][pl.ds(at, tokens), :] = whole[rows].astype(jnp.bfloat16)

    def key_part(group, first, count):
        heads = stacked(query_ref, group, first, count)
        lanes = slice(first * tokens, (first + count) * tokens)
        return dot_nn(dscore_ref[:, lanes], heads)

    def value_part(group, first, count):
        heads = stacked(grad_ref, group, first, count)
        lanes = slice(first * tokens, (first + count) * tokens)
        return dot_nn(probs_ref[:, lanes], heads)

    def query_part(keys_across, group, pair):
        lanes = slice(2 * pair * tokens, (2 * pair + 2) * tokens)
        across = dot_nn(keys_across, dscore_ref[:, lanes]) * factor
        rows = jnp.transpose(across.astype(jnp.bfloat16))
        for half in range(2):
            at = (2 * pair + half) * WIDTH
            query_grad_ref[group, :, at : at + WIDTH] = rows[half * tokens : (half + 1) * tokens]

    @pl.loop(0, groups)
    def _(group):
        keys = remote_blocks(0, group)
        values = remote_blocks(1, group)
        value_ext = jnp.concatenate([values, jnp.full(values.shape, -1.0, jnp.bfloat16)], axis=1)
        own_key = key_ref[:, pl.ds(pl.multiple_of(group * WIDTH, WIDTH), WIDTH)]
        keys_across = jnp.transpose(jnp.concatenate([own_key, keys], axis=0))
        half_heads = heads_per_group // 2
        raws = [dot_nt(keys, stacked(query_ref, group, 0, 2))]
        for pair in range(pairs):
            grad_pair = stacked(grad_ref, group, 2 * pair, 2)
            product_pair = stacked(product_ref, group, 2 * pair, 2)
            grad_ext = jnp.concatenate([grad_pair, product_pair], axis=1)
            raw = raws.pop(0)
            if pair + 1 < pairs:
                raws.append(dot_nt(keys, stacked(query_ref, group, 2 * pair + 2, 2)))
            if pair:
                part = key_part(group, 2 * pair - 2, 2)
                key_acc[...] = part if pair == 1 else key_acc[...] + part
            scales = [weigh(group, pair, raw, half) for half in range(2)]
            if pair:
                part = value_part(group, 2 * pair - 2, 2)
                value_acc[...] = part if pair == 1 else value_acc[...] + part
            if pair:
                query_part(keys_across, group, pair - 1)
            centred = dot_nt(value_ext, grad_ext)
            for half in range(2):
                differentiate(group, pair, centred, scales[half], half)
        key_whole = key_acc[...] + key_part(group, heads_per_group - 2, 2)
        put_part(group, 0, key_whole * factor)
        put_part(group, 1, value_acc[...] + value_part(group, heads_per_group - 2, 2))
        query_part(keys_across, group, pairs - 1)
        store(group).start()

    slope_sum = jnp.sum(slope_rows[...], axis=1, keepdims=True)
    gain_sum = jnp.sum(gain_rows[...], axis=1, keepdims=True)
    shape = slope_rows.shape
    lane = lax.broadcasted_iota(jnp.int32, shape, 1)
    row = lax.broadcasted_iota(jnp.int32, shape, 0)
    replicas, parts, rows_here, local = bias_ref.shape
    local_heads = shape[0] // parts
    kind = lax.broadcasted_iota(jnp.int32, (rows_here, local), 0)
    for part in range(parts):
        mine = (lane == row - part * local_heads) & (lane < local_heads)
        slope_line = jnp.sum(jnp.where(mine, slope_sum, 0.0), axis=0, keepdims=True)
        gain_line = jnp.sum(jnp.where(mine, gain_sum, 0.0), axis=0, keepdims=True)
        tile = jnp.where(kind == 0, slope_line, jnp.where(kind == 1, gain_line, 0.0))
        bias_ref[:, part] = jnp.broadcast_to(tile[None], (replicas, rows_here, local))
    for group in range(groups):
        store(group).wait()


def gather_parts_kernel(*refs):
    total = refs[0][...].astype(jnp.float32)
    for part in refs[1:-1]:
        total = total + part[...].astype(jnp.float32)
    refs[-1][...] = total


def combine_kernel(sum_ref, part_ref, bias_parts, key_out, value_out, bias_out):
    tokens = key_out.shape[0]
    groups = key_out.shape[1] // WIDTH
    for kind, out in enumerate((key_out, value_out)):
        for group in range(groups):
            at = (kind * groups + group) * tokens
            rows = slice(at, at + tokens)
            total = sum_ref[rows, :] + part_ref[rows, :].astype(jnp.float32)
            out[:, group * WIDTH : (group + 1) * WIDTH] = total.astype(jnp.bfloat16)
    bias_out[...] = jnp.sum(bias_parts[...], axis=0)[0:2, 0 : bias_out.shape[1]]


def body(
    queries,
    key_rows,
    values,
    outputs,
    out_grads,
    depths,
    subtree_end,
    file_lengths,
    slopes,
    ancestor_gain,
):
    blocks = lax.axis_size("ctx")
    replicas = lax.axis_size("dp")
    tokens, width_all = queries.shape[1:]
    kv_width = key_rows.shape[2]
    heads_all = width_all // WIDTH
    groups = kv_width // WIDTH
    heads_per_group = heads_all // groups
    group_columns = heads_per_group * WIDTH
    local_heads = heads_all // blocks
    keys_seen = blocks * tokens
    bf16, f32 = jnp.bfloat16, jnp.float32
    vmem = pl.BlockSpec(memory_space=pltpu.VMEM)
    smem = pl.BlockSpec(memory_space=pltpu.SMEM)
    hbm = pl.BlockSpec(memory_space=pltpu.HBM)
    params = pltpu.CompilerParams(vmem_limit_bytes=(24 if blocks <= 4 else 44) * 1024 * 1024)

    def hold(array):
        return pltpu.with_memory_space_constraint(array, pltpu.HBM)

    key_held, value_held = hold(key_rows[0]), hold(values[0])
    depth_held, end_held = hold(depths), hold(subtree_end)
    message_rows = 2 * groups * tokens
    message = pl.pallas_call(
        functools.partial(pack_kernel, blocks),
        out_shape=jax.ShapeDtypeStruct((message_rows + META_ROWS, WIDTH), bf16),
        in_specs=[hbm] * 4,
        out_specs=vmem,
        scratch_shapes=[
            pltpu.VMEM((1, tokens), jnp.int32),
            pltpu.VMEM((1, tokens), jnp.int32),
            pltpu.SemaphoreType.DMA((2 + 2 * groups,)),
        ],
        compiler_params=params,
        name="pack",
    )(key_held, value_held, depth_held, end_held)
    shifts = list(range(1, blocks))
    arrived = [
        lax.ppermute(message, "ctx", [(i, i ^ s) for i in range(blocks) if i < i ^ s])
        for s in shifts
    ]

    lengths_held, slope_held, gain_held = hold(file_lengths), hold(slopes), hold(ancestor_gain)
    own_table = jax.ShapeDtypeStruct((tokens, tokens), f32)
    own_scores = jax.ShapeDtypeStruct((tokens, heads_all * tokens), f32)
    query_here, grad_here, product_here, _, _, own_weight, own_dscore, own_rows = pl.pallas_call(
        functools.partial(prepare_kernel, heads_per_group, groups),
        out_shape=[jax.ShapeDtypeStruct((tokens, width_all), bf16)] * 3
        + [own_table, own_table, own_scores, own_scores]
        + [jax.ShapeDtypeStruct((4, heads_all, tokens), f32)],
        in_specs=[smem] * 3 + [vmem] * 7,
        out_specs=[vmem] * 8,
        compiler_params=params,
        cost_estimate=pl.CostEstimate(
            flops=4 * tokens * tokens * width_all,
            bytes_accessed=12 * tokens * width_all,
            transcendentals=tokens * tokens * heads_all,
        ),
        name="prepare",
    )(
        lengths_held,
        slope_held,
        gain_held,
        depth_held,
        end_held,
        hold(queries[0]),
        hold(outputs[0]),
        hold(out_grads[0]),
        key_held,
        value_held,
    )

    bias_shape = (replicas, blocks, 8, WIDTH)
    matmul_flops = 2 * tokens * keys_seen * WIDTH * heads_all
    results = pl.pallas_call(
        functools.partial(main_kernel, blocks, heads_per_group, groups, shifts),
        out_shape=[jax.ShapeDtypeStruct((tokens, width_all), bf16)]
        + [jax.ShapeDtypeStruct((message_rows, WIDTH), bf16)] * blocks
        + [jax.ShapeDtypeStruct(bias_shape, f32)],
        in_specs=[smem] * 3 + [vmem] * (7 + blocks),
        out_specs=[hbm] + [vmem] * (blocks + 1),
        scratch_shapes=[
            pltpu.VMEM((groups, tokens, group_columns), bf16),
            pltpu.VMEM((keys_seen - tokens, tokens), f32),
            pltpu.VMEM((keys_seen - tokens, tokens), f32),
            pltpu.VMEM((heads_all, tokens), f32),
            pltpu.VMEM((heads_all, tokens), f32),
            pltpu.VMEM((keys_seen, WIDTH), f32),
            pltpu.VMEM((keys_seen, WIDTH), f32),
            pltpu.VMEM((2, keys_seen - tokens, 2 * tokens), f32),
            pltpu.VMEM((keys_seen, group_columns), bf16),
            pltpu.VMEM((keys_seen, group_columns), bf16),
            pltpu.SemaphoreType.DMA((groups,)),
        ],
        compiler_params=params,
        cost_estimate=pl.CostEstimate(
            flops=5 * matmul_flops,
            bytes_accessed=10 * tokens * width_all,
            transcendentals=tokens * keys_seen * heads_all,
        ),
        name="attend",
    )(
        lengths_held,
        slope_held,
        gain_held,
        depth_held,
        query_here,
        grad_here,
        product_here,
        own_weight,
        own_dscore,
        own_rows,
        key_held,
        *arrived,
    )
    query_grads = results[0]
    parts = list(results[1 : 1 + blocks])
    bias_parts = results[1 + blocks].reshape(replicas * blocks, 8, WIDTH)
    for s in [2] + [s for s in range(1, blocks) if s != 2]:
        back = [(i, i ^ s) for i in range(blocks) if i > i ^ s]
        parts[s] = lax.ppermute(parts[s], "ctx", back)
    bias_parts = lax.all_to_all(bias_parts, ("dp", "ctx"), split_axis=0, concat_axis=0, tiled=True)

    early = [parts[0], parts[2], parts[1], *parts[3:-1]] if blocks > 3 else parts[:-1]
    parts_sum = pl.pallas_call(
        gather_parts_kernel,
        out_shape=jax.ShapeDtypeStruct((message_rows, WIDTH), f32),
        in_specs=[vmem] * len(early),
        out_specs=vmem,
        compiler_params=params,
        cost_estimate=pl.CostEstimate(
            flops=2 * message_rows * WIDTH * blocks,
            bytes_accessed=2 * message_rows * WIDTH * (blocks + 1),
            transcendentals=0,
        ),
        name="sum_parts",
    )(*early)
    key_grads, value_grads, bias_grads = pl.pallas_call(
        combine_kernel,
        out_shape=[jax.ShapeDtypeStruct((tokens, kv_width), bf16)] * 2
        + [jax.ShapeDtypeStruct((2, local_heads), f32)],
        in_specs=[vmem] * 3,
        out_specs=[vmem] * 3,
        compiler_params=params,
        name="combine",
    )(parts_sum, parts[-1], bias_parts)
    return (query_grads[None], key_grads[None], value_grads[None], bias_grads.T)


def solution(mesh):
    in_specs = (
        P("dp", "ctx", None),
        P("dp", "ctx", None),
        P("dp", "ctx", None),
        P("dp", "ctx", None),
        P("dp", "ctx", None),
        P("dp", "ctx"),
        P("dp", "ctx"),
        P("dp", None),
        P(),
        P(),
    )
    out_specs = (P("dp", "ctx", None), P("dp", "ctx", None), P("dp", "ctx", None), P("ctx", None))
    return jax.shard_map(body, mesh=mesh, in_specs=in_specs, out_specs=out_specs, check_vma=False)
```
